32 devices in a mesh: gx: 8 (over z, x), gy: 4 (over y, core).
Axes of the slice: x: 2, y: 2, z: 4, core: 2. Of those that a mesh axis runs over, the one named last changes fastest.
Arguments:
- trans: float32 [13, 16, 4096], P(None, 'gx', 'gy'), may hold values from 0.1 to 1
- storage: float32 [16, 4096], P('gx', 'gy'), may hold values from 0.05 to 1
- fault_cells: int32 [8, 4, 512], P('gx', 'gy'), may hold values from 0 to 2047, as said below
- fault_count: int32 [8, 4], P('gx', 'gy'), may hold values from 0 to 512, as said below
- fault_trans: float32 [8, 4, 512], P('gx', 'gy'), may hold values from 0.1 to 1, as said below
Outputs:
- coarse_columns: float32 [125, 8, 1024], P(None, 'gx', 'gy')
The draws below stay inside these ranges and needn't reach their ends.
Inputs may be any that keep to these rules, and one draw needn't show every extreme that they name: `fault_cells`: on a device with even gx index every slot's cell lies at x' = 1, on one with odd gx index at x' = 0; slot k of the partners with gx indices 2j and 2j + 1 (same gy index) has equal y' and layers z differing by at most 8. `fault_count`: equal on devices whose gx indices are 2j and 2j + 1 with the same gy index; some device has 512. `fault_trans`: equal slot by slot on devices whose gx indices are 2j and 2j + 1 with the same gy index.
All inputs are finite; a program needn't handle non-finite values.
Results may differ from the reference program's by a relative error of at most 0.0003.
Values sent between devices are 32-bit elements; how exact they have to be, the bound alone decides.
No kernel may reach another device: no remote copies, remote signals or barrier semaphores. Data moves between devices by JAX's collectives and lax.ppermute only.
A program may use at most 64 MiB of HBM per device.

```python
import math
import jax
import jax.numpy as jnp
from jax import lax

CX = 2
CY = 8
NZ = 128
FMAX = 512
COLORS = 125
NX = 16
NY = 32
GX_HALF = 4
GY_COUNT = 4
N_GX = 8
N_GY = 4


def draw_fault_cells(key, part):
    base = jax.random.fold_in(key, 5)
    shape = (GX_HALF, GY_COUNT, FMAX)
    column = jax.random.randint(jax.random.fold_in(base, 1), shape, 0, CY)
    depth = jax.random.randint(jax.random.fold_in(base, 2), shape, 0, NZ)
    throw = jax.random.randint(jax.random.fold_in(base, 3), shape, -8, 9)
    facing = jnp.clip(depth + throw, 0, NZ - 1)
    lower = ((CX - 1) * CY + column) * NZ + depth
    upper = column * NZ + facing
    joined = jnp.stack([lower, upper], axis=1)
    return joined.reshape(2 * GX_HALF, GY_COUNT, FMAX).astype(jnp.int32)


def draw_fault_count(key, part):
    level = jax.random.randint(key, (GX_HALF, GY_COUNT), 0, 8)
    base = FMAX * (1 + level * level) // 50
    base = base.at[0, 0].set(FMAX)
    return jnp.repeat(base, 2, axis=0).astype(jnp.int32)


def draw_fault_trans(key, part):
    spread = jax.random.uniform(jax.random.fold_in(key, 17), (GX_HALF, GY_COUNT, FMAX), jnp.float32)
    base = jnp.exp(jnp.log(0.1) + jnp.log(10.0) * spread)
    base = jnp.clip(base, 0.1, 1.0)
    return jnp.repeat(base, 2, axis=0).astype(jnp.float32)


def level_of(rng, dims, cuts, smallest, top_value):
    def one(position, shards_of):
        heights = jax.random.uniform(jax.random.fold_in(jax.random.fold_in(rng, 6), position), (shards_of,), jnp.float32, smallest / len(cuts), top_value / len(cuts))
        return jnp.repeat(jnp.exp(heights), dims[position] // shards_of).reshape((-1,) + (1,) * (len(dims) - position - 1))

    loudness = one(*cuts[0])
    for cut in cuts[1:]:
        loudness = loudness * one(*cut)
    return loudness


def setup_inputs(seed: int = 0) -> dict:
    arg_keys = jax.random.split(jax.random.key(seed), 6)
    return {
        "trans": jnp.clip(jnp.exp(math.log(1.0) - 2.3025851 * jax.random.uniform(arg_keys[0], (13, NX, NY * NZ), jnp.float32) ** level_of(arg_keys[0], (13, NX, NY * NZ), ((1, 8), (2, 4)), -0.2, 0.2)), 0.1, 1.0),
        "storage": jnp.clip(jnp.exp(math.log(1.0) - 2.9957323 * jax.random.uniform(arg_keys[1], (NX, NY * NZ), jnp.float32) ** level_of(arg_keys[1], (NX, NY * NZ), ((0, 8), (1, 4)), -0.2, 0.2)), 0.05, 1.0),
        "fault_cells": draw_fault_cells(jax.random.fold_in(arg_keys[5], 71), 0),
        "fault_count": draw_fault_count(jax.random.fold_in(arg_keys[5], 71), 0),
        "fault_trans": draw_fault_trans(jax.random.fold_in(arg_keys[5], 71), 0),
    }


FORWARD = ((0, 0, 1), (0, 1, -1), (0, 1, 0), (0, 1, 1), (1, -1, -1), (1, -1, 0), (1, -1, 1), (1, 0, -1), (1, 0, 0), (1, 0, 1), (1, 1, -1), (1, 1, 0), (1, 1, 1))
damping = 2.0 / 3.0
tentative_value = 0.35355339059327373


def shifted(padded, step_x, step_y, step_z, size_x, size_y, size_z):
    return padded[..., 1 + step_x:1 + step_x + size_x, 1 + step_y:1 + step_y + size_y, 1 + step_z:1 + step_z + size_z]


def global_index(local_cells, grid_y, layers):
    device_x = jnp.arange(N_GX, dtype=jnp.int32)[:, None, None]
    device_y = jnp.arange(N_GY, dtype=jnp.int32)[None, :, None]
    place_x = device_x * CX + local_cells // (CY * NZ)
    place_y = device_y * CY + (local_cells // NZ) % CY
    place_z = local_cells % NZ
    return ((place_x * grid_y + place_y) * layers + place_z).astype(jnp.int32)


def reference(trans, storage, fault_cells, fault_count, fault_trans):
    layers = NZ
    grid_x = storage.shape[0]
    grid_y = storage.shape[1] // layers
    cell_count = grid_x * grid_y * layers
    coord_x = jnp.arange(grid_x, dtype=jnp.int32)[:, None, None]
    coord_y = jnp.arange(grid_y, dtype=jnp.int32)[None, :, None]
    coord_z = jnp.arange(layers, dtype=jnp.int32)[None, None, :]
    weights = trans.reshape(13, grid_x, grid_y, layers)
    pieces = []
    for offset, step in enumerate(FORWARD):
        inside = (coord_x + step[0] >= 0) & (coord_x + step[0] < grid_x) & (coord_y + step[1] >= 0) & (coord_y + step[1] < grid_y) & (coord_z + step[2] >= 0) & (coord_z + step[2] < layers)
        pieces.append(jnp.where(inside, weights[offset], jnp.float32(0.0)))
    masked = jnp.stack(pieces)
    widened = jnp.pad(masked, ((0, 0), (1, 1), (1, 1), (1, 1)))
    behind_sum = jnp.zeros((grid_x, grid_y, layers), jnp.float32)
    for offset, step in enumerate(FORWARD):
        behind_sum = behind_sum + shifted(widened[offset], -step[0], -step[1], -step[2], grid_x, grid_y, layers)
    slots = jnp.arange(FMAX, dtype=jnp.int32)[None, None, :]
    live_trans = jnp.where(slots < fault_count[:, :, None], fault_trans, jnp.float32(0.0))
    own_grid = global_index(fault_cells, grid_y, layers)
    own_index = own_grid.reshape(-1)
    partner_index = jnp.flip(own_grid.reshape(GX_HALF, 2, N_GY, FMAX), axis=1).reshape(-1).astype(jnp.int32)
    live_flat = live_trans.reshape(-1)
    fault_diag = jnp.zeros((cell_count,), jnp.float32).at[own_index].add(live_flat).reshape(grid_x, grid_y, layers)
    diagonal = storage.reshape(grid_x, grid_y, layers) + jnp.sum(masked, 0) + behind_sum + fault_diag

    def apply_operator(field):
        padded = jnp.pad(field, 1)
        summed = diagonal * field
        for offset, step in enumerate(FORWARD):
            summed = summed - masked[offset] * shifted(padded, step[0], step[1], step[2], grid_x, grid_y, layers) - shifted(widened[offset], -step[0], -step[1], -step[2], grid_x, grid_y, layers) * shifted(padded, -step[0], -step[1], -step[2], grid_x, grid_y, layers)
        across = jnp.zeros((cell_count,), jnp.float32).at[own_index].add(live_flat * field.reshape(-1)[partner_index])
        return summed - across.reshape(grid_x, grid_y, layers)

    def one_colour(colour):
        agrees = ((coord_x // 2) % 5 == colour // 25) & ((coord_y // 2) % 5 == (colour // 5) % 5) & ((coord_z // 2) % 5 == colour % 5)
        probes = jnp.where(agrees, jnp.float32(tentative_value), jnp.float32(0.0))
        first = apply_operator(probes)
        smoothed = probes - damping * first / diagonal
        applied = apply_operator(smoothed)
        scaled = applied / diagonal
        result = applied - damping * apply_operator(scaled)
        coarse = result.reshape(grid_x // 2, 2, grid_y // 2, 2, layers // 2, 2).sum((1, 3, 5))
        return (tentative_value * coarse).reshape(grid_x // 2, (grid_y // 2) * (layers // 2))

    return lax.map(one_colour, jnp.arange(COLORS, dtype=jnp.int32))
```

```python
import functools

import jax
import jax.numpy as jnp
from jax import lax
from jax.experimental import pallas as pl
from jax.experimental.pallas import tpu as pltpu
from jax.sharding import PartitionSpec as P

NZ = 128
CY = 8
SLOTS = 512

FORWARD = (
    (0, 0, 1),
    (0, 1, -1),
    (0, 1, 0),
    (0, 1, 1),
    (1, -1, -1),
    (1, -1, 0),
    (1, -1, 1),
    (1, 0, -1),
    (1, 0, 0),
    (1, 0, 1),
    (1, 1, -1),
    (1, 1, 0),
    (1, 1, 1),
)
OFFSET = {step: k for k, step in enumerate(FORWARD)}
damping = 2.0 / 3.0

ROWS = 24
PER = 14
COLBLOCK = 93
FAULT_ROW = 280
YROWS = 320

f32 = jnp.float32
bf16 = jnp.bfloat16


def dot_nt(a, b):
    return lax.dot_general(a, b, (((1,), (1,)), ((), ())), preferred_element_type=f32)


def dot_nn(a, b):
    return lax.dot_general(a, b, (((1,), (0,)), ((), ())), preferred_element_type=f32)


def split(value):
    high = value.astype(bf16)
    return high, (value - high.astype(f32)).astype(bf16)


def pack_kernel(peers, trans, storage, cells, count, ftrans, block, plane, far_cells):
    last_x = lax.axis_index("gx") == peers[0] - 1
    first_y = lax.axis_index("gy") == 0
    last_y = lax.axis_index("gy") == peers[1] - 1
    depth = lax.broadcasted_iota(jnp.int32, (8, NZ), 1)
    row = lax.broadcasted_iota(jnp.int32, (8, NZ), 0)
    for x in range(2):
        for o in range(PER):
            base = (x * PER + o) * 8
            for y in range(CY):
                lanes = slice(y * NZ, (y + 1) * NZ)
                if o < 13:
                    value = trans[o, x : x + 1, lanes]
                else:
                    value = storage[x : x + 1, lanes]
                block[base + y : base + y + 1, :] = value
            if o == 13:
                continue
            step = FORWARD[o]
            keep = None
            if step[2] == 1:
                keep = depth < NZ - 1
            if step[2] == -1:
                keep = depth > 0
            if step[1] == 1:
                inside = (row < CY - 1) | jnp.logical_not(last_y)
                keep = inside if keep is None else keep & inside
            if step[1] == -1:
                inside = (row > 0) | jnp.logical_not(first_y)
                keep = inside if keep is None else keep & inside
            if step[0] == 1 and x == 1:
                inside = (row >= 0) & jnp.logical_not(last_x)
                keep = inside if keep is None else keep & inside
            if keep is not None:
                block[base : base + 8, :] = jnp.where(keep, block[base : base + 8, :], 0.0)
    live = count[0, 0]
    lane = lax.broadcasted_iota(jnp.int32, (1, NZ), 1)
    base = 2 * PER * 8
    for r in range(4):
        lanes = slice(r * NZ, (r + 1) * NZ)
        block[base + r : base + r + 1, :] = cells[0, :, lanes].astype(f32)
        block[base + 4 + r : base + 5 + r, :] = jnp.where(
            lane + r * NZ < live, ftrans[0, :, lanes], 0.0
        )
    plane[0:72, :] = block[(PER + 4) * 8 : (PER + 13) * 8, :]
    plane[72:80, :] = block[base : base + 8, :]
    far_cells[...] = block[base : base + 8, :]


def column_kernel(own, lo, hi, lo2, hi2, up, down):
    for out, first in ((up, CY - 3), (down, 0)):
        for c in range(3):
            y = first + c
            base = c * COLBLOCK
            out[base : base + 9, :] = lo2[pl.ds(y, 9, stride=8), :]
            for k, ref in enumerate((lo, own, hi)):
                start = base + 9 + 28 * k
                out[start : start + 28, :] = ref[pl.ds(y, 28, stride=8), :]
        for k, (ref, start) in enumerate(((own, 224), (lo, 224), (hi, 224), (lo2, 72), (hi2, 0))):
            out[FAULT_ROW + 8 * k : FAULT_ROW + 8 * k + 8, :] = ref[start : start + 8, :]


def lists_of(even, read):
    own, lo, hi, lo2, hi2 = (read(k) for k in range(5))
    partner = jnp.where(even, hi, lo)
    other = jnp.where(even, lo, hi)
    beyond = jnp.where(even, lo2, hi2)

    def flat(tile, start):
        return jnp.concatenate([tile[start + r : start + r + 1, :] for r in range(4)], axis=1)

    def whole(tile):
        return flat(tile, 0).astype(jnp.int32)

    return (whole(own), whole(partner), flat(own, 4)), (whole(other), whole(beyond), flat(other, 4))


def main_kernel(
    peers,
    own,
    lo,
    hi,
    lo2,
    hi2,
    yl,
    yh,
    out,
    w,
    wr,
    qc,
    inv,
    diag,
    fd,
    rf,
    qe,
    ap,
    tt,
    fh,
    fl,
):
    gx = lax.axis_index("gx")
    gy = lax.axis_index("gy")
    par = lax.rem(gx, 2)
    even = par == 0
    sgn = 1 - 2 * par
    p_own = jnp.where(even, 3, 2)
    p_far = jnp.where(even, 4, 1)
    p_third = jnp.where(even, 0, 5)

    def place(ref, count, first):
        for k in range(count):
            base = (first + k) * ROWS
            w[base + 3 : base + 11, :] = ref[8 * k : 8 * k + 8, :]

    place(lo2, 9, 4)
    for k, ref in enumerate((lo, own, hi)):
        place(ref, 28, PER * (1 + 2 * k))
    for ref, row in ((yl, 0), (yh, 11)):
        for c in range(3):
            base = c * COLBLOCK
            w[pl.ds(4 * ROWS + row + c, 9, stride=ROWS), :] = ref[base : base + 9, :]
            w[pl.ds(PER * ROWS + row + c, 84, stride=ROWS), :] = ref[base + 9 : base + 93, :]
    for p in range(7):
        for o, step in enumerate(FORWARD):
            if step[2] == 0 or (p == 0 and o < 4):
                continue
            base = (p * PER + o) * ROWS
            shift = 1 if step[2] == 1 else NZ - 1
            wr[base : base + ROWS, :] = pltpu.roll(w[base : base + ROWS, :], shift, 1)

    z128 = lax.broadcasted_iota(jnp.int32, (NZ, SLOTS), 0)
    z8 = lax.broadcasted_iota(jnp.int32, (8, NZ), 1)
    e8 = lax.broadcasted_iota(jnp.int32, (8, NZ), 0)

    def colour(z):
        half = z >> 1
        return half - 5 * ((half * 205) >> 10)

    one_all = jnp.where((e8 == colour(z8)) | (e8 == 5), 1.0, 0.0).astype(bf16)
    es = lax.broadcasted_iota(jnp.int32, (8, SLOTS), 0)

    fd[...] = jnp.zeros_like(fd)

    def prepare(lists):
        (c_own, c_far, live), (c_other, c_beyond, live_o) = lists
        live_h = live.astype(bf16).astype(f32)
        live_l = live - live_h
        match = (c_far & 127) == z128
        far2 = jnp.concatenate(
            [jnp.where(match, live_h, 0.0), jnp.where(match, live_l, 0.0)], axis=0
        ).astype(bf16)
        lo_h = live_o.astype(bf16).astype(f32)
        lo_l = live_o - lo_h
        same = (es == colour(c_beyond & 127)) | (es == 5)
        other2 = jnp.concatenate(
            [jnp.where(same, lo_h, 0.0), jnp.where(same, lo_l, 0.0)], axis=0
        ).astype(bf16)
        return c_own & 1023, far2, c_other & 1023, other2

    def build(column, y, ready):
        at_own, far2, at_other, other2 = ready
        hot = jnp.where(at_own == z128 + y * NZ, 1.0, 0.0).astype(bf16)
        both = dot_nt(hot, far2)
        f_h, f_l = split(both[:, :NZ] + both[:, NZ:])
        fh[column] = f_h
        fl[column] = f_l
        to_own = dot_nt(one_all, f_h) + dot_nt(one_all, f_l)
        to_far = dot_nn(one_all, f_h) + dot_nn(one_all, f_l)
        hot_o = jnp.where(at_other == z128 + y * NZ, 1.0, 0.0).astype(bf16)
        pieces = dot_nt(other2, hot_o)
        to_third = pieces[:8] + pieces[8:]
        for k, (plane, value) in enumerate(((p_own, to_own), (p_far, to_far), (p_third, to_third))):
            rf[k, column] = value
            fd[pl.ds(plane * 16 + column, 1), :] = value[5:6, :]

    tiles = ((own, 224), (lo, 224), (hi, 224), (lo2, 72), (hi2, 0))
    ready = prepare(lists_of(even, lambda k: tiles[k][0][tiles[k][1] : tiles[k][1] + 8, :]))

    def build_own(y, carry):
        build(y + 2, y, ready)
        return carry

    lax.fori_loop(0, CY, build_own, 0)
    for ref, columns in ((yl, ((0, 6), (1, 7))), (yh, ((10, 0), (11, 1)))):
        ready_y = prepare(
            lists_of(even, lambda k: ref[FAULT_ROW + 8 * k : FAULT_ROW + 8 * k + 8, :])
        )
        for column, y in columns:
            build(column, y, ready_y)

    r16 = lax.broadcasted_iota(jnp.int32, (16, NZ), 0)
    z16 = lax.broadcasted_iota(jnp.int32, (16, NZ), 1)
    even_y = (r16 & 1) == 0
    even_z = (z16 & 1) == 0
    for p in range(6):
        base = p + 1

        def weight(dx, dy, dz):
            if (dx, dy, dz) in OFFSET:
                start = (base * PER + OFFSET[dx, dy, dz]) * ROWS + 1
                return w[start : start + 16, :]
            o = OFFSET[-dx, -dy, -dz]
            start = ((base + dx) * PER + o) * ROWS + 1 + dy
            return (w if dz == 0 else wr)[start : start + 16, :]

        near = 1 if p % 2 == 0 else -1
        sums = {}
        for dz in (-1, 0, 1):
            got = {}
            for dx in (-1, 0, 1):
                below, above = weight(dx, -1, dz), weight(dx, 1, dz)
                got[dx, 0] = jnp.where(even_y, above, below)
                if (dx, dz) != (0, 0):
                    got[dx, 0] = got[dx, 0] + weight(dx, 0, dz)
                got[dx, 1] = jnp.where(even_y, below, above)
            for sy in range(2):
                sums[0, sy, dz] = got[0, sy] + got[near, sy]
                sums[1, sy, dz] = got[-near, sy]
        total = w[(base * PER + 13) * ROWS + 1 : (base * PER + 13) * ROWS + 17, :]
        total = total + fd[p * 16 : p * 16 + 16, :]
        r = []
        for sx in range(2):
            for sy in range(2):
                down, same, up = (sums[sx, sy, dz] for dz in (-1, 0, 1))
                r.append(same + jnp.where(even_z, up, down))
                r.append(jnp.where(even_z, down, up))
        for value in r:
            total = total + value
        total = jnp.where(total == 0.0, 1.0, total)
        scale = damping / total
        diag[p * 16 : p * 16 + 16, :] = total
        inv[p * 16 : p * 16 + 16, :] = scale
        for k, value in enumerate(r):
            value = value * scale
            if k == 0:
                value = value + (1.0 - damping)
            qc[(p * 8 + k) * 16 : (p * 8 + k) * 16 + 16, :] = value

    beside = jnp.where((z8 & 1) == 0, z8 - 1, z8 + 1)
    mask_own = jnp.where(e8 == colour(z8), 1.0, 0.0)
    mask_oth = jnp.where(e8 == colour(beside + 10), 1.0, 0.0)
    rows5 = jnp.where(e8 < 5, 1.0, 0.0)

    def spread(c, carry):
        for p in range(6):
            for lat in range(4):
                at = (p * 8 + 2 * lat) * 16 + c
                qe[p, c, lat] = (
                    qc[pl.ds(at, 1), :] * mask_own + qc[pl.ds(at + 16, 1), :] * mask_oth
                )
        for k, plane in enumerate((p_own, p_far, p_third)):
            qe[plane, c, 2] = qe[plane, c, 2] + rf[k, c] * (
                inv[pl.ds(plane * 16 + c, 1), :] * rows5
            )
        return carry

    lax.fori_loop(0, 12, spread, 0)

    def apply_column(p, y, odd_y):
        odd_x = p % 2
        acc = {}
        for dx in (-1, 0, 1):
            for dy in (-1, 0, 1):
                q = [qe[p + dx, y + dy, lat] for lat in range(4)]
                own_x = dx if (dx == 1 and odd_x) or (dx == -1 and not odd_x) else 0
                own_y = dy if (dy == 1 and odd_y) or (dy == -1 and not odd_y) else 0
                oth_x = own_x + (1 if (p + dx) % 2 else -1)
                oth_y = own_y + (1 if (odd_y + dy) % 2 else -1)
                for dz in (-1, 0, 1):
                    if (dx, dy, dz) == (0, 0, 0):
                        continue
                    if (dx, dy, dz) in OFFSET:
                        at = ((p + 1) * PER + OFFSET[dx, dy, dz]) * ROWS + y + 1
                        ref = w if dz == 0 else wr
                    else:
                        at = ((p + 1 + dx) * PER + OFFSET[-dx, -dy, -dz]) * ROWS + y + 1 + dy
                        ref = w
                    wt = ref[pl.ds(at, 1), :]
                    for lat in range(4):
                        lx = oth_x if lat >= 2 else own_x
                        ly = oth_y if lat % 2 else own_y
                        value = wt * q[lat]
                        key = (lx, ly, dz)
                        acc[key] = acc[key] + value if key in acc else value
        centre = diag[pl.ds(p * 16 + y, 1), :]
        for lx in (-1, 0, 1):
            for ly in (-1, 0, 1):
                total = acc[lx, ly, 0]
                total = total + pltpu.roll(acc[lx, ly, 1], NZ - 1, 1)
                total = total + pltpu.roll(acc[lx, ly, -1], 1, 1)
                own_lat = None
                sx = {0: 0, (1 if odd_x else -1): 1}.get(lx)
                sy = {0: 0, (1 if odd_y else -1): 1}.get(ly)
                if sx is not None and sy is not None:
                    own_lat = 2 * sx + sy
                if own_lat is None:
                    total = -total
                else:
                    total = centre * qe[p, y, own_lat] - total
                ap[p - 1, y - 1, lx + 1, ly + 1] = total

    def apply_pair(k, carry):
        for p in range(1, 5):
            apply_column(p, 2 * k + 1, 1)
            apply_column(p, 2 * k + 2, 0)
        return carry

    lax.fori_loop(0, 5, apply_pair, 0)

    def fault_apply(c, carry):
        both = jnp.concatenate([fh[c], fl[c]], axis=0)
        ly_oth = 2 * lax.rem(c, 2)
        for plane, source, x_own, forward in (
            (p_own, p_far, 1 + sgn, True),
            (p_far, p_own, 1 - sgn, False),
        ):
            high, low = split(qe[source, c].reshape(32, NZ))
            if forward:
                got = dot_nt(jnp.concatenate([high, low], axis=0), both)
                total = got[:32, :NZ] + got[:32, NZ:] + got[32:, :NZ]
            else:
                total = dot_nn(high, fh[c]) + dot_nn(high, fl[c]) + dot_nn(low, fh[c])
            for lat in range(4):
                lx = 1 if lat >= 2 else x_own
                ly = ly_oth if lat % 2 else 1
                ap[plane - 1, c - 1, lx, ly] = ap[plane - 1, c - 1, lx, ly] - total[8 * lat : 8 * lat + 8]
        return carry

    lax.fori_loop(1, 11, fault_apply, 0)

    x_coarse = lax.rem(gx, 5) + 5
    a_of = [lax.rem(x_coarse + d, 5) for d in range(-2, 3)]

    def b_of(coarse_y, d):
        return lax.rem(gy * (CY // 2) + coarse_y + d + 5, 5)

    def gather(pair, carry):
        for half in range(2):
            coarse_y = 2 * pair + half
            columns = []
            for x in range(-1, 3):
                for y in range(-1, 3):
                    sx = 0 if x in (0, 1) else 1
                    sy = 0 if y in (0, 1) else 1
                    columns.append((x, y, 2 * sx + sy, (-1, 0, 0, 1)[x + 1], (-1, 0, 0, 1)[y + 1]))
            for zk in range(2):
                acc = {}
                for x, y, lat, ax, ay in columns:
                    c = 2 * coarse_y + y + 2
                    q = qc[pl.ds(((x + 2) * 8 + 2 * lat + zk) * 16 + c, 1), :]
                    for lx in range(3):
                        for ly in range(3):
                            value = q * ap[x + 1, c - 1, lx, ly]
                            key = (ax + lx - 1, ay + ly - 1)
                            acc[key] = acc[key] + value if key in acc else value
                lane = half * 256 + zk * NZ
                for (dx, dy), value in acc.items():
                    tt[pair, a_of[dx + 2], b_of(coarse_y, dy), :, lane : lane + NZ] = value
        return carry

    lax.fori_loop(0, 2, gather, 0)

    for y in range(CY):
        c = y + 2
        coarse_y = y // 2
        lane = (coarse_y % 2) * 256
        both = jnp.concatenate([fh[c], fl[c]], axis=0)
        value = ap[p_far - 1, c - 1].reshape(72, NZ) * inv[pl.ds(p_far * 16 + c, 1), :]
        high, low = split(value)

        def add(total):
            for lx in range(3):
                a = lax.rem(x_coarse + lx - 1 + sgn, 5)
                for ly in range(3):
                    b = b_of(coarse_y, ly - 1)
                    at = 8 * (3 * lx + ly)
                    place_at = tt.at[coarse_y // 2, a, b, :, lane : lane + NZ]
                    place_at[...] = place_at[...] + total[at : at + 8]

        got = dot_nt(jnp.concatenate([high, low], axis=0), both)
        add(got[:72, :NZ] + got[:72, NZ:] + got[72:, :NZ])

    kz = lax.broadcasted_iota(jnp.int32, (512, NZ), 0)
    kout = lax.broadcasted_iota(jnp.int32, (512, NZ), 1)
    z_in = kz & 127
    is_oth = ((kz >> 7) & 1) == 1
    target = jnp.where(
        is_oth, (z_in >> 1) + jnp.where((z_in & 1) == 0, -1, 1), z_in >> 1
    )
    fits = (target == (kout & 63)) & ((kz >> 8) == (kout >> 6))
    collect = jnp.where(fits, 1.0, 0.0).astype(bf16)
    for pair in range(2):
        high, low = split(tt[pair].reshape(200, 512))
        got = (dot_nn(high, collect) + dot_nn(low, collect)) * 0.125
        for k in range(25):
            out[5 * k : 5 * k + 5, 0, pair * NZ : (pair + 1) * NZ] = got[8 * k : 8 * k + 5]


def shift(value, axis, distance):
    peers = lax.axis_size(axis)
    pairs = [(i, i + distance) for i in range(peers) if 0 <= i + distance < peers]
    return lax.ppermute(value, axis, pairs)


VMEM = pl.BlockSpec(memory_space=pltpu.VMEM)
SMEM = pl.BlockSpec(memory_space=pltpu.SMEM)
PARAMS = pltpu.CompilerParams(vmem_limit_bytes=48 * 1024 * 1024)


def sds(*shape):
    return jax.ShapeDtypeStruct(shape, f32)


def per_device(trans, storage, fault_cells, fault_count, fault_trans):
    peers = (lax.axis_size("gx"), lax.axis_size("gy"))
    own, plane, cells = pl.pallas_call(
        functools.partial(pack_kernel, peers),
        out_shape=(sds(232, NZ), sds(80, NZ), sds(8, NZ)),
        in_specs=[VMEM, VMEM, VMEM, SMEM, VMEM],
        out_specs=(VMEM, VMEM, VMEM),
        compiler_params=PARAMS,
        name="pack",
    )(trans, storage, fault_cells, fault_count, fault_trans)
    lo = shift(own, "gx", 1)
    hi = shift(own, "gx", -1)
    lo2 = shift(plane, "gx", 2)
    hi2 = shift(cells, "gx", -2)
    up, down = pl.pallas_call(
        column_kernel,
        out_shape=(sds(YROWS, NZ), sds(YROWS, NZ)),
        in_specs=[VMEM] * 5,
        out_specs=(VMEM, VMEM),
        compiler_params=PARAMS,
        name="columns",
    )(own, lo, hi, lo2, hi2)
    yl = shift(up, "gy", 1)
    yh = shift(down, "gy", -1)
    return pl.pallas_call(
        functools.partial(main_kernel, peers),
        out_shape=sds(125, 1, 256),
        in_specs=[VMEM] * 7,
        out_specs=VMEM,
        scratch_shapes=[
            pltpu.VMEM((7 * PER * ROWS, NZ), f32),
            pltpu.VMEM((7 * PER * ROWS, NZ), f32),
            pltpu.VMEM((6 * 8 * 16, NZ), f32),
            pltpu.VMEM((6 * 16, NZ), f32),
            pltpu.VMEM((6 * 16, NZ), f32),
            pltpu.VMEM((6 * 16, NZ), f32),
            pltpu.VMEM((3, 12, 8, NZ), f32),
            pltpu.VMEM((6, 12, 4, 8, NZ), f32),
            pltpu.VMEM((4, 10, 3, 3, 8, NZ), f32),
            pltpu.VMEM((2, 5, 5, 8, 512), f32),
            pltpu.VMEM((12, NZ, NZ), bf16),
            pltpu.VMEM((12, NZ, NZ), bf16),
        ],
        compiler_params=PARAMS,
        name="galerkin",
    )(own, lo, hi, lo2, hi2, yl, yh)


def solution(mesh):
    placed = (
        P(None, "gx", "gy"),
        P("gx", "gy"),
        P("gx", "gy", None),
        P("gx", "gy"),
        P("gx", "gy", None),
    )
    return jax.shard_map(
        per_device, mesh=mesh, in_specs=placed, out_specs=P(None, "gx", "gy"), check_vma=False
    )
```

```python
import functools

import jax
import jax.numpy as jnp
from jax import lax
from jax.experimental import pallas as pl
from jax.experimental.pallas import tpu as pltpu
from jax.sharding import PartitionSpec as P

NZ = 128
CY = 8
SLOTS = 512

FORWARD = (
    (0, 0, 1),
    (0, 1, -1),
    (0, 1, 0),
    (0, 1, 1),
    (1, -1, -1),
    (1, -1, 0),
    (1, -1, 1),
    (1, 0, -1),
    (1, 0, 0),
    (1, 0, 1),
    (1, 1, -1),
    (1, 1, 0),
    (1, 1, 1),
)
OFFSET = {step: k for k, step in enumerate(FORWARD)}
damping = 2.0 / 3.0

ROWS = 24
PER = 14
COLBLOCK = 93
THIRD = 2 * COLBLOCK
UP_FAULT, UP_ROWS = 232, 256
DOWN_FAULT, DOWN_ROWS = 208, 232

f32 = jnp.float32
bf16 = jnp.bfloat16


def dot_nt(a, b):
    return lax.dot_general(a, b, (((1,), (1,)), ((), ())), preferred_element_type=f32)


def dot_nn(a, b):
    return lax.dot_general(a, b, (((1,), (0,)), ((), ())), preferred_element_type=f32)


def split(value):
    high = value.astype(bf16)
    return high, (value - high.astype(f32)).astype(bf16)


def pack_kernel(peers, count, *refs):
    sources, (block, plane), targets, sems = refs[:4], refs[4:6], refs[6:10], refs[10]
    copies = [
        pltpu.make_async_copy(src, dst, sems.at[k])
        for k, (src, dst) in enumerate(zip(sources, targets))
    ]
    for copy in copies:
        copy.start()
    for copy in copies:
        copy.wait()
    trans, storage, cells, ftrans = targets
    last_x = lax.axis_index("gx") == peers[0] - 1
    first_y = lax.axis_index("gy") == 0
    last_y = lax.axis_index("gy") == peers[1] - 1
    depth = lax.broadcasted_iota(jnp.int32, (8, NZ), 1)
    row = lax.broadcasted_iota(jnp.int32, (8, NZ), 0)
    for x in range(2):
        for o in range(PER):
            base = (x * PER + o) * 8
            for y in range(CY):
                lanes = slice(y * NZ, (y + 1) * NZ)
                if o < 13:
                    value = trans[o, x : x + 1, lanes]
                else:
                    value = storage[x : x + 1, lanes]
                block[base + y : base + y + 1, :] = value
            if o == 13:
                continue
            step = FORWARD[o]
            keep = None
            if step[2] == 1:
                keep = depth < NZ - 1
            if step[2] == -1:
                keep = depth > 0
            if step[1] == 1:
                inside = (row < CY - 1) | jnp.logical_not(last_y)
                keep = inside if keep is None else keep & inside
            if step[1] == -1:
                inside = (row > 0) | jnp.logical_not(first_y)
                keep = inside if keep is None else keep & inside
            if step[0] == 1 and x == 1:
                inside = (row >= 0) & jnp.logical_not(last_x)
                keep = inside if keep is None else keep & inside
            if keep is not None:
                block[base : base + 8, :] = jnp.where(keep, block[base : base + 8, :], 0.0)
    live = count[0, 0]
    lane = lax.broadcasted_iota(jnp.int32, (1, NZ), 1)
    base = 2 * PER * 8
    for r in range(4):
        lanes = slice(r * NZ, (r + 1) * NZ)
        block[base + r : base + r + 1, :] = cells[0, :, lanes].astype(f32)
        block[base + 4 + r : base + 5 + r, :] = jnp.where(
            lane + r * NZ < live, ftrans[0, :, lanes], 0.0
        )
    plane[0:72, :] = block[(PER + 4) * 8 : (PER + 13) * 8, :]
    plane[72:80, :] = block[base : base + 8, :]


def column_kernel(own, lo, hi, lo2, hi2, up, down, fb):
    even = lax.rem(lax.axis_index("gx"), 2) == 0
    tile_own, tile_lo, tile_hi = (ref[224:232, :] for ref in (own, lo, hi))
    partner = jnp.where(even, tile_hi, tile_lo)
    other = jnp.where(even, tile_lo, tile_hi)
    fb[0:4, :] = tile_own[0:4]
    fb[4:8, :] = partner[0:4]
    fb[8:12, :] = tile_own[4:8]
    fb[12:16, :] = other[0:4]
    for r in range(4):
        beyond = hi2[0, :, r * NZ : (r + 1) * NZ].astype(f32)
        fb[16 + r : 17 + r, :] = jnp.where(even, lo2[72 + r : 73 + r, :], beyond)
    fb[20:24, :] = other[4:8]
    up[UP_FAULT : UP_FAULT + 24, :] = fb[...]
    down[DOWN_FAULT : DOWN_FAULT + 24, :] = fb[...]
    for out, first, third, runs in ((up, CY - 2, CY - 3, (1, 10)), (down, 0, 2, (4,))):
        for c in range(2):
            y = first + c
            base = c * COLBLOCK
            out[base : base + 9, :] = lo2[pl.ds(y, 9, stride=8), :]
            for k, ref in enumerate((lo, own, hi)):
                start = base + 9 + 28 * k
                out[start : start + 28, :] = ref[pl.ds(y, 28, stride=8), :]
        at = THIRD
        out[at : at + 3, :] = lo2[pl.ds((runs[-1] - 4) * 8 + third, 3, stride=8), :]
        at += 3
        for ref in (lo, own, hi):
            for x in range(2):
                for o in runs:
                    out[at : at + 3, :] = ref[pl.ds((x * PER + o) * 8 + third, 3, stride=8), :]
                    at += 3


def colour(z):
    half = z >> 1
    return half - 5 * ((half * 205) >> 10)


def prepare(tile, far2, eo):
    columns = jnp.transpose(tile)
    lane = lax.broadcasted_iota(jnp.int32, (NZ, NZ), 1)
    for r in range(4):
        rows = slice(r * NZ, (r + 1) * NZ)

        def column(k):
            return columns[:, 4 * k + r : 4 * k + r + 1]

        match = (column(1).astype(jnp.int32) & 127) == lane
        high = column(2).astype(bf16).astype(f32)
        far2[rows, 0:NZ] = jnp.where(match, high, 0.0).astype(bf16)
        far2[rows, NZ : 2 * NZ] = jnp.where(match, column(2) - high, 0.0).astype(bf16)
        tint = colour(column(4).astype(jnp.int32) & 127)
        high = column(5).astype(bf16).astype(f32)
        value = jnp.where((lane == tint) | (lane == 5), high, 0.0)
        value = jnp.where((lane == tint + 8) | (lane == 13), column(5) - high, value)
        eo[rows, :] = value.astype(bf16)

    def flat(k):
        row = jnp.concatenate([tile[4 * k + r : 4 * k + r + 1, :] for r in range(4)], axis=1)
        return row.astype(jnp.int32) & 1023

    return flat(0), flat(3)


def build(y, at_own, at_other, far2, eo):
    z128 = lax.broadcasted_iota(jnp.int32, (NZ, SLOTS), 0)
    z8 = lax.broadcasted_iota(jnp.int32, (8, NZ), 1)
    e8 = lax.broadcasted_iota(jnp.int32, (8, NZ), 0)
    one = jnp.where((e8 == colour(z8)) | (e8 == 5), 1.0, 0.0).astype(bf16)
    one2 = jnp.concatenate([one, one], axis=1)
    hot = jnp.where(at_own == z128 + y * NZ, 1.0, 0.0).astype(bf16)
    both = dot_nn(hot, far2[...])
    matrix = both[:, :NZ] + both[:, NZ:]
    f2 = jnp.concatenate(split(matrix), axis=0)
    ft2 = jnp.concatenate(split(jnp.transpose(matrix)), axis=0)
    hot_o = jnp.where(at_other == z128 + y * NZ, 1.0, 0.0).astype(bf16)
    pieces = jnp.transpose(dot_nn(hot_o, eo[...]))
    return f2, ft2, (dot_nn(one2, ft2), dot_nn(one2, f2), pieces[:8] + pieces[8:16])


def fault_kernel(fb, f2, ft2, rf, far2, eo):
    at_own, at_other = prepare(fb[...], far2, eo)

    def column(y, carry):
        f2[y], ft2[y], sums = build(y, at_own, at_other, far2, eo)
        for k in range(3):
            rf[k, y] = sums[k]
        return carry

    lax.fori_loop(0, CY, column, 0)


def through(value, matrix2):
    rows = value.shape[0]
    high, low = split(value)
    left = jnp.concatenate(
        [jnp.concatenate([high, high], axis=1), jnp.concatenate([low, low], axis=1)], axis=0
    )
    got = dot_nn(left, matrix2)
    return got[:rows] + got[rows:]


def main_kernel(
    peers,
    own,
    lo,
    hi,
    lo2,
    yl,
    yh,
    f2,
    ft2,
    rf_in,
    out,
    w,
    wr,
    qc,
    inv,
    diag,
    fd,
    rf,
    qe,
    ap,
    tt,
    f2h,
    ft2h,
    far2,
    eo,
):
    gx = lax.axis_index("gx")
    gy = lax.axis_index("gy")
    par = lax.rem(gx, 2)
    even = par == 0
    sgn = 1 - 2 * par
    p_own = jnp.where(even, 3, 2)
    p_far = jnp.where(even, 4, 1)
    p_third = jnp.where(even, 0, 5)
    p_fault = (p_own, p_far, p_third)
    z8 = lax.broadcasted_iota(jnp.int32, (8, NZ), 1)
    e8 = lax.broadcasted_iota(jnp.int32, (8, NZ), 0)

    def place(ref, count, first):
        for k in range(count):
            base = (first + k) * ROWS
            w[base + 3 : base + 11, :] = ref[8 * k : 8 * k + 8, :]

    place(lo2, 9, 4)
    for k, ref in enumerate((lo, own, hi)):
        place(ref, 28, PER * (1 + 2 * k))
    for ref, row, third, runs in ((yl, 1, 0, (1, 10)), (yh, 11, 13, (4,))):
        for c in range(2):
            base = c * COLBLOCK
            w[pl.ds(4 * ROWS + row + c, 9, stride=ROWS), :] = ref[base : base + 9, :]
            w[pl.ds(PER * ROWS + row + c, 84, stride=ROWS), :] = ref[base + 9 : base + 93, :]
        at = THIRD
        for plane in range(7):
            for o in runs[-1:] if plane == 0 else runs:
                start = (plane * PER + o) * ROWS + third
                w[pl.ds(start, 3, stride=ROWS), :] = ref[at : at + 3, :]
                at += 3
    for p in range(7):
        for o, step in enumerate(FORWARD):
            if step[2] == 0 or (p == 0 and o < 4):
                continue
            base = (p * PER + o) * ROWS
            shift = 1 if step[2] == 1 else NZ - 1
            wr[base : base + ROWS, :] = pltpu.roll(w[base : base + ROWS, :], shift, 1)

    fd[...] = jnp.zeros_like(fd)

    def put(column, k, value):
        rf[k, column] = value
        fd[pl.ds(p_fault[k] * 16 + column, 1), :] = value[5:6, :]

    for y in range(CY):
        for k in range(3):
            put(y + 2, k, rf_in[k, y])
    for ref, start, columns in ((yl, UP_FAULT, ((0, 6), (1, 7))), (yh, DOWN_FAULT, ((10, 0), (11, 1)))):
        at_own, at_other = prepare(ref[start : start + 24, :], far2, eo)
        for column, y in columns:
            near, near_t, values = build(y, at_own, at_other, far2, eo)
            if column in (1, 10):
                f2h[column // 10] = near
                ft2h[column // 10] = near_t
            for k in range(3):
                put(column, k, values[k])

    r16 = lax.broadcasted_iota(jnp.int32, (16, NZ), 0)
    z16 = lax.broadcasted_iota(jnp.int32, (16, NZ), 1)
    even_y = (r16 & 1) == 0
    even_z = (z16 & 1) == 0
    for p in range(6):
        base = p + 1

        def weight(dx, dy, dz):
            if (dx, dy, dz) in OFFSET:
                start = (base * PER + OFFSET[dx, dy, dz]) * ROWS + 1
                return w[start : start + 16, :]
            o = OFFSET[-dx, -dy, -dz]
            start = ((base + dx) * PER + o) * ROWS + 1 + dy
            return (w if dz == 0 else wr)[start : start + 16, :]

        near = 1 if p % 2 == 0 else -1
        sums = {}
        for dz in (-1, 0, 1):
            got = {}
            for dx in (-1, 0, 1):
                below, above = weight(dx, -1, dz), weight(dx, 1, dz)
                got[dx, 0] = jnp.where(even_y, above, below)
                if (dx, dz) != (0, 0):
                    got[dx, 0] = got[dx, 0] + weight(dx, 0, dz)
                got[dx, 1] = jnp.where(even_y, below, above)
            for sy in range(2):
                sums[0, sy, dz] = got[0, sy] + got[near, sy]
                sums[1, sy, dz] = got[-near, sy]
        total = w[(base * PER + 13) * ROWS + 1 : (base * PER + 13) * ROWS + 17, :]
        total = total + fd[p * 16 : p * 16 + 16, :]
        r = []
        for sx in range(2):
            for sy in range(2):
                down, same, up = (sums[sx, sy, dz] for dz in (-1, 0, 1))
                r.append(same + jnp.where(even_z, up, down))
                r.append(jnp.where(even_z, down, up))
        for value in r:
            total = total + value
        total = jnp.where(total == 0.0, 1.0, total)
        scale = damping / total
        diag[p * 16 : p * 16 + 16, :] = total
        inv[p * 16 : p * 16 + 16, :] = scale
        for k, value in enumerate(r):
            value = value * scale
            if k == 0:
                value = value + (1.0 - damping)
            qc[(p * 8 + k) * 16 : (p * 8 + k) * 16 + 16, :] = value

    beside = jnp.where((z8 & 1) == 0, z8 - 1, z8 + 1)
    mask_own = jnp.where(e8 == colour(z8), 1.0, 0.0)
    mask_oth = jnp.where(e8 == colour(beside + 10), 1.0, 0.0)
    rows5 = jnp.where(e8 < 5, 1.0, 0.0)

    def spread(c, carry):
        for p in range(6):
            for lat in range(4):
                at = (p * 8 + 2 * lat) * 16 + c
                qe[p, c, lat] = (
                    qc[pl.ds(at, 1), :] * mask_own + qc[pl.ds(at + 16, 1), :] * mask_oth
                )
        for k, plane in enumerate(p_fault):
            qe[plane, c, 2] = qe[plane, c, 2] + rf[k, c] * (
                inv[pl.ds(plane * 16 + c, 1), :] * rows5
            )
        return carry

    lax.fori_loop(0, 12, spread, 0)

    def apply_column(p, y, odd_y):
        odd_x = p % 2
        acc = {}
        for dx in (-1, 0, 1):
            for dy in (-1, 0, 1):
                q = [qe[p + dx, y + dy, lat] for lat in range(4)]
                own_x = dx if (dx == 1 and odd_x) or (dx == -1 and not odd_x) else 0
                own_y = dy if (dy == 1 and odd_y) or (dy == -1 and not odd_y) else 0
                oth_x = own_x + (1 if (p + dx) % 2 else -1)
                oth_y = own_y + (1 if (odd_y + dy) % 2 else -1)
                for dz in (-1, 0, 1):
                    if (dx, dy, dz) == (0, 0, 0):
                        continue
                    if (dx, dy, dz) in OFFSET:
                        at = ((p + 1) * PER + OFFSET[dx, dy, dz]) * ROWS + y + 1
                        ref = w if dz == 0 else wr
                    else:
                        at = ((p + 1 + dx) * PER + OFFSET[-dx, -dy, -dz]) * ROWS + y + 1 + dy
                        ref = w
                    wt = ref[pl.ds(at, 1), :]
                    for lat in range(4):
                        lx = oth_x if lat >= 2 else own_x
                        ly = oth_y if lat % 2 else own_y
                        value = wt * q[lat]
                        key = (lx, ly, dz)
                        acc[key] = acc[key] + value if key in acc else value
        centre = diag[pl.ds(p * 16 + y, 1), :]
        for lx in (-1, 0, 1):
            for ly in (-1, 0, 1):
                total = acc[lx, ly, 0]
                total = total + pltpu.roll(acc[lx, ly, 1], NZ - 1, 1)
                total = total + pltpu.roll(acc[lx, ly, -1], 1, 1)
                own_lat = None
                sx = {0: 0, (1 if odd_x else -1): 1}.get(lx)
                sy = {0: 0, (1 if odd_y else -1): 1}.get(ly)
                if sx is not None and sy is not None:
                    own_lat = 2 * sx + sy
                if own_lat is None:
                    total = -total
                else:
                    total = centre * qe[p, y, own_lat] - total
                ap[p - 1, y - 1, lx + 1, ly + 1] = total

    def apply_pair(k, carry):
        for p in range(1, 5):
            apply_column(p, 2 * k + 1, 1)
            apply_column(p, 2 * k + 2, 0)
        return carry

    lax.fori_loop(0, 5, apply_pair, 0)

    def fault_apply(c, f2c, ft2c):
        ly_oth = 2 * lax.rem(c, 2)
        for plane, source, x_own, matrix in (
            (p_own, p_far, 1 + sgn, ft2c),
            (p_far, p_own, 1 - sgn, f2c),
        ):
            total = through(qe[source, c].reshape(32, NZ), matrix)
            for lat in range(4):
                lx = 1 if lat >= 2 else x_own
                ly = ly_oth if lat % 2 else 1
                ap[plane - 1, c - 1, lx, ly] = ap[plane - 1, c - 1, lx, ly] - total[8 * lat : 8 * lat + 8]

    def fault_own(y, carry):
        fault_apply(y + 2, f2[y], ft2[y])
        return carry

    lax.fori_loop(0, CY, fault_own, 0)
    fault_apply(1, f2h[0], ft2h[0])
    fault_apply(10, f2h[1], ft2h[1])

    x_coarse = lax.rem(gx, 5) + 5
    a_of = [lax.rem(x_coarse + d, 5) for d in range(-2, 3)]

    def b_of(coarse_y, d):
        return lax.rem(gy * (CY // 2) + coarse_y + d + 5, 5)

    def gather(pair, carry):
        for half in range(2):
            coarse_y = 2 * pair + half
            columns = []
            for x in range(-1, 3):
                for y in range(-1, 3):
                    sx = 0 if x in (0, 1) else 1
                    sy = 0 if y in (0, 1) else 1
                    columns.append((x, y, 2 * sx + sy, (-1, 0, 0, 1)[x + 1], (-1, 0, 0, 1)[y + 1]))
            for zk in range(2):
                acc = {}
                for x, y, lat, ax, ay in columns:
                    c = 2 * coarse_y + y + 2
                    q = qc[pl.ds(((x + 2) * 8 + 2 * lat + zk) * 16 + c, 1), :]
                    for lx in range(3):
                        for ly in range(3):
                            value = q * ap[x + 1, c - 1, lx, ly]
                            key = (ax + lx - 1, ay + ly - 1)
                            acc[key] = acc[key] + value if key in acc else value
                lane = half * 256 + zk * NZ
                for (dx, dy), value in acc.items():
                    tt[pair, a_of[dx + 2], b_of(coarse_y, dy), :, lane : lane + NZ] = value
        return carry

    lax.fori_loop(0, 2, gather, 0)

    for y in range(CY):
        c = y + 2
        coarse_y = y // 2
        lane = (coarse_y % 2) * 256
        value = ap[p_far - 1, c - 1].reshape(72, NZ) * inv[pl.ds(p_far * 16 + c, 1), :]
        total = through(value, ft2[y])
        for lx in range(3):
            a = lax.rem(x_coarse + lx - 1 + sgn, 5)
            for ly in range(3):
                b = b_of(coarse_y, ly - 1)
                at = 8 * (3 * lx + ly)
                place_at = tt.at[coarse_y // 2, a, b, :, lane : lane + NZ]
                place_at[...] = place_at[...] + total[at : at + 8]

    kz = lax.broadcasted_iota(jnp.int32, (512, NZ), 0)
    kout = lax.broadcasted_iota(jnp.int32, (512, NZ), 1)
    z_in = kz & 127
    is_oth = ((kz >> 7) & 1) == 1
    target = jnp.where(
        is_oth, (z_in >> 1) + jnp.where((z_in & 1) == 0, -1, 1), z_in >> 1
    )
    fits = (target == (kout & 63)) & ((kz >> 8) == (kout >> 6))
    collect = jnp.where(fits, 1.0, 0.0).astype(bf16)
    for pair in range(2):
        high, low = split(tt[pair].reshape(200, 512))
        got = (dot_nn(high, collect) + dot_nn(low, collect)) * 0.125
        for k in range(25):
            out[5 * k : 5 * k + 5, 0, pair * NZ : (pair + 1) * NZ] = got[8 * k : 8 * k + 5]


def shift(value, axis, distance):
    peers = lax.axis_size(axis)
    pairs = [(i, i + distance) for i in range(peers) if 0 <= i + distance < peers]
    return lax.ppermute(value, axis, pairs)


VMEM = pl.BlockSpec(memory_space=pltpu.VMEM)
HBM = pl.BlockSpec(memory_space=pltpu.HBM)


def params(mib):
    return pltpu.CompilerParams(vmem_limit_bytes=mib * 1024 * 1024)


def sds(*shape, dtype=f32):
    return jax.ShapeDtypeStruct(shape, dtype)


def per_device(trans, storage, fault_cells, fault_count, fault_trans):
    peers = (lax.axis_size("gx"), lax.axis_size("gy"))
    hi2 = shift(fault_cells, "gx", -2)
    sources = [
        pltpu.with_memory_space_constraint(array, pltpu.HBM)
        for array in (trans, storage, fault_cells, fault_trans)
    ]
    own, plane = pl.pallas_call(
        functools.partial(pack_kernel, peers),
        out_shape=(sds(232, NZ), sds(80, NZ)),
        in_specs=[pl.BlockSpec(memory_space=pltpu.SMEM)] + [HBM] * 4,
        out_specs=(VMEM, VMEM),
        scratch_shapes=[pltpu.VMEM(array.shape, array.dtype) for array in sources]
        + [pltpu.SemaphoreType.DMA((4,))],
        compiler_params=params(16),
        name="pack",
    )(fault_count, *sources)
    lo2 = shift(plane, "gx", 2)
    lo = shift(own, "gx", 1)
    hi = shift(own, "gx", -1)
    up, down, fb = pl.pallas_call(
        column_kernel,
        out_shape=(sds(UP_ROWS, NZ), sds(DOWN_ROWS, NZ), sds(24, NZ)),
        in_specs=[VMEM] * 5,
        out_specs=(VMEM,) * 3,
        compiler_params=params(16),
        name="columns",
    )(own, lo, hi, lo2, hi2)
    yl = shift(up, "gy", 1)
    yh = shift(down, "gy", -1)
    pieces = sds(CY, 2 * NZ, NZ, dtype=bf16)
    f2, ft2, rf = pl.pallas_call(
        fault_kernel,
        out_shape=(pieces, pieces, sds(3, CY, 8, NZ)),
        in_specs=[VMEM],
        out_specs=(VMEM,) * 3,
        scratch_shapes=[pltpu.VMEM((SLOTS, 2 * NZ), bf16), pltpu.VMEM((SLOTS, NZ), bf16)],
        compiler_params=params(16),
        cost_estimate=pl.CostEstimate(flops=2 * 10**9, bytes_accessed=2**21, transcendentals=0),
        name="faults",
    )(fb)
    return pl.pallas_call(
        functools.partial(main_kernel, peers),
        out_shape=sds(125, 1, 256),
        in_specs=[VMEM] * 9,
        out_specs=VMEM,
        scratch_shapes=[
            pltpu.VMEM((7 * PER * ROWS, NZ), f32),
            pltpu.VMEM((7 * PER * ROWS, NZ), f32),
            pltpu.VMEM((6 * 8 * 16, NZ), f32),
            pltpu.VMEM((6 * 16, NZ), f32),
            pltpu.VMEM((6 * 16, NZ), f32),
            pltpu.VMEM((6 * 16, NZ), f32),
            pltpu.VMEM((3, 12, 8, NZ), f32),
            pltpu.VMEM((6, 12, 4, 8, NZ), f32),
            pltpu.VMEM((4, 10, 3, 3, 8, NZ), f32),
            pltpu.VMEM((2, 5, 5, 8, 512), f32),
            pltpu.VMEM((2, 2 * NZ, NZ), bf16),
            pltpu.VMEM((2, 2 * NZ, NZ), bf16),
            pltpu.VMEM((SLOTS, 2 * NZ), bf16),
            pltpu.VMEM((SLOTS, NZ), bf16),
        ],
        compiler_params=params(24),
        name="galerkin",
    )(own, lo, hi, lo2, yl, yh, f2, ft2, rf)


def solution(mesh):
    placed = (
        P(None, "gx", "gy"),
        P("gx", "gy"),
        P("gx", "gy", None),
        P("gx", "gy"),
        P("gx", "gy", None),
    )
    return jax.shard_map(
        per_device, mesh=mesh, in_specs=placed, out_specs=P(None, "gx", "gy"), check_vma=False
    )
```

```python
import functools

import jax
import jax.numpy as jnp
from jax import lax
from jax.experimental import pallas as pl
from jax.experimental.pallas import tpu as pltpu
from jax.sharding import PartitionSpec as P

NZ = 128
CY = 8
SLOTS = 512

FORWARD = (
    (0, 0, 1),
    (0, 1, -1),
    (0, 1, 0),
    (0, 1, 1),
    (1, -1, -1),
    (1, -1, 0),
    (1, -1, 1),
    (1, 0, -1),
    (1, 0, 0),
    (1, 0, 1),
    (1, 1, -1),
    (1, 1, 0),
    (1, 1, 1),
)
OFFSET = {step: k for k, step in enumerate(FORWARD)}
damping = 2.0 / 3.0

ROWS = 24
PER = 14
COLBLOCK = 93
THIRD = 2 * COLBLOCK
FAULT_ROW, Y_ROWS = 232, 256

f32 = jnp.float32
bf16 = jnp.bfloat16


def dot_nn(a, b):
    return lax.dot_general(a, b, (((1,), (0,)), ((), ())), preferred_element_type=f32)


def split(value):
    high = value.astype(bf16)
    return high, (value - high.astype(f32)).astype(bf16)


def pack_kernel(peers, count, *refs):
    sources, (block, plane), targets, sems = refs[:4], refs[4:6], refs[6:10], refs[10]
    copies = [
        pltpu.make_async_copy(src, dst, sems.at[k])
        for k, (src, dst) in enumerate(zip(sources, targets))
    ]
    for copy in copies:
        copy.start()
    for copy in copies:
        copy.wait()
    trans, storage, cells, ftrans = targets
    last_x = lax.axis_index("gx") == peers[0] - 1
    first_y = lax.axis_index("gy") == 0
    last_y = lax.axis_index("gy") == peers[1] - 1
    depth = lax.broadcasted_iota(jnp.int32, (8, NZ), 1)
    row = lax.broadcasted_iota(jnp.int32, (8, NZ), 0)
    for x in range(2):
        for o in range(PER):
            base = (x * PER + o) * 8
            for y in range(CY):
                lanes = slice(y * NZ, (y + 1) * NZ)
                if o < 13:
                    value = trans[o, x : x + 1, lanes]
                else:
                    value = storage[x : x + 1, lanes]
                block[base + y : base + y + 1, :] = value
            if o == 13:
                continue
            step = FORWARD[o]
            keep = None
            if step[2] == 1:
                keep = depth < NZ - 1
            if step[2] == -1:
                keep = depth > 0
            if step[1] == 1:
                inside = (row < CY - 1) | jnp.logical_not(last_y)
                keep = inside if keep is None else keep & inside
            if step[1] == -1:
                inside = (row > 0) | jnp.logical_not(first_y)
                keep = inside if keep is None else keep & inside
            if step[0] == 1 and x == 1:
                inside = (row >= 0) & jnp.logical_not(last_x)
                keep = inside if keep is None else keep & inside
            if keep is not None:
                block[base : base + 8, :] = jnp.where(keep, block[base : base + 8, :], 0.0)
    live = count[0, 0]
    lane = lax.broadcasted_iota(jnp.int32, (1, NZ), 1)
    base = 2 * PER * 8
    for r in range(4):
        lanes = slice(r * NZ, (r + 1) * NZ)
        block[base + r : base + r + 1, :] = cells[0, :, lanes].astype(f32)
        block[base + 4 + r : base + 5 + r, :] = jnp.where(
            lane + r * NZ < live, ftrans[0, :, lanes], 0.0
        )
    plane[0:72, :] = block[(PER + 4) * 8 : (PER + 13) * 8, :]
    plane[72:80, :] = block[base : base + 8, :]


def by_parity(axis, body):
    odd = lax.rem(lax.axis_index(axis), 2)
    for k in range(2):
        pl.when(odd == k)(functools.partial(body, k))


def column_kernel(own, rp, ro, rd, re, to_core, to_chip):
    tile = own[224:232, :]
    other = ro[224:232, :]
    parts = (tile[0:4], rp[224:228, :], tile[4:8], other[0:4], rd[72:76, :], other[4:8])
    for out in (to_core, to_chip):
        for k, part in enumerate(parts):
            out[FAULT_ROW + 4 * k : FAULT_ROW + 4 * k + 4, :] = part

    def fill(out, lo, hi, lo2, first, third, runs):
        for c in range(2):
            y = first + c
            base = c * COLBLOCK
            out[base : base + 9, :] = lo2[pl.ds(y, 9, stride=8), :]
            for k, ref in enumerate((lo, own, hi)):
                start = base + 9 + 28 * k
                out[start : start + 28, :] = ref[pl.ds(y, 28, stride=8), :]
        at = THIRD
        out[at : at + 3, :] = lo2[pl.ds((runs[-1] - 4) * 8 + third, 3, stride=8), :]
        at += 3
        for ref in (lo, own, hi):
            for x in range(2):
                for o in runs:
                    out[at : at + 3, :] = ref[pl.ds((x * PER + o) * 8 + third, 3, stride=8), :]
                    at += 3

    def for_x(odd_x):
        lo, hi, lo2 = (rp, ro, re) if odd_x else (ro, rp, rd)

        def for_y(odd_y):
            up, down = (to_chip, to_core) if odd_y else (to_core, to_chip)
            fill(up, lo, hi, lo2, CY - 2, CY - 3, (1, 10))
            fill(down, lo, hi, lo2, 0, 2, (4,))

        by_parity("gy", for_y)

    by_parity("gx", for_x)


def colour(z):
    half = z >> 1
    return half - 5 * ((half * 205) >> 10)


def slot_columns(rows):
    tall = jnp.transpose(jnp.concatenate(rows, axis=0))
    return [[tall[:, 4 * k + r : 4 * k + r + 1] for r in range(4)] for k in range(len(rows))]


def flat_cells(rows):
    row = jnp.concatenate([rows[r : r + 1] for r in range(4)], axis=1)
    return row.astype(jnp.int32) & 1023


def fill_far(far2, partner, live):
    lane = lax.broadcasted_iota(jnp.int32, (NZ, NZ), 1)
    for r in range(4):
        rows = slice(r * NZ, (r + 1) * NZ)
        match = (partner[r].astype(jnp.int32) & 127) == lane
        high = live[r].astype(bf16).astype(f32)
        far2[rows, 0:NZ] = jnp.where(match, high, 0.0).astype(bf16)
        far2[rows, NZ : 2 * NZ] = jnp.where(match, live[r] - high, 0.0).astype(bf16)


def fill_tint(eo, beyond, live):
    lane = lax.broadcasted_iota(jnp.int32, (NZ, NZ), 1)
    for r in range(4):
        tint = colour(beyond[r].astype(jnp.int32) & 127)
        high = live[r].astype(bf16).astype(f32)
        value = jnp.where((lane == tint) | (lane == 5), high, 0.0)
        value = jnp.where((lane == tint + 8) | (lane == 13), live[r] - high, value)
        eo[r * NZ : (r + 1) * NZ, :] = value.astype(bf16)


def fill_hot(hot, cells, columns):
    z128 = lax.broadcasted_iota(jnp.int32, (NZ, SLOTS), 0)
    for k, y in enumerate(columns):
        value = jnp.where(cells == z128 + y * NZ, 1.0, 0.0)
        hot[k * NZ : (k + 1) * NZ, :] = value.astype(bf16)


def pair_matrix(both):
    z8 = lax.broadcasted_iota(jnp.int32, (8, NZ), 1)
    e8 = lax.broadcasted_iota(jnp.int32, (8, NZ), 0)
    one = jnp.where((e8 == colour(z8)) | (e8 == 5), 1.0, 0.0).astype(bf16)
    one2 = jnp.concatenate([one, one], axis=1)
    matrix = both[:, :NZ] + both[:, NZ:]
    f2 = jnp.concatenate(split(matrix), axis=0)
    ft2 = jnp.concatenate(split(jnp.transpose(matrix)), axis=0)
    return f2, ft2, dot_nn(one2, ft2), dot_nn(one2, f2)


def fault_kernel(own, rp, f2, ft2, rf, far2, hot, both):
    partner, live = slot_columns([rp[224:228, :], own[228:232, :]])
    fill_far(far2, partner, live)
    fill_hot(hot, flat_cells(own[224:228, :]), range(CY))
    both[...] = dot_nn(hot[...], far2[...])
    for y in range(CY):
        f2[y], ft2[y], rf[0, y], rf[1, y] = pair_matrix(both[y * NZ : (y + 1) * NZ, :])


def third_kernel(ro, rd, rf, eo, hot, both):
    beyond, live = slot_columns([rd[72:76, :], ro[228:232, :]])
    fill_tint(eo, beyond, live)
    fill_hot(hot, flat_cells(ro[224:228, :]), range(CY))
    both[...] = dot_nn(hot[...], eo[...])
    for y in range(CY):
        pieces = jnp.transpose(both[y * NZ : (y + 1) * NZ, :])
        rf[y] = pieces[:8] + pieces[8:16]


def through(value, matrix2):
    rows = value.shape[0]
    high, low = split(value)
    left = jnp.concatenate(
        [jnp.concatenate([high, high], axis=1), jnp.concatenate([low, low], axis=1)], axis=0
    )
    got = dot_nn(left, matrix2)
    return got[:rows] + got[rows:]


def main_kernel(
    own,
    rp,
    ro,
    rd,
    re,
    from_core,
    from_chip,
    f2,
    ft2,
    rf_pair,
    rf_third,
    out,
    w,
    wr,
    qc,
    inv,
    diag,
    fd,
    rf,
    qe,
    ap,
    tt,
    f2h,
    ft2h,
    far2,
    eo,
    hot,
):
    gx = lax.axis_index("gx")
    gy = lax.axis_index("gy")
    par = lax.rem(gx, 2)
    even = par == 0
    sgn = 1 - 2 * par
    p_own = jnp.where(even, 3, 2)
    p_far = jnp.where(even, 4, 1)
    p_third = jnp.where(even, 0, 5)
    p_fault = (p_own, p_far, p_third)
    z8 = lax.broadcasted_iota(jnp.int32, (8, NZ), 1)
    e8 = lax.broadcasted_iota(jnp.int32, (8, NZ), 0)

    def place(ref, count, first):
        for k in range(count):
            base = (first + k) * ROWS
            w[base + 3 : base + 11, :] = ref[8 * k : 8 * k + 8, :]

    def place_x(odd):
        lo, hi, lo2 = (rp, ro, re) if odd else (ro, rp, rd)
        place(lo2, 9, 4)
        place(lo, 28, PER)
        place(hi, 28, 5 * PER)

    place(own, 28, 3 * PER)
    by_parity("gx", place_x)

    def place_y(odd):
        yl, yh = (from_core, from_chip) if odd else (from_chip, from_core)
        for ref, row, third, runs in ((yl, 1, 0, (1, 10)), (yh, 11, 13, (4,))):
            for c in range(2):
                base = c * COLBLOCK
                w[pl.ds(4 * ROWS + row + c, 9, stride=ROWS), :] = ref[base : base + 9, :]
                w[pl.ds(PER * ROWS + row + c, 84, stride=ROWS), :] = ref[base + 9 : base + 93, :]
            at = THIRD
            for plane in range(7):
                for o in runs[-1:] if plane == 0 else runs:
                    start = (plane * PER + o) * ROWS + third
                    w[pl.ds(start, 3, stride=ROWS), :] = ref[at : at + 3, :]
                    at += 3

    by_parity("gy", place_y)
    for p in range(7):
        for o, step in enumerate(FORWARD):
            if step[2] == 0 or (p == 0 and o < 4):
                continue
            base = (p * PER + o) * ROWS
            shift = 1 if step[2] == 1 else NZ - 1
            wr[base : base + ROWS, :] = pltpu.roll(w[base : base + ROWS, :], shift, 1)

    fd[...] = jnp.zeros_like(fd)

    def put(column, k, value):
        rf[k, column] = value
        fd[pl.ds(p_fault[k] * 16 + column, 1), :] = value[5:6, :]

    for y in range(CY):
        put(y + 2, 0, rf_pair[0, y])
        put(y + 2, 1, rf_pair[1, y])
        put(y + 2, 2, rf_third[y])
    core_rows = from_core[FAULT_ROW : FAULT_ROW + 24, :]
    chip_rows = from_chip[FAULT_ROW : FAULT_ROW + 24, :]
    odd_y = lax.rem(gy, 2) == 1
    for side, first, second, columns in (
        (0, core_rows, chip_rows, ((0, 6), (1, 7))),
        (1, chip_rows, core_rows, ((10, 0), (11, 1))),
    ):
        rows = jnp.where(odd_y, first, second)
        cells, far, weight, cells_o, far_o, weight_o = (rows[4 * k : 4 * k + 4] for k in range(6))
        partner, live, beyond, live_o = slot_columns([far, weight, far_o, weight_o])
        fill_far(far2.at[side], partner, live)
        fill_tint(eo.at[side], beyond, live_o)
        ys = [y for _, y in columns]
        fill_hot(hot.at[side, 0], flat_cells(cells), ys)
        fill_hot(hot.at[side, 1], flat_cells(cells_o), ys)
        pair = dot_nn(hot[side, 0], far2[side])
        third = dot_nn(hot[side, 1], eo[side])
        for k, (column, y) in enumerate(columns):
            near, near_t, at_own, at_far = pair_matrix(pair[k * NZ : (k + 1) * NZ])
            if column in (1, 10):
                f2h[side] = near
                ft2h[side] = near_t
            put(column, 0, at_own)
            put(column, 1, at_far)
            pieces = jnp.transpose(third[k * NZ : (k + 1) * NZ])
            put(column, 2, pieces[:8] + pieces[8:16])

    r16 = lax.broadcasted_iota(jnp.int32, (16, NZ), 0)
    z16 = lax.broadcasted_iota(jnp.int32, (16, NZ), 1)
    even_y = (r16 & 1) == 0
    even_z = (z16 & 1) == 0
    for p in range(6):
        base = p + 1

        def weight(dx, dy, dz):
            if (dx, dy, dz) in OFFSET:
                start = (base * PER + OFFSET[dx, dy, dz]) * ROWS + 1
                return w[start : start + 16, :]
            o = OFFSET[-dx, -dy, -dz]
            start = ((base + dx) * PER + o) * ROWS + 1 + dy
            return (w if dz == 0 else wr)[start : start + 16, :]

        near = 1 if p % 2 == 0 else -1
        sums = {}
        for dz in (-1, 0, 1):
            got = {}
            for dx in (-1, 0, 1):
                below, above = weight(dx, -1, dz), weight(dx, 1, dz)
                got[dx, 0] = jnp.where(even_y, above, below)
                if (dx, dz) != (0, 0):
                    got[dx, 0] = got[dx, 0] + weight(dx, 0, dz)
                got[dx, 1] = jnp.where(even_y, below, above)
            for sy in range(2):
                sums[0, sy, dz] = got[0, sy] + got[near, sy]
                sums[1, sy, dz] = got[-near, sy]
        total = w[(base * PER + 13) * ROWS + 1 : (base * PER + 13) * ROWS + 17, :]
        total = total + fd[p * 16 : p * 16 + 16, :]
        r = []
        for sx in range(2):
            for sy in range(2):
                down, same, up = (sums[sx, sy, dz] for dz in (-1, 0, 1))
                r.append(same + jnp.where(even_z, up, down))
                r.append(jnp.where(even_z, down, up))
        for value in r:
            total = total + value
        total = jnp.where(total == 0.0, 1.0, total)
        scale = damping / total
        diag[p * 16 : p * 16 + 16, :] = total
        inv[p * 16 : p * 16 + 16, :] = scale
        for k, value in enumerate(r):
            value = value * scale
            if k == 0:
                value = value + (1.0 - damping)
            qc[(p * 8 + k) * 16 : (p * 8 + k) * 16 + 16, :] = value

    beside = jnp.where((z8 & 1) == 0, z8 - 1, z8 + 1)
    mask_own = jnp.where(e8 == colour(z8), 1.0, 0.0)
    mask_oth = jnp.where(e8 == colour(beside + 10), 1.0, 0.0)
    rows5 = jnp.where(e8 < 5, 1.0, 0.0)

    def spread(c, carry):
        for p in range(6):
            for lat in range(4):
                at = (p * 8 + 2 * lat) * 16 + c
                qe[p, c, lat] = (
                    qc[pl.ds(at, 1), :] * mask_own + qc[pl.ds(at + 16, 1), :] * mask_oth
                )
        for k, plane in enumerate(p_fault):
            qe[plane, c, 2] = qe[plane, c, 2] + rf[k, c] * (
                inv[pl.ds(plane * 16 + c, 1), :] * rows5
            )
        return carry

    lax.fori_loop(0, 12, spread, 0)

    def apply_column(p, y, odd_y):
        odd_x = p % 2
        acc = {}
        for dx in (-1, 0, 1):
            for dy in (-1, 0, 1):
                q = [qe[p + dx, y + dy, lat] for lat in range(4)]
                own_x = dx if (dx == 1 and odd_x) or (dx == -1 and not odd_x) else 0
                own_y = dy if (dy == 1 and odd_y) or (dy == -1 and not odd_y) else 0
                oth_x = own_x + (1 if (p + dx) % 2 else -1)
                oth_y = own_y + (1 if (odd_y + dy) % 2 else -1)
                for dz in (-1, 0, 1):
                    if (dx, dy, dz) == (0, 0, 0):
                        continue
                    if (dx, dy, dz) in OFFSET:
                        at = ((p + 1) * PER + OFFSET[dx, dy, dz]) * ROWS + y + 1
                        ref = w if dz == 0 else wr
                    else:
                        at = ((p + 1 + dx) * PER + OFFSET[-dx, -dy, -dz]) * ROWS + y + 1 + dy
                        ref = w
                    wt = ref[pl.ds(at, 1), :]
                    for lat in range(4):
                        lx = oth_x if lat >= 2 else own_x
                        ly = oth_y if lat % 2 else own_y
                        value = wt * q[lat]
                        key = (lx, ly, dz)
                        acc[key] = acc[key] + value if key in acc else value
        centre = diag[pl.ds(p * 16 + y, 1), :]
        for lx in (-1, 0, 1):
            for ly in (-1, 0, 1):
                total = acc[lx, ly, 0]
                total = total + pltpu.roll(acc[lx, ly, 1], NZ - 1, 1)
                total = total + pltpu.roll(acc[lx, ly, -1], 1, 1)
                own_lat = None
                sx = {0: 0, (1 if odd_x else -1): 1}.get(lx)
                sy = {0: 0, (1 if odd_y else -1): 1}.get(ly)
                if sx is not None and sy is not None:
                    own_lat = 2 * sx + sy
                if own_lat is None:
                    total = -total
                else:
                    total = centre * qe[p, y, own_lat] - total
                ap[p - 1, y - 1, lx + 1, ly + 1] = total

    def apply_pair(k, carry):
        for p in range(1, 5):
            apply_column(p, 2 * k + 1, 1)
            apply_column(p, 2 * k + 2, 0)
        return carry

    lax.fori_loop(0, 5, apply_pair, 0)

    def fault_apply(c, f2c, ft2c):
        ly_oth = 2 * (c % 2)
        for plane, source, x_own, matrix in (
            (p_own, p_far, 1 + sgn, ft2c),
            (p_far, p_own, 1 - sgn, f2c),
        ):
            total = through(qe[source, c].reshape(32, NZ), matrix)
            for lat in range(4):
                lx = 1 if lat >= 2 else x_own
                ly = ly_oth if lat % 2 else 1
                ap[plane - 1, c - 1, lx, ly] = ap[plane - 1, c - 1, lx, ly] - total[8 * lat : 8 * lat + 8]

    for y in range(CY):
        fault_apply(y + 2, f2[y], ft2[y])
    fault_apply(1, f2h[0], ft2h[0])
    fault_apply(10, f2h[1], ft2h[1])

    x_coarse = lax.rem(gx, 5) + 5
    a_of = [lax.rem(x_coarse + d, 5) for d in range(-2, 3)]

    def b_of(coarse_y, d):
        return lax.rem(gy * (CY // 2) + coarse_y + d + 5, 5)

    def gather(pair, carry):
        for half in range(2):
            coarse_y = 2 * pair + half
            columns = []
            for x in range(-1, 3):
                for y in range(-1, 3):
                    sx = 0 if x in (0, 1) else 1
                    sy = 0 if y in (0, 1) else 1
                    columns.append((x, y, 2 * sx + sy, (-1, 0, 0, 1)[x + 1], (-1, 0, 0, 1)[y + 1]))
            for zk in range(2):
                acc = {}
                for x, y, lat, ax, ay in columns:
                    c = 2 * coarse_y + y + 2
                    q = qc[pl.ds(((x + 2) * 8 + 2 * lat + zk) * 16 + c, 1), :]
                    for lx in range(3):
                        for ly in range(3):
                            value = q * ap[x + 1, c - 1, lx, ly]
                            key = (ax + lx - 1, ay + ly - 1)
                            acc[key] = acc[key] + value if key in acc else value
                lane = half * 256 + zk * NZ
                for (dx, dy), value in acc.items():
                    tt[pair, a_of[dx + 2], b_of(coarse_y, dy), :, lane : lane + NZ] = value
        return carry

    lax.fori_loop(0, 2, gather, 0)

    for y in range(CY):
        c = y + 2
        coarse_y = y // 2
        lane = (coarse_y % 2) * 256
        value = ap[p_far - 1, c - 1].reshape(72, NZ) * inv[pl.ds(p_far * 16 + c, 1), :]
        total = through(value, ft2[y])
        for lx in range(3):
            a = lax.rem(x_coarse + lx - 1 + sgn, 5)
            for ly in range(3):
                b = b_of(coarse_y, ly - 1)
                at = 8 * (3 * lx + ly)
                place_at = tt.at[coarse_y // 2, a, b, :, lane : lane + NZ]
                place_at[...] = place_at[...] + total[at : at + 8]

    kz = lax.broadcasted_iota(jnp.int32, (512, NZ), 0)
    kout = lax.broadcasted_iota(jnp.int32, (512, NZ), 1)
    z_in = kz & 127
    is_oth = ((kz >> 7) & 1) == 1
    target = jnp.where(
        is_oth, (z_in >> 1) + jnp.where((z_in & 1) == 0, -1, 1), z_in >> 1
    )
    fits = (target == (kout & 63)) & ((kz >> 8) == (kout >> 6))
    collect = jnp.where(fits, 1.0, 0.0).astype(bf16)
    for pair in range(2):
        high, low = split(tt[pair].reshape(200, 512))
        got = (dot_nn(high, collect) + dot_nn(low, collect)) * 0.125
        for k in range(25):
            out[5 * k : 5 * k + 5, 0, pair * NZ : (pair + 1) * NZ] = got[8 * k : 8 * k + 5]


def send(value, axis, target):
    peers = lax.axis_size(axis)
    pairs = [(i, target(i)) for i in range(peers) if target(i) is not None]
    return lax.ppermute(value, axis, [(i, j) for i, j in pairs if 0 <= j < peers])


def partner_of(i):
    return i ^ 1


def other_of(i):
    return i + 1 if i % 2 else i - 1


def beyond_of(i):
    return i - 2 if i % 2 else i + 2


def odd_after(i):
    return i + 2 if i % 2 else None


VMEM = pl.BlockSpec(memory_space=pltpu.VMEM)
HBM = pl.BlockSpec(memory_space=pltpu.HBM)


def params(mib):
    return pltpu.CompilerParams(vmem_limit_bytes=mib * 1024 * 1024)


def sds(*shape, dtype=f32):
    return jax.ShapeDtypeStruct(shape, dtype)


def per_device(trans, storage, fault_cells, fault_count, fault_trans):
    peers = (lax.axis_size("gx"), lax.axis_size("gy"))
    sources = [
        pltpu.with_memory_space_constraint(array, pltpu.HBM)
        for array in (trans, storage, fault_cells, fault_trans)
    ]
    own, plane = pl.pallas_call(
        functools.partial(pack_kernel, peers),
        out_shape=(sds(232, NZ), sds(80, NZ)),
        in_specs=[pl.BlockSpec(memory_space=pltpu.SMEM)] + [HBM] * 4,
        out_specs=(VMEM, VMEM),
        scratch_shapes=[pltpu.VMEM(array.shape, array.dtype) for array in sources]
        + [pltpu.SemaphoreType.DMA((4,))],
        compiler_params=params(16),
        name="pack",
    )(fault_count, *sources)
    rp = send(own, "gx", partner_of)
    rd = send(plane, "gx", beyond_of)
    re = send(plane, "gx", odd_after)
    ro = send(own, "gx", other_of)
    pieces = sds(CY, 2 * NZ, NZ, dtype=bf16)
    f2, ft2, rf_pair = pl.pallas_call(
        fault_kernel,
        out_shape=(pieces, pieces, sds(2, CY, 8, NZ)),
        in_specs=[VMEM] * 2,
        out_specs=(VMEM,) * 3,
        scratch_shapes=[
            pltpu.VMEM((SLOTS, 2 * NZ), bf16),
            pltpu.VMEM((CY * NZ, SLOTS), bf16),
            pltpu.VMEM((CY * NZ, 2 * NZ), f32),
        ],
        compiler_params=params(16),
        cost_estimate=pl.CostEstimate(flops=2 * 10**9, bytes_accessed=2**21, transcendentals=0),
        name="faults",
    )(own, rp)
    to_core, to_chip = pl.pallas_call(
        column_kernel,
        out_shape=(sds(Y_ROWS, NZ), sds(Y_ROWS, NZ)),
        in_specs=[VMEM] * 5,
        out_specs=(VMEM,) * 2,
        compiler_params=params(16),
        name="columns",
    )(own, rp, ro, rd, re)
    from_chip = send(to_chip, "gy", other_of)
    from_core = send(to_core, "gy", partner_of)
    rf_third = pl.pallas_call(
        third_kernel,
        out_shape=sds(CY, 8, NZ),
        in_specs=[VMEM] * 2,
        out_specs=VMEM,
        scratch_shapes=[
            pltpu.VMEM((SLOTS, NZ), bf16),
            pltpu.VMEM((CY * NZ, SLOTS), bf16),
            pltpu.VMEM((CY * NZ, NZ), f32),
        ],
        compiler_params=params(16),
        cost_estimate=pl.CostEstimate(flops=10**9, bytes_accessed=2**20, transcendentals=0),
        name="third",
    )(ro, rd)
    return pl.pallas_call(
        main_kernel,
        out_shape=sds(125, 1, 256),
        in_specs=[VMEM] * 11,
        out_specs=VMEM,
        scratch_shapes=[
            pltpu.VMEM((7 * PER * ROWS, NZ), f32),
            pltpu.VMEM((7 * PER * ROWS, NZ), f32),
            pltpu.VMEM((6 * 8 * 16, NZ), f32),
            pltpu.VMEM((6 * 16, NZ), f32),
            pltpu.VMEM((6 * 16, NZ), f32),
            pltpu.VMEM((6 * 16, NZ), f32),
            pltpu.VMEM((3, 12, 8, NZ), f32),
            pltpu.VMEM((6, 12, 4, 8, NZ), f32),
            pltpu.VMEM((4, 10, 3, 3, 8, NZ), f32),
            pltpu.VMEM((2, 5, 5, 8, 512), f32),
            pltpu.VMEM((2, 2 * NZ, NZ), bf16),
            pltpu.VMEM((2, 2 * NZ, NZ), bf16),
            pltpu.VMEM((2, SLOTS, 2 * NZ), bf16),
            pltpu.VMEM((2, SLOTS, NZ), bf16),
            pltpu.VMEM((2, 2, 2 * NZ, SLOTS), bf16),
        ],
        compiler_params=params(24),
        name="galerkin",
    )(own, rp, ro, rd, re, from_core, from_chip, f2, ft2, rf_pair, rf_third)


def solution(mesh):
    placed = (
        P(None, "gx", "gy"),
        P("gx", "gy"),
        P("gx", "gy", None),
        P("gx", "gy"),
        P("gx", "gy", None),
    )
    return jax.shard_map(
        per_device, mesh=mesh, in_specs=placed, out_specs=P(None, "gx", "gy"), check_vma=False
    )
```

```python
import functools

import jax
import jax.numpy as jnp
from jax import lax
from jax.experimental import pallas as pl
from jax.experimental.pallas import tpu as pltpu
from jax.sharding import PartitionSpec as P

NZ = 128
CY = 8
SLOTS = 512

FORWARD = (
    (0, 0, 1),
    (0, 1, -1),
    (0, 1, 0),
    (0, 1, 1),
    (1, -1, -1),
    (1, -1, 0),
    (1, -1, 1),
    (1, 0, -1),
    (1, 0, 0),
    (1, 0, 1),
    (1, 1, -1),
    (1, 1, 0),
    (1, 1, 1),
)
OFFSET = {step: k for k, step in enumerate(FORWARD)}
damping = 2.0 / 3.0

ROWS = 24
PER = 14
COLBLOCK = 93
THIRD = 2 * COLBLOCK
FAULT_ROW, Y_ROWS = 232, 256

f32 = jnp.float32
bf16 = jnp.bfloat16


def dot_nn(a, b):
    return lax.dot_general(a, b, (((1,), (0,)), ((), ())), preferred_element_type=f32)


def split(value):
    high = value.astype(bf16)
    return high, (value - high.astype(f32)).astype(bf16)


def pack_kernel(peers, count, *refs):
    sources, (block, plane), targets, sems = refs[:4], refs[4:6], refs[6:10], refs[10]
    copies = [
        pltpu.make_async_copy(src, dst, sems.at[k])
        for k, (src, dst) in enumerate(zip(sources, targets))
    ]
    for copy in copies:
        copy.start()
    for copy in copies:
        copy.wait()
    trans, storage, cells, ftrans = targets
    last_x = lax.axis_index("gx") == peers[0] - 1
    first_y = lax.axis_index("gy") == 0
    last_y = lax.axis_index("gy") == peers[1] - 1
    depth = lax.broadcasted_iota(jnp.int32, (8, NZ), 1)
    row = lax.broadcasted_iota(jnp.int32, (8, NZ), 0)
    for x in range(2):
        for o in range(PER):
            base = (x * PER + o) * 8
            for y in range(CY):
                lanes = slice(y * NZ, (y + 1) * NZ)
                if o < 13:
                    value = trans[o, x : x + 1, lanes]
                else:
                    value = storage[x : x + 1, lanes]
                block[base + y : base + y + 1, :] = value
            if o == 13:
                continue
            step = FORWARD[o]
            keep = None
            if step[2] == 1:
                keep = depth < NZ - 1
            if step[2] == -1:
                keep = depth > 0
            if step[1] == 1:
                inside = (row < CY - 1) | jnp.logical_not(last_y)
                keep = inside if keep is None else keep & inside
            if step[1] == -1:
                inside = (row > 0) | jnp.logical_not(first_y)
                keep = inside if keep is None else keep & inside
            if step[0] == 1 and x == 1:
                inside = (row >= 0) & jnp.logical_not(last_x)
                keep = inside if keep is None else keep & inside
            if keep is not None:
                block[base : base + 8, :] = jnp.where(keep, block[base : base + 8, :], 0.0)
    live = count[0, 0]
    lane = lax.broadcasted_iota(jnp.int32, (1, NZ), 1)
    base = 2 * PER * 8
    for r in range(4):
        lanes = slice(r * NZ, (r + 1) * NZ)
        block[base + r : base + r + 1, :] = cells[0, :, lanes].astype(f32)
        block[base + 4 + r : base + 5 + r, :] = jnp.where(
            lane + r * NZ < live, ftrans[0, :, lanes], 0.0
        )
    plane[0:72, :] = block[(PER + 4) * 8 : (PER + 13) * 8, :]


def by_parity(axis, body):
    odd = lax.rem(lax.axis_index(axis), 2)
    for k in range(2):
        pl.when(odd == k)(functools.partial(body, k))


def cells_at(cells, device):
    at = jnp.clip(device, 0, cells.shape[0] - 1)
    row = cells[at]
    return jnp.concatenate([row[:, r * NZ : (r + 1) * NZ] for r in range(4)], axis=0).astype(f32)


def partner_cells(cells):
    gx = lax.axis_index("gx")
    return cells_at(cells, gx + 1 - 2 * lax.rem(gx, 2))


def beyond_cells(cells):
    gx = lax.axis_index("gx")
    return cells_at(cells, gx - 2 + 4 * lax.rem(gx, 2))


def column_kernel(own, rp, ro, planes, cells, to_core, to_chip):
    gx = lax.axis_index("gx")
    lo2_base = jnp.maximum(gx // 2 - 1, 0) * 72
    has_lo2 = gx >= 2
    tile = own[224:232, :]
    other = ro[224:232, :]
    parts = (tile[0:4], partner_cells(cells), tile[4:8], other[0:4], beyond_cells(cells), other[4:8])
    for out in (to_core, to_chip):
        for k, part in enumerate(parts):
            out[FAULT_ROW + 4 * k : FAULT_ROW + 4 * k + 4, :] = part

    def fill(out, lo, hi, first, third, runs):
        for c in range(2):
            y = first + c
            base = c * COLBLOCK
            out[base : base + 9, :] = jnp.where(has_lo2, planes[pl.ds(lo2_base + y, 9, stride=8), :], 0.0)
            for k, ref in enumerate((lo, own, hi)):
                start = base + 9 + 28 * k
                out[start : start + 28, :] = ref[pl.ds(y, 28, stride=8), :]
        at = THIRD
        start = lo2_base + (runs[-1] - 4) * 8 + third
        out[at : at + 3, :] = jnp.where(has_lo2, planes[pl.ds(start, 3, stride=8), :], 0.0)
        at += 3
        for ref in (lo, own, hi):
            for x in range(2):
                for o in runs:
                    out[at : at + 3, :] = ref[pl.ds((x * PER + o) * 8 + third, 3, stride=8), :]
                    at += 3

    def for_x(odd_x):
        lo, hi = (rp, ro) if odd_x else (ro, rp)

        def for_y(odd_y):
            up, down = (to_chip, to_core) if odd_y else (to_core, to_chip)
            fill(up, lo, hi, CY - 2, CY - 3, (1, 10))
            fill(down, lo, hi, 0, 2, (4,))

        by_parity("gy", for_y)

    by_parity("gx", for_x)


def colour(z):
    half = z >> 1
    return half - 5 * ((half * 205) >> 10)


def slot_columns(rows):
    tall = jnp.transpose(jnp.concatenate(rows, axis=0))
    return [[tall[:, 4 * k + r : 4 * k + r + 1] for r in range(4)] for k in range(len(rows))]


def flat_cells(rows):
    row = jnp.concatenate([rows[r : r + 1] for r in range(4)], axis=1)
    return row.astype(jnp.int32) & 1023


def fill_far(far2, partner, live):
    lane = lax.broadcasted_iota(jnp.int32, (NZ, NZ), 1)
    for r in range(4):
        rows = slice(r * NZ, (r + 1) * NZ)
        match = (partner[r].astype(jnp.int32) & 127) == lane
        high = live[r].astype(bf16).astype(f32)
        far2[rows, 0:NZ] = jnp.where(match, high, 0.0).astype(bf16)
        far2[rows, NZ : 2 * NZ] = jnp.where(match, live[r] - high, 0.0).astype(bf16)


def fill_tint(eo, beyond, live):
    lane = lax.broadcasted_iota(jnp.int32, (NZ, NZ), 1)
    for r in range(4):
        tint = colour(beyond[r].astype(jnp.int32) & 127)
        high = live[r].astype(bf16).astype(f32)
        value = jnp.where((lane == tint) | (lane == 5), high, 0.0)
        value = jnp.where((lane == tint + 8) | (lane == 13), live[r] - high, value)
        eo[r * NZ : (r + 1) * NZ, :] = value.astype(bf16)


def fill_hot(hot, cells, columns):
    z128 = lax.broadcasted_iota(jnp.int32, (NZ, SLOTS), 0)
    for k, y in enumerate(columns):
        value = jnp.where(cells == z128 + y * NZ, 1.0, 0.0)
        hot[k * NZ : (k + 1) * NZ, :] = value.astype(bf16)


def pair_matrix(both):
    z8 = lax.broadcasted_iota(jnp.int32, (8, NZ), 1)
    e8 = lax.broadcasted_iota(jnp.int32, (8, NZ), 0)
    one = jnp.where((e8 == colour(z8)) | (e8 == 5), 1.0, 0.0).astype(bf16)
    one2 = jnp.concatenate([one, one], axis=1)
    matrix = both[:, :NZ] + both[:, NZ:]
    f2 = jnp.concatenate(split(matrix), axis=0)
    ft2 = jnp.concatenate(split(jnp.transpose(matrix)), axis=0)
    return f2, ft2, dot_nn(one2, ft2), dot_nn(one2, f2)


def fault_kernel(own, cells, f2, ft2, rf, far2, hot, both):
    partner, live = slot_columns([partner_cells(cells), own[228:232, :]])
    fill_far(far2, partner, live)
    fill_hot(hot, flat_cells(own[224:228, :]), range(CY))
    both[...] = dot_nn(hot[...], far2[...])
    for y in range(CY):
        f2[y], ft2[y], rf[0, y], rf[1, y] = pair_matrix(both[y * NZ : (y + 1) * NZ, :])


def third_kernel(ro, cells, rf, eo, hot, both):
    beyond, live = slot_columns([beyond_cells(cells), ro[228:232, :]])
    fill_tint(eo, beyond, live)
    fill_hot(hot, flat_cells(ro[224:228, :]), range(CY))
    both[...] = dot_nn(hot[...], eo[...])
    for y in range(CY):
        pieces = jnp.transpose(both[y * NZ : (y + 1) * NZ, :])
        rf[y] = pieces[:8] + pieces[8:16]


def through(value, matrix2):
    rows = value.shape[0]
    high, low = split(value)
    left = jnp.concatenate(
        [jnp.concatenate([high, high], axis=1), jnp.concatenate([low, low], axis=1)], axis=0
    )
    got = dot_nn(left, matrix2)
    return got[:rows] + got[rows:]


def main_kernel(
    own,
    rp,
    ro,
    planes,
    from_core,
    from_chip,
    f2,
    ft2,
    rf_pair,
    rf_third,
    out,
    w,
    wr,
    qc,
    inv,
    diag,
    fd,
    rf,
    qe,
    ap,
    tt,
    f2h,
    ft2h,
    far2,
    eo,
    hot,
):
    gx = lax.axis_index("gx")
    gy = lax.axis_index("gy")
    par = lax.rem(gx, 2)
    even = par == 0
    sgn = 1 - 2 * par
    p_own = jnp.where(even, 3, 2)
    p_far = jnp.where(even, 4, 1)
    p_third = jnp.where(even, 0, 5)
    p_fault = (p_own, p_far, p_third)
    z8 = lax.broadcasted_iota(jnp.int32, (8, NZ), 1)
    e8 = lax.broadcasted_iota(jnp.int32, (8, NZ), 0)

    def place(ref, count, first):
        for k in range(count):
            base = (first + k) * ROWS
            w[base + 3 : base + 11, :] = ref[8 * k : 8 * k + 8, :]

    def place_x(odd):
        lo, hi = (rp, ro) if odd else (ro, rp)
        place(lo, 28, PER)
        place(hi, 28, 5 * PER)

    lo2_base = jnp.maximum(gx // 2 - 1, 0) * 72
    for k in range(9):
        base = (4 + k) * ROWS
        value = planes[pl.ds(pl.multiple_of(lo2_base + 8 * k, 8), 8), :]
        w[base + 3 : base + 11, :] = jnp.where(gx >= 2, value, 0.0)
    place(own, 28, 3 * PER)
    by_parity("gx", place_x)

    def place_y(odd):
        yl, yh = (from_core, from_chip) if odd else (from_chip, from_core)
        for ref, row, third, runs in ((yl, 1, 0, (1, 10)), (yh, 11, 13, (4,))):
            for c in range(2):
                base = c * COLBLOCK
                w[pl.ds(4 * ROWS + row + c, 9, stride=ROWS), :] = ref[base : base + 9, :]
                w[pl.ds(PER * ROWS + row + c, 84, stride=ROWS), :] = ref[base + 9 : base + 93, :]
            at = THIRD
            for plane in range(7):
                for o in runs[-1:] if plane == 0 else runs:
                    start = (plane * PER + o) * ROWS + third
                    w[pl.ds(start, 3, stride=ROWS), :] = ref[at : at + 3, :]
                    at += 3

    by_parity("gy", place_y)
    for p in range(7):
        for o, step in enumerate(FORWARD):
            if step[2] == 0 or (p == 0 and o < 4):
                continue
            base = (p * PER + o) * ROWS
            shift = 1 if step[2] == 1 else NZ - 1
            wr[base : base + ROWS, :] = pltpu.roll(w[base : base + ROWS, :], shift, 1)

    fd[...] = jnp.zeros_like(fd)

    def put(column, k, value):
        rf[k, column] = value
        fd[pl.ds(p_fault[k] * 16 + column, 1), :] = value[5:6, :]

    for y in range(CY):
        put(y + 2, 0, rf_pair[0, y])
        put(y + 2, 1, rf_pair[1, y])
        put(y + 2, 2, rf_third[y])
    core_rows = from_core[FAULT_ROW : FAULT_ROW + 24, :]
    chip_rows = from_chip[FAULT_ROW : FAULT_ROW + 24, :]
    odd_y = lax.rem(gy, 2) == 1
    for side, first, second, columns in (
        (0, core_rows, chip_rows, ((0, 6), (1, 7))),
        (1, chip_rows, core_rows, ((10, 0), (11, 1))),
    ):
        rows = jnp.where(odd_y, first, second)
        cells, far, weight, cells_o, far_o, weight_o = (rows[4 * k : 4 * k + 4] for k in range(6))
        partner, live, beyond, live_o = slot_columns([far, weight, far_o, weight_o])
        fill_far(far2.at[side], partner, live)
        fill_tint(eo.at[side], beyond, live_o)
        ys = [y for _, y in columns]
        fill_hot(hot.at[side, 0], flat_cells(cells), ys)
        fill_hot(hot.at[side, 1], flat_cells(cells_o), ys)
        pair = dot_nn(hot[side, 0], far2[side])
        third = dot_nn(hot[side, 1], eo[side])
        for k, (column, y) in enumerate(columns):
            near, near_t, at_own, at_far = pair_matrix(pair[k * NZ : (k + 1) * NZ])
            if column in (1, 10):
                f2h[side] = near
                ft2h[side] = near_t
            put(column, 0, at_own)
            put(column, 1, at_far)
            pieces = jnp.transpose(third[k * NZ : (k + 1) * NZ])
            put(column, 2, pieces[:8] + pieces[8:16])

    r16 = lax.broadcasted_iota(jnp.int32, (16, NZ), 0)
    z16 = lax.broadcasted_iota(jnp.int32, (16, NZ), 1)
    even_y = (r16 & 1) == 0
    even_z = (z16 & 1) == 0
    for p in range(6):
        base = p + 1

        def weight(dx, dy, dz):
            if (dx, dy, dz) in OFFSET:
                start = (base * PER + OFFSET[dx, dy, dz]) * ROWS + 1
                return w[start : start + 16, :]
            o = OFFSET[-dx, -dy, -dz]
            start = ((base + dx) * PER + o) * ROWS + 1 + dy
            return (w if dz == 0 else wr)[start : start + 16, :]

        near = 1 if p % 2 == 0 else -1
        sums = {}
        for dz in (-1, 0, 1):
            got = {}
            for dx in (-1, 0, 1):
                below, above = weight(dx, -1, dz), weight(dx, 1, dz)
                got[dx, 0] = jnp.where(even_y, above, below)
                if (dx, dz) != (0, 0):
                    got[dx, 0] = got[dx, 0] + weight(dx, 0, dz)
                got[dx, 1] = jnp.where(even_y, below, above)
            for sy in range(2):
                sums[0, sy, dz] = got[0, sy] + got[near, sy]
                sums[1, sy, dz] = got[-near, sy]
        total = w[(base * PER + 13) * ROWS + 1 : (base * PER + 13) * ROWS + 17, :]
        total = total + fd[p * 16 : p * 16 + 16, :]
        r = []
        for sx in range(2):
            for sy in range(2):
                down, same, up = (sums[sx, sy, dz] for dz in (-1, 0, 1))
                r.append(same + jnp.where(even_z, up, down))
                r.append(jnp.where(even_z, down, up))
        for value in r:
            total = total + value
        total = jnp.where(total == 0.0, 1.0, total)
        scale = damping / total
        diag[p * 16 : p * 16 + 16, :] = total
        inv[p * 16 : p * 16 + 16, :] = scale
        for k, value in enumerate(r):
            value = value * scale
            if k == 0:
                value = value + (1.0 - damping)
            qc[(p * 8 + k) * 16 : (p * 8 + k) * 16 + 16, :] = value

    beside = jnp.where((z8 & 1) == 0, z8 - 1, z8 + 1)
    mask_own = jnp.where(e8 == colour(z8), 1.0, 0.0)
    mask_oth = jnp.where(e8 == colour(beside + 10), 1.0, 0.0)
    rows5 = jnp.where(e8 < 5, 1.0, 0.0)

    def spread(c, carry):
        for p in range(6):
            for lat in range(4):
                at = (p * 8 + 2 * lat) * 16 + c
                qe[p, c, lat] = (
                    qc[pl.ds(at, 1), :] * mask_own + qc[pl.ds(at + 16, 1), :] * mask_oth
                )
        for k, plane in enumerate(p_fault):
            qe[plane, c, 2] = qe[plane, c, 2] + rf[k, c] * (
                inv[pl.ds(plane * 16 + c, 1), :] * rows5
            )
        return carry

    lax.fori_loop(0, 12, spread, 0)

    def apply_column(p, y, odd_y):
        odd_x = p % 2
        acc = {}
        for dx in (-1, 0, 1):
            for dy in (-1, 0, 1):
                q = [qe[p + dx, y + dy, lat] for lat in range(4)]
                own_x = dx if (dx == 1 and odd_x) or (dx == -1 and not odd_x) else 0
                own_y = dy if (dy == 1 and odd_y) or (dy == -1 and not odd_y) else 0
                oth_x = own_x + (1 if (p + dx) % 2 else -1)
                oth_y = own_y + (1 if (odd_y + dy) % 2 else -1)
                for dz in (-1, 0, 1):
                    if (dx, dy, dz) == (0, 0, 0):
                        continue
                    if (dx, dy, dz) in OFFSET:
                        at = ((p + 1) * PER + OFFSET[dx, dy, dz]) * ROWS + y + 1
                        ref = w if dz == 0 else wr
                    else:
                        at = ((p + 1 + dx) * PER + OFFSET[-dx, -dy, -dz]) * ROWS + y + 1 + dy
                        ref = w
                    wt = ref[pl.ds(at, 1), :]
                    for lat in range(4):
                        lx = oth_x if lat >= 2 else own_x
                        ly = oth_y if lat % 2 else own_y
                        value = wt * q[lat]
                        key = (lx, ly, dz)
                        acc[key] = acc[key] + value if key in acc else value
        centre = diag[pl.ds(p * 16 + y, 1), :]
        for lx in (-1, 0, 1):
            for ly in (-1, 0, 1):
                total = acc[lx, ly, 0]
                total = total + pltpu.roll(acc[lx, ly, 1], NZ - 1, 1)
                total = total + pltpu.roll(acc[lx, ly, -1], 1, 1)
                own_lat = None
                sx = {0: 0, (1 if odd_x else -1): 1}.get(lx)
                sy = {0: 0, (1 if odd_y else -1): 1}.get(ly)
                if sx is not None and sy is not None:
                    own_lat = 2 * sx + sy
                if own_lat is None:
                    total = -total
                else:
                    total = centre * qe[p, y, own_lat] - total
                ap[p - 1, y - 1, lx + 1, ly + 1] = total

    def apply_pair(k, carry):
        for p in range(1, 5):
            apply_column(p, 2 * k + 1, 1)
            apply_column(p, 2 * k + 2, 0)
        return carry

    lax.fori_loop(0, 5, apply_pair, 0)

    def fault_apply(c, f2c, ft2c):
        ly_oth = 2 * (c % 2)
        for plane, source, x_own, matrix in (
            (p_own, p_far, 1 + sgn, ft2c),
            (p_far, p_own, 1 - sgn, f2c),
        ):
            total = through(qe[source, c].reshape(32, NZ), matrix)
            for lat in range(4):
                lx = 1 if lat >= 2 else x_own
                ly = ly_oth if lat % 2 else 1
                ap[plane - 1, c - 1, lx, ly] = ap[plane - 1, c - 1, lx, ly] - total[8 * lat : 8 * lat + 8]

    for y in range(CY):
        fault_apply(y + 2, f2[y], ft2[y])
    fault_apply(1, f2h[0], ft2h[0])
    fault_apply(10, f2h[1], ft2h[1])

    x_coarse = lax.rem(gx, 5) + 5
    a_of = [lax.rem(x_coarse + d, 5) for d in range(-2, 3)]

    def b_of(coarse_y, d):
        return lax.rem(gy * (CY // 2) + coarse_y + d + 5, 5)

    def gather(pair, carry):
        for half in range(2):
            coarse_y = 2 * pair + half
            columns = []
            for x in range(-1, 3):
                for y in range(-1, 3):
                    sx = 0 if x in (0, 1) else 1
                    sy = 0 if y in (0, 1) else 1
                    columns.append((x, y, 2 * sx + sy, (-1, 0, 0, 1)[x + 1], (-1, 0, 0, 1)[y + 1]))
            for zk in range(2):
                acc = {}
                for x, y, lat, ax, ay in columns:
                    c = 2 * coarse_y + y + 2
                    q = qc[pl.ds(((x + 2) * 8 + 2 * lat + zk) * 16 + c, 1), :]
                    for lx in range(3):
                        for ly in range(3):
                            value = q * ap[x + 1, c - 1, lx, ly]
                            key = (ax + lx - 1, ay + ly - 1)
                            acc[key] = acc[key] + value if key in acc else value
                lane = half * 256 + zk * NZ
                for (dx, dy), value in acc.items():
                    tt[pair, a_of[dx + 2], b_of(coarse_y, dy), :, lane : lane + NZ] = value
        return carry

    lax.fori_loop(0, 2, gather, 0)

    for y in range(CY):
        c = y + 2
        coarse_y = y // 2
        lane = (coarse_y % 2) * 256
        value = ap[p_far - 1, c - 1].reshape(72, NZ) * inv[pl.ds(p_far * 16 + c, 1), :]
        total = through(value, ft2[y])
        for lx in range(3):
            a = lax.rem(x_coarse + lx - 1 + sgn, 5)
            for ly in range(3):
                b = b_of(coarse_y, ly - 1)
                at = 8 * (3 * lx + ly)
                place_at = tt.at[coarse_y // 2, a, b, :, lane : lane + NZ]
                place_at[...] = place_at[...] + total[at : at + 8]

    kz = lax.broadcasted_iota(jnp.int32, (512, NZ), 0)
    kout = lax.broadcasted_iota(jnp.int32, (512, NZ), 1)
    z_in = kz & 127
    is_oth = ((kz >> 7) & 1) == 1
    target = jnp.where(
        is_oth, (z_in >> 1) + jnp.where((z_in & 1) == 0, -1, 1), z_in >> 1
    )
    fits = (target == (kout & 63)) & ((kz >> 8) == (kout >> 6))
    collect = jnp.where(fits, 1.0, 0.0).astype(bf16)
    for pair in range(2):
        high, low = split(tt[pair].reshape(200, 512))
        got = (dot_nn(high, collect) + dot_nn(low, collect)) * 0.125
        for k in range(25):
            out[5 * k : 5 * k + 5, 0, pair * NZ : (pair + 1) * NZ] = got[8 * k : 8 * k + 5]


def send(value, axis, target):
    peers = lax.axis_size(axis)
    pairs = [(i, target(i)) for i in range(peers) if target(i) is not None]
    return lax.ppermute(value, axis, [(i, j) for i, j in pairs if 0 <= j < peers])


def partner_of(i):
    return i ^ 1


def other_of(i):
    return i + 1 if i % 2 else i - 1


VMEM = pl.BlockSpec(memory_space=pltpu.VMEM)
HBM = pl.BlockSpec(memory_space=pltpu.HBM)


def params(mib):
    return pltpu.CompilerParams(vmem_limit_bytes=mib * 1024 * 1024)


def sds(*shape, dtype=f32):
    return jax.ShapeDtypeStruct(shape, dtype)


def per_device(trans, storage, fault_cells, fault_count, fault_trans):
    peers = (lax.axis_size("gx"), lax.axis_size("gy"))
    cells = lax.all_gather(fault_cells, "gx", tiled=True)
    sources = [
        pltpu.with_memory_space_constraint(array, pltpu.HBM)
        for array in (trans, storage, fault_cells, fault_trans)
    ]
    own, plane = pl.pallas_call(
        functools.partial(pack_kernel, peers),
        out_shape=(sds(232, NZ), sds(72, NZ)),
        in_specs=[pl.BlockSpec(memory_space=pltpu.SMEM)] + [HBM] * 4,
        out_specs=(VMEM, VMEM),
        scratch_shapes=[pltpu.VMEM(array.shape, array.dtype) for array in sources]
        + [pltpu.SemaphoreType.DMA((4,))],
        compiler_params=params(16),
        name="pack",
    )(fault_count, *sources)
    groups = [list(range(k, peers[0], 2)) for k in range(2)]
    planes = lax.all_gather(plane, "gx", axis_index_groups=groups, tiled=True)
    rp = send(own, "gx", partner_of)
    ro = send(own, "gx", other_of)
    pieces = sds(CY, 2 * NZ, NZ, dtype=bf16)
    f2, ft2, rf_pair = pl.pallas_call(
        fault_kernel,
        out_shape=(pieces, pieces, sds(2, CY, 8, NZ)),
        in_specs=[VMEM] * 2,
        out_specs=(VMEM,) * 3,
        scratch_shapes=[
            pltpu.VMEM((SLOTS, 2 * NZ), bf16),
            pltpu.VMEM((CY * NZ, SLOTS), bf16),
            pltpu.VMEM((CY * NZ, 2 * NZ), f32),
        ],
        compiler_params=params(16),
        cost_estimate=pl.CostEstimate(flops=2 * 10**9, bytes_accessed=2**21, transcendentals=0),
        name="faults",
    )(own, cells)
    to_core, to_chip = pl.pallas_call(
        column_kernel,
        out_shape=(sds(Y_ROWS, NZ), sds(Y_ROWS, NZ)),
        in_specs=[VMEM] * 5,
        out_specs=(VMEM,) * 2,
        compiler_params=params(16),
        name="columns",
    )(own, rp, ro, planes, cells)
    from_chip = send(to_chip, "gy", other_of)
    from_core = send(to_core, "gy", partner_of)
    rf_third = pl.pallas_call(
        third_kernel,
        out_shape=sds(CY, 8, NZ),
        in_specs=[VMEM] * 2,
        out_specs=VMEM,
        scratch_shapes=[
            pltpu.VMEM((SLOTS, NZ), bf16),
            pltpu.VMEM((CY * NZ, SLOTS), bf16),
            pltpu.VMEM((CY * NZ, NZ), f32),
        ],
        compiler_params=params(16),
        cost_estimate=pl.CostEstimate(flops=10**9, bytes_accessed=2**20, transcendentals=0),
        name="third",
    )(ro, cells)
    return pl.pallas_call(
        main_kernel,
        out_shape=sds(125, 1, 256),
        in_specs=[VMEM] * 10,
        out_specs=VMEM,
        scratch_shapes=[
            pltpu.VMEM((7 * PER * ROWS, NZ), f32),
            pltpu.VMEM((7 * PER * ROWS, NZ), f32),
            pltpu.VMEM((6 * 8 * 16, NZ), f32),
            pltpu.VMEM((6 * 16, NZ), f32),
            pltpu.VMEM((6 * 16, NZ), f32),
            pltpu.VMEM((6 * 16, NZ), f32),
            pltpu.VMEM((3, 12, 8, NZ), f32),
            pltpu.VMEM((6, 12, 4, 8, NZ), f32),
            pltpu.VMEM((4, 10, 3, 3, 8, NZ), f32),
            pltpu.VMEM((2, 5, 5, 8, 512), f32),
            pltpu.VMEM((2, 2 * NZ, NZ), bf16),
            pltpu.VMEM((2, 2 * NZ, NZ), bf16),
            pltpu.VMEM((2, SLOTS, 2 * NZ), bf16),
            pltpu.VMEM((2, SLOTS, NZ), bf16),
            pltpu.VMEM((2, 2, 2 * NZ, SLOTS), bf16),
        ],
        compiler_params=params(24),
        name="galerkin",
    )(own, rp, ro, planes, from_core, from_chip, f2, ft2, rf_pair, rf_third)


def solution(mesh):
    placed = (
        P(None, "gx", "gy"),
        P("gx", "gy"),
        P("gx", "gy", None),
        P("gx", "gy"),
        P("gx", "gy", None),
    )
    return jax.shard_map(
        per_device, mesh=mesh, in_specs=placed, out_specs=P(None, "gx", "gy"), check_vma=False
    )
```

```python
import functools

import jax
import jax.numpy as jnp
from jax import lax
from jax.experimental import pallas as pl
from jax.experimental.pallas import tpu as pltpu
from jax.sharding import PartitionSpec as P

NZ = 128
CY = 8
SLOTS = 512

FORWARD = (
    (0, 0, 1),
    (0, 1, -1),
    (0, 1, 0),
    (0, 1, 1),
    (1, -1, -1),
    (1, -1, 0),
    (1, -1, 1),
    (1, 0, -1),
    (1, 0, 0),
    (1, 0, 1),
    (1, 1, -1),
    (1, 1, 0),
    (1, 1, 1),
)
OFFSET = {step: k for k, step in enumerate(FORWARD)}
damping = 2.0 / 3.0

ROWS = 24
PER = 14
COLBLOCK = 93
THIRD = 2 * COLBLOCK
FAULT_ROW, Y_ROWS = 232, 256

f32 = jnp.float32
bf16 = jnp.bfloat16


def dot_nn(a, b):
    return lax.dot_general(a, b, (((1,), (0,)), ((), ())), preferred_element_type=f32)


def split(value):
    high = value.astype(bf16)
    return high, (value - high.astype(f32)).astype(bf16)


def pack_kernel(peers, count, *refs):
    sources, (block, plane, tile), targets, sems = refs[:4], refs[4:7], refs[7:11], refs[11]
    copies = [
        pltpu.make_async_copy(src, dst, sems.at[k])
        for k, (src, dst) in enumerate(zip(sources, targets))
    ]
    for copy in copies:
        copy.start()
    for copy in copies:
        copy.wait()
    trans, storage, cells, ftrans = targets
    last_x = lax.axis_index("gx") == peers[0] - 1
    first_y = lax.axis_index("gy") == 0
    last_y = lax.axis_index("gy") == peers[1] - 1
    depth = lax.broadcasted_iota(jnp.int32, (8, NZ), 1)
    row = lax.broadcasted_iota(jnp.int32, (8, NZ), 0)
    for x in range(2):
        for o in range(PER):
            base = (x * PER + o) * 8
            for y in range(CY):
                lanes = slice(y * NZ, (y + 1) * NZ)
                if o < 13:
                    value = trans[o, x : x + 1, lanes]
                else:
                    value = storage[x : x + 1, lanes]
                block[base + y : base + y + 1, :] = value
            if o == 13:
                continue
            step = FORWARD[o]
            keep = None
            if step[2] == 1:
                keep = depth < NZ - 1
            if step[2] == -1:
                keep = depth > 0
            if step[1] == 1:
                inside = (row < CY - 1) | jnp.logical_not(last_y)
                keep = inside if keep is None else keep & inside
            if step[1] == -1:
                inside = (row > 0) | jnp.logical_not(first_y)
                keep = inside if keep is None else keep & inside
            if step[0] == 1 and x == 1:
                inside = (row >= 0) & jnp.logical_not(last_x)
                keep = inside if keep is None else keep & inside
            if keep is not None:
                block[base : base + 8, :] = jnp.where(keep, block[base : base + 8, :], 0.0)
    live = count[0, 0]
    lane = lax.broadcasted_iota(jnp.int32, (1, NZ), 1)
    base = 2 * PER * 8
    for r in range(4):
        lanes = slice(r * NZ, (r + 1) * NZ)
        block[base + r : base + r + 1, :] = cells[0, :, lanes].astype(f32)
        block[base + 4 + r : base + 5 + r, :] = jnp.where(
            lane + r * NZ < live, ftrans[0, :, lanes], 0.0
        )
    plane[0:72, :] = block[(PER + 4) * 8 : (PER + 13) * 8, :]
    plane[72:80, :] = block[base : base + 8, :]
    tile[...] = block[base : base + 8, :]


def by_parity(axis, body):
    odd = lax.rem(lax.axis_index(axis), 2)
    for k in range(2):
        pl.when(odd == k)(functools.partial(body, k))


class Masked:
    def __init__(self, ref, due):
        self.ref, self.due = ref, due

    def __getitem__(self, index):
        return jnp.where(self.due, self.ref[index], 0.0)


def has_other(axis, peers):
    at = lax.axis_index(axis)
    return jnp.where(lax.rem(at, 2) == 0, at > 0, at < peers - 1)


def column_kernel(peers, own, rp, ro, rs, rt, to_core, to_chip):
    ro = Masked(ro, has_other("gx", peers[0]))
    lo2 = Masked(rs, lax.axis_index("gx") >= 2)
    tile = own[224:232, :]
    other = ro[224:232, :]
    parts = (tile[0:4], rp[224:228, :], tile[4:8], other[0:4], beyond_cells(rs, rt), other[4:8])
    for out in (to_core, to_chip):
        for k, part in enumerate(parts):
            out[FAULT_ROW + 4 * k : FAULT_ROW + 4 * k + 4, :] = part

    def fill(out, lo, hi, first, third, runs):
        for c in range(2):
            y = first + c
            base = c * COLBLOCK
            out[base : base + 9, :] = lo2[pl.ds(y, 9, stride=8), :]
            for k, ref in enumerate((lo, own, hi)):
                start = base + 9 + 28 * k
                out[start : start + 28, :] = ref[pl.ds(y, 28, stride=8), :]
        at = THIRD
        out[at : at + 3, :] = lo2[pl.ds((runs[-1] - 4) * 8 + third, 3, stride=8), :]
        at += 3
        for ref in (lo, own, hi):
            for x in range(2):
                for o in runs:
                    out[at : at + 3, :] = ref[pl.ds((x * PER + o) * 8 + third, 3, stride=8), :]
                    at += 3

    def for_x(odd_x):
        lo, hi = (rp, ro) if odd_x else (ro, rp)

        def for_y(odd_y):
            up, down = (to_chip, to_core) if odd_y else (to_core, to_chip)
            fill(up, lo, hi, CY - 2, CY - 3, (1, 10))
            fill(down, lo, hi, 0, 2, (4,))

        by_parity("gy", for_y)

    by_parity("gx", for_x)


def colour(z):
    half = z >> 1
    return half - 5 * ((half * 205) >> 10)


def slot_columns(rows):
    tall = jnp.transpose(jnp.concatenate(rows, axis=0))
    return [[tall[:, 4 * k + r : 4 * k + r + 1] for r in range(4)] for k in range(len(rows))]


def flat_cells(rows):
    row = jnp.concatenate([rows[r : r + 1] for r in range(4)], axis=1)
    return row.astype(jnp.int32) & 1023


def fill_far(far2, partner, live):
    lane = lax.broadcasted_iota(jnp.int32, (NZ, NZ), 1)
    for r in range(4):
        rows = slice(r * NZ, (r + 1) * NZ)
        match = (partner[r].astype(jnp.int32) & 127) == lane
        high = live[r].astype(bf16).astype(f32)
        far2[rows, 0:NZ] = jnp.where(match, high, 0.0).astype(bf16)
        far2[rows, NZ : 2 * NZ] = jnp.where(match, live[r] - high, 0.0).astype(bf16)


def fill_tint(eo, beyond, live):
    lane = lax.broadcasted_iota(jnp.int32, (NZ, NZ), 1)
    for r in range(4):
        tint = colour(beyond[r].astype(jnp.int32) & 127)
        high = live[r].astype(bf16).astype(f32)
        value = jnp.where((lane == tint) | (lane == 5), high, 0.0)
        value = jnp.where((lane == tint + 8) | (lane == 13), live[r] - high, value)
        eo[r * NZ : (r + 1) * NZ, :] = value.astype(bf16)


def fill_hot(hot, cells, columns):
    z128 = lax.broadcasted_iota(jnp.int32, (NZ, SLOTS), 0)
    for k, y in enumerate(columns):
        value = jnp.where(cells == z128 + y * NZ, 1.0, 0.0)
        hot[k * NZ : (k + 1) * NZ, :] = value.astype(bf16)


def pair_matrix(both):
    z8 = lax.broadcasted_iota(jnp.int32, (8, NZ), 1)
    e8 = lax.broadcasted_iota(jnp.int32, (8, NZ), 0)
    one = jnp.where((e8 == colour(z8)) | (e8 == 5), 1.0, 0.0).astype(bf16)
    one2 = jnp.concatenate([one, one], axis=1)
    matrix = both[:, :NZ] + both[:, NZ:]
    f2 = jnp.concatenate(split(matrix), axis=0)
    ft2 = jnp.concatenate(split(jnp.transpose(matrix)), axis=0)
    return f2, ft2, dot_nn(one2, ft2), dot_nn(one2, f2)


def fault_kernel(own, rp, f2, ft2, rf, far2, hot, both):
    partner, live = slot_columns([rp[224:228, :], own[228:232, :]])
    fill_far(far2, partner, live)
    fill_hot(hot, flat_cells(own[224:228, :]), range(CY))
    both[...] = dot_nn(hot[...], far2[...])
    for y in range(CY):
        f2[y], ft2[y], rf[0, y], rf[1, y] = pair_matrix(both[y * NZ : (y + 1) * NZ, :])


def beyond_cells(rs, rt):
    return jnp.where(lax.rem(lax.axis_index("gx"), 2) == 0, rs[72:76, :], rt[0:4, :])


def third_kernel(peers, ro, rs, rt, rf, eo, hot, both):
    ro = Masked(ro, has_other("gx", peers[0]))
    beyond, live = slot_columns([beyond_cells(rs, rt), ro[228:232, :]])
    fill_tint(eo, beyond, live)
    fill_hot(hot, flat_cells(ro[224:228, :]), range(CY))
    both[...] = dot_nn(hot[...], eo[...])
    for y in range(CY):
        pieces = jnp.transpose(both[y * NZ : (y + 1) * NZ, :])
        rf[y] = pieces[:8] + pieces[8:16]


def through(value, matrix2):
    rows = value.shape[0]
    high, low = split(value)
    left = jnp.concatenate(
        [jnp.concatenate([high, high], axis=1), jnp.concatenate([low, low], axis=1)], axis=0
    )
    got = dot_nn(left, matrix2)
    return got[:rows] + got[rows:]


def main_kernel(
    peers,
    own,
    rp,
    ro,
    rs,
    from_core,
    from_chip,
    f2,
    ft2,
    rf_pair,
    rf_third,
    out,
    w,
    wr,
    qc,
    inv,
    diag,
    fd,
    rf,
    qe,
    ap,
    tt,
    f2h,
    ft2h,
    far2,
    eo,
    hot,
):
    gx = lax.axis_index("gx")
    gy = lax.axis_index("gy")
    ro = Masked(ro, has_other("gx", peers[0]))
    from_chip = Masked(from_chip, has_other("gy", peers[1]))
    par = lax.rem(gx, 2)
    even = par == 0
    sgn = 1 - 2 * par
    p_own = jnp.where(even, 3, 2)
    p_far = jnp.where(even, 4, 1)
    p_third = jnp.where(even, 0, 5)
    p_fault = (p_own, p_far, p_third)
    z8 = lax.broadcasted_iota(jnp.int32, (8, NZ), 1)
    e8 = lax.broadcasted_iota(jnp.int32, (8, NZ), 0)

    def place(ref, count, first):
        for k in range(count):
            base = (first + k) * ROWS
            w[base + 3 : base + 11, :] = ref[8 * k : 8 * k + 8, :]

    def place_x(odd):
        lo, hi = (rp, ro) if odd else (ro, rp)
        place(lo, 28, PER)
        place(hi, 28, 5 * PER)

    place(Masked(rs, gx >= 2), 9, 4)
    place(own, 28, 3 * PER)
    by_parity("gx", place_x)

    def place_y(odd):
        yl, yh = (from_core, from_chip) if odd else (from_chip, from_core)
        for ref, row, third, runs in ((yl, 1, 0, (1, 10)), (yh, 11, 13, (4,))):
            for c in range(2):
                base = c * COLBLOCK
                w[pl.ds(4 * ROWS + row + c, 9, stride=ROWS), :] = ref[base : base + 9, :]
                w[pl.ds(PER * ROWS + row + c, 84, stride=ROWS), :] = ref[base + 9 : base + 93, :]
            at = THIRD
            for plane in range(7):
                for o in runs[-1:] if plane == 0 else runs:
                    start = (plane * PER + o) * ROWS + third
                    w[pl.ds(start, 3, stride=ROWS), :] = ref[at : at + 3, :]
                    at += 3

    by_parity("gy", place_y)
    for p in range(7):
        for o, step in enumerate(FORWARD):
            if step[2] == 0 or (p == 0 and o < 4):
                continue
            base = (p * PER + o) * ROWS
            shift = 1 if step[2] == 1 else NZ - 1
            wr[base : base + ROWS, :] = pltpu.roll(w[base : base + ROWS, :], shift, 1)

    fd[...] = jnp.zeros_like(fd)

    def put(column, k, value):
        rf[k, column] = value
        fd[pl.ds(p_fault[k] * 16 + column, 1), :] = value[5:6, :]

    for y in range(CY):
        put(y + 2, 0, rf_pair[0, y])
        put(y + 2, 1, rf_pair[1, y])
        put(y + 2, 2, rf_third[y])
    core_rows = from_core[FAULT_ROW : FAULT_ROW + 24, :]
    chip_rows = from_chip[FAULT_ROW : FAULT_ROW + 24, :]
    odd_y = lax.rem(gy, 2) == 1
    for side, first, second, columns in (
        (0, core_rows, chip_rows, ((0, 6), (1, 7))),
        (1, chip_rows, core_rows, ((10, 0), (11, 1))),
    ):
        rows = jnp.where(odd_y, first, second)
        cells, far, weight, cells_o, far_o, weight_o = (rows[4 * k : 4 * k + 4] for k in range(6))
        partner, live, beyond, live_o = slot_columns([far, weight, far_o, weight_o])
        fill_far(far2.at[side], partner, live)
        fill_tint(eo.at[side], beyond, live_o)
        ys = [y for _, y in columns]
        fill_hot(hot.at[side, 0], flat_cells(cells), ys)
        fill_hot(hot.at[side, 1], flat_cells(cells_o), ys)
        pair = dot_nn(hot[side, 0], far2[side])
        third = dot_nn(hot[side, 1], eo[side])
        for k, (column, y) in enumerate(columns):
            near, near_t, at_own, at_far = pair_matrix(pair[k * NZ : (k + 1) * NZ])
            if column in (1, 10):
                f2h[side] = near
                ft2h[side] = near_t
            put(column, 0, at_own)
            put(column, 1, at_far)
            pieces = jnp.transpose(third[k * NZ : (k + 1) * NZ])
            put(column, 2, pieces[:8] + pieces[8:16])

    r16 = lax.broadcasted_iota(jnp.int32, (16, NZ), 0)
    z16 = lax.broadcasted_iota(jnp.int32, (16, NZ), 1)
    even_y = (r16 & 1) == 0
    even_z = (z16 & 1) == 0
    for p in range(6):
        base = p + 1

        def weight(dx, dy, dz):
            if (dx, dy, dz) in OFFSET:
                start = (base * PER + OFFSET[dx, dy, dz]) * ROWS + 1
                return w[start : start + 16, :]
            o = OFFSET[-dx, -dy, -dz]
            start = ((base + dx) * PER + o) * ROWS + 1 + dy
            return (w if dz == 0 else wr)[start : start + 16, :]

        near = 1 if p % 2 == 0 else -1
        sums = {}
        for dz in (-1, 0, 1):
            got = {}
            for dx in (-1, 0, 1):
                below, above = weight(dx, -1, dz), weight(dx, 1, dz)
                got[dx, 0] = jnp.where(even_y, above, below)
                if (dx, dz) != (0, 0):
                    got[dx, 0] = got[dx, 0] + weight(dx, 0, dz)
                got[dx, 1] = jnp.where(even_y, below, above)
            for sy in range(2):
                sums[0, sy, dz] = got[0, sy] + got[near, sy]
                sums[1, sy, dz] = got[-near, sy]
        total = w[(base * PER + 13) * ROWS + 1 : (base * PER + 13) * ROWS + 17, :]
        total = total + fd[p * 16 : p * 16 + 16, :]
        r = []
        for sx in range(2):
            for sy in range(2):
                down, same, up = (sums[sx, sy, dz] for dz in (-1, 0, 1))
                r.append(same + jnp.where(even_z, up, down))
                r.append(jnp.where(even_z, down, up))
        for value in r:
            total = total + value
        total = jnp.where(total == 0.0, 1.0, total)
        scale = damping / total
        diag[p * 16 : p * 16 + 16, :] = total
        inv[p * 16 : p * 16 + 16, :] = scale
        for k, value in enumerate(r):
            value = value * scale
            if k == 0:
                value = value + (1.0 - damping)
            qc[(p * 8 + k) * 16 : (p * 8 + k) * 16 + 16, :] = value

    beside = jnp.where((z8 & 1) == 0, z8 - 1, z8 + 1)
    mask_own = jnp.where(e8 == colour(z8), 1.0, 0.0)
    mask_oth = jnp.where(e8 == colour(beside + 10), 1.0, 0.0)
    rows5 = jnp.where(e8 < 5, 1.0, 0.0)

    def spread(c, carry):
        for p in range(6):
            for lat in range(4):
                at = (p * 8 + 2 * lat) * 16 + c
                qe[p, c, lat] = (
                    qc[pl.ds(at, 1), :] * mask_own + qc[pl.ds(at + 16, 1), :] * mask_oth
                )
        for k, plane in enumerate(p_fault):
            qe[plane, c, 2] = qe[plane, c, 2] + rf[k, c] * (
                inv[pl.ds(plane * 16 + c, 1), :] * rows5
            )
        return carry

    lax.fori_loop(0, 12, spread, 0)

    def apply_column(p, y, odd_y):
        odd_x = p % 2
        acc = {}
        for dx in (-1, 0, 1):
            for dy in (-1, 0, 1):
                q = [qe[p + dx, y + dy, lat] for lat in range(4)]
                own_x = dx if (dx == 1 and odd_x) or (dx == -1 and not odd_x) else 0
                own_y = dy if (dy == 1 and odd_y) or (dy == -1 and not odd_y) else 0
                oth_x = own_x + (1 if (p + dx) % 2 else -1)
                oth_y = own_y + (1 if (odd_y + dy) % 2 else -1)
                for dz in (-1, 0, 1):
                    if (dx, dy, dz) == (0, 0, 0):
                        continue
                    if (dx, dy, dz) in OFFSET:
                        at = ((p + 1) * PER + OFFSET[dx, dy, dz]) * ROWS + y + 1
                        ref = w if dz == 0 else wr
                    else:
                        at = ((p + 1 + dx) * PER + OFFSET[-dx, -dy, -dz]) * ROWS + y + 1 + dy
                        ref = w
                    wt = ref[pl.ds(at, 1), :]
                    for lat in range(4):
                        lx = oth_x if lat >= 2 else own_x
                        ly = oth_y if lat % 2 else own_y
                        value = wt * q[lat]
                        key = (lx, ly, dz)
                        acc[key] = acc[key] + value if key in acc else value
        centre = diag[pl.ds(p * 16 + y, 1), :]
        for lx in (-1, 0, 1):
            for ly in (-1, 0, 1):
                total = acc[lx, ly, 0]
                total = total + pltpu.roll(acc[lx, ly, 1], NZ - 1, 1)
                total = total + pltpu.roll(acc[lx, ly, -1], 1, 1)
                own_lat = None
                sx = {0: 0, (1 if odd_x else -1): 1}.get(lx)
                sy = {0: 0, (1 if odd_y else -1): 1}.get(ly)
                if sx is not None and sy is not None:
                    own_lat = 2 * sx + sy
                if own_lat is None:
                    total = -total
                else:
                    total = centre * qe[p, y, own_lat] - total
                ap[p - 1, y - 1, lx + 1, ly + 1] = total

    def apply_pair(k, carry):
        for p in range(1, 5):
            apply_column(p, 2 * k + 1, 1)
            apply_column(p, 2 * k + 2, 0)
        return carry

    lax.fori_loop(0, 5, apply_pair, 0)

    def fault_apply(c, f2c, ft2c):
        ly_oth = 2 * (c % 2)
        for plane, source, x_own, matrix in (
            (p_own, p_far, 1 + sgn, ft2c),
            (p_far, p_own, 1 - sgn, f2c),
        ):
            total = through(qe[source, c].reshape(32, NZ), matrix)
            for lat in range(4):
                lx = 1 if lat >= 2 else x_own
                ly = ly_oth if lat % 2 else 1
                ap[plane - 1, c - 1, lx, ly] = ap[plane - 1, c - 1, lx, ly] - total[8 * lat : 8 * lat + 8]

    for y in range(CY):
        fault_apply(y + 2, f2[y], ft2[y])
    fault_apply(1, f2h[0], ft2h[0])
    fault_apply(10, f2h[1], ft2h[1])

    x_coarse = lax.rem(gx, 5) + 5
    a_of = [lax.rem(x_coarse + d, 5) for d in range(-2, 3)]

    def b_of(coarse_y, d):
        return lax.rem(gy * (CY // 2) + coarse_y + d + 5, 5)

    def gather(pair, carry):
        for half in range(2):
            coarse_y = 2 * pair + half
            columns = []
            for x in range(-1, 3):
                for y in range(-1, 3):
                    sx = 0 if x in (0, 1) else 1
                    sy = 0 if y in (0, 1) else 1
                    columns.append((x, y, 2 * sx + sy, (-1, 0, 0, 1)[x + 1], (-1, 0, 0, 1)[y + 1]))
            for zk in range(2):
                acc = {}
                for x, y, lat, ax, ay in columns:
                    c = 2 * coarse_y + y + 2
                    q = qc[pl.ds(((x + 2) * 8 + 2 * lat + zk) * 16 + c, 1), :]
                    for lx in range(3):
                        for ly in range(3):
                            value = q * ap[x + 1, c - 1, lx, ly]
                            key = (ax + lx - 1, ay + ly - 1)
                            acc[key] = acc[key] + value if key in acc else value
                lane = half * 256 + zk * NZ
                for (dx, dy), value in acc.items():
                    tt[pair, a_of[dx + 2], b_of(coarse_y, dy), :, lane : lane + NZ] = value
        return carry

    lax.fori_loop(0, 2, gather, 0)

    for y in range(CY):
        c = y + 2
        coarse_y = y // 2
        lane = (coarse_y % 2) * 256
        value = ap[p_far - 1, c - 1].reshape(72, NZ) * inv[pl.ds(p_far * 16 + c, 1), :]
        total = through(value, ft2[y])
        for lx in range(3):
            a = lax.rem(x_coarse + lx - 1 + sgn, 5)
            for ly in range(3):
                b = b_of(coarse_y, ly - 1)
                at = 8 * (3 * lx + ly)
                place_at = tt.at[coarse_y // 2, a, b, :, lane : lane + NZ]
                place_at[...] = place_at[...] + total[at : at + 8]

    kz = lax.broadcasted_iota(jnp.int32, (512, NZ), 0)
    kout = lax.broadcasted_iota(jnp.int32, (512, NZ), 1)
    z_in = kz & 127
    is_oth = ((kz >> 7) & 1) == 1
    target = jnp.where(
        is_oth, (z_in >> 1) + jnp.where((z_in & 1) == 0, -1, 1), z_in >> 1
    )
    fits = (target == (kout & 63)) & ((kz >> 8) == (kout >> 6))
    collect = jnp.where(fits, 1.0, 0.0).astype(bf16)
    for pair in range(2):
        high, low = split(tt[pair].reshape(200, 512))
        got = (dot_nn(high, collect) + dot_nn(low, collect)) * 0.125
        for k in range(25):
            out[5 * k : 5 * k + 5, 0, pair * NZ : (pair + 1) * NZ] = got[8 * k : 8 * k + 5]


def send(value, axis, target):
    peers = lax.axis_size(axis)
    return lax.ppermute(value, axis, [(i, target(i, peers)) for i in range(peers)])


def partner_of(i, peers):
    return i ^ 1


def other_of(i, peers):
    j = i + 1 if i % 2 else i - 1
    return j if 0 <= j < peers else i


def ahead_of(i, peers):
    return (i + 2) % peers


def odd_behind(i, peers):
    return (i - 2) % peers if i % 2 else i


VMEM = pl.BlockSpec(memory_space=pltpu.VMEM)
HBM = pl.BlockSpec(memory_space=pltpu.HBM)


def params(mib):
    return pltpu.CompilerParams(vmem_limit_bytes=mib * 1024 * 1024)


def sds(*shape, dtype=f32):
    return jax.ShapeDtypeStruct(shape, dtype)


def per_device(trans, storage, fault_cells, fault_count, fault_trans):
    peers = (lax.axis_size("gx"), lax.axis_size("gy"))
    sources = [
        pltpu.with_memory_space_constraint(array, pltpu.HBM)
        for array in (trans, storage, fault_cells, fault_trans)
    ]
    own, plane, tile = pl.pallas_call(
        functools.partial(pack_kernel, peers),
        out_shape=(sds(232, NZ), sds(80, NZ), sds(8, NZ)),
        in_specs=[pl.BlockSpec(memory_space=pltpu.SMEM)] + [HBM] * 4,
        out_specs=(VMEM,) * 3,
        scratch_shapes=[pltpu.VMEM(array.shape, array.dtype) for array in sources]
        + [pltpu.SemaphoreType.DMA((4,))],
        compiler_params=params(16),
        name="pack",
    )(fault_count, *sources)
    rp = send(own, "gx", partner_of)
    rs = send(plane, "gx", ahead_of)
    rt = send(tile, "gx", odd_behind)
    ro = send(own, "gx", other_of)
    pieces = sds(CY, 2 * NZ, NZ, dtype=bf16)
    f2, ft2, rf_pair = pl.pallas_call(
        fault_kernel,
        out_shape=(pieces, pieces, sds(2, CY, 8, NZ)),
        in_specs=[VMEM] * 2,
        out_specs=(VMEM,) * 3,
        scratch_shapes=[
            pltpu.VMEM((SLOTS, 2 * NZ), bf16),
            pltpu.VMEM((CY * NZ, SLOTS), bf16),
            pltpu.VMEM((CY * NZ, 2 * NZ), f32),
        ],
        compiler_params=params(16),
        cost_estimate=pl.CostEstimate(flops=2 * 10**9, bytes_accessed=2**21, transcendentals=0),
        name="faults",
    )(own, rp)
    to_core, to_chip = pl.pallas_call(
        functools.partial(column_kernel, peers),
        out_shape=(sds(Y_ROWS, NZ), sds(Y_ROWS, NZ)),
        in_specs=[VMEM] * 5,
        out_specs=(VMEM,) * 2,
        compiler_params=params(16),
        name="columns",
    )(own, rp, ro, rs, rt)
    from_chip = send(to_chip, "gy", other_of)
    from_core = send(to_core, "gy", partner_of)
    rf_third = pl.pallas_call(
        functools.partial(third_kernel, peers),
        out_shape=sds(CY, 8, NZ),
        in_specs=[VMEM] * 3,
        out_specs=VMEM,
        scratch_shapes=[
            pltpu.VMEM((SLOTS, NZ), bf16),
            pltpu.VMEM((CY * NZ, SLOTS), bf16),
            pltpu.VMEM((CY * NZ, NZ), f32),
        ],
        compiler_params=params(16),
        cost_estimate=pl.CostEstimate(flops=10**9, bytes_accessed=2**20, transcendentals=0),
        name="third",
    )(ro, rs, rt)
    return pl.pallas_call(
        functools.partial(main_kernel, peers),
        out_shape=sds(125, 1, 256),
        in_specs=[VMEM] * 10,
        out_specs=VMEM,
        scratch_shapes=[
            pltpu.VMEM((7 * PER * ROWS, NZ), f32),
            pltpu.VMEM((7 * PER * ROWS, NZ), f32),
            pltpu.VMEM((6 * 8 * 16, NZ), f32),
            pltpu.VMEM((6 * 16, NZ), f32),
            pltpu.VMEM((6 * 16, NZ), f32),
            pltpu.VMEM((6 * 16, NZ), f32),
            pltpu.VMEM((3, 12, 8, NZ), f32),
            pltpu.VMEM((6, 12, 4, 8, NZ), f32),
            pltpu.VMEM((4, 10, 3, 3, 8, NZ), f32),
            pltpu.VMEM((2, 5, 5, 8, 512), f32),
            pltpu.VMEM((2, 2 * NZ, NZ), bf16),
            pltpu.VMEM((2, 2 * NZ, NZ), bf16),
            pltpu.VMEM((2, SLOTS, 2 * NZ), bf16),
            pltpu.VMEM((2, SLOTS, NZ), bf16),
            pltpu.VMEM((2, 2, 2 * NZ, SLOTS), bf16),
        ],
        compiler_params=params(24),
        name="galerkin",
    )(own, rp, ro, rs, from_core, from_chip, f2, ft2, rf_pair, rf_third)


def solution(mesh):
    placed = (
        P(None, "gx", "gy"),
        P("gx", "gy"),
        P("gx", "gy", None),
        P("gx", "gy"),
        P("gx", "gy", None),
    )
    return jax.shard_map(
        per_device, mesh=mesh, in_specs=placed, out_specs=P(None, "gx", "gy"), check_vma=False
    )
```

```python
import functools

import jax
import jax.numpy as jnp
from jax import lax
from jax.experimental import pallas as pl
from jax.experimental.pallas import tpu as pltpu
from jax.sharding import PartitionSpec as P

NZ = 128
CY = 8
SLOTS = 512

FORWARD = (
    (0, 0, 1),
    (0, 1, -1),
    (0, 1, 0),
    (0, 1, 1),
    (1, -1, -1),
    (1, -1, 0),
    (1, -1, 1),
    (1, 0, -1),
    (1, 0, 0),
    (1, 0, 1),
    (1, 1, -1),
    (1, 1, 0),
    (1, 1, 1),
)
OFFSET = {step: k for k, step in enumerate(FORWARD)}
damping = 2.0 / 3.0

ROWS = 24
PER = 14
COLBLOCK = 93
THIRD = 2 * COLBLOCK
FAULT_ROW, Y_ROWS = 232, 256

f32 = jnp.float32
bf16 = jnp.bfloat16


def dot_nn(a, b):
    return lax.dot_general(a, b, (((1,), (0,)), ((), ())), preferred_element_type=f32)


def split(value):
    high = value.astype(bf16)
    return high, (value - high.astype(f32)).astype(bf16)


def pack_kernel(peers, count, *refs):
    sources, (block, plane, tile), targets, sems = refs[:4], refs[4:7], refs[7:11], refs[11]
    copies = [
        pltpu.make_async_copy(src, dst, sems.at[k])
        for k, (src, dst) in enumerate(zip(sources, targets))
    ]
    for copy in copies:
        copy.start()
    for copy in copies:
        copy.wait()
    trans, storage, cells, ftrans = targets
    last_x = lax.axis_index("gx") == peers[0] - 1
    first_y = lax.axis_index("gy") == 0
    last_y = lax.axis_index("gy") == peers[1] - 1
    depth = lax.broadcasted_iota(jnp.int32, (8, NZ), 1)
    row = lax.broadcasted_iota(jnp.int32, (8, NZ), 0)
    for x in range(2):
        for o in range(PER):
            base = (x * PER + o) * 8
            for y in range(CY):
                lanes = slice(y * NZ, (y + 1) * NZ)
                if o < 13:
                    value = trans[o, x : x + 1, lanes]
                else:
                    value = storage[x : x + 1, lanes]
                block[base + y : base + y + 1, :] = value
            if o == 13:
                continue
            step = FORWARD[o]
            keep = None
            if step[2] == 1:
                keep = depth < NZ - 1
            if step[2] == -1:
                keep = depth > 0
            if step[1] == 1:
                inside = (row < CY - 1) | jnp.logical_not(last_y)
                keep = inside if keep is None else keep & inside
            if step[1] == -1:
                inside = (row > 0) | jnp.logical_not(first_y)
                keep = inside if keep is None else keep & inside
            if step[0] == 1 and x == 1:
                inside = (row >= 0) & jnp.logical_not(last_x)
                keep = inside if keep is None else keep & inside
            if keep is not None:
                block[base : base + 8, :] = jnp.where(keep, block[base : base + 8, :], 0.0)
    live = count[0, 0]
    lane = lax.broadcasted_iota(jnp.int32, (1, NZ), 1)
    base = 2 * PER * 8
    for r in range(4):
        lanes = slice(r * NZ, (r + 1) * NZ)
        block[base + r : base + r + 1, :] = cells[0, :, lanes].astype(f32)
        block[base + 4 + r : base + 5 + r, :] = jnp.where(
            lane + r * NZ < live, ftrans[0, :, lanes], 0.0
        )
    plane[0:72, :] = block[(PER + 4) * 8 : (PER + 13) * 8, :]
    plane[72:80, :] = block[base : base + 8, :]
    tile[...] = block[base : base + 8, :]


def by_parity(axis, body):
    odd = lax.rem(lax.axis_index(axis), 2)
    for k in range(2):
        pl.when(odd == k)(functools.partial(body, k))


class Masked:
    def __init__(self, ref, due):
        self.ref, self.due = ref, due

    def __getitem__(self, index):
        return jnp.where(self.due, self.ref[index], 0.0)


def has_other(axis, peers):
    at = lax.axis_index(axis)
    return jnp.where(lax.rem(at, 2) == 0, at > 0, at < peers - 1)


def column_kernel(peers, own, rp, ro, rs, rt, after, to_core, to_chip):
    del after
    ro = Masked(ro, has_other("gx", peers[0]))
    lo2 = Masked(rs, lax.axis_index("gx") >= 2)
    tile = own[224:232, :]
    other = ro[224:232, :]
    parts = (tile[0:4], rp[224:228, :], tile[4:8], other[0:4], beyond_cells(rs, rt), other[4:8])
    for out in (to_core, to_chip):
        for k, part in enumerate(parts):
            out[FAULT_ROW + 4 * k : FAULT_ROW + 4 * k + 4, :] = part

    def fill(out, lo, hi, first, third, runs):
        for c in range(2):
            y = first + c
            base = c * COLBLOCK
            out[base : base + 9, :] = lo2[pl.ds(y, 9, stride=8), :]
            for k, ref in enumerate((lo, own, hi)):
                start = base + 9 + 28 * k
                out[start : start + 28, :] = ref[pl.ds(y, 28, stride=8), :]
        at = THIRD
        out[at : at + 3, :] = lo2[pl.ds((runs[-1] - 4) * 8 + third, 3, stride=8), :]
        at += 3
        for ref in (lo, own, hi):
            for x in range(2):
                for o in runs:
                    out[at : at + 3, :] = ref[pl.ds((x * PER + o) * 8 + third, 3, stride=8), :]
                    at += 3

    def for_x(odd_x):
        lo, hi = (rp, ro) if odd_x else (ro, rp)

        def for_y(odd_y):
            up, down = (to_chip, to_core) if odd_y else (to_core, to_chip)
            fill(up, lo, hi, CY - 2, CY - 3, (1, 10))
            fill(down, lo, hi, 0, 2, (4,))

        by_parity("gy", for_y)

    by_parity("gx", for_x)


def colour(z):
    half = z >> 1
    return half - 5 * ((half * 205) >> 10)


def slot_columns(rows):
    tall = jnp.transpose(jnp.concatenate(rows, axis=0))
    return [[tall[:, 4 * k + r : 4 * k + r + 1] for r in range(4)] for k in range(len(rows))]


def flat_cells(rows):
    row = jnp.concatenate([rows[r : r + 1] for r in range(4)], axis=1)
    return row.astype(jnp.int32) & 1023


def fill_far(far2, partner, live):
    lane = lax.broadcasted_iota(jnp.int32, (NZ, NZ), 1)
    for r in range(4):
        rows = slice(r * NZ, (r + 1) * NZ)
        match = (partner[r].astype(jnp.int32) & 127) == lane
        high = live[r].astype(bf16).astype(f32)
        far2[rows, 0:NZ] = jnp.where(match, high, 0.0).astype(bf16)
        far2[rows, NZ : 2 * NZ] = jnp.where(match, live[r] - high, 0.0).astype(bf16)


def fill_tint(eo, beyond, live):
    lane = lax.broadcasted_iota(jnp.int32, (NZ, NZ), 1)
    for r in range(4):
        tint = colour(beyond[r].astype(jnp.int32) & 127)
        high = live[r].astype(bf16).astype(f32)
        value = jnp.where((lane == tint) | (lane == 5), high, 0.0)
        value = jnp.where((lane == tint + 8) | (lane == 13), live[r] - high, value)
        eo[r * NZ : (r + 1) * NZ, :] = value.astype(bf16)


def fill_hot(hot, cells, columns):
    z128 = lax.broadcasted_iota(jnp.int32, (NZ, SLOTS), 0)
    for k, y in enumerate(columns):
        value = jnp.where(cells == z128 + y * NZ, 1.0, 0.0)
        hot[k * NZ : (k + 1) * NZ, :] = value.astype(bf16)


def pair_matrix(both):
    z8 = lax.broadcasted_iota(jnp.int32, (8, NZ), 1)
    e8 = lax.broadcasted_iota(jnp.int32, (8, NZ), 0)
    one = jnp.where((e8 == colour(z8)) | (e8 == 5), 1.0, 0.0).astype(bf16)
    one2 = jnp.concatenate([one, one], axis=1)
    matrix = both[:, :NZ] + both[:, NZ:]
    f2 = jnp.concatenate(split(matrix), axis=0)
    ft2 = jnp.concatenate(split(jnp.transpose(matrix)), axis=0)
    return f2, ft2, dot_nn(one2, ft2), dot_nn(one2, f2)


def fault_kernel(own, rp, f2, ft2, rf, far2, hot, both):
    partner, live = slot_columns([rp[224:228, :], own[228:232, :]])
    fill_far(far2, partner, live)
    fill_hot(hot, flat_cells(own[224:228, :]), range(CY))
    both[...] = dot_nn(hot[...], far2[...])
    for y in range(CY):
        f2[y], ft2[y], rf[0, y], rf[1, y] = pair_matrix(both[y * NZ : (y + 1) * NZ, :])


def beyond_cells(rs, rt):
    return jnp.where(lax.rem(lax.axis_index("gx"), 2) == 0, rs[72:76, :], rt[0:4, :])


def third_kernel(peers, ro, rs, rt, rf, eo, hot, both):
    ro = Masked(ro, has_other("gx", peers[0]))
    beyond, live = slot_columns([beyond_cells(rs, rt), ro[228:232, :]])
    fill_tint(eo, beyond, live)
    fill_hot(hot, flat_cells(ro[224:228, :]), range(CY))
    both[...] = dot_nn(hot[...], eo[...])
    for y in range(CY):
        pieces = jnp.transpose(both[y * NZ : (y + 1) * NZ, :])
        rf[y] = pieces[:8] + pieces[8:16]


def through(value, matrix2):
    rows = value.shape[0]
    high, low = split(value)
    left = jnp.concatenate(
        [jnp.concatenate([high, high], axis=1), jnp.concatenate([low, low], axis=1)], axis=0
    )
    got = dot_nn(left, matrix2)
    return got[:rows] + got[rows:]


def main_kernel(
    peers,
    own,
    rp,
    ro,
    rs,
    from_core,
    from_chip,
    f2,
    ft2,
    rf_pair,
    rf_third,
    out,
    w,
    wr,
    qc,
    inv,
    diag,
    fd,
    rf,
    qe,
    ap,
    tt,
    f2h,
    ft2h,
    far2,
    eo,
    hot,
):
    gx = lax.axis_index("gx")
    gy = lax.axis_index("gy")
    ro = Masked(ro, has_other("gx", peers[0]))
    from_chip = Masked(from_chip, has_other("gy", peers[1]))
    par = lax.rem(gx, 2)
    even = par == 0
    sgn = 1 - 2 * par
    p_own = jnp.where(even, 3, 2)
    p_far = jnp.where(even, 4, 1)
    p_third = jnp.where(even, 0, 5)
    p_fault = (p_own, p_far, p_third)
    z8 = lax.broadcasted_iota(jnp.int32, (8, NZ), 1)
    e8 = lax.broadcasted_iota(jnp.int32, (8, NZ), 0)

    def place(ref, count, first):
        for k in range(count):
            base = (first + k) * ROWS
            w[base + 3 : base + 11, :] = ref[8 * k : 8 * k + 8, :]

    def place_x(odd):
        lo, hi = (rp, ro) if odd else (ro, rp)
        place(lo, 28, PER)
        place(hi, 28, 5 * PER)

    place(Masked(rs, gx >= 2), 9, 4)
    place(own, 28, 3 * PER)
    by_parity("gx", place_x)

    def place_y(odd):
        yl, yh = (from_core, from_chip) if odd else (from_chip, from_core)
        for ref, row, third, runs in ((yl, 1, 0, (1, 10)), (yh, 11, 13, (4,))):
            for c in range(2):
                base = c * COLBLOCK
                w[pl.ds(4 * ROWS + row + c, 9, stride=ROWS), :] = ref[base : base + 9, :]
                w[pl.ds(PER * ROWS + row + c, 84, stride=ROWS), :] = ref[base + 9 : base + 93, :]
            at = THIRD
            for plane in range(7):
                for o in runs[-1:] if plane == 0 else runs:
                    start = (plane * PER + o) * ROWS + third
                    w[pl.ds(start, 3, stride=ROWS), :] = ref[at : at + 3, :]
                    at += 3

    by_parity("gy", place_y)
    for p in range(7):
        for o, step in enumerate(FORWARD):
            if step[2] == 0 or (p == 0 and o < 4):
                continue
            base = (p * PER + o) * ROWS
            shift = 1 if step[2] == 1 else NZ - 1
            wr[base : base + ROWS, :] = pltpu.roll(w[base : base + ROWS, :], shift, 1)

    fd[...] = jnp.zeros_like(fd)

    def put(column, k, value):
        rf[k, column] = value
        fd[pl.ds(p_fault[k] * 16 + column, 1), :] = value[5:6, :]

    for y in range(CY):
        put(y + 2, 0, rf_pair[0, y])
        put(y + 2, 1, rf_pair[1, y])
        put(y + 2, 2, rf_third[y])
    core_rows = from_core[FAULT_ROW : FAULT_ROW + 24, :]
    chip_rows = from_chip[FAULT_ROW : FAULT_ROW + 24, :]
    odd_y = lax.rem(gy, 2) == 1
    for side, first, second, columns in (
        (0, core_rows, chip_rows, ((0, 6), (1, 7))),
        (1, chip_rows, core_rows, ((10, 0), (11, 1))),
    ):
        rows = jnp.where(odd_y, first, second)
        cells, far, weight, cells_o, far_o, weight_o = (rows[4 * k : 4 * k + 4] for k in range(6))
        partner, live, beyond, live_o = slot_columns([far, weight, far_o, weight_o])
        fill_far(far2.at[side], partner, live)
        fill_tint(eo.at[side], beyond, live_o)
        ys = [y for _, y in columns]
        fill_hot(hot.at[side, 0], flat_cells(cells), ys)
        fill_hot(hot.at[side, 1], flat_cells(cells_o), ys)
        pair = dot_nn(hot[side, 0], far2[side])
        third = dot_nn(hot[side, 1], eo[side])
        for k, (column, y) in enumerate(columns):
            near, near_t, at_own, at_far = pair_matrix(pair[k * NZ : (k + 1) * NZ])
            if column in (1, 10):
                f2h[side] = near
                ft2h[side] = near_t
            put(column, 0, at_own)
            put(column, 1, at_far)
            pieces = jnp.transpose(third[k * NZ : (k + 1) * NZ])
            put(column, 2, pieces[:8] + pieces[8:16])

    r16 = lax.broadcasted_iota(jnp.int32, (16, NZ), 0)
    z16 = lax.broadcasted_iota(jnp.int32, (16, NZ), 1)
    even_y = (r16 & 1) == 0
    even_z = (z16 & 1) == 0
    for p in range(6):
        base = p + 1

        def weight(dx, dy, dz):
            if (dx, dy, dz) in OFFSET:
                start = (base * PER + OFFSET[dx, dy, dz]) * ROWS + 1
                return w[start : start + 16, :]
            o = OFFSET[-dx, -dy, -dz]
            start = ((base + dx) * PER + o) * ROWS + 1 + dy
            return (w if dz == 0 else wr)[start : start + 16, :]

        near = 1 if p % 2 == 0 else -1
        sums = {}
        for dz in (-1, 0, 1):
            got = {}
            for dx in (-1, 0, 1):
                below, above = weight(dx, -1, dz), weight(dx, 1, dz)
                got[dx, 0] = jnp.where(even_y, above, below)
                if (dx, dz) != (0, 0):
                    got[dx, 0] = got[dx, 0] + weight(dx, 0, dz)
                got[dx, 1] = jnp.where(even_y, below, above)
            for sy in range(2):
                sums[0, sy, dz] = got[0, sy] + got[near, sy]
                sums[1, sy, dz] = got[-near, sy]
        total = w[(base * PER + 13) * ROWS + 1 : (base * PER + 13) * ROWS + 17, :]
        total = total + fd[p * 16 : p * 16 + 16, :]
        r = []
        for sx in range(2):
            for sy in range(2):
                down, same, up = (sums[sx, sy, dz] for dz in (-1, 0, 1))
                r.append(same + jnp.where(even_z, up, down))
                r.append(jnp.where(even_z, down, up))
        for value in r:
            total = total + value
        total = jnp.where(total == 0.0, 1.0, total)
        scale = damping / total
        diag[p * 16 : p * 16 + 16, :] = total
        inv[p * 16 : p * 16 + 16, :] = scale
        for k, value in enumerate(r):
            value = value * scale
            if k == 0:
                value = value + (1.0 - damping)
            qc[(p * 8 + k) * 16 : (p * 8 + k) * 16 + 16, :] = value

    beside = jnp.where((z8 & 1) == 0, z8 - 1, z8 + 1)
    mask_own = jnp.where(e8 == colour(z8), 1.0, 0.0)
    mask_oth = jnp.where(e8 == colour(beside + 10), 1.0, 0.0)
    rows5 = jnp.where(e8 < 5, 1.0, 0.0)

    def spread(c, carry):
        for p in range(6):
            for lat in range(4):
                at = (p * 8 + 2 * lat) * 16 + c
                qe[p, c, lat] = (
                    qc[pl.ds(at, 1), :] * mask_own + qc[pl.ds(at + 16, 1), :] * mask_oth
                )
        for k, plane in enumerate(p_fault):
            qe[plane, c, 2] = qe[plane, c, 2] + rf[k, c] * (
                inv[pl.ds(plane * 16 + c, 1), :] * rows5
            )
        return carry

    lax.fori_loop(0, 12, spread, 0)

    def apply_column(p, y, odd_y):
        odd_x = p % 2
        acc = {}
        for dx in (-1, 0, 1):
            for dy in (-1, 0, 1):
                q = [qe[p + dx, y + dy, lat] for lat in range(4)]
                own_x = dx if (dx == 1 and odd_x) or (dx == -1 and not odd_x) else 0
                own_y = dy if (dy == 1 and odd_y) or (dy == -1 and not odd_y) else 0
                oth_x = own_x + (1 if (p + dx) % 2 else -1)
                oth_y = own_y + (1 if (odd_y + dy) % 2 else -1)
                for dz in (-1, 0, 1):
                    if (dx, dy, dz) == (0, 0, 0):
                        continue
                    if (dx, dy, dz) in OFFSET:
                        at = ((p + 1) * PER + OFFSET[dx, dy, dz]) * ROWS + y + 1
                        ref = w if dz == 0 else wr
                    else:
                        at = ((p + 1 + dx) * PER + OFFSET[-dx, -dy, -dz]) * ROWS + y + 1 + dy
                        ref = w
                    wt = ref[pl.ds(at, 1), :]
                    for lat in range(4):
                        lx = oth_x if lat >= 2 else own_x
                        ly = oth_y if lat % 2 else own_y
                        value = wt * q[lat]
                        key = (lx, ly, dz)
                        acc[key] = acc[key] + value if key in acc else value
        centre = diag[pl.ds(p * 16 + y, 1), :]
        for lx in (-1, 0, 1):
            for ly in (-1, 0, 1):
                total = acc[lx, ly, 0]
                total = total + pltpu.roll(acc[lx, ly, 1], NZ - 1, 1)
                total = total + pltpu.roll(acc[lx, ly, -1], 1, 1)
                own_lat = None
                sx = {0: 0, (1 if odd_x else -1): 1}.get(lx)
                sy = {0: 0, (1 if odd_y else -1): 1}.get(ly)
                if sx is not None and sy is not None:
                    own_lat = 2 * sx + sy
                if own_lat is None:
                    total = -total
                else:
                    total = centre * qe[p, y, own_lat] - total
                ap[p - 1, y - 1, lx + 1, ly + 1] = total

    def apply_pair(k, carry):
        for p in range(1, 5):
            apply_column(p, 2 * k + 1, 1)
            apply_column(p, 2 * k + 2, 0)
        return carry

    lax.fori_loop(0, 5, apply_pair, 0)

    def fault_apply(c, f2c, ft2c):
        ly_oth = 2 * (c % 2)
        for plane, source, x_own, matrix in (
            (p_own, p_far, 1 + sgn, ft2c),
            (p_far, p_own, 1 - sgn, f2c),
        ):
            total = through(qe[source, c].reshape(32, NZ), matrix)
            for lat in range(4):
                lx = 1 if lat >= 2 else x_own
                ly = ly_oth if lat % 2 else 1
                ap[plane - 1, c - 1, lx, ly] = ap[plane - 1, c - 1, lx, ly] - total[8 * lat : 8 * lat + 8]

    for y in range(CY):
        fault_apply(y + 2, f2[y], ft2[y])
    fault_apply(1, f2h[0], ft2h[0])
    fault_apply(10, f2h[1], ft2h[1])

    x_coarse = lax.rem(gx, 5) + 5
    a_of = [lax.rem(x_coarse + d, 5) for d in range(-2, 3)]

    def b_of(coarse_y, d):
        return lax.rem(gy * (CY // 2) + coarse_y + d + 5, 5)

    def gather(pair, carry):
        for half in range(2):
            coarse_y = 2 * pair + half
            columns = []
            for x in range(-1, 3):
                for y in range(-1, 3):
                    sx = 0 if x in (0, 1) else 1
                    sy = 0 if y in (0, 1) else 1
                    columns.append((x, y, 2 * sx + sy, (-1, 0, 0, 1)[x + 1], (-1, 0, 0, 1)[y + 1]))
            for zk in range(2):
                acc = {}
                for x, y, lat, ax, ay in columns:
                    c = 2 * coarse_y + y + 2
                    q = qc[pl.ds(((x + 2) * 8 + 2 * lat + zk) * 16 + c, 1), :]
                    for lx in range(3):
                        for ly in range(3):
                            value = q * ap[x + 1, c - 1, lx, ly]
                            key = (ax + lx - 1, ay + ly - 1)
                            acc[key] = acc[key] + value if key in acc else value
                lane = half * 256 + zk * NZ
                for (dx, dy), value in acc.items():
                    tt[pair, a_of[dx + 2], b_of(coarse_y, dy), :, lane : lane + NZ] = value
        return carry

    lax.fori_loop(0, 2, gather, 0)

    for y in range(CY):
        c = y + 2
        coarse_y = y // 2
        lane = (coarse_y % 2) * 256
        value = ap[p_far - 1, c - 1].reshape(72, NZ) * inv[pl.ds(p_far * 16 + c, 1), :]
        total = through(value, ft2[y])
        for lx in range(3):
            a = lax.rem(x_coarse + lx - 1 + sgn, 5)
            for ly in range(3):
                b = b_of(coarse_y, ly - 1)
                at = 8 * (3 * lx + ly)
                place_at = tt.at[coarse_y // 2, a, b, :, lane : lane + NZ]
                place_at[...] = place_at[...] + total[at : at + 8]

    kz = lax.broadcasted_iota(jnp.int32, (512, NZ), 0)
    kout = lax.broadcasted_iota(jnp.int32, (512, NZ), 1)
    z_in = kz & 127
    is_oth = ((kz >> 7) & 1) == 1
    target = jnp.where(
        is_oth, (z_in >> 1) + jnp.where((z_in & 1) == 0, -1, 1), z_in >> 1
    )
    fits = (target == (kout & 63)) & ((kz >> 8) == (kout >> 6))
    collect = jnp.where(fits, 1.0, 0.0).astype(bf16)
    for pair in range(2):
        high, low = split(tt[pair].reshape(200, 512))
        got = (dot_nn(high, collect) + dot_nn(low, collect)) * 0.125
        for k in range(25):
            out[5 * k : 5 * k + 5, 0, pair * NZ : (pair + 1) * NZ] = got[8 * k : 8 * k + 5]


def send(value, axis, target):
    peers = lax.axis_size(axis)
    return lax.ppermute(value, axis, [(i, target(i, peers)) for i in range(peers)])


def partner_of(i, peers):
    return i ^ 1


def other_of(i, peers):
    j = i + 1 if i % 2 else i - 1
    return j if 0 <= j < peers else i


def ahead_of(i, peers):
    return (i + 2) % peers


def odd_behind(i, peers):
    return (i - 2) % peers if i % 2 else i


VMEM = pl.BlockSpec(memory_space=pltpu.VMEM)
HBM = pl.BlockSpec(memory_space=pltpu.HBM)


def params(mib):
    return pltpu.CompilerParams(vmem_limit_bytes=mib * 1024 * 1024)


def sds(*shape, dtype=f32):
    return jax.ShapeDtypeStruct(shape, dtype)


def per_device(trans, storage, fault_cells, fault_count, fault_trans):
    peers = (lax.axis_size("gx"), lax.axis_size("gy"))
    sources = [
        pltpu.with_memory_space_constraint(array, pltpu.HBM)
        for array in (trans, storage, fault_cells, fault_trans)
    ]
    own, plane, tile = pl.pallas_call(
        functools.partial(pack_kernel, peers),
        out_shape=(sds(232, NZ), sds(80, NZ), sds(8, NZ)),
        in_specs=[pl.BlockSpec(memory_space=pltpu.SMEM)] + [HBM] * 4,
        out_specs=(VMEM,) * 3,
        scratch_shapes=[pltpu.VMEM(array.shape, array.dtype) for array in sources]
        + [pltpu.SemaphoreType.DMA((4,))],
        compiler_params=params(16),
        name="pack",
    )(fault_count, *sources)
    ro = send(own, "gx", other_of)
    rt = send(tile, "gx", odd_behind)
    rs = send(plane, "gx", ahead_of)
    rp = send(own, "gx", partner_of)
    pieces = sds(CY, 2 * NZ, NZ, dtype=bf16)
    f2, ft2, rf_pair = pl.pallas_call(
        fault_kernel,
        out_shape=(pieces, pieces, sds(2, CY, 8, NZ)),
        in_specs=[VMEM] * 2,
        out_specs=(VMEM,) * 3,
        scratch_shapes=[
            pltpu.VMEM((SLOTS, 2 * NZ), bf16),
            pltpu.VMEM((CY * NZ, SLOTS), bf16),
            pltpu.VMEM((CY * NZ, 2 * NZ), f32),
        ],
        compiler_params=params(16),
        cost_estimate=pl.CostEstimate(flops=2 * 10**9, bytes_accessed=2**21, transcendentals=0),
        name="faults",
    )(own, rp)
    to_core, to_chip = pl.pallas_call(
        functools.partial(column_kernel, peers),
        out_shape=(sds(Y_ROWS, NZ), sds(Y_ROWS, NZ)),
        in_specs=[VMEM] * 6,
        out_specs=(VMEM,) * 2,
        compiler_params=params(16),
        name="columns",
    )(own, rp, ro, rs, rt, rf_pair)
    from_chip = send(to_chip, "gy", other_of)
    from_core = send(to_core, "gy", partner_of)
    rf_third = pl.pallas_call(
        functools.partial(third_kernel, peers),
        out_shape=sds(CY, 8, NZ),
        in_specs=[VMEM] * 3,
        out_specs=VMEM,
        scratch_shapes=[
            pltpu.VMEM((SLOTS, NZ), bf16),
            pltpu.VMEM((CY * NZ, SLOTS), bf16),
            pltpu.VMEM((CY * NZ, NZ), f32),
        ],
        compiler_params=params(16),
        cost_estimate=pl.CostEstimate(flops=10**9, bytes_accessed=2**20, transcendentals=0),
        name="third",
    )(ro, rs, rt)
    return pl.pallas_call(
        functools.partial(main_kernel, peers),
        out_shape=sds(125, 1, 256),
        in_specs=[VMEM] * 10,
        out_specs=VMEM,
        scratch_shapes=[
            pltpu.VMEM((7 * PER * ROWS, NZ), f32),
            pltpu.VMEM((7 * PER * ROWS, NZ), f32),
            pltpu.VMEM((6 * 8 * 16, NZ), f32),
            pltpu.VMEM((6 * 16, NZ), f32),
            pltpu.VMEM((6 * 16, NZ), f32),
            pltpu.VMEM((6 * 16, NZ), f32),
            pltpu.VMEM((3, 12, 8, NZ), f32),
            pltpu.VMEM((6, 12, 4, 8, NZ), f32),
            pltpu.VMEM((4, 10, 3, 3, 8, NZ), f32),
            pltpu.VMEM((2, 5, 5, 8, 512), f32),
            pltpu.VMEM((2, 2 * NZ, NZ), bf16),
            pltpu.VMEM((2, 2 * NZ, NZ), bf16),
            pltpu.VMEM((2, SLOTS, 2 * NZ), bf16),
            pltpu.VMEM((2, SLOTS, NZ), bf16),
            pltpu.VMEM((2, 2, 2 * NZ, SLOTS), bf16),
        ],
        compiler_params=params(24),
        name="galerkin",
    )(own, rp, ro, rs, from_core, from_chip, f2, ft2, rf_pair, rf_third)


def solution(mesh):
    placed = (
        P(None, "gx", "gy"),
        P("gx", "gy"),
        P("gx", "gy", None),
        P("gx", "gy"),
        P("gx", "gy", None),
    )
    return jax.shard_map(
        per_device, mesh=mesh, in_specs=placed, out_specs=P(None, "gx", "gy"), check_vma=False
    )
```

```python
import functools

import jax
import jax.numpy as jnp
from jax import lax
from jax.experimental import pallas as pl
from jax.experimental.pallas import tpu as pltpu
from jax.sharding import PartitionSpec as P

NZ = 128
CY = 8
SLOTS = 512

FORWARD = (
    (0, 0, 1),
    (0, 1, -1),
    (0, 1, 0),
    (0, 1, 1),
    (1, -1, -1),
    (1, -1, 0),
    (1, -1, 1),
    (1, 0, -1),
    (1, 0, 0),
    (1, 0, 1),
    (1, 1, -1),
    (1, 1, 0),
    (1, 1, 1),
)
OFFSET = {step: k for k, step in enumerate(FORWARD)}
damping = 2.0 / 3.0

ROWS = 24
PER = 14
COLBLOCK = 93
THIRD = 2 * COLBLOCK
FAULT_ROW, Y_ROWS = 232, 256

f32 = jnp.float32
bf16 = jnp.bfloat16


def dot_nn(a, b):
    return lax.dot_general(a, b, (((1,), (0,)), ((), ())), preferred_element_type=f32)


def split(value):
    high = value.astype(bf16)
    return high, (value - high.astype(f32)).astype(bf16)


def pack_kernel(peers, count, *refs):
    sources, (block, plane), targets, sems = refs[:4], refs[4:6], refs[6:10], refs[10]
    copies = [
        pltpu.make_async_copy(src, dst, sems.at[k])
        for k, (src, dst) in enumerate(zip(sources, targets))
    ]
    for copy in copies:
        copy.start()
    for copy in copies:
        copy.wait()
    trans, storage, cells, ftrans = targets
    last_x = lax.axis_index("gx") == peers[0] - 1
    first_y = lax.axis_index("gy") == 0
    last_y = lax.axis_index("gy") == peers[1] - 1
    depth = lax.broadcasted_iota(jnp.int32, (8, NZ), 1)
    row = lax.broadcasted_iota(jnp.int32, (8, NZ), 0)
    for x in range(2):
        for o in range(PER):
            base = (x * PER + o) * 8
            for y in range(CY):
                lanes = slice(y * NZ, (y + 1) * NZ)
                if o < 13:
                    value = trans[o, x : x + 1, lanes]
                else:
                    value = storage[x : x + 1, lanes]
                block[base + y : base + y + 1, :] = value
            if o == 13:
                continue
            step = FORWARD[o]
            keep = None
            if step[2] == 1:
                keep = depth < NZ - 1
            if step[2] == -1:
                keep = depth > 0
            if step[1] == 1:
                inside = (row < CY - 1) | jnp.logical_not(last_y)
                keep = inside if keep is None else keep & inside
            if step[1] == -1:
                inside = (row > 0) | jnp.logical_not(first_y)
                keep = inside if keep is None else keep & inside
            if step[0] == 1 and x == 1:
                inside = (row >= 0) & jnp.logical_not(last_x)
                keep = inside if keep is None else keep & inside
            if keep is not None:
                block[base : base + 8, :] = jnp.where(keep, block[base : base + 8, :], 0.0)
    live = count[0, 0]
    lane = lax.broadcasted_iota(jnp.int32, (1, NZ), 1)
    base = 2 * PER * 8
    for r in range(4):
        lanes = slice(r * NZ, (r + 1) * NZ)
        block[base + r : base + r + 1, :] = cells[0, :, lanes].astype(f32)
        block[base + 4 + r : base + 5 + r, :] = jnp.where(
            lane + r * NZ < live, ftrans[0, :, lanes], 0.0
        )
    plane[...] = block[(PER + 4) * 8 : (PER + 13) * 8, :]


def partner_rows(cells):
    return jnp.concatenate(
        [cells[0, :, r * NZ : (r + 1) * NZ] for r in range(4)], axis=0
    ).astype(f32)


def join_kernel(own, cells, joined):
    joined[0:232, :] = own[...]
    joined[232:236, :] = partner_rows(cells)
    joined[236:240, :] = jnp.zeros((4, NZ), f32)


def by_parity(axis, body):
    odd = lax.rem(lax.axis_index(axis), 2)
    for k in range(2):
        pl.when(odd == k)(functools.partial(body, k))


class Masked:
    def __init__(self, ref, due):
        self.ref, self.due = ref, due

    def __getitem__(self, index):
        return jnp.where(self.due, self.ref[index], 0.0)


def has_other(axis, peers):
    at = lax.axis_index(axis)
    return jnp.where(lax.rem(at, 2) == 0, at > 0, at < peers - 1)


def column_kernel(peers, own, rp, ro, rs, cells, after, to_core, to_chip):
    del after
    ro = Masked(ro, has_other("gx", peers[0]))
    lo2 = Masked(rs, lax.axis_index("gx") >= 2)
    tile = own[224:232, :]
    other = ro[224:232, :]
    parts = (tile[0:4], partner_rows(cells), tile[4:8], other[0:4], ro[232:236, :], other[4:8])
    for out in (to_core, to_chip):
        for k, part in enumerate(parts):
            out[FAULT_ROW + 4 * k : FAULT_ROW + 4 * k + 4, :] = part

    def fill(out, lo, hi, first, third, runs):
        for c in range(2):
            y = first + c
            base = c * COLBLOCK
            out[base : base + 9, :] = lo2[pl.ds(y, 9, stride=8), :]
            for k, ref in enumerate((lo, own, hi)):
                start = base + 9 + 28 * k
                out[start : start + 28, :] = ref[pl.ds(y, 28, stride=8), :]
        at = THIRD
        out[at : at + 3, :] = lo2[pl.ds((runs[-1] - 4) * 8 + third, 3, stride=8), :]
        at += 3
        for ref in (lo, own, hi):
            for x in range(2):
                for o in runs:
                    out[at : at + 3, :] = ref[pl.ds((x * PER + o) * 8 + third, 3, stride=8), :]
                    at += 3

    def for_x(odd_x):
        lo, hi = (rp, ro) if odd_x else (ro, rp)

        def for_y(odd_y):
            up, down = (to_chip, to_core) if odd_y else (to_core, to_chip)
            fill(up, lo, hi, CY - 2, CY - 3, (1, 10))
            fill(down, lo, hi, 0, 2, (4,))

        by_parity("gy", for_y)

    by_parity("gx", for_x)


def colour(z):
    half = z >> 1
    return half - 5 * ((half * 205) >> 10)


def slot_columns(rows):
    tall = jnp.transpose(jnp.concatenate(rows, axis=0))
    return [[tall[:, 4 * k + r : 4 * k + r + 1] for r in range(4)] for k in range(len(rows))]


def flat_cells(rows):
    row = jnp.concatenate([rows[r : r + 1] for r in range(4)], axis=1)
    return row.astype(jnp.int32) & 1023


def fill_far(far2, partner, live):
    lane = lax.broadcasted_iota(jnp.int32, (NZ, NZ), 1)
    for r in range(4):
        rows = slice(r * NZ, (r + 1) * NZ)
        match = (partner[r].astype(jnp.int32) & 127) == lane
        high = live[r].astype(bf16).astype(f32)
        far2[rows, 0:NZ] = jnp.where(match, high, 0.0).astype(bf16)
        far2[rows, NZ : 2 * NZ] = jnp.where(match, live[r] - high, 0.0).astype(bf16)


def fill_tint(eo, beyond, live):
    lane = lax.broadcasted_iota(jnp.int32, (NZ, NZ), 1)
    for r in range(4):
        tint = colour(beyond[r].astype(jnp.int32) & 127)
        high = live[r].astype(bf16).astype(f32)
        value = jnp.where((lane == tint) | (lane == 5), high, 0.0)
        value = jnp.where((lane == tint + 8) | (lane == 13), live[r] - high, value)
        eo[r * NZ : (r + 1) * NZ, :] = value.astype(bf16)


def fill_hot(hot, cells, columns):
    z128 = lax.broadcasted_iota(jnp.int32, (NZ, SLOTS), 0)
    for k, y in enumerate(columns):
        value = jnp.where(cells == z128 + y * NZ, 1.0, 0.0)
        hot[k * NZ : (k + 1) * NZ, :] = value.astype(bf16)


def pair_matrix(both):
    z8 = lax.broadcasted_iota(jnp.int32, (8, NZ), 1)
    e8 = lax.broadcasted_iota(jnp.int32, (8, NZ), 0)
    one = jnp.where((e8 == colour(z8)) | (e8 == 5), 1.0, 0.0).astype(bf16)
    one2 = jnp.concatenate([one, one], axis=1)
    matrix = both[:, :NZ] + both[:, NZ:]
    f2 = jnp.concatenate(split(matrix), axis=0)
    ft2 = jnp.concatenate(split(jnp.transpose(matrix)), axis=0)
    return f2, ft2, dot_nn(one2, ft2), dot_nn(one2, f2)


def fault_kernel(own, cells, f2, ft2, rf, far2, hot, both):
    partner, live = slot_columns([partner_rows(cells), own[228:232, :]])
    fill_far(far2, partner, live)
    fill_hot(hot, flat_cells(own[224:228, :]), range(CY))
    both[...] = dot_nn(hot[...], far2[...])
    for y in range(CY):
        f2[y], ft2[y], rf[0, y], rf[1, y] = pair_matrix(both[y * NZ : (y + 1) * NZ, :])


def third_kernel(peers, ro, rf, eo, hot, both):
    ro = Masked(ro, has_other("gx", peers[0]))
    beyond, live = slot_columns([ro[232:236, :], ro[228:232, :]])
    fill_tint(eo, beyond, live)
    fill_hot(hot, flat_cells(ro[224:228, :]), range(CY))
    both[...] = dot_nn(hot[...], eo[...])
    for y in range(CY):
        pieces = jnp.transpose(both[y * NZ : (y + 1) * NZ, :])
        rf[y] = pieces[:8] + pieces[8:16]


def through(value, matrix2):
    rows = value.shape[0]
    high, low = split(value)
    left = jnp.concatenate(
        [jnp.concatenate([high, high], axis=1), jnp.concatenate([low, low], axis=1)], axis=0
    )
    got = dot_nn(left, matrix2)
    return got[:rows] + got[rows:]


def main_kernel(
    peers,
    own,
    rp,
    ro,
    rs,
    from_core,
    from_chip,
    f2,
    ft2,
    rf_pair,
    rf_third,
    out,
    w,
    wr,
    qc,
    inv,
    diag,
    fd,
    rf,
    qe,
    ap,
    tt,
    f2h,
    ft2h,
    far2,
    eo,
    hot,
):
    gx = lax.axis_index("gx")
    gy = lax.axis_index("gy")
    ro = Masked(ro, has_other("gx", peers[0]))
    from_chip = Masked(from_chip, has_other("gy", peers[1]))
    par = lax.rem(gx, 2)
    even = par == 0
    sgn = 1 - 2 * par
    p_own = jnp.where(even, 3, 2)
    p_far = jnp.where(even, 4, 1)
    p_third = jnp.where(even, 0, 5)
    p_fault = (p_own, p_far, p_third)
    z8 = lax.broadcasted_iota(jnp.int32, (8, NZ), 1)
    e8 = lax.broadcasted_iota(jnp.int32, (8, NZ), 0)

    def place(ref, count, first):
        for k in range(count):
            base = (first + k) * ROWS
            w[base + 3 : base + 11, :] = ref[8 * k : 8 * k + 8, :]

    def place_x(odd):
        lo, hi = (rp, ro) if odd else (ro, rp)
        place(lo, 28, PER)
        place(hi, 28, 5 * PER)

    place(Masked(rs, gx >= 2), 9, 4)
    place(own, 28, 3 * PER)
    by_parity("gx", place_x)

    def place_y(odd):
        yl, yh = (from_core, from_chip) if odd else (from_chip, from_core)
        for ref, row, third, runs in ((yl, 1, 0, (1, 10)), (yh, 11, 13, (4,))):
            for c in range(2):
                base = c * COLBLOCK
                w[pl.ds(4 * ROWS + row + c, 9, stride=ROWS), :] = ref[base : base + 9, :]
                w[pl.ds(PER * ROWS + row + c, 84, stride=ROWS), :] = ref[base + 9 : base + 93, :]
            at = THIRD
            for plane in range(7):
                for o in runs[-1:] if plane == 0 else runs:
                    start = (plane * PER + o) * ROWS + third
                    w[pl.ds(start, 3, stride=ROWS), :] = ref[at : at + 3, :]
                    at += 3

    by_parity("gy", place_y)
    for p in range(7):
        for o, step in enumerate(FORWARD):
            if step[2] == 0 or (p == 0 and o < 4):
                continue
            base = (p * PER + o) * ROWS
            shift = 1 if step[2] == 1 else NZ - 1
            wr[base : base + ROWS, :] = pltpu.roll(w[base : base + ROWS, :], shift, 1)

    fd[...] = jnp.zeros_like(fd)

    def put(column, k, value):
        rf[k, column] = value
        fd[pl.ds(p_fault[k] * 16 + column, 1), :] = value[5:6, :]

    for y in range(CY):
        put(y + 2, 0, rf_pair[0, y])
        put(y + 2, 1, rf_pair[1, y])
        put(y + 2, 2, rf_third[y])
    core_rows = from_core[FAULT_ROW : FAULT_ROW + 24, :]
    chip_rows = from_chip[FAULT_ROW : FAULT_ROW + 24, :]
    odd_y = lax.rem(gy, 2) == 1
    for side, first, second, columns in (
        (0, core_rows, chip_rows, ((0, 6), (1, 7))),
        (1, chip_rows, core_rows, ((10, 0), (11, 1))),
    ):
        rows = jnp.where(odd_y, first, second)
        cells, far, weight, cells_o, far_o, weight_o = (rows[4 * k : 4 * k + 4] for k in range(6))
        partner, live, beyond, live_o = slot_columns([far, weight, far_o, weight_o])
        fill_far(far2.at[side], partner, live)
        fill_tint(eo.at[side], beyond, live_o)
        ys = [y for _, y in columns]
        fill_hot(hot.at[side, 0], flat_cells(cells), ys)
        fill_hot(hot.at[side, 1], flat_cells(cells_o), ys)
        pair = dot_nn(hot[side, 0], far2[side])
        third = dot_nn(hot[side, 1], eo[side])
        for k, (column, y) in enumerate(columns):
            near, near_t, at_own, at_far = pair_matrix(pair[k * NZ : (k + 1) * NZ])
            if column in (1, 10):
                f2h[side] = near
                ft2h[side] = near_t
            put(column, 0, at_own)
            put(column, 1, at_far)
            pieces = jnp.transpose(third[k * NZ : (k + 1) * NZ])
            put(column, 2, pieces[:8] + pieces[8:16])

    r16 = lax.broadcasted_iota(jnp.int32, (16, NZ), 0)
    z16 = lax.broadcasted_iota(jnp.int32, (16, NZ), 1)
    even_y = (r16 & 1) == 0
    even_z = (z16 & 1) == 0
    for p in range(6):
        base = p + 1

        def weight(dx, dy, dz):
            if (dx, dy, dz) in OFFSET:
                start = (base * PER + OFFSET[dx, dy, dz]) * ROWS + 1
                return w[start : start + 16, :]
            o = OFFSET[-dx, -dy, -dz]
            start = ((base + dx) * PER + o) * ROWS + 1 + dy
            return (w if dz == 0 else wr)[start : start + 16, :]

        near = 1 if p % 2 == 0 else -1
        sums = {}
        for dz in (-1, 0, 1):
            got = {}
            for dx in (-1, 0, 1):
                below, above = weight(dx, -1, dz), weight(dx, 1, dz)
                got[dx, 0] = jnp.where(even_y, above, below)
                if (dx, dz) != (0, 0):
                    got[dx, 0] = got[dx, 0] + weight(dx, 0, dz)
                got[dx, 1] = jnp.where(even_y, below, above)
            for sy in range(2):
                sums[0, sy, dz] = got[0, sy] + got[near, sy]
                sums[1, sy, dz] = got[-near, sy]
        total = w[(base * PER + 13) * ROWS + 1 : (base * PER + 13) * ROWS + 17, :]
        total = total + fd[p * 16 : p * 16 + 16, :]
        r = []
        for sx in range(2):
            for sy in range(2):
                down, same, up = (sums[sx, sy, dz] for dz in (-1, 0, 1))
                r.append(same + jnp.where(even_z, up, down))
                r.append(jnp.where(even_z, down, up))
        for value in r:
            total = total + value
        total = jnp.where(total == 0.0, 1.0, total)
        scale = damping / total
        diag[p * 16 : p * 16 + 16, :] = total
        inv[p * 16 : p * 16 + 16, :] = scale
        for k, value in enumerate(r):
            value = value * scale
            if k == 0:
                value = value + (1.0 - damping)
            qc[(p * 8 + k) * 16 : (p * 8 + k) * 16 + 16, :] = value

    beside = jnp.where((z8 & 1) == 0, z8 - 1, z8 + 1)
    mask_own = jnp.where(e8 == colour(z8), 1.0, 0.0)
    mask_oth = jnp.where(e8 == colour(beside + 10), 1.0, 0.0)
    rows5 = jnp.where(e8 < 5, 1.0, 0.0)

    def spread(c, carry):
        for p in range(6):
            for lat in range(4):
                at = (p * 8 + 2 * lat) * 16 + c
                qe[p, c, lat] = (
                    qc[pl.ds(at, 1), :] * mask_own + qc[pl.ds(at + 16, 1), :] * mask_oth
                )
        for k, plane in enumerate(p_fault):
            qe[plane, c, 2] = qe[plane, c, 2] + rf[k, c] * (
                inv[pl.ds(plane * 16 + c, 1), :] * rows5
            )
        return carry

    lax.fori_loop(0, 12, spread, 0)

    def apply_column(p, y, odd_y):
        odd_x = p % 2
        acc = {}
        for dx in (-1, 0, 1):
            for dy in (-1, 0, 1):
                q = [qe[p + dx, y + dy, lat] for lat in range(4)]
                own_x = dx if (dx == 1 and odd_x) or (dx == -1 and not odd_x) else 0
                own_y = dy if (dy == 1 and odd_y) or (dy == -1 and not odd_y) else 0
                oth_x = own_x + (1 if (p + dx) % 2 else -1)
                oth_y = own_y + (1 if (odd_y + dy) % 2 else -1)
                for dz in (-1, 0, 1):
                    if (dx, dy, dz) == (0, 0, 0):
                        continue
                    if (dx, dy, dz) in OFFSET:
                        at = ((p + 1) * PER + OFFSET[dx, dy, dz]) * ROWS + y + 1
                        ref = w if dz == 0 else wr
                    else:
                        at = ((p + 1 + dx) * PER + OFFSET[-dx, -dy, -dz]) * ROWS + y + 1 + dy
                        ref = w
                    wt = ref[pl.ds(at, 1), :]
                    for lat in range(4):
                        lx = oth_x if lat >= 2 else own_x
                        ly = oth_y if lat % 2 else own_y
                        value = wt * q[lat]
                        key = (lx, ly, dz)
                        acc[key] = acc[key] + value if key in acc else value
        centre = diag[pl.ds(p * 16 + y, 1), :]
        for lx in (-1, 0, 1):
            for ly in (-1, 0, 1):
                total = acc[lx, ly, 0]
                total = total + pltpu.roll(acc[lx, ly, 1], NZ - 1, 1)
                total = total + pltpu.roll(acc[lx, ly, -1], 1, 1)
                own_lat = None
                sx = {0: 0, (1 if odd_x else -1): 1}.get(lx)
                sy = {0: 0, (1 if odd_y else -1): 1}.get(ly)
                if sx is not None and sy is not None:
                    own_lat = 2 * sx + sy
                if own_lat is None:
                    total = -total
                else:
                    total = centre * qe[p, y, own_lat] - total
                ap[p - 1, y - 1, lx + 1, ly + 1] = total

    def apply_pair(k, carry):
        for p in range(1, 5):
            apply_column(p, 2 * k + 1, 1)
            apply_column(p, 2 * k + 2, 0)
        return carry

    lax.fori_loop(0, 5, apply_pair, 0)

    def fault_apply(c, f2c, ft2c):
        ly_oth = 2 * (c % 2)
        for plane, source, x_own, matrix in (
            (p_own, p_far, 1 + sgn, ft2c),
            (p_far, p_own, 1 - sgn, f2c),
        ):
            total = through(qe[source, c].reshape(32, NZ), matrix)
            for lat in range(4):
                lx = 1 if lat >= 2 else x_own
                ly = ly_oth if lat % 2 else 1
                ap[plane - 1, c - 1, lx, ly] = ap[plane - 1, c - 1, lx, ly] - total[8 * lat : 8 * lat + 8]

    for y in range(CY):
        fault_apply(y + 2, f2[y], ft2[y])
    fault_apply(1, f2h[0], ft2h[0])
    fault_apply(10, f2h[1], ft2h[1])

    x_coarse = lax.rem(gx, 5) + 5
    a_of = [lax.rem(x_coarse + d, 5) for d in range(-2, 3)]

    def b_of(coarse_y, d):
        return lax.rem(gy * (CY // 2) + coarse_y + d + 5, 5)

    def gather(pair, carry):
        for half in range(2):
            coarse_y = 2 * pair + half
            columns = []
            for x in range(-1, 3):
                for y in range(-1, 3):
                    sx = 0 if x in (0, 1) else 1
                    sy = 0 if y in (0, 1) else 1
                    columns.append((x, y, 2 * sx + sy, (-1, 0, 0, 1)[x + 1], (-1, 0, 0, 1)[y + 1]))
            for zk in range(2):
                acc = {}
                for x, y, lat, ax, ay in columns:
                    c = 2 * coarse_y + y + 2
                    q = qc[pl.ds(((x + 2) * 8 + 2 * lat + zk) * 16 + c, 1), :]
                    for lx in range(3):
                        for ly in range(3):
                            value = q * ap[x + 1, c - 1, lx, ly]
                            key = (ax + lx - 1, ay + ly - 1)
                            acc[key] = acc[key] + value if key in acc else value
                lane = half * 256 + zk * NZ
                for (dx, dy), value in acc.items():
                    tt[pair, a_of[dx + 2], b_of(coarse_y, dy), :, lane : lane + NZ] = value
        return carry

    lax.fori_loop(0, 2, gather, 0)

    for y in range(CY):
        c = y + 2
        coarse_y = y // 2
        lane = (coarse_y % 2) * 256
        value = ap[p_far - 1, c - 1].reshape(72, NZ) * inv[pl.ds(p_far * 16 + c, 1), :]
        total = through(value, ft2[y])
        for lx in range(3):
            a = lax.rem(x_coarse + lx - 1 + sgn, 5)
            for ly in range(3):
                b = b_of(coarse_y, ly - 1)
                at = 8 * (3 * lx + ly)
                place_at = tt.at[coarse_y // 2, a, b, :, lane : lane + NZ]
                place_at[...] = place_at[...] + total[at : at + 8]

    kz = lax.broadcasted_iota(jnp.int32, (512, NZ), 0)
    kout = lax.broadcasted_iota(jnp.int32, (512, NZ), 1)
    z_in = kz & 127
    is_oth = ((kz >> 7) & 1) == 1
    target = jnp.where(
        is_oth, (z_in >> 1) + jnp.where((z_in & 1) == 0, -1, 1), z_in >> 1
    )
    fits = (target == (kout & 63)) & ((kz >> 8) == (kout >> 6))
    collect = jnp.where(fits, 1.0, 0.0).astype(bf16)
    for pair in range(2):
        high, low = split(tt[pair].reshape(200, 512))
        got = (dot_nn(high, collect) + dot_nn(low, collect)) * 0.125
        for k in range(25):
            out[5 * k : 5 * k + 5, 0, pair * NZ : (pair + 1) * NZ] = got[8 * k : 8 * k + 5]


def send(value, axis, target):
    peers = lax.axis_size(axis)
    return lax.ppermute(value, axis, [(i, target(i, peers)) for i in range(peers)])


def partner_of(i, peers):
    return i ^ 1


def other_of(i, peers):
    j = i + 1 if i % 2 else i - 1
    return j if 0 <= j < peers else i


def ahead_of(i, peers):
    return (i + 2) % peers


VMEM = pl.BlockSpec(memory_space=pltpu.VMEM)
HBM = pl.BlockSpec(memory_space=pltpu.HBM)


def params(mib):
    return pltpu.CompilerParams(vmem_limit_bytes=mib * 1024 * 1024)


def sds(*shape, dtype=f32):
    return jax.ShapeDtypeStruct(shape, dtype)


def per_device(trans, storage, fault_cells, fault_count, fault_trans):
    peers = (lax.axis_size("gx"), lax.axis_size("gy"))
    cells = send(fault_cells, "gx", partner_of)
    sources = [
        pltpu.with_memory_space_constraint(array, pltpu.HBM)
        for array in (trans, storage, fault_cells, fault_trans)
    ]
    own, plane = pl.pallas_call(
        functools.partial(pack_kernel, peers),
        out_shape=(sds(232, NZ), sds(72, NZ)),
        in_specs=[pl.BlockSpec(memory_space=pltpu.SMEM)] + [HBM] * 4,
        out_specs=(VMEM,) * 2,
        scratch_shapes=[pltpu.VMEM(array.shape, array.dtype) for array in sources]
        + [pltpu.SemaphoreType.DMA((4,))],
        compiler_params=params(16),
        name="pack",
    )(fault_count, *sources)
    joined = pl.pallas_call(
        join_kernel,
        out_shape=sds(240, NZ),
        in_specs=[VMEM] * 2,
        out_specs=VMEM,
        compiler_params=params(16),
        name="join",
    )(own, cells)
    ro = send(joined, "gx", other_of)
    rs = send(plane, "gx", ahead_of)
    rp = send(own, "gx", partner_of)
    pieces = sds(CY, 2 * NZ, NZ, dtype=bf16)
    f2, ft2, rf_pair = pl.pallas_call(
        fault_kernel,
        out_shape=(pieces, pieces, sds(2, CY, 8, NZ)),
        in_specs=[VMEM] * 2,
        out_specs=(VMEM,) * 3,
        scratch_shapes=[
            pltpu.VMEM((SLOTS, 2 * NZ), bf16),
            pltpu.VMEM((CY * NZ, SLOTS), bf16),
            pltpu.VMEM((CY * NZ, 2 * NZ), f32),
        ],
        compiler_params=params(16),
        cost_estimate=pl.CostEstimate(flops=2 * 10**9, bytes_accessed=2**21, transcendentals=0),
        name="faults",
    )(own, cells)
    to_core, to_chip = pl.pallas_call(
        functools.partial(column_kernel, peers),
        out_shape=(sds(Y_ROWS, NZ), sds(Y_ROWS, NZ)),
        in_specs=[VMEM] * 6,
        out_specs=(VMEM,) * 2,
        compiler_params=params(16),
        name="columns",
    )(own, rp, ro, rs, cells, rf_pair)
    from_chip = send(to_chip, "gy", other_of)
    from_core = send(to_core, "gy", partner_of)
    rf_third = pl.pallas_call(
        functools.partial(third_kernel, peers),
        out_shape=sds(CY, 8, NZ),
        in_specs=[VMEM],
        out_specs=VMEM,
        scratch_shapes=[
            pltpu.VMEM((SLOTS, NZ), bf16),
            pltpu.VMEM((CY * NZ, SLOTS), bf16),
            pltpu.VMEM((CY * NZ, NZ), f32),
        ],
        compiler_params=params(16),
        cost_estimate=pl.CostEstimate(flops=10**9, bytes_accessed=2**20, transcendentals=0),
        name="third",
    )(ro)
    return pl.pallas_call(
        functools.partial(main_kernel, peers),
        out_shape=sds(125, 1, 256),
        in_specs=[VMEM] * 10,
        out_specs=VMEM,
        scratch_shapes=[
            pltpu.VMEM((7 * PER * ROWS, NZ), f32),
            pltpu.VMEM((7 * PER * ROWS, NZ), f32),
            pltpu.VMEM((6 * 8 * 16, NZ), f32),
            pltpu.VMEM((6 * 16, NZ), f32),
            pltpu.VMEM((6 * 16, NZ), f32),
            pltpu.VMEM((6 * 16, NZ), f32),
            pltpu.VMEM((3, 12, 8, NZ), f32),
            pltpu.VMEM((6, 12, 4, 8, NZ), f32),
            pltpu.VMEM((4, 10, 3, 3, 8, NZ), f32),
            pltpu.VMEM((2, 5, 5, 8, 512), f32),
            pltpu.VMEM((2, 2 * NZ, NZ), bf16),
            pltpu.VMEM((2, 2 * NZ, NZ), bf16),
            pltpu.VMEM((2, SLOTS, 2 * NZ), bf16),
            pltpu.VMEM((2, SLOTS, NZ), bf16),
            pltpu.VMEM((2, 2, 2 * NZ, SLOTS), bf16),
        ],
        compiler_params=params(24),
        name="galerkin",
    )(own, rp, ro, rs, from_core, from_chip, f2, ft2, rf_pair, rf_third)


def solution(mesh):
    placed = (
        P(None, "gx", "gy"),
        P("gx", "gy"),
        P("gx", "gy", None),
        P("gx", "gy"),
        P("gx", "gy", None),
    )
    return jax.shard_map(
        per_device, mesh=mesh, in_specs=placed, out_specs=P(None, "gx", "gy"), check_vma=False
    )
```

```python
import functools

import jax
import jax.numpy as jnp
from jax import lax
from jax.experimental import pallas as pl
from jax.experimental.pallas import tpu as pltpu
from jax.sharding import PartitionSpec as P

NZ = 128
CY = 8
SLOTS = 512

FORWARD = (
    (0, 0, 1),
    (0, 1, -1),
    (0, 1, 0),
    (0, 1, 1),
    (1, -1, -1),
    (1, -1, 0),
    (1, -1, 1),
    (1, 0, -1),
    (1, 0, 0),
    (1, 0, 1),
    (1, 1, -1),
    (1, 1, 0),
    (1, 1, 1),
)
OFFSET = {step: k for k, step in enumerate(FORWARD)}
damping = 2.0 / 3.0

ROWS = 24
PER = 14
COLBLOCK = 93
THIRD = 2 * COLBLOCK
FAULT_ROW, Y_ROWS = 232, 256

f32 = jnp.float32
bf16 = jnp.bfloat16


def dot_nn(a, b):
    return lax.dot_general(a, b, (((1,), (0,)), ((), ())), preferred_element_type=f32)


def split(value):
    high = value.astype(bf16)
    return high, (value - high.astype(f32)).astype(bf16)


def pack_kernel(peers, count, *refs):
    sources, (block, plane), targets, sems = refs[:4], refs[4:6], refs[6:10], refs[10]
    copies = [
        pltpu.make_async_copy(src, dst, sems.at[k])
        for k, (src, dst) in enumerate(zip(sources, targets))
    ]
    for copy in copies:
        copy.start()
    for copy in copies:
        copy.wait()
    trans, storage, cells, ftrans = targets
    last_x = lax.axis_index("gx") == peers[0] - 1
    first_y = lax.axis_index("gy") == 0
    last_y = lax.axis_index("gy") == peers[1] - 1
    depth = lax.broadcasted_iota(jnp.int32, (8, NZ), 1)
    row = lax.broadcasted_iota(jnp.int32, (8, NZ), 0)
    for x in range(2):
        for o in range(PER):
            base = (x * PER + o) * 8
            for y in range(CY):
                lanes = slice(y * NZ, (y + 1) * NZ)
                if o < 13:
                    value = trans[o, x : x + 1, lanes]
                else:
                    value = storage[x : x + 1, lanes]
                block[base + y : base + y + 1, :] = value
            if o == 13:
                continue
            step = FORWARD[o]
            keep = None
            if step[2] == 1:
                keep = depth < NZ - 1
            if step[2] == -1:
                keep = depth > 0
            if step[1] == 1:
                inside = (row < CY - 1) | jnp.logical_not(last_y)
                keep = inside if keep is None else keep & inside
            if step[1] == -1:
                inside = (row > 0) | jnp.logical_not(first_y)
                keep = inside if keep is None else keep & inside
            if step[0] == 1 and x == 1:
                inside = (row >= 0) & jnp.logical_not(last_x)
                keep = inside if keep is None else keep & inside
            if keep is not None:
                block[base : base + 8, :] = jnp.where(keep, block[base : base + 8, :], 0.0)
    live = count[0, 0]
    lane = lax.broadcasted_iota(jnp.int32, (1, NZ), 1)
    base = 2 * PER * 8
    for r in range(4):
        lanes = slice(r * NZ, (r + 1) * NZ)
        block[base + r : base + r + 1, :] = cells[0, :, lanes].astype(f32)
        block[base + 4 + r : base + 5 + r, :] = jnp.where(
            lane + r * NZ < live, ftrans[0, :, lanes], 0.0
        )
    plane[...] = block[(PER + 4) * 8 : (PER + 13) * 8, :]


def partner_rows(cells):
    return jnp.concatenate(
        [cells[0, :, r * NZ : (r + 1) * NZ] for r in range(4)], axis=0
    ).astype(f32)


def join_kernel(own, cells, joined):
    joined[0:232, :] = own[...]
    joined[232:236, :] = partner_rows(cells)
    joined[236:240, :] = jnp.zeros((4, NZ), f32)


def by_parity(axis, body):
    odd = lax.rem(lax.axis_index(axis), 2)
    for k in range(2):
        pl.when(odd == k)(functools.partial(body, k))


class Masked:
    def __init__(self, ref, due):
        self.ref, self.due = ref, due

    def __getitem__(self, index):
        return jnp.where(self.due, self.ref[index], 0.0)


def has_other(axis, peers):
    at = lax.axis_index(axis)
    return jnp.where(lax.rem(at, 2) == 0, at > 0, at < peers - 1)


def column_kernel(peers, own, rp, ro, rs, cells, after, to_core, to_chip):
    del after
    ro = Masked(ro, has_other("gx", peers[0]))
    lo2 = Masked(rs, lax.axis_index("gx") >= 2)
    tile = own[224:232, :]
    other = ro[224:232, :]
    parts = (tile[0:4], partner_rows(cells), tile[4:8], other[0:4], ro[232:236, :], other[4:8])
    for out in (to_core, to_chip):
        for k, part in enumerate(parts):
            out[FAULT_ROW + 4 * k : FAULT_ROW + 4 * k + 4, :] = part

    def fill(out, lo, hi, first, third, runs):
        for c in range(2):
            y = first + c
            base = c * COLBLOCK
            out[base : base + 9, :] = lo2[pl.ds(y, 9, stride=8), :]
            for k, ref in enumerate((lo, own, hi)):
                start = base + 9 + 28 * k
                out[start : start + 28, :] = ref[pl.ds(y, 28, stride=8), :]
        at = THIRD
        out[at : at + 3, :] = lo2[pl.ds((runs[-1] - 4) * 8 + third, 3, stride=8), :]
        at += 3
        for ref in (lo, own, hi):
            for x in range(2):
                for o in runs:
                    out[at : at + 3, :] = ref[pl.ds((x * PER + o) * 8 + third, 3, stride=8), :]
                    at += 3

    def for_x(odd_x):
        lo, hi = (rp, ro) if odd_x else (ro, rp)

        def for_y(odd_y):
            up, down = (to_chip, to_core) if odd_y else (to_core, to_chip)
            fill(up, lo, hi, CY - 2, CY - 3, (1, 10))
            fill(down, lo, hi, 0, 2, (4,))

        by_parity("gy", for_y)

    by_parity("gx", for_x)


def colour(z):
    half = z >> 1
    return half - 5 * ((half * 205) >> 10)


def slot_columns(rows):
    tall = jnp.transpose(jnp.concatenate(rows, axis=0))
    return [[tall[:, 4 * k + r : 4 * k + r + 1] for r in range(4)] for k in range(len(rows))]


def flat_cells(rows):
    row = jnp.concatenate([rows[r : r + 1] for r in range(4)], axis=1)
    return row.astype(jnp.int32) & 1023


def fill_far(far2, partner, live):
    lane = lax.broadcasted_iota(jnp.int32, (NZ, NZ), 1)
    for r in range(4):
        rows = slice(r * NZ, (r + 1) * NZ)
        match = (partner[r].astype(jnp.int32) & 127) == lane
        high = live[r].astype(bf16).astype(f32)
        far2[rows, 0:NZ] = jnp.where(match, high, 0.0).astype(bf16)
        far2[rows, NZ : 2 * NZ] = jnp.where(match, live[r] - high, 0.0).astype(bf16)


def fill_tint(eo, beyond, live):
    lane = lax.broadcasted_iota(jnp.int32, (NZ, NZ), 1)
    for r in range(4):
        tint = colour(beyond[r].astype(jnp.int32) & 127)
        high = live[r].astype(bf16).astype(f32)
        value = jnp.where((lane == tint) | (lane == 5), high, 0.0)
        value = jnp.where((lane == tint + 8) | (lane == 13), live[r] - high, value)
        eo[r * NZ : (r + 1) * NZ, :] = value.astype(bf16)


def fill_hot(hot, cells, columns):
    z128 = lax.broadcasted_iota(jnp.int32, (NZ, SLOTS), 0)
    for k, y in enumerate(columns):
        value = jnp.where(cells == z128 + y * NZ, 1.0, 0.0)
        hot[k * NZ : (k + 1) * NZ, :] = value.astype(bf16)


def pair_matrix(both):
    z8 = lax.broadcasted_iota(jnp.int32, (8, NZ), 1)
    e8 = lax.broadcasted_iota(jnp.int32, (8, NZ), 0)
    one = jnp.where((e8 == colour(z8)) | (e8 == 5), 1.0, 0.0).astype(bf16)
    one2 = jnp.concatenate([one, one], axis=1)
    matrix = both[:, :NZ] + both[:, NZ:]
    f2 = jnp.concatenate(split(matrix), axis=0)
    ft2 = jnp.concatenate(split(jnp.transpose(matrix)), axis=0)
    return f2, ft2, dot_nn(one2, ft2), dot_nn(one2, f2)


def fault_kernel(own, plane, cells, f2, ft2, rf, plane_out, far2, hot, both):
    plane_out[...] = plane[...]
    partner, live = slot_columns([partner_rows(cells), own[228:232, :]])
    fill_far(far2, partner, live)
    fill_hot(hot, flat_cells(own[224:228, :]), range(CY))
    both[...] = dot_nn(hot[...], far2[...])
    for y in range(CY):
        f2[y], ft2[y], rf[0, y], rf[1, y] = pair_matrix(both[y * NZ : (y + 1) * NZ, :])


def through(value, matrix2):
    rows = value.shape[0]
    high, low = split(value)
    left = jnp.concatenate(
        [jnp.concatenate([high, high], axis=1), jnp.concatenate([low, low], axis=1)], axis=0
    )
    got = dot_nn(left, matrix2)
    return got[:rows] + got[rows:]


class Place:
    def __init__(self):
        self.gx = lax.axis_index("gx")
        self.gy = lax.axis_index("gy")
        par = lax.rem(self.gx, 2)
        even = par == 0
        self.sgn = 1 - 2 * par
        self.p_own = jnp.where(even, 3, 2)
        self.p_far = jnp.where(even, 4, 1)
        self.p_third = jnp.where(even, 0, 5)
        self.p_fault = (self.p_own, self.p_far, self.p_third)
        self.x_coarse = lax.rem(self.gx, 5) + 5

    def a_of(self, d):
        return lax.rem(self.x_coarse + d, 5)

    def b_of(self, coarse_y, d):
        return lax.rem(self.gy * (CY // 2) + coarse_y + d + 5, 5)


def roll_weights(w, wr, first, count):
    for p in range(7):
        for o, step in enumerate(FORWARD):
            if step[2] == 0 or (p == 0 and o < 4):
                continue
            at = (p * PER + o) * ROWS + first
            distance = 1 if step[2] == 1 else NZ - 1
            wr[at : at + count, :] = pltpu.roll(w[at : at + count, :], distance, 1)


def smooth(w, wr, fd, qc, inv, diag, first, count):
    even_y = (lax.broadcasted_iota(jnp.int32, (count, NZ), 0) & 1) == 0
    even_z = (lax.broadcasted_iota(jnp.int32, (count, NZ), 1) & 1) == 0
    for p in range(6):
        base = p + 1

        def weight(dx, dy, dz):
            if (dx, dy, dz) in OFFSET:
                start = (base * PER + OFFSET[dx, dy, dz]) * ROWS + 1 + first
                return w[start : start + count, :]
            o = OFFSET[-dx, -dy, -dz]
            start = ((base + dx) * PER + o) * ROWS + 1 + first + dy
            return (w if dz == 0 else wr)[start : start + count, :]

        near = 1 if p % 2 == 0 else -1
        sums = {}
        for dz in (-1, 0, 1):
            got = {}
            for dx in (-1, 0, 1):
                below, above = weight(dx, -1, dz), weight(dx, 1, dz)
                got[dx, 0] = jnp.where(even_y, above, below)
                if (dx, dz) != (0, 0):
                    got[dx, 0] = got[dx, 0] + weight(dx, 0, dz)
                got[dx, 1] = jnp.where(even_y, below, above)
            for sy in range(2):
                sums[0, sy, dz] = got[0, sy] + got[near, sy]
                sums[1, sy, dz] = got[-near, sy]
        start = (base * PER + 13) * ROWS + 1 + first
        at = p * 16 + first
        total = w[start : start + count, :] + fd[at : at + count, :]
        r = []
        for sx in range(2):
            for sy in range(2):
                down, same, up = (sums[sx, sy, dz] for dz in (-1, 0, 1))
                r.append(same + jnp.where(even_z, up, down))
                r.append(jnp.where(even_z, down, up))
        for value in r:
            total = total + value
        total = jnp.where(total == 0.0, 1.0, total)
        scale = damping / total
        diag[at : at + count, :] = total
        inv[at : at + count, :] = scale
        for k, value in enumerate(r):
            value = value * scale
            if k == 0:
                value = value + (1.0 - damping)
            at = (p * 8 + k) * 16 + first
            qc[at : at + count, :] = value


def spread(here, qc, inv, qe, rf_at, columns, count):
    z8 = lax.broadcasted_iota(jnp.int32, (8, NZ), 1)
    e8 = lax.broadcasted_iota(jnp.int32, (8, NZ), 0)
    beside = jnp.where((z8 & 1) == 0, z8 - 1, z8 + 1)
    mask_own = jnp.where(e8 == colour(z8), 1.0, 0.0)
    mask_oth = jnp.where(e8 == colour(beside + 10), 1.0, 0.0)
    rows5 = jnp.where(e8 < 5, 1.0, 0.0)

    def one(k, carry):
        c = columns(k)
        for p in range(6):
            for lat in range(4):
                at = (p * 8 + 2 * lat) * 16 + c
                qe[p, c, lat] = (
                    qc[pl.ds(at, 1), :] * mask_own + qc[pl.ds(at + 16, 1), :] * mask_oth
                )
        for k, plane in enumerate(here.p_fault):
            qe[plane, c, 2] = qe[plane, c, 2] + rf_at(k, c) * (
                inv[pl.ds(plane * 16 + c, 1), :] * rows5
            )
        return carry

    lax.fori_loop(0, count, one, 0)


def apply_column(w, wr, diag, qe, ap, p, y, odd_y):
    odd_x = p % 2
    acc = {}
    for dx in (-1, 0, 1):
        for dy in (-1, 0, 1):
            q = [qe[p + dx, y + dy, lat] for lat in range(4)]
            own_x = dx if (dx == 1 and odd_x) or (dx == -1 and not odd_x) else 0
            own_y = dy if (dy == 1 and odd_y) or (dy == -1 and not odd_y) else 0
            oth_x = own_x + (1 if (p + dx) % 2 else -1)
            oth_y = own_y + (1 if (odd_y + dy) % 2 else -1)
            for dz in (-1, 0, 1):
                if (dx, dy, dz) == (0, 0, 0):
                    continue
                if (dx, dy, dz) in OFFSET:
                    at = ((p + 1) * PER + OFFSET[dx, dy, dz]) * ROWS + y + 1
                    ref = w if dz == 0 else wr
                else:
                    at = ((p + 1 + dx) * PER + OFFSET[-dx, -dy, -dz]) * ROWS + y + 1 + dy
                    ref = w
                wt = ref[pl.ds(at, 1), :]
                for lat in range(4):
                    lx = oth_x if lat >= 2 else own_x
                    ly = oth_y if lat % 2 else own_y
                    value = wt * q[lat]
                    key = (lx, ly, dz)
                    acc[key] = acc[key] + value if key in acc else value
    centre = diag[pl.ds(p * 16 + y, 1), :]
    for lx in (-1, 0, 1):
        for ly in (-1, 0, 1):
            total = acc[lx, ly, 0]
            total = total + pltpu.roll(acc[lx, ly, 1], NZ - 1, 1)
            total = total + pltpu.roll(acc[lx, ly, -1], 1, 1)
            own_lat = None
            sx = {0: 0, (1 if odd_x else -1): 1}.get(lx)
            sy = {0: 0, (1 if odd_y else -1): 1}.get(ly)
            if sx is not None and sy is not None:
                own_lat = 2 * sx + sy
            if own_lat is None:
                total = -total
            else:
                total = centre * qe[p, y, own_lat] - total
            ap[p - 1, y - 1, lx + 1, ly + 1] = total


def fault_apply(here, qe, ap, c, f2c, ft2c):
    ly_oth = 2 * (c % 2)
    for plane, source, x_own, matrix in (
        (here.p_own, here.p_far, 1 + here.sgn, ft2c),
        (here.p_far, here.p_own, 1 - here.sgn, f2c),
    ):
        total = through(qe[source, c].reshape(32, NZ), matrix)
        for lat in range(4):
            lx = 1 if lat >= 2 else x_own
            ly = ly_oth if lat % 2 else 1
            ap[plane - 1, c - 1, lx, ly] = ap[plane - 1, c - 1, lx, ly] - total[8 * lat : 8 * lat + 8]


def gather(here, qc, ap, tt, coarse_y, rows, add):
    shift = (-1, 0, 0, 1)
    for zk in range(2):
        acc = {}
        for x in range(-1, 3):
            for y in rows:
                lat = 2 * (x not in (0, 1)) + (y not in (0, 1))
                c = 2 * coarse_y + y + 2
                at = ((x + 2) * 8 + 2 * lat + zk) * 16 + c
                q = qc[at : at + 1, :]
                for lx in range(3):
                    for ly in range(3):
                        value = q * ap[x + 1, c - 1, lx, ly]
                        key = (shift[x + 1] + lx - 1, shift[y + 1] + ly - 1)
                        acc[key] = acc[key] + value if key in acc else value
        lane = (coarse_y % 2) * 256 + zk * NZ
        for (dx, dy), value in acc.items():
            at = (coarse_y // 2, here.a_of(dx), here.b_of(coarse_y, dy), slice(None), slice(lane, lane + NZ))
            tt[at] = tt[at] + value if add else value


def gather_fault(here, inv, ap, tt, y, ft2c):
    c = y + 2
    coarse_y = y // 2
    lane = (coarse_y % 2) * 256
    value = ap[here.p_far - 1, c - 1].reshape(72, NZ) * inv[pl.ds(here.p_far * 16 + c, 1), :]
    total = through(value, ft2c)
    for lx in range(3):
        a = here.a_of(lx - 1 + here.sgn)
        for ly in range(3):
            at = (coarse_y // 2, a, here.b_of(coarse_y, ly - 1), slice(None), slice(lane, lane + NZ))
            row = 8 * (3 * lx + ly)
            tt[at] = tt[at] + total[row : row + 8]


INNER = (2, 3, 4, 5)


def rows_of(coarse_y, inner):
    return [y for y in range(-1, 3) if (2 * coarse_y + y in INNER) == inner]


def inner_kernel(
    peers, own, rp, ro, rs, f2, ft2, rf_pair, w, wr, qe, ap, tt, rf_third, qc, inv, diag, fd, eo, hot, both
):
    here = Place()
    ro = Masked(ro, has_other("gx", peers[0]))

    def place(ref, count, first):
        for k in range(count):
            base = (first + k) * ROWS
            w[base + 3 : base + 11, :] = ref[8 * k : 8 * k + 8, :]

    def place_x(odd):
        lo, hi = (rp, ro) if odd else (ro, rp)
        place(lo, 28, PER)
        place(hi, 28, 5 * PER)

    by_parity("gx", place_x)
    place(Masked(rs, here.gx >= 2), 9, 4)
    place(own, 28, 3 * PER)

    beyond, live = slot_columns([ro[232:236, :], ro[228:232, :]])
    fill_tint(eo, beyond, live)
    fill_hot(hot, flat_cells(ro[224:228, :]), range(CY))
    both[...] = dot_nn(hot[...], eo[...])
    fd[...] = jnp.zeros_like(fd)
    for y in range(CY):
        pieces = jnp.transpose(both[y * NZ : (y + 1) * NZ, :])
        rf_third[y] = pieces[:8] + pieces[8:16]
        for plane, value in zip(here.p_fault, (rf_pair[0, y], rf_pair[1, y], rf_third[y])):
            fd[pl.ds(plane * 16 + y + 2, 1), :] = value[5:6, :]

    roll_weights(w, wr, 3, 8)
    smooth(w, wr, fd, qc, inv, diag, 2, 8)
    spread(
        here, qc, inv, qe, lambda k, c: rf_third[c - 2] if k == 2 else rf_pair[k, c - 2], lambda k: k + 3, 6
    )

    def pair(k, carry):
        for p in range(1, 5):
            apply_column(w, wr, diag, qe, ap, p, 2 * k + 4, 0)
            apply_column(w, wr, diag, qe, ap, p, 2 * k + 5, 1)
        return carry

    lax.fori_loop(0, 2, pair, 0)
    for y in INNER:
        fault_apply(here, qe, ap, y + 2, f2[y], ft2[y])
    tt[...] = jnp.zeros_like(tt)
    for coarse_y in range(CY // 2):
        gather(here, qc, ap, tt, coarse_y, rows_of(coarse_y, True), False)
    for y in INNER:
        gather_fault(here, inv, ap, tt, y, ft2[y])


def main_kernel(
    peers,
    from_core,
    from_chip,
    f2,
    ft2,
    rf_pair,
    rf_third,
    w_in,
    wr_in,
    qe_in,
    ap_in,
    tt_in,
    out,
    w,
    wr,
    qe,
    ap,
    tt,
    qc,
    inv,
    diag,
    fd,
    rf,
    f2h,
    ft2h,
    far2,
    eo,
    hot,
):
    del w_in, wr_in, qe_in, ap_in, tt_in
    here = Place()
    from_chip = Masked(from_chip, has_other("gy", peers[1]))

    def place_y(odd):
        yl, yh = (from_core, from_chip) if odd else (from_chip, from_core)
        for ref, row, third, runs in ((yl, 1, 0, (1, 10)), (yh, 11, 13, (4,))):
            for c in range(2):
                base = c * COLBLOCK
                w[pl.ds(4 * ROWS + row + c, 9, stride=ROWS), :] = ref[base : base + 9, :]
                w[pl.ds(PER * ROWS + row + c, 84, stride=ROWS), :] = ref[base + 9 : base + 93, :]
            at = THIRD
            for plane in range(7):
                for o in runs[-1:] if plane == 0 else runs:
                    start = (plane * PER + o) * ROWS + third
                    w[pl.ds(start, 3, stride=ROWS), :] = ref[at : at + 3, :]
                    at += 3

    by_parity("gy", place_y)
    roll_weights(w, wr, 0, 16)

    fd[...] = jnp.zeros_like(fd)

    def put(column, k, value):
        rf[k, column] = value
        fd[pl.ds(here.p_fault[k] * 16 + column, 1), :] = value[5:6, :]

    for y in range(CY):
        put(y + 2, 0, rf_pair[0, y])
        put(y + 2, 1, rf_pair[1, y])
        put(y + 2, 2, rf_third[y])
    core_rows = from_core[FAULT_ROW : FAULT_ROW + 24, :]
    chip_rows = from_chip[FAULT_ROW : FAULT_ROW + 24, :]
    odd_y = lax.rem(here.gy, 2) == 1
    for side, first, second, columns in (
        (0, core_rows, chip_rows, ((0, 6), (1, 7))),
        (1, chip_rows, core_rows, ((10, 0), (11, 1))),
    ):
        rows = jnp.where(odd_y, first, second)
        cells, far, weight, cells_o, far_o, weight_o = (rows[4 * k : 4 * k + 4] for k in range(6))
        partner, live, beyond, live_o = slot_columns([far, weight, far_o, weight_o])
        fill_far(far2.at[side], partner, live)
        fill_tint(eo.at[side], beyond, live_o)
        ys = [y for _, y in columns]
        fill_hot(hot.at[side, 0], flat_cells(cells), ys)
        fill_hot(hot.at[side, 1], flat_cells(cells_o), ys)
        pair = dot_nn(hot[side, 0], far2[side])
        third = dot_nn(hot[side, 1], eo[side])
        for k, (column, y) in enumerate(columns):
            near, near_t, at_own, at_far = pair_matrix(pair[k * NZ : (k + 1) * NZ])
            if column in (1, 10):
                f2h[side] = near
                ft2h[side] = near_t
            put(column, 0, at_own)
            put(column, 1, at_far)
            pieces = jnp.transpose(third[k * NZ : (k + 1) * NZ])
            put(column, 2, pieces[:8] + pieces[8:16])

    smooth(w, wr, fd, qc, inv, diag, 0, 16)
    spread(
        here, qc, inv, qe, lambda k, c: rf[k, c], lambda k: jnp.where(k < 3, k, k + 6), 6
    )

    def outer_pair(k, carry):
        odd_y = 1 + 2 * k + 4 * (k // 2)
        even_y = 2 + 6 * jnp.minimum(k, 1) + 2 * (k // 2)
        for p in range(1, 5):
            apply_column(w, wr, diag, qe, ap, p, odd_y, 1)
            apply_column(w, wr, diag, qe, ap, p, even_y, 0)
        return carry

    lax.fori_loop(0, 3, outer_pair, 0)
    outer = [y for y in range(CY) if y not in INNER]
    for y in outer:
        fault_apply(here, qe, ap, y + 2, f2[y], ft2[y])
    fault_apply(here, qe, ap, 1, f2h[0], ft2h[0])
    fault_apply(here, qe, ap, 10, f2h[1], ft2h[1])
    for coarse_y in range(CY // 2):
        gather(here, qc, ap, tt, coarse_y, rows_of(coarse_y, False), True)
    for y in outer:
        gather_fault(here, inv, ap, tt, y, ft2[y])

    kz = lax.broadcasted_iota(jnp.int32, (512, NZ), 0)
    kout = lax.broadcasted_iota(jnp.int32, (512, NZ), 1)
    z_in = kz & 127
    is_oth = ((kz >> 7) & 1) == 1
    target = jnp.where(
        is_oth, (z_in >> 1) + jnp.where((z_in & 1) == 0, -1, 1), z_in >> 1
    )
    fits = (target == (kout & 63)) & ((kz >> 8) == (kout >> 6))
    collect = jnp.where(fits, 1.0, 0.0).astype(bf16)
    for pair in range(2):
        high, low = split(tt[pair].reshape(200, 512))
        got = (dot_nn(high, collect) + dot_nn(low, collect)) * 0.125
        for k in range(25):
            out[5 * k : 5 * k + 5, 0, pair * NZ : (pair + 1) * NZ] = got[8 * k : 8 * k + 5]


def send(value, axis, target):
    peers = lax.axis_size(axis)
    return lax.ppermute(value, axis, [(i, target(i, peers)) for i in range(peers)])


def partner_of(i, peers):
    return i ^ 1


def other_of(i, peers):
    j = i + 1 if i % 2 else i - 1
    return j if 0 <= j < peers else i


def ahead_of(i, peers):
    return (i + 2) % peers


VMEM = pl.BlockSpec(memory_space=pltpu.VMEM)
HBM = pl.BlockSpec(memory_space=pltpu.HBM)


def params(mib):
    return pltpu.CompilerParams(vmem_limit_bytes=mib * 1024 * 1024)


def sds(*shape, dtype=f32):
    return jax.ShapeDtypeStruct(shape, dtype)


def per_device(trans, storage, fault_cells, fault_count, fault_trans):
    peers = (lax.axis_size("gx"), lax.axis_size("gy"))
    cells = send(fault_cells, "gx", partner_of)
    sources = [
        pltpu.with_memory_space_constraint(array, pltpu.HBM)
        for array in (trans, storage, fault_cells, fault_trans)
    ]
    own, plane = pl.pallas_call(
        functools.partial(pack_kernel, peers),
        out_shape=(sds(232, NZ), sds(72, NZ)),
        in_specs=[pl.BlockSpec(memory_space=pltpu.SMEM)] + [HBM] * 4,
        out_specs=(VMEM,) * 2,
        scratch_shapes=[pltpu.VMEM(array.shape, array.dtype) for array in sources]
        + [pltpu.SemaphoreType.DMA((4,))],
        compiler_params=params(16),
        name="pack",
    )(fault_count, *sources)
    joined = pl.pallas_call(
        join_kernel,
        out_shape=sds(240, NZ),
        in_specs=[VMEM] * 2,
        out_specs=VMEM,
        compiler_params=params(16),
        name="join",
    )(own, cells)
    ro = send(joined, "gx", other_of)
    rp = send(own, "gx", partner_of)
    pieces = sds(CY, 2 * NZ, NZ, dtype=bf16)
    f2, ft2, rf_pair, plane = pl.pallas_call(
        fault_kernel,
        out_shape=(pieces, pieces, sds(2, CY, 8, NZ), sds(72, NZ)),
        in_specs=[VMEM] * 3,
        out_specs=(VMEM,) * 4,
        scratch_shapes=[
            pltpu.VMEM((SLOTS, 2 * NZ), bf16),
            pltpu.VMEM((CY * NZ, SLOTS), bf16),
            pltpu.VMEM((CY * NZ, 2 * NZ), f32),
        ],
        compiler_params=params(16),
        cost_estimate=pl.CostEstimate(flops=2 * 10**9, bytes_accessed=2**21, transcendentals=0),
        name="faults",
    )(own, plane, cells)
    rs = send(plane, "gx", ahead_of)
    to_core, to_chip = pl.pallas_call(
        functools.partial(column_kernel, peers),
        out_shape=(sds(Y_ROWS, NZ), sds(Y_ROWS, NZ)),
        in_specs=[VMEM] * 6,
        out_specs=(VMEM,) * 2,
        compiler_params=params(16),
        name="columns",
    )(own, rp, ro, rs, cells, rf_pair)
    from_chip = send(to_chip, "gy", other_of)
    from_core = send(to_core, "gy", partner_of)
    work = (
        sds(7 * PER * ROWS, NZ),
        sds(7 * PER * ROWS, NZ),
        sds(6, 12, 4, 8, NZ),
        sds(4, 10, 3, 3, 8, NZ),
        sds(2, 5, 5, 8, 512),
    )
    fields = [
        pltpu.VMEM((6 * 8 * 16, NZ), f32),
        pltpu.VMEM((6 * 16, NZ), f32),
        pltpu.VMEM((6 * 16, NZ), f32),
        pltpu.VMEM((6 * 16, NZ), f32),
    ]
    *work_in, rf_third = pl.pallas_call(
        functools.partial(inner_kernel, peers),
        out_shape=work + (sds(CY, 8, NZ),),
        in_specs=[VMEM] * 7,
        out_specs=(VMEM,) * 6,
        scratch_shapes=fields
        + [
            pltpu.VMEM((SLOTS, NZ), bf16),
            pltpu.VMEM((CY * NZ, SLOTS), bf16),
            pltpu.VMEM((CY * NZ, NZ), f32),
        ],
        compiler_params=params(16),
        cost_estimate=pl.CostEstimate(flops=4 * 10**9, bytes_accessed=2**21, transcendentals=0),
        name="inner",
    )(own, rp, ro, rs, f2, ft2, rf_pair)
    result, *_ = pl.pallas_call(
        functools.partial(main_kernel, peers),
        out_shape=(sds(125, 1, 256),) + work,
        in_specs=[VMEM] * 11,
        out_specs=(VMEM,) * 6,
        scratch_shapes=fields
        + [
            pltpu.VMEM((3, 12, 8, NZ), f32),
            pltpu.VMEM((2, 2 * NZ, NZ), bf16),
            pltpu.VMEM((2, 2 * NZ, NZ), bf16),
            pltpu.VMEM((2, SLOTS, 2 * NZ), bf16),
            pltpu.VMEM((2, SLOTS, NZ), bf16),
            pltpu.VMEM((2, 2, 2 * NZ, SLOTS), bf16),
        ],
        input_output_aliases={6 + k: 1 + k for k in range(5)},
        compiler_params=params(16),
        name="galerkin",
    )(from_core, from_chip, f2, ft2, rf_pair, rf_third, *work_in)
    return result


def solution(mesh):
    placed = (
        P(None, "gx", "gy"),
        P("gx", "gy"),
        P("gx", "gy", None),
        P("gx", "gy"),
        P("gx", "gy", None),
    )
    return jax.shard_map(
        per_device, mesh=mesh, in_specs=placed, out_specs=P(None, "gx", "gy"), check_vma=False
    )
```

```python
import functools

import jax
import jax.numpy as jnp
from jax import lax
from jax.experimental import pallas as pl
from jax.experimental.pallas import tpu as pltpu
from jax.sharding import PartitionSpec as P

NZ = 128
CY = 8
SLOTS = 512

FORWARD = (
    (0, 0, 1),
    (0, 1, -1),
    (0, 1, 0),
    (0, 1, 1),
    (1, -1, -1),
    (1, -1, 0),
    (1, -1, 1),
    (1, 0, -1),
    (1, 0, 0),
    (1, 0, 1),
    (1, 1, -1),
    (1, 1, 0),
    (1, 1, 1),
)
OFFSET = {step: k for k, step in enumerate(FORWARD)}
damping = 2.0 / 3.0

ROWS = 24
PER = 14
COLBLOCK = 93
THIRD = 2 * COLBLOCK
FAULT_ROW = 225
BAND_ROW, SUM_ROW, Y_ROWS = 237, 254, 280
REACH = 8
DIAGONALS = 2 * REACH + 1

f32 = jnp.float32
bf16 = jnp.bfloat16


def dot_nt(a, b):
    return lax.dot_general(a, b, (((1,), (1,)), ((), ())), preferred_element_type=f32)


def dot_nn(a, b):
    return lax.dot_general(a, b, (((1,), (0,)), ((), ())), preferred_element_type=f32)


def split(value):
    high = value.astype(bf16)
    return high, (value - high.astype(f32)).astype(bf16)


def pack_kernel(peers, count, *refs):
    sources, (block, plane), targets, sems = refs[:4], refs[4:6], refs[6:10], refs[10]
    copies = [
        pltpu.make_async_copy(src, dst, sems.at[k])
        for k, (src, dst) in enumerate(zip(sources, targets))
    ]
    for copy in copies:
        copy.start()
    for copy in copies:
        copy.wait()
    trans, storage, cells, ftrans = targets
    last_x = lax.axis_index("gx") == peers[0] - 1
    first_y = lax.axis_index("gy") == 0
    last_y = lax.axis_index("gy") == peers[1] - 1
    depth = lax.broadcasted_iota(jnp.int32, (8, NZ), 1)
    row = lax.broadcasted_iota(jnp.int32, (8, NZ), 0)
    for x in range(2):
        for o in range(PER):
            base = (x * PER + o) * 8
            for y in range(CY):
                lanes = slice(y * NZ, (y + 1) * NZ)
                if o < 13:
                    value = trans[o, x : x + 1, lanes]
                else:
                    value = storage[x : x + 1, lanes]
                block[base + y : base + y + 1, :] = value
            if o == 13:
                continue
            step = FORWARD[o]
            keep = None
            if step[2] == 1:
                keep = depth < NZ - 1
            if step[2] == -1:
                keep = depth > 0
            if step[1] == 1:
                inside = (row < CY - 1) | jnp.logical_not(last_y)
                keep = inside if keep is None else keep & inside
            if step[1] == -1:
                inside = (row > 0) | jnp.logical_not(first_y)
                keep = inside if keep is None else keep & inside
            if step[0] == 1 and x == 1:
                inside = (row >= 0) & jnp.logical_not(last_x)
                keep = inside if keep is None else keep & inside
            if keep is not None:
                block[base : base + 8, :] = jnp.where(keep, block[base : base + 8, :], 0.0)
    live = count[0, 0]
    lane = lax.broadcasted_iota(jnp.int32, (1, NZ), 1)
    base = 2 * PER * 8
    for r in range(4):
        lanes = slice(r * NZ, (r + 1) * NZ)
        block[base + r : base + r + 1, :] = cells[0, :, lanes].astype(f32)
        block[base + 4 + r : base + 5 + r, :] = jnp.where(
            lane + r * NZ < live, ftrans[0, :, lanes], 0.0
        )
    plane[...] = block[(PER + 4) * 8 : (PER + 13) * 8, :]


def partner_rows(cells):
    return jnp.concatenate(
        [cells[0, :, r * NZ : (r + 1) * NZ] for r in range(4)], axis=0
    ).astype(f32)


def join_kernel(own, cells, joined):
    joined[0:232, :] = own[...]
    joined[232:236, :] = partner_rows(cells)
    joined[236:240, :] = jnp.zeros((4, NZ), f32)


def by_parity(axis, body):
    odd = lax.rem(lax.axis_index(axis), 2)
    for k in range(2):
        pl.when(odd == k)(functools.partial(body, k))


class Masked:
    def __init__(self, ref, due):
        self.ref, self.due = ref, due

    def __getitem__(self, index):
        return jnp.where(self.due, self.ref[index], 0.0)


def has_other(axis, peers):
    at = lax.axis_index(axis)
    return jnp.where(lax.rem(at, 2) == 0, at > 0, at < peers - 1)


def column_kernel(peers, own, rp, ro, rs, band, sums, to_core, to_chip):
    ro = Masked(ro, has_other("gx", peers[0]))
    lo2 = Masked(rs, lax.axis_index("gx") >= 2)

    def fill(out, lo, hi, first, third, runs):
        for c in range(2):
            y = first + c
            base = c * COLBLOCK
            out[base : base + 9, :] = lo2[pl.ds(y, 9, stride=8), :]
            for k, ref in enumerate((lo, own, hi)):
                start = base + 9 + 28 * k
                out[start : start + 28, :] = ref[pl.ds(y, 28, stride=8), :]
        at = THIRD
        out[at : at + 3, :] = lo2[pl.ds((runs[-1] - 4) * 8 + third, 3, stride=8), :]
        at += 3
        for ref in (lo, own, hi):
            for x in range(2):
                for o in runs:
                    out[at : at + 3, :] = ref[pl.ds((x * PER + o) * 8 + third, 3, stride=8), :]
                    at += 3
        for k, start in enumerate((224, 232, 228)):
            out[FAULT_ROW + 4 * k : FAULT_ROW + 4 * k + 4, :] = ro[start : start + 4, :]
        out[BAND_ROW : BAND_ROW + DIAGONALS, :] = band[int(first > 0), 0:DIAGONALS, :]
        for c in range(2):
            for k in range(2):
                at = SUM_ROW + (2 * c + k) * 6
                out[at : at + 6, :] = sums[k, first + c, 0:6, :]
        out[SUM_ROW + 24 : Y_ROWS, :] = jnp.zeros((Y_ROWS - SUM_ROW - 24, NZ), f32)

    def for_x(odd_x):
        lo, hi = (rp, ro) if odd_x else (ro, rp)

        def for_y(odd_y):
            up, down = (to_chip, to_core) if odd_y else (to_core, to_chip)
            fill(up, lo, hi, CY - 2, CY - 3, (1, 10))
            fill(down, lo, hi, 0, 2, (4,))

        by_parity("gy", for_y)

    by_parity("gx", for_x)


def colour(z):
    half = z >> 1
    return half - 5 * ((half * 205) >> 10)


def slot_columns(rows):
    tall = jnp.transpose(jnp.concatenate(rows, axis=0))
    return [[tall[:, 4 * k + r : 4 * k + r + 1] for r in range(4)] for k in range(len(rows))]


def flat_cells(rows):
    row = jnp.concatenate([rows[r : r + 1] for r in range(4)], axis=1)
    return row.astype(jnp.int32) & 1023


def fill_far(far2, partner, live):
    lane = lax.broadcasted_iota(jnp.int32, (NZ, NZ), 1)
    for r in range(4):
        rows = slice(r * NZ, (r + 1) * NZ)
        match = (partner[r].astype(jnp.int32) & 127) == lane
        high = live[r].astype(bf16).astype(f32)
        far2[rows, 0:NZ] = jnp.where(match, high, 0.0).astype(bf16)
        far2[rows, NZ : 2 * NZ] = jnp.where(match, live[r] - high, 0.0).astype(bf16)


def flat_rows(rows):
    return jnp.concatenate([rows[r : r + 1] for r in range(4)], axis=1)


def colour_sums(hot, beyond, live):
    e16 = lax.broadcasted_iota(jnp.int32, (16, SLOTS), 0)
    tint = colour(flat_rows(beyond).astype(jnp.int32) & 127)
    live = flat_rows(live)
    high = live.astype(bf16).astype(f32)
    value = jnp.where((e16 == tint) | (e16 == 5), high, 0.0)
    value = jnp.where((e16 == tint + 8) | (e16 == 13), live - high, value)
    got = dot_nt(value.astype(bf16), hot)
    return got[:8] + got[8:]


def diagonals(hot, own, far, live):
    d24 = lax.broadcasted_iota(jnp.int32, (24, SLOTS), 0)
    step = (flat_rows(far).astype(jnp.int32) & 127) - (flat_rows(own).astype(jnp.int32) & 127)
    live = flat_rows(live)
    high = live.astype(bf16).astype(f32)
    match = step + REACH == d24
    both = [jnp.where(match, value, 0.0) for value in (high, live - high)]
    got = dot_nt(jnp.concatenate(both, axis=0).astype(bf16), hot)
    return got[:24] + got[24:]


def fill_hot(hot, cells, columns):
    z128 = lax.broadcasted_iota(jnp.int32, (NZ, SLOTS), 0)
    for k, y in enumerate(columns):
        value = jnp.where(cells == z128 + y * NZ, 1.0, 0.0)
        hot[k * NZ : (k + 1) * NZ, :] = value.astype(bf16)


def pair_matrix(both):
    z8 = lax.broadcasted_iota(jnp.int32, (8, NZ), 1)
    e8 = lax.broadcasted_iota(jnp.int32, (8, NZ), 0)
    one = jnp.where((e8 == colour(z8)) | (e8 == 5), 1.0, 0.0).astype(bf16)
    one2 = jnp.concatenate([one, one], axis=1)
    matrix = both[:, :NZ] + both[:, NZ:]
    f2 = jnp.concatenate(split(matrix), axis=0)
    ft2 = jnp.concatenate(split(jnp.transpose(matrix)), axis=0)
    return f2, ft2, dot_nn(one2, ft2), dot_nn(one2, f2)


def fault_kernel(own, cells, f2, ft2, rf, band, far2, hot, both):
    partner, live = slot_columns([partner_rows(cells), own[228:232, :]])
    fill_far(far2, partner, live)
    fill_hot(hot, flat_cells(own[224:228, :]), range(CY))
    both[...] = dot_nn(hot[...], far2[...])
    for y in range(CY):
        f2[y], ft2[y], rf[0, y], rf[1, y] = pair_matrix(both[y * NZ : (y + 1) * NZ, :])
    for k, y in enumerate((0, CY - 1)):
        band[k] = diagonals(
            hot[y * NZ : (y + 1) * NZ, :], own[224:228, :], partner_rows(cells), own[228:232, :]
        )


def through(value, matrix2):
    rows = value.shape[0]
    high, low = split(value)
    left = jnp.concatenate(
        [jnp.concatenate([high, high], axis=1), jnp.concatenate([low, low], axis=1)], axis=0
    )
    got = dot_nn(left, matrix2)
    return got[:rows] + got[rows:]


class Place:
    def __init__(self):
        self.gx = lax.axis_index("gx")
        self.gy = lax.axis_index("gy")
        par = lax.rem(self.gx, 2)
        even = par == 0
        self.sgn = 1 - 2 * par
        self.p_own = jnp.where(even, 3, 2)
        self.p_far = jnp.where(even, 4, 1)
        self.p_third = jnp.where(even, 0, 5)
        self.p_fault = (self.p_own, self.p_far, self.p_third)
        self.x_coarse = lax.rem(self.gx, 5) + 5

    def a_of(self, d):
        return lax.rem(self.x_coarse + d, 5)

    def b_of(self, coarse_y, d):
        return lax.rem(self.gy * (CY // 2) + coarse_y + d + 5, 5)


def roll_weights(w, wr, first, count):
    for p in range(7):
        for o, step in enumerate(FORWARD):
            if step[2] == 0 or (p == 0 and o < 4):
                continue
            at = (p * PER + o) * ROWS + first
            distance = 1 if step[2] == 1 else NZ - 1
            wr[at : at + count, :] = pltpu.roll(w[at : at + count, :], distance, 1)


def smooth(w, wr, fd, qc, inv, diag, first, count):
    even_y = (lax.broadcasted_iota(jnp.int32, (count, NZ), 0) & 1) == 0
    even_z = (lax.broadcasted_iota(jnp.int32, (count, NZ), 1) & 1) == 0
    for p in range(6):
        base = p + 1

        def weight(dx, dy, dz):
            if (dx, dy, dz) in OFFSET:
                start = (base * PER + OFFSET[dx, dy, dz]) * ROWS + 1 + first
                return w[start : start + count, :]
            o = OFFSET[-dx, -dy, -dz]
            start = ((base + dx) * PER + o) * ROWS + 1 + first + dy
            return (w if dz == 0 else wr)[start : start + count, :]

        near = 1 if p % 2 == 0 else -1
        sums = {}
        for dz in (-1, 0, 1):
            got = {}
            for dx in (-1, 0, 1):
                below, above = weight(dx, -1, dz), weight(dx, 1, dz)
                got[dx, 0] = jnp.where(even_y, above, below)
                if (dx, dz) != (0, 0):
                    got[dx, 0] = got[dx, 0] + weight(dx, 0, dz)
                got[dx, 1] = jnp.where(even_y, below, above)
            for sy in range(2):
                sums[0, sy, dz] = got[0, sy] + got[near, sy]
                sums[1, sy, dz] = got[-near, sy]
        start = (base * PER + 13) * ROWS + 1 + first
        at = p * 16 + first
        total = w[start : start + count, :] + fd[at : at + count, :]
        r = []
        for sx in range(2):
            for sy in range(2):
                down, same, up = (sums[sx, sy, dz] for dz in (-1, 0, 1))
                r.append(same + jnp.where(even_z, up, down))
                r.append(jnp.where(even_z, down, up))
        for value in r:
            total = total + value
        total = jnp.where(total == 0.0, 1.0, total)
        scale = damping / total
        diag[at : at + count, :] = total
        inv[at : at + count, :] = scale
        for k, value in enumerate(r):
            value = value * scale
            if k == 0:
                value = value + (1.0 - damping)
            at = (p * 8 + k) * 16 + first
            qc[at : at + count, :] = value


def spread(here, qc, inv, qe, rf_at, columns, count):
    z8 = lax.broadcasted_iota(jnp.int32, (8, NZ), 1)
    e8 = lax.broadcasted_iota(jnp.int32, (8, NZ), 0)
    beside = jnp.where((z8 & 1) == 0, z8 - 1, z8 + 1)
    mask_own = jnp.where(e8 == colour(z8), 1.0, 0.0)
    mask_oth = jnp.where(e8 == colour(beside + 10), 1.0, 0.0)
    rows5 = jnp.where(e8 < 5, 1.0, 0.0)

    def one(k, carry):
        c = columns(k)
        for p in range(6):
            for lat in range(4):
                at = (p * 8 + 2 * lat) * 16 + c
                qe[p, c, lat] = (
                    qc[pl.ds(at, 1), :] * mask_own + qc[pl.ds(at + 16, 1), :] * mask_oth
                )
        for k, plane in enumerate(here.p_fault):
            qe[plane, c, 2] = qe[plane, c, 2] + rf_at(k, c) * (
                inv[pl.ds(plane * 16 + c, 1), :] * rows5
            )
        return carry

    lax.fori_loop(0, count, one, 0)


def apply_column(w, wr, diag, qe, ap, p, y, odd_y):
    odd_x = p % 2
    acc = {}
    for dx in (-1, 0, 1):
        for dy in (-1, 0, 1):
            q = [qe[p + dx, y + dy, lat] for lat in range(4)]
            own_x = dx if (dx == 1 and odd_x) or (dx == -1 and not odd_x) else 0
            own_y = dy if (dy == 1 and odd_y) or (dy == -1 and not odd_y) else 0
            oth_x = own_x + (1 if (p + dx) % 2 else -1)
            oth_y = own_y + (1 if (odd_y + dy) % 2 else -1)
            for dz in (-1, 0, 1):
                if (dx, dy, dz) == (0, 0, 0):
                    continue
                if (dx, dy, dz) in OFFSET:
                    at = ((p + 1) * PER + OFFSET[dx, dy, dz]) * ROWS + y + 1
                    ref = w if dz == 0 else wr
                else:
                    at = ((p + 1 + dx) * PER + OFFSET[-dx, -dy, -dz]) * ROWS + y + 1 + dy
                    ref = w
                wt = ref[pl.ds(at, 1), :]
                for lat in range(4):
                    lx = oth_x if lat >= 2 else own_x
                    ly = oth_y if lat % 2 else own_y
                    value = wt * q[lat]
                    key = (lx, ly, dz)
                    acc[key] = acc[key] + value if key in acc else value
    centre = diag[pl.ds(p * 16 + y, 1), :]
    for lx in (-1, 0, 1):
        for ly in (-1, 0, 1):
            total = acc[lx, ly, 0]
            total = total + pltpu.roll(acc[lx, ly, 1], NZ - 1, 1)
            total = total + pltpu.roll(acc[lx, ly, -1], 1, 1)
            own_lat = None
            sx = {0: 0, (1 if odd_x else -1): 1}.get(lx)
            sy = {0: 0, (1 if odd_y else -1): 1}.get(ly)
            if sx is not None and sy is not None:
                own_lat = 2 * sx + sy
            if own_lat is None:
                total = -total
            else:
                total = centre * qe[p, y, own_lat] - total
            ap[p - 1, y - 1, lx + 1, ly + 1] = total


def fault_apply(here, qe, ap, c, f2c, ft2c):
    ly_oth = 2 * (c % 2)
    for plane, source, x_own, matrix in (
        (here.p_own, here.p_far, 1 + here.sgn, ft2c),
        (here.p_far, here.p_own, 1 - here.sgn, f2c),
    ):
        total = through(qe[source, c].reshape(32, NZ), matrix)
        for lat in range(4):
            lx = 1 if lat >= 2 else x_own
            ly = ly_oth if lat % 2 else 1
            ap[plane - 1, c - 1, lx, ly] = ap[plane - 1, c - 1, lx, ly] - total[8 * lat : 8 * lat + 8]


def fault_apply_band(here, qe, ap, c, band):
    ly_oth = 2 * (c % 2)
    to_own, to_far = [0.0] * 4, [0.0] * 4
    for d in range(DIAGONALS):
        weight = band[d : d + 1, :]
        for lat in range(4):
            ahead = pltpu.roll(qe[here.p_far, c, lat], (REACH - d) % NZ, 1)
            to_own[lat] = to_own[lat] + weight * ahead
            back = weight * qe[here.p_own, c, lat]
            to_far[lat] = to_far[lat] + pltpu.roll(back, (d - REACH) % NZ, 1)
    for plane, x_own, total in (
        (here.p_own, 1 + here.sgn, to_own),
        (here.p_far, 1 - here.sgn, to_far),
    ):
        for lat in range(4):
            lx = 1 if lat >= 2 else x_own
            ly = ly_oth if lat % 2 else 1
            ap[plane - 1, c - 1, lx, ly] = ap[plane - 1, c - 1, lx, ly] - total[lat]


def gather(here, qc, ap, tt, coarse_y, rows, add):
    shift = (-1, 0, 0, 1)
    for zk in range(2):
        acc = {}
        for x in range(-1, 3):
            for y in rows:
                lat = 2 * (x not in (0, 1)) + (y not in (0, 1))
                c = 2 * coarse_y + y + 2
                at = ((x + 2) * 8 + 2 * lat + zk) * 16 + c
                q = qc[at : at + 1, :]
                for lx in range(3):
                    for ly in range(3):
                        value = q * ap[x + 1, c - 1, lx, ly]
                        key = (shift[x + 1] + lx - 1, shift[y + 1] + ly - 1)
                        acc[key] = acc[key] + value if key in acc else value
        lane = (coarse_y % 2) * 256 + zk * NZ
        for (dx, dy), value in acc.items():
            at = (coarse_y // 2, here.a_of(dx), here.b_of(coarse_y, dy), slice(None), slice(lane, lane + NZ))
            tt[at] = tt[at] + value if add else value


def gather_fault(here, inv, ap, tt, y, ft2c):
    c = y + 2
    coarse_y = y // 2
    lane = (coarse_y % 2) * 256
    value = ap[here.p_far - 1, c - 1].reshape(72, NZ) * inv[pl.ds(here.p_far * 16 + c, 1), :]
    total = through(value, ft2c)
    for lx in range(3):
        a = here.a_of(lx - 1 + here.sgn)
        for ly in range(3):
            at = (coarse_y // 2, a, here.b_of(coarse_y, ly - 1), slice(None), slice(lane, lane + NZ))
            row = 8 * (3 * lx + ly)
            tt[at] = tt[at] + total[row : row + 8]


INNER = (2, 3, 4, 5)


def rows_of(coarse_y, inner):
    return [y for y in range(-1, 3) if (2 * coarse_y + y in INNER) == inner]


def inner_kernel(
    peers, own, rp, ro, rs, f2, ft2, rf_pair, w, wr, qe, ap, tt, rf_third, qc, inv, diag, fd, hot
):
    here = Place()
    ro = Masked(ro, has_other("gx", peers[0]))

    def place(ref, count, first):
        for k in range(count):
            base = (first + k) * ROWS
            w[base + 3 : base + 11, :] = ref[8 * k : 8 * k + 8, :]

    def place_x(odd):
        lo, hi = (rp, ro) if odd else (ro, rp)
        place(lo, 28, PER)
        place(hi, 28, 5 * PER)

    by_parity("gx", place_x)
    place(Masked(rs, here.gx >= 2), 9, 4)
    place(own, 28, 3 * PER)

    fill_hot(hot, flat_cells(ro[224:228, :]), range(CY))
    got = colour_sums(hot[...], ro[232:236, :], ro[228:232, :])
    fd[...] = jnp.zeros_like(fd)
    for y in range(CY):
        rf_third[y] = got[:, y * NZ : (y + 1) * NZ]
        for plane, value in zip(here.p_fault, (rf_pair[0, y], rf_pair[1, y], rf_third[y])):
            fd[pl.ds(plane * 16 + y + 2, 1), :] = value[5:6, :]

    roll_weights(w, wr, 3, 8)
    smooth(w, wr, fd, qc, inv, diag, 2, 8)
    spread(
        here, qc, inv, qe, lambda k, c: rf_third[c - 2] if k == 2 else rf_pair[k, c - 2], lambda k: k + 3, 6
    )

    def pair(k, carry):
        for p in range(1, 5):
            apply_column(w, wr, diag, qe, ap, p, 2 * k + 4, 0)
            apply_column(w, wr, diag, qe, ap, p, 2 * k + 5, 1)
        return carry

    lax.fori_loop(0, 2, pair, 0)
    for y in INNER:
        fault_apply(here, qe, ap, y + 2, f2[y], ft2[y])
    tt[...] = jnp.zeros_like(tt)
    for coarse_y in range(CY // 2):
        gather(here, qc, ap, tt, coarse_y, rows_of(coarse_y, True), False)
    for y in INNER:
        gather_fault(here, inv, ap, tt, y, ft2[y])


def main_kernel(
    peers,
    from_core,
    from_chip,
    f2,
    ft2,
    rf_pair,
    rf_third,
    w_in,
    wr_in,
    qe_in,
    ap_in,
    tt_in,
    out,
    w,
    wr,
    qe,
    ap,
    tt,
    qc,
    inv,
    diag,
    fd,
    rf,
    band,
    hot,
):
    del w_in, wr_in, qe_in, ap_in, tt_in
    here = Place()
    from_chip = Masked(from_chip, has_other("gy", peers[1]))

    def place_y(odd):
        yl, yh = (from_core, from_chip) if odd else (from_chip, from_core)
        for ref, row, third, runs in ((yl, 1, 0, (1, 10)), (yh, 11, 13, (4,))):
            for c in range(2):
                base = c * COLBLOCK
                w[pl.ds(4 * ROWS + row + c, 9, stride=ROWS), :] = ref[base : base + 9, :]
                w[pl.ds(PER * ROWS + row + c, 84, stride=ROWS), :] = ref[base + 9 : base + 93, :]
            at = THIRD
            for plane in range(7):
                for o in runs[-1:] if plane == 0 else runs:
                    start = (plane * PER + o) * ROWS + third
                    w[pl.ds(start, 3, stride=ROWS), :] = ref[at : at + 3, :]
                    at += 3

    by_parity("gy", place_y)
    roll_weights(w, wr, 0, 16)

    fd[...] = jnp.zeros_like(fd)

    def put(column, k, value):
        rf[k, column] = value
        fd[pl.ds(here.p_fault[k] * 16 + column, 1), :] = value[5:6, :]

    for y in range(CY):
        put(y + 2, 0, rf_pair[0, y])
        put(y + 2, 1, rf_pair[1, y])
        put(y + 2, 2, rf_third[y])
    odd_y = lax.rem(here.gy, 2) == 1
    for side, first, second, columns in (
        (0, from_core, from_chip, ((0, 6), (1, 7))),
        (1, from_chip, from_core, ((10, 0), (11, 1))),
    ):

        def rows(start, count):
            here_rows = slice(start, start + count)
            return jnp.where(odd_y, first[here_rows, :], second[here_rows, :])

        band[side, 0:DIAGONALS, :] = rows(BAND_ROW, DIAGONALS)
        lists = rows(FAULT_ROW, 12)
        fill_hot(hot.at[side], flat_cells(lists[0:4]), [y for _, y in columns])
        third = colour_sums(hot[side], lists[4:8], lists[8:12])
        for c, (column, _) in enumerate(columns):
            for k in range(2):
                value = rows(SUM_ROW + (2 * c + k) * 6, 6)
                put(column, k, jnp.concatenate([value, jnp.zeros((2, NZ), f32)], axis=0))
            put(column, 2, third[:, c * NZ : (c + 1) * NZ])

    smooth(w, wr, fd, qc, inv, diag, 0, 16)
    spread(
        here, qc, inv, qe, lambda k, c: rf[k, c], lambda k: jnp.where(k < 3, k, k + 6), 6
    )

    def outer_pair(k, carry):
        odd_y = 1 + 2 * k + 4 * (k // 2)
        even_y = 2 + 6 * jnp.minimum(k, 1) + 2 * (k // 2)
        for p in range(1, 5):
            apply_column(w, wr, diag, qe, ap, p, odd_y, 1)
            apply_column(w, wr, diag, qe, ap, p, even_y, 0)
        return carry

    lax.fori_loop(0, 3, outer_pair, 0)
    outer = [y for y in range(CY) if y not in INNER]
    for y in outer:
        fault_apply(here, qe, ap, y + 2, f2[y], ft2[y])
    fault_apply_band(here, qe, ap, 1, band.at[0])
    fault_apply_band(here, qe, ap, 10, band.at[1])
    for coarse_y in range(CY // 2):
        gather(here, qc, ap, tt, coarse_y, rows_of(coarse_y, False), True)
    for y in outer:
        gather_fault(here, inv, ap, tt, y, ft2[y])

    kz = lax.broadcasted_iota(jnp.int32, (512, NZ), 0)
    kout = lax.broadcasted_iota(jnp.int32, (512, NZ), 1)
    z_in = kz & 127
    is_oth = ((kz >> 7) & 1) == 1
    target = jnp.where(
        is_oth, (z_in >> 1) + jnp.where((z_in & 1) == 0, -1, 1), z_in >> 1
    )
    fits = (target == (kout & 63)) & ((kz >> 8) == (kout >> 6))
    collect = jnp.where(fits, 1.0, 0.0).astype(bf16)
    for pair in range(2):
        high, low = split(tt[pair].reshape(200, 512))
        got = (dot_nn(high, collect) + dot_nn(low, collect)) * 0.125
        for k in range(25):
            out[5 * k : 5 * k + 5, 0, pair * NZ : (pair + 1) * NZ] = got[8 * k : 8 * k + 5]


def send(value, axis, target):
    peers = lax.axis_size(axis)
    return lax.ppermute(value, axis, [(i, target(i, peers)) for i in range(peers)])


def partner_of(i, peers):
    return i ^ 1


def other_of(i, peers):
    j = i + 1 if i % 2 else i - 1
    return j if 0 <= j < peers else i


def ahead_of(i, peers):
    return (i + 2) % peers


VMEM = pl.BlockSpec(memory_space=pltpu.VMEM)
HBM = pl.BlockSpec(memory_space=pltpu.HBM)


def params(mib):
    return pltpu.CompilerParams(vmem_limit_bytes=mib * 1024 * 1024)


def sds(*shape, dtype=f32):
    return jax.ShapeDtypeStruct(shape, dtype)


def per_device(trans, storage, fault_cells, fault_count, fault_trans):
    peers = (lax.axis_size("gx"), lax.axis_size("gy"))
    cells = send(fault_cells, "gx", partner_of)
    sources = [
        pltpu.with_memory_space_constraint(array, pltpu.HBM)
        for array in (trans, storage, fault_cells, fault_trans)
    ]
    own, plane = pl.pallas_call(
        functools.partial(pack_kernel, peers),
        out_shape=(sds(232, NZ), sds(72, NZ)),
        in_specs=[pl.BlockSpec(memory_space=pltpu.SMEM)] + [HBM] * 4,
        out_specs=(VMEM,) * 2,
        scratch_shapes=[pltpu.VMEM(array.shape, array.dtype) for array in sources]
        + [pltpu.SemaphoreType.DMA((4,))],
        compiler_params=params(16),
        name="pack",
    )(fault_count, *sources)
    rs = send(plane, "gx", ahead_of)
    joined = pl.pallas_call(
        join_kernel,
        out_shape=sds(240, NZ),
        in_specs=[VMEM] * 2,
        out_specs=VMEM,
        compiler_params=params(16),
        name="join",
    )(own, cells)
    ro = send(joined, "gx", other_of)
    rp = send(own, "gx", partner_of)
    pieces = sds(CY, 2 * NZ, NZ, dtype=bf16)
    f2, ft2, rf_pair, band = pl.pallas_call(
        fault_kernel,
        out_shape=(pieces, pieces, sds(2, CY, 8, NZ), sds(2, 24, NZ)),
        in_specs=[VMEM] * 2,
        out_specs=(VMEM,) * 4,
        scratch_shapes=[
            pltpu.VMEM((SLOTS, 2 * NZ), bf16),
            pltpu.VMEM((CY * NZ, SLOTS), bf16),
            pltpu.VMEM((CY * NZ, 2 * NZ), f32),
        ],
        compiler_params=params(16),
        cost_estimate=pl.CostEstimate(flops=2 * 10**9, bytes_accessed=2**21, transcendentals=0),
        name="faults",
    )(own, cells)
    to_core, to_chip = pl.pallas_call(
        functools.partial(column_kernel, peers),
        out_shape=(sds(Y_ROWS, NZ), sds(Y_ROWS, NZ)),
        in_specs=[VMEM] * 6,
        out_specs=(VMEM,) * 2,
        compiler_params=params(16),
        name="columns",
    )(own, rp, ro, rs, band, rf_pair)
    from_chip = send(to_chip, "gy", other_of)
    from_core = send(to_core, "gy", partner_of)
    work = (
        sds(7 * PER * ROWS, NZ),
        sds(7 * PER * ROWS, NZ),
        sds(6, 12, 4, 8, NZ),
        sds(4, 10, 3, 3, 8, NZ),
        sds(2, 5, 5, 8, 512),
    )
    fields = [
        pltpu.VMEM((6 * 8 * 16, NZ), f32),
        pltpu.VMEM((6 * 16, NZ), f32),
        pltpu.VMEM((6 * 16, NZ), f32),
        pltpu.VMEM((6 * 16, NZ), f32),
    ]
    *work_in, rf_third = pl.pallas_call(
        functools.partial(inner_kernel, peers),
        out_shape=work + (sds(CY, 8, NZ),),
        in_specs=[VMEM] * 7,
        out_specs=(VMEM,) * 6,
        scratch_shapes=fields + [pltpu.VMEM((CY * NZ, SLOTS), bf16)],
        compiler_params=params(16),
        cost_estimate=pl.CostEstimate(flops=4 * 10**9, bytes_accessed=2**21, transcendentals=0),
        name="inner",
    )(own, rp, ro, rs, f2, ft2, rf_pair)
    result, *_ = pl.pallas_call(
        functools.partial(main_kernel, peers),
        out_shape=(sds(125, 1, 256),) + work,
        in_specs=[VMEM] * 11,
        out_specs=(VMEM,) * 6,
        scratch_shapes=fields
        + [
            pltpu.VMEM((3, 12, 8, NZ), f32),
            pltpu.VMEM((2, 24, NZ), f32),
            pltpu.VMEM((2, 2 * NZ, SLOTS), bf16),
        ],
        input_output_aliases={6 + k: 1 + k for k in range(5)},
        compiler_params=params(16),
        name="galerkin",
    )(from_core, from_chip, f2, ft2, rf_pair, rf_third, *work_in)
    return result


def solution(mesh):
    placed = (
        P(None, "gx", "gy"),
        P("gx", "gy"),
        P("gx", "gy", None),
        P("gx", "gy"),
        P("gx", "gy", None),
    )
    return jax.shard_map(
        per_device, mesh=mesh, in_specs=placed, out_specs=P(None, "gx", "gy"), check_vma=False
    )
```

```python
import functools

import jax
import jax.numpy as jnp
from jax import lax
from jax.experimental import pallas as pl
from jax.experimental.pallas import tpu as pltpu
from jax.sharding import PartitionSpec as P

NZ = 128
CY = 8
SLOTS = 512

FORWARD = (
    (0, 0, 1),
    (0, 1, -1),
    (0, 1, 0),
    (0, 1, 1),
    (1, -1, -1),
    (1, -1, 0),
    (1, -1, 1),
    (1, 0, -1),
    (1, 0, 0),
    (1, 0, 1),
    (1, 1, -1),
    (1, 1, 0),
    (1, 1, 1),
)
OFFSET = {step: k for k, step in enumerate(FORWARD)}
damping = 2.0 / 3.0

ROWS = 24
PER = 14
COLBLOCK = 93
THIRD = 2 * COLBLOCK
FAULT_ROW = 225
BAND_ROW, SUM_ROW, Y_ROWS = 237, 254, 280
REACH = 8
DIAGONALS = 2 * REACH + 1

f32 = jnp.float32
bf16 = jnp.bfloat16


def dot_nt(a, b):
    return lax.dot_general(a, b, (((1,), (1,)), ((), ())), preferred_element_type=f32)


def dot_nn(a, b):
    return lax.dot_general(a, b, (((1,), (0,)), ((), ())), preferred_element_type=f32)


def split(value):
    high = value.astype(bf16)
    return high, (value - high.astype(f32)).astype(bf16)


def pack_kernel(peers, count, *refs):
    sources, (block, plane), targets, sems = refs[:4], refs[4:6], refs[6:10], refs[10]
    copies = [
        pltpu.make_async_copy(src, dst, sems.at[k])
        for k, (src, dst) in enumerate(zip(sources, targets))
    ]
    for copy in copies:
        copy.start()
    for copy in copies:
        copy.wait()
    trans, storage, cells, ftrans = targets
    last_x = lax.axis_index("gx") == peers[0] - 1
    first_y = lax.axis_index("gy") == 0
    last_y = lax.axis_index("gy") == peers[1] - 1
    depth = lax.broadcasted_iota(jnp.int32, (8, NZ), 1)
    row = lax.broadcasted_iota(jnp.int32, (8, NZ), 0)
    for x in range(2):
        for o in range(PER):
            base = (x * PER + o) * 8
            for y in range(CY):
                lanes = slice(y * NZ, (y + 1) * NZ)
                if o < 13:
                    value = trans[o, x : x + 1, lanes]
                else:
                    value = storage[x : x + 1, lanes]
                block[base + y : base + y + 1, :] = value
            if o == 13:
                continue
            step = FORWARD[o]
            keep = None
            if step[2] == 1:
                keep = depth < NZ - 1
            if step[2] == -1:
                keep = depth > 0
            if step[1] == 1:
                inside = (row < CY - 1) | jnp.logical_not(last_y)
                keep = inside if keep is None else keep & inside
            if step[1] == -1:
                inside = (row > 0) | jnp.logical_not(first_y)
                keep = inside if keep is None else keep & inside
            if step[0] == 1 and x == 1:
                inside = (row >= 0) & jnp.logical_not(last_x)
                keep = inside if keep is None else keep & inside
            if keep is not None:
                block[base : base + 8, :] = jnp.where(keep, block[base : base + 8, :], 0.0)
    live = count[0, 0]
    lane = lax.broadcasted_iota(jnp.int32, (1, NZ), 1)
    base = 2 * PER * 8
    for r in range(4):
        lanes = slice(r * NZ, (r + 1) * NZ)
        block[base + r : base + r + 1, :] = cells[0, :, lanes].astype(f32)
        block[base + 4 + r : base + 5 + r, :] = jnp.where(
            lane + r * NZ < live, ftrans[0, :, lanes], 0.0
        )
    plane[...] = block[(PER + 4) * 8 : (PER + 13) * 8, :]


def partner_rows(cells):
    return jnp.concatenate(
        [cells[0, :, r * NZ : (r + 1) * NZ] for r in range(4)], axis=0
    ).astype(f32)


def join_kernel(own, cells, joined):
    joined[0:232, :] = own[...]
    joined[232:236, :] = partner_rows(cells)
    joined[236:240, :] = jnp.zeros((4, NZ), f32)


def by_parity(axis, body):
    odd = lax.rem(lax.axis_index(axis), 2)
    for k in range(2):
        pl.when(odd == k)(functools.partial(body, k))


class Masked:
    def __init__(self, ref, due):
        self.ref, self.due = ref, due

    def __getitem__(self, index):
        return jnp.where(self.due, self.ref[index], 0.0)


def has_other(axis, peers):
    at = lax.axis_index(axis)
    return jnp.where(lax.rem(at, 2) == 0, at > 0, at < peers - 1)


def column_kernel(peers, own, rp, ro, rs, band, sums, to_core, to_chip):
    ro = Masked(ro, has_other("gx", peers[0]))
    lo2 = Masked(rs, lax.axis_index("gx") >= 2)

    def fill(out, lo, hi, first, third, runs):
        for c in range(2):
            y = first + c
            base = c * COLBLOCK
            out[base : base + 9, :] = lo2[pl.ds(y, 9, stride=8), :]
            for k, ref in enumerate((lo, own, hi)):
                start = base + 9 + 28 * k
                out[start : start + 28, :] = ref[pl.ds(y, 28, stride=8), :]
        at = THIRD
        out[at : at + 3, :] = lo2[pl.ds((runs[-1] - 4) * 8 + third, 3, stride=8), :]
        at += 3
        for ref in (lo, own, hi):
            for x in range(2):
                for o in runs:
                    out[at : at + 3, :] = ref[pl.ds((x * PER + o) * 8 + third, 3, stride=8), :]
                    at += 3
        for k, start in enumerate((224, 232, 228)):
            out[FAULT_ROW + 4 * k : FAULT_ROW + 4 * k + 4, :] = ro[start : start + 4, :]
        out[BAND_ROW : BAND_ROW + DIAGONALS, :] = band[int(first > 0), 0:DIAGONALS, :]
        for c in range(2):
            for k in range(2):
                at = SUM_ROW + (2 * c + k) * 6
                out[at : at + 6, :] = sums[k, first + c, 0:6, :]
        out[SUM_ROW + 24 : Y_ROWS, :] = jnp.zeros((Y_ROWS - SUM_ROW - 24, NZ), f32)

    def for_x(odd_x):
        lo, hi = (rp, ro) if odd_x else (ro, rp)

        def for_y(odd_y):
            up, down = (to_chip, to_core) if odd_y else (to_core, to_chip)
            fill(up, lo, hi, CY - 2, CY - 3, (1, 10))
            fill(down, lo, hi, 0, 2, (4,))

        by_parity("gy", for_y)

    by_parity("gx", for_x)


def colour(z):
    half = z >> 1
    return half - 5 * ((half * 205) >> 10)


def slot_columns(rows):
    tall = jnp.transpose(jnp.concatenate(rows, axis=0))
    return [[tall[:, 4 * k + r : 4 * k + r + 1] for r in range(4)] for k in range(len(rows))]


def flat_cells(rows):
    row = jnp.concatenate([rows[r : r + 1] for r in range(4)], axis=1)
    return row.astype(jnp.int32) & 1023


def fill_far(far2, partner, live):
    lane = lax.broadcasted_iota(jnp.int32, (NZ, NZ), 1)
    for r in range(4):
        rows = slice(r * NZ, (r + 1) * NZ)
        match = (partner[r].astype(jnp.int32) & 127) == lane
        high = live[r].astype(bf16).astype(f32)
        far2[rows, 0:NZ] = jnp.where(match, high, 0.0).astype(bf16)
        far2[rows, NZ : 2 * NZ] = jnp.where(match, live[r] - high, 0.0).astype(bf16)


def flat_rows(rows):
    return jnp.concatenate([rows[r : r + 1] for r in range(4)], axis=1)


def colour_sums(hot, beyond, live):
    e16 = lax.broadcasted_iota(jnp.int32, (16, SLOTS), 0)
    tint = colour(flat_rows(beyond).astype(jnp.int32) & 127)
    live = flat_rows(live)
    high = live.astype(bf16).astype(f32)
    value = jnp.where((e16 == tint) | (e16 == 5), high, 0.0)
    value = jnp.where((e16 == tint + 8) | (e16 == 13), live - high, value)
    got = dot_nt(value.astype(bf16), hot)
    return got[:8] + got[8:]


def diagonals(hot, own, far, live):
    d24 = lax.broadcasted_iota(jnp.int32, (24, SLOTS), 0)
    step = (flat_rows(far).astype(jnp.int32) & 127) - (flat_rows(own).astype(jnp.int32) & 127)
    live = flat_rows(live)
    high = live.astype(bf16).astype(f32)
    match = step + REACH == d24
    both = [jnp.where(match, value, 0.0) for value in (high, live - high)]
    got = dot_nt(jnp.concatenate(both, axis=0).astype(bf16), hot)
    return got[:24] + got[24:]


def fill_hot(hot, cells, columns):
    z128 = lax.broadcasted_iota(jnp.int32, (NZ, SLOTS), 0)
    for k, y in enumerate(columns):
        value = jnp.where(cells == z128 + y * NZ, 1.0, 0.0)
        hot[k * NZ : (k + 1) * NZ, :] = value.astype(bf16)


def pair_matrix(both):
    z8 = lax.broadcasted_iota(jnp.int32, (8, NZ), 1)
    e8 = lax.broadcasted_iota(jnp.int32, (8, NZ), 0)
    one = jnp.where((e8 == colour(z8)) | (e8 == 5), 1.0, 0.0).astype(bf16)
    one2 = jnp.concatenate([one, one], axis=1)
    matrix = both[:, :NZ] + both[:, NZ:]
    f2 = jnp.concatenate(split(matrix), axis=0)
    ft2 = jnp.concatenate(split(jnp.transpose(matrix)), axis=0)
    return f2, ft2, dot_nn(one2, ft2), dot_nn(one2, f2)


def fault_kernel(own, cells, f2, ft2, rf, band, far2, hot, both):
    partner, live = slot_columns([partner_rows(cells), own[228:232, :]])
    fill_far(far2, partner, live)
    fill_hot(hot, flat_cells(own[224:228, :]), range(CY))
    both[...] = dot_nn(hot[...], far2[...])
    for y in range(CY):
        f2[y], ft2[y], rf[0, y], rf[1, y] = pair_matrix(both[y * NZ : (y + 1) * NZ, :])
    for k, y in enumerate((0, CY - 1)):
        band[k] = diagonals(
            hot[y * NZ : (y + 1) * NZ, :], own[224:228, :], partner_rows(cells), own[228:232, :]
        )


def through(value, matrix2):
    rows = value.shape[0]
    high, low = split(value)
    left = jnp.concatenate(
        [jnp.concatenate([high, high], axis=1), jnp.concatenate([low, low], axis=1)], axis=0
    )
    got = dot_nn(left, matrix2)
    return got[:rows] + got[rows:]


class Place:
    def __init__(self):
        self.gx = lax.axis_index("gx")
        self.gy = lax.axis_index("gy")
        par = lax.rem(self.gx, 2)
        even = par == 0
        self.sgn = 1 - 2 * par
        self.p_own = jnp.where(even, 3, 2)
        self.p_far = jnp.where(even, 4, 1)
        self.p_third = jnp.where(even, 0, 5)
        self.p_fault = (self.p_own, self.p_far, self.p_third)
        self.x_coarse = lax.rem(self.gx, 5) + 5

    def a_of(self, d):
        return lax.rem(self.x_coarse + d, 5)

    def b_of(self, coarse_y, d):
        return lax.rem(self.gy * (CY // 2) + coarse_y + d + 5, 5)


def roll_weights(w, wr, first, count):
    for p in range(7):
        for o, step in enumerate(FORWARD):
            if step[2] == 0 or (p == 0 and o < 4):
                continue
            at = (p * PER + o) * ROWS + first
            distance = 1 if step[2] == 1 else NZ - 1
            wr[at : at + count, :] = pltpu.roll(w[at : at + count, :], distance, 1)


def smooth(w, wr, fd, qc, inv, diag, first, count):
    even_y = (lax.broadcasted_iota(jnp.int32, (count, NZ), 0) & 1) == 0
    even_z = (lax.broadcasted_iota(jnp.int32, (count, NZ), 1) & 1) == 0
    for p in range(6):
        base = p + 1

        def weight(dx, dy, dz):
            if (dx, dy, dz) in OFFSET:
                start = (base * PER + OFFSET[dx, dy, dz]) * ROWS + 1 + first
                return w[start : start + count, :]
            o = OFFSET[-dx, -dy, -dz]
            start = ((base + dx) * PER + o) * ROWS + 1 + first + dy
            return (w if dz == 0 else wr)[start : start + count, :]

        near = 1 if p % 2 == 0 else -1
        sums = {}
        for dz in (-1, 0, 1):
            got = {}
            for dx in (-1, 0, 1):
                below, above = weight(dx, -1, dz), weight(dx, 1, dz)
                got[dx, 0] = jnp.where(even_y, above, below)
                if (dx, dz) != (0, 0):
                    got[dx, 0] = got[dx, 0] + weight(dx, 0, dz)
                got[dx, 1] = jnp.where(even_y, below, above)
            for sy in range(2):
                sums[0, sy, dz] = got[0, sy] + got[near, sy]
                sums[1, sy, dz] = got[-near, sy]
        start = (base * PER + 13) * ROWS + 1 + first
        at = p * 16 + first
        total = w[start : start + count, :] + fd[at : at + count, :]
        r = []
        for sx in range(2):
            for sy in range(2):
                down, same, up = (sums[sx, sy, dz] for dz in (-1, 0, 1))
                r.append(same + jnp.where(even_z, up, down))
                r.append(jnp.where(even_z, down, up))
        for value in r:
            total = total + value
        total = jnp.where(total == 0.0, 1.0, total)
        scale = damping / total
        diag[at : at + count, :] = total
        inv[at : at + count, :] = scale
        for k, value in enumerate(r):
            value = value * scale
            if k == 0:
                value = value + (1.0 - damping)
            at = (p * 8 + k) * 16 + first
            qc[at : at + count, :] = value


def spread(here, qc, inv, qe, rf_at, columns, count):
    z8 = lax.broadcasted_iota(jnp.int32, (8, NZ), 1)
    e8 = lax.broadcasted_iota(jnp.int32, (8, NZ), 0)
    beside = jnp.where((z8 & 1) == 0, z8 - 1, z8 + 1)
    mask_own = jnp.where(e8 == colour(z8), 1.0, 0.0)
    mask_oth = jnp.where(e8 == colour(beside + 10), 1.0, 0.0)
    rows5 = jnp.where(e8 < 5, 1.0, 0.0)

    def one(k, carry):
        c = columns(k)
        for p in range(6):
            for lat in range(4):
                at = (p * 8 + 2 * lat) * 16 + c
                qe[p, c, lat] = (
                    qc[pl.ds(at, 1), :] * mask_own + qc[pl.ds(at + 16, 1), :] * mask_oth
                )
        for k, plane in enumerate(here.p_fault):
            qe[plane, c, 2] = qe[plane, c, 2] + rf_at(k, c) * (
                inv[pl.ds(plane * 16 + c, 1), :] * rows5
            )
        return carry

    lax.fori_loop(0, count, one, 0)


def apply_column(w, wr, diag, qe, ap, p, y, odd_x, odd_y):
    acc = {}
    for dx in (-1, 0, 1):
        for dy in (-1, 0, 1):
            q = [qe[p + dx, y + dy, lat] for lat in range(4)]
            own_x = dx if (dx == 1 and odd_x) or (dx == -1 and not odd_x) else 0
            own_y = dy if (dy == 1 and odd_y) or (dy == -1 and not odd_y) else 0
            oth_x = own_x + (1 if (odd_x + dx) % 2 else -1)
            oth_y = own_y + (1 if (odd_y + dy) % 2 else -1)
            for dz in (-1, 0, 1):
                if (dx, dy, dz) == (0, 0, 0):
                    continue
                if (dx, dy, dz) in OFFSET:
                    at = ((p + 1) * PER + OFFSET[dx, dy, dz]) * ROWS + y + 1
                    ref = w if dz == 0 else wr
                else:
                    at = ((p + 1 + dx) * PER + OFFSET[-dx, -dy, -dz]) * ROWS + y + 1 + dy
                    ref = w
                wt = ref[pl.ds(at, 1), :]
                for lat in range(4):
                    lx = oth_x if lat >= 2 else own_x
                    ly = oth_y if lat % 2 else own_y
                    value = wt * q[lat]
                    key = (lx, ly, dz)
                    acc[key] = acc[key] + value if key in acc else value
    centre = diag[pl.ds(p * 16 + y, 1), :]
    for lx in (-1, 0, 1):
        for ly in (-1, 0, 1):
            total = acc[lx, ly, 0]
            total = total + pltpu.roll(acc[lx, ly, 1], NZ - 1, 1)
            total = total + pltpu.roll(acc[lx, ly, -1], 1, 1)
            own_lat = None
            sx = {0: 0, (1 if odd_x else -1): 1}.get(lx)
            sy = {0: 0, (1 if odd_y else -1): 1}.get(ly)
            if sx is not None and sy is not None:
                own_lat = 2 * sx + sy
            if own_lat is None:
                total = -total
            else:
                total = centre * qe[p, y, own_lat] - total
            ap[p - 1, y - 1, lx + 1, ly + 1] = total


def fault_apply(here, qe, ap, c, f2c, ft2c):
    ly_oth = 2 * (c % 2)
    for plane, source, x_own, matrix in (
        (here.p_own, here.p_far, 1 + here.sgn, ft2c),
        (here.p_far, here.p_own, 1 - here.sgn, f2c),
    ):
        total = through(qe[source, c].reshape(32, NZ), matrix)
        for lat in range(4):
            lx = 1 if lat >= 2 else x_own
            ly = ly_oth if lat % 2 else 1
            ap[plane - 1, c - 1, lx, ly] = ap[plane - 1, c - 1, lx, ly] - total[8 * lat : 8 * lat + 8]


def fault_apply_band(here, qe, ap, c, band):
    ly_oth = 2 * (c % 2)
    to_own, to_far = [0.0] * 4, [0.0] * 4
    for d in range(DIAGONALS):
        weight = band[d : d + 1, :]
        for lat in range(4):
            ahead = pltpu.roll(qe[here.p_far, c, lat], (REACH - d) % NZ, 1)
            to_own[lat] = to_own[lat] + weight * ahead
            back = weight * qe[here.p_own, c, lat]
            to_far[lat] = to_far[lat] + pltpu.roll(back, (d - REACH) % NZ, 1)
    for plane, x_own, total in (
        (here.p_own, 1 + here.sgn, to_own),
        (here.p_far, 1 - here.sgn, to_far),
    ):
        for lat in range(4):
            lx = 1 if lat >= 2 else x_own
            ly = ly_oth if lat % 2 else 1
            ap[plane - 1, c - 1, lx, ly] = ap[plane - 1, c - 1, lx, ly] - total[lat]


def gather(here, qc, ap, tt, coarse_y, rows, add):
    shift = (-1, 0, 0, 1)
    for zk in range(2):
        acc = {}
        for x in range(-1, 3):
            for y in rows:
                lat = 2 * (x not in (0, 1)) + (y not in (0, 1))
                c = 2 * coarse_y + y + 2
                at = ((x + 2) * 8 + 2 * lat + zk) * 16 + c
                q = qc[at : at + 1, :]
                for lx in range(3):
                    for ly in range(3):
                        value = q * ap[x + 1, c - 1, lx, ly]
                        key = (shift[x + 1] + lx - 1, shift[y + 1] + ly - 1)
                        acc[key] = acc[key] + value if key in acc else value
        lane = (coarse_y % 2) * 256 + zk * NZ
        for (dx, dy), value in acc.items():
            at = (coarse_y // 2, here.a_of(dx), here.b_of(coarse_y, dy), slice(None), slice(lane, lane + NZ))
            tt[at] = tt[at] + value if add else value


def gather_fault(here, inv, ap, tt, y, ft2c):
    c = y + 2
    coarse_y = y // 2
    lane = (coarse_y % 2) * 256
    value = ap[here.p_far - 1, c - 1].reshape(72, NZ) * inv[pl.ds(here.p_far * 16 + c, 1), :]
    total = through(value, ft2c)
    for lx in range(3):
        a = here.a_of(lx - 1 + here.sgn)
        for ly in range(3):
            at = (coarse_y // 2, a, here.b_of(coarse_y, ly - 1), slice(None), slice(lane, lane + NZ))
            row = 8 * (3 * lx + ly)
            tt[at] = tt[at] + total[row : row + 8]


INNER = (2, 3, 4, 5)


def rows_of(coarse_y, inner):
    return [y for y in range(-1, 3) if (2 * coarse_y + y in INNER) == inner]


def inner_kernel(
    peers, own, rp, ro, rs, f2, ft2, rf_pair, w, wr, qe, ap, tt, rf_third, qc, inv, diag, fd, hot
):
    here = Place()
    ro = Masked(ro, has_other("gx", peers[0]))

    def place(ref, count, first):
        for k in range(count):
            base = (first + k) * ROWS
            w[base + 3 : base + 11, :] = ref[8 * k : 8 * k + 8, :]

    def place_x(odd):
        lo, hi = (rp, ro) if odd else (ro, rp)
        place(lo, 28, PER)
        place(hi, 28, 5 * PER)

    by_parity("gx", place_x)
    place(Masked(rs, here.gx >= 2), 9, 4)
    place(own, 28, 3 * PER)

    fill_hot(hot, flat_cells(ro[224:228, :]), range(CY))
    got = colour_sums(hot[...], ro[232:236, :], ro[228:232, :])
    fd[...] = jnp.zeros_like(fd)
    for y in range(CY):
        rf_third[y] = got[:, y * NZ : (y + 1) * NZ]
        for plane, value in zip(here.p_fault, (rf_pair[0, y], rf_pair[1, y], rf_third[y])):
            fd[pl.ds(plane * 16 + y + 2, 1), :] = value[5:6, :]

    roll_weights(w, wr, 3, 8)
    smooth(w, wr, fd, qc, inv, diag, 2, 8)
    spread(
        here, qc, inv, qe, lambda k, c: rf_third[c - 2] if k == 2 else rf_pair[k, c - 2], lambda k: k + 3, 6
    )

    def pair(k, carry):
        for p in range(1, 5):
            apply_column(w, wr, diag, qe, ap, p, 2 * k + 4, p % 2, 0)
            apply_column(w, wr, diag, qe, ap, p, 2 * k + 5, p % 2, 1)
        return carry

    lax.fori_loop(0, 2, pair, 0)
    for y in INNER:
        fault_apply(here, qe, ap, y + 2, f2[y], ft2[y])
    tt[...] = jnp.zeros_like(tt)
    for coarse_y in range(CY // 2):
        gather(here, qc, ap, tt, coarse_y, rows_of(coarse_y, True), False)
    for y in INNER:
        gather_fault(here, inv, ap, tt, y, ft2[y])


def side(high, halo, f2, ft2, rf_pair, rf_third, work, fields, rf, band, hot):
    here = Place()
    w, wr, qe, ap, tt = work
    qc, inv, diag, fd = fields
    first = 6 if high else 0
    columns = (10, 11) if high else (0, 1)
    row, third, runs = (11, 13, (4,)) if high else (1, 0, (1, 10))

    for c in range(2):
        base = c * COLBLOCK
        w[pl.ds(4 * ROWS + row + c, 9, stride=ROWS), :] = halo[base : base + 9, :]
        w[pl.ds(PER * ROWS + row + c, 84, stride=ROWS), :] = halo[base + 9 : base + 93, :]
    at = THIRD
    for plane in range(7):
        for o in runs[-1:] if plane == 0 else runs:
            start = (plane * PER + o) * ROWS + third
            w[pl.ds(start, 3, stride=ROWS), :] = halo[at : at + 3, :]
            at += 3
    roll_weights(w, wr, 8 if high else 0, 8)

    fd[...] = jnp.zeros_like(fd)

    def put(column, k, value):
        rf[k, column - first] = value
        fd[pl.ds(here.p_fault[k] * 16 + column, 1), :] = value[5:6, :]

    for column in range(first, first + 8):
        y = column - 2
        if 0 <= y < CY:
            put(column, 0, rf_pair[0, y])
            put(column, 1, rf_pair[1, y])
            put(column, 2, rf_third[y])
    band[0:DIAGONALS, :] = halo[BAND_ROW : BAND_ROW + DIAGONALS, :]
    lists = halo[FAULT_ROW : FAULT_ROW + 12, :]
    fill_hot(hot, flat_cells(lists[0:4]), (0, 1) if high else (CY - 2, CY - 1))
    got = colour_sums(hot[...], lists[4:8], lists[8:12])
    for c, column in enumerate(columns):
        for k in range(2):
            at = SUM_ROW + (2 * c + k) * 6
            value = halo[at : at + 6, :]
            put(column, k, jnp.concatenate([value, jnp.zeros((2, NZ), f32)], axis=0))
        put(column, 2, got[:, c * NZ : (c + 1) * NZ])

    smooth(w, wr, fd, qc, inv, diag, first, 8)
    spread(
        here, qc, inv, qe, lambda k, c: rf[k, c - first], lambda k: k + (9 if high else 0), 3
    )

    def planes(k, carry):
        for odd_x in (1, 0):
            p = 2 * k + 2 - odd_x
            for y in (8, 9, 10) if high else (1, 2, 3):
                apply_column(w, wr, diag, qe, ap, p, y, odd_x, y % 2)
        return carry

    lax.fori_loop(0, 2, planes, 0)
    own = (6, 7) if high else (0, 1)
    for y in own:
        fault_apply(here, qe, ap, y + 2, f2[y], ft2[y])
    fault_apply_band(here, qe, ap, 10 if high else 1, band)
    parts = ((3, (0, 1, 2)), (2, (2,))) if high else ((0, (-1, 0, 1)), (1, (-1,)))
    for coarse_y, rows in parts:
        gather(here, qc, ap, tt, coarse_y, rows, True)
    for y in own:
        gather_fault(here, inv, ap, tt, y, ft2[y])


def core_kernel(halo, f2, ft2, rf_pair, rf_third, *refs):
    work, fields, rest = refs[5:10], refs[10:14], refs[14:]

    def body(odd):
        side(not odd, halo, f2, ft2, rf_pair, rf_third, work, fields, *rest)

    by_parity("gy", body)


def main_kernel(peers, halo, f2, ft2, rf_pair, rf_third, *refs):
    out, work, fields, rest = refs[5], refs[6:11], refs[11:15], refs[15:]
    halo = Masked(halo, has_other("gy", peers[1]))

    def body(odd):
        side(odd, halo, f2, ft2, rf_pair, rf_third, work, fields, *rest)

    by_parity("gy", body)
    tt = work[4]

    kz = lax.broadcasted_iota(jnp.int32, (512, NZ), 0)
    kout = lax.broadcasted_iota(jnp.int32, (512, NZ), 1)
    z_in = kz & 127
    is_oth = ((kz >> 7) & 1) == 1
    target = jnp.where(
        is_oth, (z_in >> 1) + jnp.where((z_in & 1) == 0, -1, 1), z_in >> 1
    )
    fits = (target == (kout & 63)) & ((kz >> 8) == (kout >> 6))
    collect = jnp.where(fits, 1.0, 0.0).astype(bf16)
    for pair in range(2):
        high, low = split(tt[pair].reshape(200, 512))
        got = (dot_nn(high, collect) + dot_nn(low, collect)) * 0.125
        for k in range(25):
            out[5 * k : 5 * k + 5, 0, pair * NZ : (pair + 1) * NZ] = got[8 * k : 8 * k + 5]


def send(value, axis, target):
    peers = lax.axis_size(axis)
    return lax.ppermute(value, axis, [(i, target(i, peers)) for i in range(peers)])


def partner_of(i, peers):
    return i ^ 1


def other_of(i, peers):
    j = i + 1 if i % 2 else i - 1
    return j if 0 <= j < peers else i


def ahead_of(i, peers):
    return (i + 2) % peers


VMEM = pl.BlockSpec(memory_space=pltpu.VMEM)
HBM = pl.BlockSpec(memory_space=pltpu.HBM)


def params(mib):
    return pltpu.CompilerParams(vmem_limit_bytes=mib * 1024 * 1024)


def sds(*shape, dtype=f32):
    return jax.ShapeDtypeStruct(shape, dtype)


def per_device(trans, storage, fault_cells, fault_count, fault_trans):
    peers = (lax.axis_size("gx"), lax.axis_size("gy"))
    cells = send(fault_cells, "gx", partner_of)
    sources = [
        pltpu.with_memory_space_constraint(array, pltpu.HBM)
        for array in (trans, storage, fault_cells, fault_trans)
    ]
    own, plane = pl.pallas_call(
        functools.partial(pack_kernel, peers),
        out_shape=(sds(232, NZ), sds(72, NZ)),
        in_specs=[pl.BlockSpec(memory_space=pltpu.SMEM)] + [HBM] * 4,
        out_specs=(VMEM,) * 2,
        scratch_shapes=[pltpu.VMEM(array.shape, array.dtype) for array in sources]
        + [pltpu.SemaphoreType.DMA((4,))],
        compiler_params=params(16),
        name="pack",
    )(fault_count, *sources)
    rs = send(plane, "gx", ahead_of)
    joined = pl.pallas_call(
        join_kernel,
        out_shape=sds(240, NZ),
        in_specs=[VMEM] * 2,
        out_specs=VMEM,
        compiler_params=params(16),
        name="join",
    )(own, cells)
    ro = send(joined, "gx", other_of)
    rp = send(own, "gx", partner_of)
    pieces = sds(CY, 2 * NZ, NZ, dtype=bf16)
    f2, ft2, rf_pair, band = pl.pallas_call(
        fault_kernel,
        out_shape=(pieces, pieces, sds(2, CY, 8, NZ), sds(2, 24, NZ)),
        in_specs=[VMEM] * 2,
        out_specs=(VMEM,) * 4,
        scratch_shapes=[
            pltpu.VMEM((SLOTS, 2 * NZ), bf16),
            pltpu.VMEM((CY * NZ, SLOTS), bf16),
            pltpu.VMEM((CY * NZ, 2 * NZ), f32),
        ],
        compiler_params=params(16),
        cost_estimate=pl.CostEstimate(flops=2 * 10**9, bytes_accessed=2**21, transcendentals=0),
        name="faults",
    )(own, cells)
    to_core, to_chip = pl.pallas_call(
        functools.partial(column_kernel, peers),
        out_shape=(sds(Y_ROWS, NZ), sds(Y_ROWS, NZ)),
        in_specs=[VMEM] * 6,
        out_specs=(VMEM,) * 2,
        compiler_params=params(16),
        name="columns",
    )(own, rp, ro, rs, band, rf_pair)
    from_chip = send(to_chip, "gy", other_of)
    from_core = send(to_core, "gy", partner_of)
    work = (
        sds(7 * PER * ROWS, NZ),
        sds(7 * PER * ROWS, NZ),
        sds(6, 12, 4, 8, NZ),
        sds(4, 10, 3, 3, 8, NZ),
        sds(2, 5, 5, 8, 512),
    )
    fields = [
        pltpu.VMEM((6 * 8 * 16, NZ), f32),
        pltpu.VMEM((6 * 16, NZ), f32),
        pltpu.VMEM((6 * 16, NZ), f32),
        pltpu.VMEM((6 * 16, NZ), f32),
    ]
    *work_in, rf_third = pl.pallas_call(
        functools.partial(inner_kernel, peers),
        out_shape=work + (sds(CY, 8, NZ),),
        in_specs=[VMEM] * 7,
        out_specs=(VMEM,) * 6,
        scratch_shapes=fields + [pltpu.VMEM((CY * NZ, SLOTS), bf16)],
        compiler_params=params(16),
        cost_estimate=pl.CostEstimate(flops=4 * 10**9, bytes_accessed=2**21, transcendentals=0),
        name="inner",
    )(own, rp, ro, rs, f2, ft2, rf_pair)
    side_scratch = fields + [
        pltpu.VMEM((3, 8, 8, NZ), f32),
        pltpu.VMEM((24, NZ), f32),
        pltpu.VMEM((2 * NZ, SLOTS), bf16),
    ]
    work_in = pl.pallas_call(
        core_kernel,
        out_shape=work,
        in_specs=[VMEM] * 10,
        out_specs=(VMEM,) * 5,
        scratch_shapes=side_scratch,
        input_output_aliases={5 + k: k for k in range(5)},
        compiler_params=params(16),
        cost_estimate=pl.CostEstimate(flops=2 * 10**9, bytes_accessed=2**20, transcendentals=0),
        name="core_side",
    )(from_core, f2, ft2, rf_pair, rf_third, *work_in)
    result, *_ = pl.pallas_call(
        functools.partial(main_kernel, peers),
        out_shape=(sds(125, 1, 256),) + work,
        in_specs=[VMEM] * 10,
        out_specs=(VMEM,) * 6,
        scratch_shapes=side_scratch,
        input_output_aliases={5 + k: 1 + k for k in range(5)},
        compiler_params=params(16),
        name="chip_side",
    )(from_chip, f2, ft2, rf_pair, rf_third, *work_in)
    return result


def solution(mesh):
    placed = (
        P(None, "gx", "gy"),
        P("gx", "gy"),
        P("gx", "gy", None),
        P("gx", "gy"),
        P("gx", "gy", None),
    )
    return jax.shard_map(
        per_device, mesh=mesh, in_specs=placed, out_specs=P(None, "gx", "gy"), check_vma=False
    )
```

```python
import functools

import jax
import jax.numpy as jnp
from jax import lax
from jax.experimental import pallas as pl
from jax.experimental.pallas import tpu as pltpu
from jax.sharding import PartitionSpec as P

NZ = 128
CY = 8
SLOTS = 512

FORWARD = (
    (0, 0, 1),
    (0, 1, -1),
    (0, 1, 0),
    (0, 1, 1),
    (1, -1, -1),
    (1, -1, 0),
    (1, -1, 1),
    (1, 0, -1),
    (1, 0, 0),
    (1, 0, 1),
    (1, 1, -1),
    (1, 1, 0),
    (1, 1, 1),
)
OFFSET = {step: k for k, step in enumerate(FORWARD)}
damping = 2.0 / 3.0

ROWS = 24
PER = 14
COLBLOCK = 93
THIRD = 2 * COLBLOCK
FAULT_ROW = 225
BAND_ROW, SUM_ROW, Y_ROWS = 237, 254, 280
REACH = 8
DIAGONALS = 2 * REACH + 1

f32 = jnp.float32
bf16 = jnp.bfloat16


def dot_nt(a, b):
    return lax.dot_general(a, b, (((1,), (1,)), ((), ())), preferred_element_type=f32)


def dot_nn(a, b):
    return lax.dot_general(a, b, (((1,), (0,)), ((), ())), preferred_element_type=f32)


def split(value):
    high = value.astype(bf16)
    return high, (value - high.astype(f32)).astype(bf16)


def pack_kernel(peers, count, *refs):
    sources, (block, plane), targets, sems = refs[:4], refs[4:6], refs[6:10], refs[10]
    copies = [
        pltpu.make_async_copy(src, dst, sems.at[k])
        for k, (src, dst) in enumerate(zip(sources, targets))
    ]
    for copy in copies:
        copy.start()
    for copy in copies:
        copy.wait()
    trans, storage, cells, ftrans = targets
    last_x = lax.axis_index("gx") == peers[0] - 1
    first_y = lax.axis_index("gy") == 0
    last_y = lax.axis_index("gy") == peers[1] - 1
    depth = lax.broadcasted_iota(jnp.int32, (8, NZ), 1)
    row = lax.broadcasted_iota(jnp.int32, (8, NZ), 0)
    for x in range(2):
        for o in range(PER):
            base = (x * PER + o) * 8
            for y in range(CY):
                lanes = slice(y * NZ, (y + 1) * NZ)
                if o < 13:
                    value = trans[o, x : x + 1, lanes]
                else:
                    value = storage[x : x + 1, lanes]
                block[base + y : base + y + 1, :] = value
            if o == 13:
                continue
            step = FORWARD[o]
            keep = None
            if step[2] == 1:
                keep = depth < NZ - 1
            if step[2] == -1:
                keep = depth > 0
            if step[1] == 1:
                inside = (row < CY - 1) | jnp.logical_not(last_y)
                keep = inside if keep is None else keep & inside
            if step[1] == -1:
                inside = (row > 0) | jnp.logical_not(first_y)
                keep = inside if keep is None else keep & inside
            if step[0] == 1 and x == 1:
                inside = (row >= 0) & jnp.logical_not(last_x)
                keep = inside if keep is None else keep & inside
            if keep is not None:
                block[base : base + 8, :] = jnp.where(keep, block[base : base + 8, :], 0.0)
    live = count[0, 0]
    lane = lax.broadcasted_iota(jnp.int32, (1, NZ), 1)
    base = 2 * PER * 8
    for r in range(4):
        lanes = slice(r * NZ, (r + 1) * NZ)
        block[base + r : base + r + 1, :] = cells[0, :, lanes].astype(f32)
        block[base + 4 + r : base + 5 + r, :] = jnp.where(
            lane + r * NZ < live, ftrans[0, :, lanes], 0.0
        )
    plane[...] = block[(PER + 4) * 8 : (PER + 13) * 8, :]


def partner_rows(cells):
    return jnp.concatenate(
        [cells[0, :, r * NZ : (r + 1) * NZ] for r in range(4)], axis=0
    ).astype(f32)


def join_kernel(own, cells, joined):
    joined[0:232, :] = own[...]
    joined[232:236, :] = partner_rows(cells)
    joined[236:240, :] = jnp.zeros((4, NZ), f32)


def by_parity(axis, body):
    odd = lax.rem(lax.axis_index(axis), 2)
    for k in range(2):
        pl.when(odd == k)(functools.partial(body, k))


class Masked:
    def __init__(self, ref, due):
        self.ref, self.due = ref, due

    def __getitem__(self, index):
        return jnp.where(self.due, self.ref[index], 0.0)


def has_other(axis, peers):
    at = lax.axis_index(axis)
    return jnp.where(lax.rem(at, 2) == 0, at > 0, at < peers - 1)


def column_kernel(peers, own, rp, ro, rs, band, sums, to_core, to_chip):
    ro = Masked(ro, has_other("gx", peers[0]))
    lo2 = Masked(rs, lax.axis_index("gx") >= 2)

    def fill(out, lo, hi, first, third, runs):
        for c in range(2):
            y = first + c
            base = c * COLBLOCK
            out[base : base + 9, :] = lo2[pl.ds(y, 9, stride=8), :]
            for k, ref in enumerate((lo, own, hi)):
                start = base + 9 + 28 * k
                out[start : start + 28, :] = ref[pl.ds(y, 28, stride=8), :]
        at = THIRD
        out[at : at + 3, :] = lo2[pl.ds((runs[-1] - 4) * 8 + third, 3, stride=8), :]
        at += 3
        for ref in (lo, own, hi):
            for x in range(2):
                for o in runs:
                    out[at : at + 3, :] = ref[pl.ds((x * PER + o) * 8 + third, 3, stride=8), :]
                    at += 3
        for k, start in enumerate((224, 232, 228)):
            out[FAULT_ROW + 4 * k : FAULT_ROW + 4 * k + 4, :] = ro[start : start + 4, :]
        out[BAND_ROW : BAND_ROW + DIAGONALS, :] = band[int(first > 0), 0:DIAGONALS, :]
        for c in range(2):
            for k in range(2):
                at = SUM_ROW + (2 * c + k) * 6
                out[at : at + 6, :] = sums[k, first + c, 0:6, :]
        out[SUM_ROW + 24 : Y_ROWS, :] = jnp.zeros((Y_ROWS - SUM_ROW - 24, NZ), f32)

    def for_x(odd_x):
        lo, hi = (rp, ro) if odd_x else (ro, rp)

        def for_y(odd_y):
            up, down = (to_chip, to_core) if odd_y else (to_core, to_chip)
            fill(up, lo, hi, CY - 2, CY - 3, (1, 10))
            fill(down, lo, hi, 0, 2, (4,))

        by_parity("gy", for_y)

    by_parity("gx", for_x)


def colour(z):
    half = z >> 1
    return half - 5 * ((half * 205) >> 10)


def slot_columns(rows):
    tall = jnp.transpose(jnp.concatenate(rows, axis=0))
    return [[tall[:, 4 * k + r : 4 * k + r + 1] for r in range(4)] for k in range(len(rows))]


def flat_cells(rows):
    row = jnp.concatenate([rows[r : r + 1] for r in range(4)], axis=1)
    return row.astype(jnp.int32) & 1023


def fill_far(far2, partner, live):
    lane = lax.broadcasted_iota(jnp.int32, (NZ, NZ), 1)
    for r in range(4):
        rows = slice(r * NZ, (r + 1) * NZ)
        match = (partner[r].astype(jnp.int32) & 127) == lane
        high = live[r].astype(bf16).astype(f32)
        far2[rows, 0:NZ] = jnp.where(match, high, 0.0).astype(bf16)
        far2[rows, NZ : 2 * NZ] = jnp.where(match, live[r] - high, 0.0).astype(bf16)


def flat_rows(rows):
    return jnp.concatenate([rows[r : r + 1] for r in range(4)], axis=1)


def colour_sums(hot, beyond, live):
    e16 = lax.broadcasted_iota(jnp.int32, (16, SLOTS), 0)
    tint = colour(flat_rows(beyond).astype(jnp.int32) & 127)
    live = flat_rows(live)
    high = live.astype(bf16).astype(f32)
    value = jnp.where((e16 == tint) | (e16 == 5), high, 0.0)
    value = jnp.where((e16 == tint + 8) | (e16 == 13), live - high, value)
    got = dot_nt(value.astype(bf16), hot)
    return got[:8] + got[8:]


def diagonals(hot, own, far, live):
    d24 = lax.broadcasted_iota(jnp.int32, (24, SLOTS), 0)
    step = (flat_rows(far).astype(jnp.int32) & 127) - (flat_rows(own).astype(jnp.int32) & 127)
    live = flat_rows(live)
    high = live.astype(bf16).astype(f32)
    match = step + REACH == d24
    both = [jnp.where(match, value, 0.0) for value in (high, live - high)]
    got = dot_nt(jnp.concatenate(both, axis=0).astype(bf16), hot)
    return got[:24] + got[24:]


def fill_hot(hot, cells, columns):
    z128 = lax.broadcasted_iota(jnp.int32, (NZ, SLOTS), 0)
    for k, y in enumerate(columns):
        value = jnp.where(cells == z128 + y * NZ, 1.0, 0.0)
        hot[k * NZ : (k + 1) * NZ, :] = value.astype(bf16)


def pair_matrix(both):
    z8 = lax.broadcasted_iota(jnp.int32, (8, NZ), 1)
    e8 = lax.broadcasted_iota(jnp.int32, (8, NZ), 0)
    one = jnp.where((e8 == colour(z8)) | (e8 == 5), 1.0, 0.0).astype(bf16)
    one2 = jnp.concatenate([one, one], axis=1)
    matrix = both[:, :NZ] + both[:, NZ:]
    f2 = jnp.concatenate(split(matrix), axis=0)
    ft2 = jnp.concatenate(split(jnp.transpose(matrix)), axis=0)
    return f2, ft2, dot_nn(one2, ft2), dot_nn(one2, f2)


def fault_kernel(own, plane, cells, f2, ft2, rf, band, plane_out, far2, hot, both):
    plane_out[...] = plane[...]
    partner, live = slot_columns([partner_rows(cells), own[228:232, :]])
    fill_far(far2, partner, live)
    fill_hot(hot, flat_cells(own[224:228, :]), range(CY))
    both[...] = dot_nn(hot[...], far2[...])
    for y in range(CY):
        f2[y], ft2[y], rf[0, y], rf[1, y] = pair_matrix(both[y * NZ : (y + 1) * NZ, :])
    for k, y in enumerate((0, CY - 1)):
        band[k] = diagonals(
            hot[y * NZ : (y + 1) * NZ, :], own[224:228, :], partner_rows(cells), own[228:232, :]
        )


def through(value, matrix2):
    rows = value.shape[0]
    high, low = split(value)
    left = jnp.concatenate(
        [jnp.concatenate([high, high], axis=1), jnp.concatenate([low, low], axis=1)], axis=0
    )
    got = dot_nn(left, matrix2)
    return got[:rows] + got[rows:]


class Place:
    def __init__(self):
        self.gx = lax.axis_index("gx")
        self.gy = lax.axis_index("gy")
        par = lax.rem(self.gx, 2)
        even = par == 0
        self.sgn = 1 - 2 * par
        self.p_own = jnp.where(even, 3, 2)
        self.p_far = jnp.where(even, 4, 1)
        self.p_third = jnp.where(even, 0, 5)
        self.p_fault = (self.p_own, self.p_far, self.p_third)
        self.x_coarse = lax.rem(self.gx, 5) + 5

    def a_of(self, d):
        return lax.rem(self.x_coarse + d, 5)

    def b_of(self, coarse_y, d):
        return lax.rem(self.gy * (CY // 2) + coarse_y + d + 5, 5)


def roll_weights(w, wr, first, count):
    for p in range(7):
        for o, step in enumerate(FORWARD):
            if step[2] == 0 or (p == 0 and o < 4):
                continue
            at = (p * PER + o) * ROWS + first
            distance = 1 if step[2] == 1 else NZ - 1
            wr[at : at + count, :] = pltpu.roll(w[at : at + count, :], distance, 1)


def smooth(w, wr, fd, qc, inv, diag, first, count):
    even_y = (lax.broadcasted_iota(jnp.int32, (count, NZ), 0) & 1) == 0
    even_z = (lax.broadcasted_iota(jnp.int32, (count, NZ), 1) & 1) == 0
    for p in range(6):
        base = p + 1

        def weight(dx, dy, dz):
            if (dx, dy, dz) in OFFSET:
                start = (base * PER + OFFSET[dx, dy, dz]) * ROWS + 1 + first
                return w[start : start + count, :]
            o = OFFSET[-dx, -dy, -dz]
            start = ((base + dx) * PER + o) * ROWS + 1 + first + dy
            return (w if dz == 0 else wr)[start : start + count, :]

        near = 1 if p % 2 == 0 else -1
        sums = {}
        for dz in (-1, 0, 1):
            got = {}
            for dx in (-1, 0, 1):
                below, above = weight(dx, -1, dz), weight(dx, 1, dz)
                got[dx, 0] = jnp.where(even_y, above, below)
                if (dx, dz) != (0, 0):
                    got[dx, 0] = got[dx, 0] + weight(dx, 0, dz)
                got[dx, 1] = jnp.where(even_y, below, above)
            for sy in range(2):
                sums[0, sy, dz] = got[0, sy] + got[near, sy]
                sums[1, sy, dz] = got[-near, sy]
        start = (base * PER + 13) * ROWS + 1 + first
        at = p * 16 + first
        total = w[start : start + count, :] + fd[at : at + count, :]
        r = []
        for sx in range(2):
            for sy in range(2):
                down, same, up = (sums[sx, sy, dz] for dz in (-1, 0, 1))
                r.append(same + jnp.where(even_z, up, down))
                r.append(jnp.where(even_z, down, up))
        for value in r:
            total = total + value
        total = jnp.where(total == 0.0, 1.0, total)
        scale = damping / total
        diag[at : at + count, :] = total
        inv[at : at + count, :] = scale
        for k, value in enumerate(r):
            value = value * scale
            if k == 0:
                value = value + (1.0 - damping)
            at = (p * 8 + k) * 16 + first
            qc[at : at + count, :] = value


def spread(here, qc, inv, qe, rf_at, columns, count):
    z8 = lax.broadcasted_iota(jnp.int32, (8, NZ), 1)
    e8 = lax.broadcasted_iota(jnp.int32, (8, NZ), 0)
    beside = jnp.where((z8 & 1) == 0, z8 - 1, z8 + 1)
    mask_own = jnp.where(e8 == colour(z8), 1.0, 0.0)
    mask_oth = jnp.where(e8 == colour(beside + 10), 1.0, 0.0)
    rows5 = jnp.where(e8 < 5, 1.0, 0.0)

    def one(k, carry):
        c = columns(k)
        for p in range(6):
            for lat in range(4):
                at = (p * 8 + 2 * lat) * 16 + c
                qe[p, c, lat] = (
                    qc[pl.ds(at, 1), :] * mask_own + qc[pl.ds(at + 16, 1), :] * mask_oth
                )
        for k, plane in enumerate(here.p_fault):
            qe[plane, c, 2] = qe[plane, c, 2] + rf_at(k, c) * (
                inv[pl.ds(plane * 16 + c, 1), :] * rows5
            )
        return carry

    lax.fori_loop(0, count, one, 0)


def apply_column(w, wr, diag, qe, ap, p, y, odd_x, odd_y):
    acc = {}
    for dx in (-1, 0, 1):
        for dy in (-1, 0, 1):
            q = [qe[p + dx, y + dy, lat] for lat in range(4)]
            own_x = dx if (dx == 1 and odd_x) or (dx == -1 and not odd_x) else 0
            own_y = dy if (dy == 1 and odd_y) or (dy == -1 and not odd_y) else 0
            oth_x = own_x + (1 if (odd_x + dx) % 2 else -1)
            oth_y = own_y + (1 if (odd_y + dy) % 2 else -1)
            for dz in (-1, 0, 1):
                if (dx, dy, dz) == (0, 0, 0):
                    continue
                if (dx, dy, dz) in OFFSET:
                    at = ((p + 1) * PER + OFFSET[dx, dy, dz]) * ROWS + y + 1
                    ref = w if dz == 0 else wr
                else:
                    at = ((p + 1 + dx) * PER + OFFSET[-dx, -dy, -dz]) * ROWS + y + 1 + dy
                    ref = w
                wt = ref[pl.ds(at, 1), :]
                for lat in range(4):
                    lx = oth_x if lat >= 2 else own_x
                    ly = oth_y if lat % 2 else own_y
                    value = wt * q[lat]
                    key = (lx, ly, dz)
                    acc[key] = acc[key] + value if key in acc else value
    centre = diag[pl.ds(p * 16 + y, 1), :]
    for lx in (-1, 0, 1):
        for ly in (-1, 0, 1):
            total = acc[lx, ly, 0]
            total = total + pltpu.roll(acc[lx, ly, 1], NZ - 1, 1)
            total = total + pltpu.roll(acc[lx, ly, -1], 1, 1)
            own_lat = None
            sx = {0: 0, (1 if odd_x else -1): 1}.get(lx)
            sy = {0: 0, (1 if odd_y else -1): 1}.get(ly)
            if sx is not None and sy is not None:
                own_lat = 2 * sx + sy
            if own_lat is None:
                total = -total
            else:
                total = centre * qe[p, y, own_lat] - total
            ap[p - 1, y - 1, lx + 1, ly + 1] = total


def fault_apply(here, qe, ap, c, f2c, ft2c):
    ly_oth = 2 * (c % 2)
    for plane, source, x_own, matrix in (
        (here.p_own, here.p_far, 1 + here.sgn, ft2c),
        (here.p_far, here.p_own, 1 - here.sgn, f2c),
    ):
        total = through(qe[source, c].reshape(32, NZ), matrix)
        for lat in range(4):
            lx = 1 if lat >= 2 else x_own
            ly = ly_oth if lat % 2 else 1
            ap[plane - 1, c - 1, lx, ly] = ap[plane - 1, c - 1, lx, ly] - total[8 * lat : 8 * lat + 8]


def fault_apply_band(here, qe, ap, c, band):
    ly_oth = 2 * (c % 2)
    to_own, to_far = [0.0] * 4, [0.0] * 4
    for d in range(DIAGONALS):
        weight = band[d : d + 1, :]
        for lat in range(4):
            ahead = pltpu.roll(qe[here.p_far, c, lat], (REACH - d) % NZ, 1)
            to_own[lat] = to_own[lat] + weight * ahead
            back = weight * qe[here.p_own, c, lat]
            to_far[lat] = to_far[lat] + pltpu.roll(back, (d - REACH) % NZ, 1)
    for plane, x_own, total in (
        (here.p_own, 1 + here.sgn, to_own),
        (here.p_far, 1 - here.sgn, to_far),
    ):
        for lat in range(4):
            lx = 1 if lat >= 2 else x_own
            ly = ly_oth if lat % 2 else 1
            ap[plane - 1, c - 1, lx, ly] = ap[plane - 1, c - 1, lx, ly] - total[lat]


def gather(here, qc, ap, tt, coarse_y, rows, add):
    shift = (-1, 0, 0, 1)
    for zk in range(2):
        acc = {}
        for x in range(-1, 3):
            for y in rows:
                lat = 2 * (x not in (0, 1)) + (y not in (0, 1))
                c = 2 * coarse_y + y + 2
                at = ((x + 2) * 8 + 2 * lat + zk) * 16 + c
                q = qc[at : at + 1, :]
                for lx in range(3):
                    for ly in range(3):
                        value = q * ap[x + 1, c - 1, lx, ly]
                        key = (shift[x + 1] + lx - 1, shift[y + 1] + ly - 1)
                        acc[key] = acc[key] + value if key in acc else value
        lane = (coarse_y % 2) * 256 + zk * NZ
        for (dx, dy), value in acc.items():
            at = (coarse_y // 2, here.a_of(dx), here.b_of(coarse_y, dy), slice(None), slice(lane, lane + NZ))
            tt[at] = tt[at] + value if add else value


def gather_fault(here, inv, ap, tt, y, ft2c):
    c = y + 2
    coarse_y = y // 2
    lane = (coarse_y % 2) * 256
    value = ap[here.p_far - 1, c - 1].reshape(72, NZ) * inv[pl.ds(here.p_far * 16 + c, 1), :]
    total = through(value, ft2c)
    for lx in range(3):
        a = here.a_of(lx - 1 + here.sgn)
        for ly in range(3):
            at = (coarse_y // 2, a, here.b_of(coarse_y, ly - 1), slice(None), slice(lane, lane + NZ))
            row = 8 * (3 * lx + ly)
            tt[at] = tt[at] + total[row : row + 8]


INNER = (2, 3, 4, 5)


def rows_of(coarse_y, inner):
    return [y for y in range(-1, 3) if (2 * coarse_y + y in INNER) == inner]


def inner_kernel(
    peers, own, rp, ro, rs, f2, ft2, rf_pair, w, wr, qe, ap, tt, rf_third, qc, inv, diag, fd, hot
):
    here = Place()
    ro = Masked(ro, has_other("gx", peers[0]))

    def place(ref, count, first):
        for k in range(count):
            base = (first + k) * ROWS
            w[base + 3 : base + 11, :] = ref[8 * k : 8 * k + 8, :]

    def place_x(odd):
        lo, hi = (rp, ro) if odd else (ro, rp)
        place(lo, 28, PER)
        place(hi, 28, 5 * PER)

    by_parity("gx", place_x)
    place(Masked(rs, here.gx >= 2), 9, 4)
    place(own, 28, 3 * PER)

    fill_hot(hot, flat_cells(ro[224:228, :]), range(CY))
    got = colour_sums(hot[...], ro[232:236, :], ro[228:232, :])
    fd[...] = jnp.zeros_like(fd)
    for y in range(CY):
        rf_third[y] = got[:, y * NZ : (y + 1) * NZ]
        for plane, value in zip(here.p_fault, (rf_pair[0, y], rf_pair[1, y], rf_third[y])):
            fd[pl.ds(plane * 16 + y + 2, 1), :] = value[5:6, :]

    roll_weights(w, wr, 3, 8)
    smooth(w, wr, fd, qc, inv, diag, 2, 8)
    spread(
        here, qc, inv, qe, lambda k, c: rf_third[c - 2] if k == 2 else rf_pair[k, c - 2], lambda k: k + 3, 6
    )

    def pair(k, carry):
        for p in range(1, 5):
            apply_column(w, wr, diag, qe, ap, p, 2 * k + 4, p % 2, 0)
            apply_column(w, wr, diag, qe, ap, p, 2 * k + 5, p % 2, 1)
        return carry

    lax.fori_loop(0, 2, pair, 0)
    for y in INNER:
        fault_apply(here, qe, ap, y + 2, f2[y], ft2[y])
    tt[...] = jnp.zeros_like(tt)
    for coarse_y in range(CY // 2):
        gather(here, qc, ap, tt, coarse_y, rows_of(coarse_y, True), False)
    for y in INNER:
        gather_fault(here, inv, ap, tt, y, ft2[y])


def side(high, halo, f2, ft2, rf_pair, rf_third, work, fields, rf, band, hot):
    here = Place()
    w, wr, qe, ap, tt = work
    qc, inv, diag, fd = fields
    first = 6 if high else 0
    columns = (10, 11) if high else (0, 1)
    row, third, runs = (11, 13, (4,)) if high else (1, 0, (1, 10))

    for c in range(2):
        base = c * COLBLOCK
        w[pl.ds(4 * ROWS + row + c, 9, stride=ROWS), :] = halo[base : base + 9, :]
        w[pl.ds(PER * ROWS + row + c, 84, stride=ROWS), :] = halo[base + 9 : base + 93, :]
    at = THIRD
    for plane in range(7):
        for o in runs[-1:] if plane == 0 else runs:
            start = (plane * PER + o) * ROWS + third
            w[pl.ds(start, 3, stride=ROWS), :] = halo[at : at + 3, :]
            at += 3
    roll_weights(w, wr, 8 if high else 0, 8)

    fd[...] = jnp.zeros_like(fd)

    def put(column, k, value):
        rf[k, column - first] = value
        fd[pl.ds(here.p_fault[k] * 16 + column, 1), :] = value[5:6, :]

    for column in range(first, first + 8):
        y = column - 2
        if 0 <= y < CY:
            put(column, 0, rf_pair[0, y])
            put(column, 1, rf_pair[1, y])
            put(column, 2, rf_third[y])
    band[0:DIAGONALS, :] = halo[BAND_ROW : BAND_ROW + DIAGONALS, :]
    lists = halo[FAULT_ROW : FAULT_ROW + 12, :]
    fill_hot(hot, flat_cells(lists[0:4]), (0, 1) if high else (CY - 2, CY - 1))
    got = colour_sums(hot[...], lists[4:8], lists[8:12])
    for c, column in enumerate(columns):
        for k in range(2):
            at = SUM_ROW + (2 * c + k) * 6
            value = halo[at : at + 6, :]
            put(column, k, jnp.concatenate([value, jnp.zeros((2, NZ), f32)], axis=0))
        put(column, 2, got[:, c * NZ : (c + 1) * NZ])

    smooth(w, wr, fd, qc, inv, diag, first, 8)
    spread(
        here, qc, inv, qe, lambda k, c: rf[k, c - first], lambda k: k + (9 if high else 0), 3
    )

    def planes(k, carry):
        for odd_x in (1, 0):
            p = 2 * k + 2 - odd_x
            for y in (8, 9, 10) if high else (1, 2, 3):
                apply_column(w, wr, diag, qe, ap, p, y, odd_x, y % 2)
        return carry

    lax.fori_loop(0, 2, planes, 0)
    own = (6, 7) if high else (0, 1)
    for y in own:
        fault_apply(here, qe, ap, y + 2, f2[y], ft2[y])
    fault_apply_band(here, qe, ap, 10 if high else 1, band)
    parts = ((3, (0, 1, 2)), (2, (2,))) if high else ((0, (-1, 0, 1)), (1, (-1,)))
    for coarse_y, rows in parts:
        gather(here, qc, ap, tt, coarse_y, rows, True)
    for y in own:
        gather_fault(here, inv, ap, tt, y, ft2[y])


def finish(tt, pair, store):
    kz = lax.broadcasted_iota(jnp.int32, (512, NZ), 0)
    kout = lax.broadcasted_iota(jnp.int32, (512, NZ), 1)
    z_in = kz & 127
    is_oth = ((kz >> 7) & 1) == 1
    target = jnp.where(
        is_oth, (z_in >> 1) + jnp.where((z_in & 1) == 0, -1, 1), z_in >> 1
    )
    fits = (target == (kout & 63)) & ((kz >> 8) == (kout >> 6))
    collect = jnp.where(fits, 1.0, 0.0).astype(bf16)
    high, low = split(tt[pair].reshape(200, 512))
    got = (dot_nn(high, collect) + dot_nn(low, collect)) * 0.125
    for k in range(25):
        store(5 * k, got[8 * k : 8 * k + 5])


def core_kernel(halo, f2, ft2, rf_pair, rf_third, *refs):
    half, work, fields, rest = refs[5], refs[6:11], refs[11:15], refs[15:]

    def body(odd):
        side(not odd, halo, f2, ft2, rf_pair, rf_third, work, fields, *rest)

        def store(row, value):
            half[row : row + 5, :] = value

        finish(work[4], 0 if odd else 1, store)

    by_parity("gy", body)


def main_kernel(peers, halo, f2, ft2, rf_pair, rf_third, half, *refs):
    out, work, fields, rest = refs[5], refs[6:11], refs[11:15], refs[15:]
    halo = Masked(halo, has_other("gy", peers[1]))

    def body(odd):
        side(odd, halo, f2, ft2, rf_pair, rf_third, work, fields, *rest)
        lanes = [slice(0, NZ), slice(NZ, 2 * NZ)]

        def store(row, value):
            out[row : row + 5, 0, lanes[odd]] = value
            out[row : row + 5, 0, lanes[1 - odd]] = half[row : row + 5, :]

        finish(work[4], odd, store)

    by_parity("gy", body)


def send(value, axis, target):
    peers = lax.axis_size(axis)
    pairs = [(i, target(i, peers)) for i in range(peers)]
    return lax.ppermute(value, axis, [(i, j) for i, j in pairs if j < peers])


def partner_of(i, peers):
    return i ^ 1


def other_of(i, peers):
    j = i + 1 if i % 2 else i - 1
    return j if 0 <= j < peers else i


def ahead_of(i, peers):
    return i + 2


VMEM = pl.BlockSpec(memory_space=pltpu.VMEM)
HBM = pl.BlockSpec(memory_space=pltpu.HBM)


def params(mib):
    return pltpu.CompilerParams(vmem_limit_bytes=mib * 1024 * 1024)


def sds(*shape, dtype=f32):
    return jax.ShapeDtypeStruct(shape, dtype)


def per_device(trans, storage, fault_cells, fault_count, fault_trans):
    peers = (lax.axis_size("gx"), lax.axis_size("gy"))
    cells = send(fault_cells, "gx", partner_of)
    sources = [
        pltpu.with_memory_space_constraint(array, pltpu.HBM)
        for array in (trans, storage, fault_cells, fault_trans)
    ]
    own, plane = pl.pallas_call(
        functools.partial(pack_kernel, peers),
        out_shape=(sds(232, NZ), sds(72, NZ)),
        in_specs=[pl.BlockSpec(memory_space=pltpu.SMEM)] + [HBM] * 4,
        out_specs=(VMEM,) * 2,
        scratch_shapes=[pltpu.VMEM(array.shape, array.dtype) for array in sources]
        + [pltpu.SemaphoreType.DMA((4,))],
        compiler_params=params(16),
        name="pack",
    )(fault_count, *sources)
    joined = pl.pallas_call(
        join_kernel,
        out_shape=sds(240, NZ),
        in_specs=[VMEM] * 2,
        out_specs=VMEM,
        compiler_params=params(16),
        name="join",
    )(own, cells)
    ro = send(joined, "gx", other_of)
    rp = send(own, "gx", partner_of)
    pieces = sds(CY, 2 * NZ, NZ, dtype=bf16)
    f2, ft2, rf_pair, band, plane = pl.pallas_call(
        fault_kernel,
        out_shape=(pieces, pieces, sds(2, CY, 8, NZ), sds(2, 24, NZ), sds(72, NZ)),
        in_specs=[VMEM] * 3,
        out_specs=(VMEM,) * 5,
        scratch_shapes=[
            pltpu.VMEM((SLOTS, 2 * NZ), bf16),
            pltpu.VMEM((CY * NZ, SLOTS), bf16),
            pltpu.VMEM((CY * NZ, 2 * NZ), f32),
        ],
        compiler_params=params(16),
        cost_estimate=pl.CostEstimate(flops=2 * 10**9, bytes_accessed=2**21, transcendentals=0),
        name="faults",
    )(own, plane, cells)
    rs = send(plane, "gx", ahead_of)
    to_core, to_chip = pl.pallas_call(
        functools.partial(column_kernel, peers),
        out_shape=(sds(Y_ROWS, NZ), sds(Y_ROWS, NZ)),
        in_specs=[VMEM] * 6,
        out_specs=(VMEM,) * 2,
        compiler_params=params(16),
        name="columns",
    )(own, rp, ro, rs, band, rf_pair)
    from_chip = send(to_chip, "gy", other_of)
    from_core = send(to_core, "gy", partner_of)
    work = (
        sds(7 * PER * ROWS, NZ),
        sds(7 * PER * ROWS, NZ),
        sds(6, 12, 4, 8, NZ),
        sds(4, 10, 3, 3, 8, NZ),
        sds(2, 5, 5, 8, 512),
    )
    fields = [
        pltpu.VMEM((6 * 8 * 16, NZ), f32),
        pltpu.VMEM((6 * 16, NZ), f32),
        pltpu.VMEM((6 * 16, NZ), f32),
        pltpu.VMEM((6 * 16, NZ), f32),
    ]
    *work_in, rf_third = pl.pallas_call(
        functools.partial(inner_kernel, peers),
        out_shape=work + (sds(CY, 8, NZ),),
        in_specs=[VMEM] * 7,
        out_specs=(VMEM,) * 6,
        scratch_shapes=fields + [pltpu.VMEM((CY * NZ, SLOTS), bf16)],
        compiler_params=params(16),
        cost_estimate=pl.CostEstimate(flops=4 * 10**9, bytes_accessed=2**21, transcendentals=0),
        name="inner",
    )(own, rp, ro, rs, f2, ft2, rf_pair)
    side_scratch = fields + [
        pltpu.VMEM((3, 8, 8, NZ), f32),
        pltpu.VMEM((24, NZ), f32),
        pltpu.VMEM((2 * NZ, SLOTS), bf16),
    ]
    half, *work_in = pl.pallas_call(
        core_kernel,
        out_shape=(sds(125, NZ),) + work,
        in_specs=[VMEM] * 10,
        out_specs=(VMEM,) * 6,
        scratch_shapes=side_scratch,
        input_output_aliases={5 + k: 1 + k for k in range(5)},
        compiler_params=params(16),
        cost_estimate=pl.CostEstimate(flops=2 * 10**9, bytes_accessed=2**20, transcendentals=0),
        name="core_side",
    )(from_core, f2, ft2, rf_pair, rf_third, *work_in)
    result, *_ = pl.pallas_call(
        functools.partial(main_kernel, peers),
        out_shape=(sds(125, 1, 256),) + work,
        in_specs=[VMEM] * 11,
        out_specs=(VMEM,) * 6,
        scratch_shapes=side_scratch,
        input_output_aliases={6 + k: 1 + k for k in range(5)},
        compiler_params=params(16),
        name="chip_side",
    )(from_chip, f2, ft2, rf_pair, rf_third, half, *work_in)
    return result


def solution(mesh):
    placed = (
        P(None, "gx", "gy"),
        P("gx", "gy"),
        P("gx", "gy", None),
        P("gx", "gy"),
        P("gx", "gy", None),
    )
    return jax.shard_map(
        per_device, mesh=mesh, in_specs=placed, out_specs=P(None, "gx", "gy"), check_vma=False
    )
```

```python
import functools

import jax
import jax.numpy as jnp
from jax import lax
from jax.experimental import pallas as pl
from jax.experimental.pallas import tpu as pltpu
from jax.sharding import PartitionSpec as P

NZ = 128
CY = 8
SLOTS = 512

FORWARD = (
    (0, 0, 1),
    (0, 1, -1),
    (0, 1, 0),
    (0, 1, 1),
    (1, -1, -1),
    (1, -1, 0),
    (1, -1, 1),
    (1, 0, -1),
    (1, 0, 0),
    (1, 0, 1),
    (1, 1, -1),
    (1, 1, 0),
    (1, 1, 1),
)
OFFSET = {step: k for k, step in enumerate(FORWARD)}
damping = 2.0 / 3.0

ROWS = 24
PER = 14
COLBLOCK = 93
THIRD = 2 * COLBLOCK
FAULT_ROW = 225
BAND_ROW, SUM_ROW, Y_ROWS = 237, 254, 280
REACH = 8
DIAGONALS = 2 * REACH + 1

f32 = jnp.float32
bf16 = jnp.bfloat16


def dot_nt(a, b):
    return lax.dot_general(a, b, (((1,), (1,)), ((), ())), preferred_element_type=f32)


def dot_nn(a, b):
    return lax.dot_general(a, b, (((1,), (0,)), ((), ())), preferred_element_type=f32)


def split(value):
    high = value.astype(bf16)
    return high, (value - high.astype(f32)).astype(bf16)


def pack_kernel(peers, count, *refs):
    sources, (block, plane), targets, sems = refs[:4], refs[4:6], refs[6:10], refs[10]
    copies = [
        pltpu.make_async_copy(src, dst, sems.at[k])
        for k, (src, dst) in enumerate(zip(sources, targets))
    ]
    for copy in copies:
        copy.start()
    for copy in copies:
        copy.wait()
    trans, storage, cells, ftrans = targets
    last_x = lax.axis_index("gx") == peers[0] - 1
    first_y = lax.axis_index("gy") == 0
    last_y = lax.axis_index("gy") == peers[1] - 1
    depth = lax.broadcasted_iota(jnp.int32, (8, NZ), 1)
    row = lax.broadcasted_iota(jnp.int32, (8, NZ), 0)
    for x in range(2):
        for o in range(PER):
            base = (x * PER + o) * 8
            for y in range(CY):
                lanes = slice(y * NZ, (y + 1) * NZ)
                if o < 13:
                    value = trans[o, x : x + 1, lanes]
                else:
                    value = storage[x : x + 1, lanes]
                block[base + y : base + y + 1, :] = value
            if o == 13:
                continue
            step = FORWARD[o]
            keep = None
            if step[2] == 1:
                keep = depth < NZ - 1
            if step[2] == -1:
                keep = depth > 0
            if step[1] == 1:
                inside = (row < CY - 1) | jnp.logical_not(last_y)
                keep = inside if keep is None else keep & inside
            if step[1] == -1:
                inside = (row > 0) | jnp.logical_not(first_y)
                keep = inside if keep is None else keep & inside
            if step[0] == 1 and x == 1:
                inside = (row >= 0) & jnp.logical_not(last_x)
                keep = inside if keep is None else keep & inside
            if keep is not None:
                block[base : base + 8, :] = jnp.where(keep, block[base : base + 8, :], 0.0)
    live = count[0, 0]
    lane = lax.broadcasted_iota(jnp.int32, (1, NZ), 1)
    base = 2 * PER * 8
    for r in range(4):
        lanes = slice(r * NZ, (r + 1) * NZ)
        block[base + r : base + r + 1, :] = cells[0, :, lanes].astype(f32)
        block[base + 4 + r : base + 5 + r, :] = jnp.where(
            lane + r * NZ < live, ftrans[0, :, lanes], 0.0
        )
    plane[...] = block[(PER + 4) * 8 : (PER + 13) * 8, :]


def partner_rows(cells):
    return jnp.concatenate(
        [cells[0, :, r * NZ : (r + 1) * NZ] for r in range(4)], axis=0
    ).astype(f32)


def join_kernel(own, cells, joined):
    joined[0:232, :] = own[...]
    joined[232:236, :] = partner_rows(cells)
    joined[236:240, :] = jnp.zeros((4, NZ), f32)


def by_parity(axis, body):
    odd = lax.rem(lax.axis_index(axis), 2)
    for k in range(2):
        pl.when(odd == k)(functools.partial(body, k))


class Masked:
    def __init__(self, ref, due):
        self.ref, self.due = ref, due

    def __getitem__(self, index):
        return jnp.where(self.due, self.ref[index], 0.0)


def has_other(axis, peers):
    at = lax.axis_index(axis)
    return jnp.where(lax.rem(at, 2) == 0, at > 0, at < peers - 1)


def column_kernel(peers, own, rp, ro, rs, band, sums, to_core, to_chip):
    ro = Masked(ro, has_other("gx", peers[0]))
    lo2 = Masked(rs, lax.axis_index("gx") >= 2)

    def fill(out, lo, hi, first, third, runs):
        for c in range(2):
            y = first + c
            base = c * COLBLOCK
            out[base : base + 9, :] = lo2[pl.ds(y, 9, stride=8), :]
            for k, ref in enumerate((lo, own, hi)):
                start = base + 9 + 28 * k
                out[start : start + 28, :] = ref[pl.ds(y, 28, stride=8), :]
        at = THIRD
        out[at : at + 3, :] = lo2[pl.ds((runs[-1] - 4) * 8 + third, 3, stride=8), :]
        at += 3
        for ref in (lo, own, hi):
            for x in range(2):
                for o in runs:
                    out[at : at + 3, :] = ref[pl.ds((x * PER + o) * 8 + third, 3, stride=8), :]
                    at += 3
        for k, start in enumerate((224, 232, 228)):
            out[FAULT_ROW + 4 * k : FAULT_ROW + 4 * k + 4, :] = ro[start : start + 4, :]
        out[BAND_ROW : BAND_ROW + DIAGONALS, :] = band[int(first > 0), 0:DIAGONALS, :]
        for c in range(2):
            for k in range(2):
                at = SUM_ROW + (2 * c + k) * 6
                out[at : at + 6, :] = sums[k, first + c, 0:6, :]
        out[SUM_ROW + 24 : Y_ROWS, :] = jnp.zeros((Y_ROWS - SUM_ROW - 24, NZ), f32)

    def for_x(odd_x):
        lo, hi = (rp, ro) if odd_x else (ro, rp)

        def for_y(odd_y):
            up, down = (to_chip, to_core) if odd_y else (to_core, to_chip)
            fill(up, lo, hi, CY - 2, CY - 3, (1, 10))
            fill(down, lo, hi, 0, 2, (4,))

        by_parity("gy", for_y)

    by_parity("gx", for_x)


def colour(z):
    half = z >> 1
    return half - 5 * ((half * 205) >> 10)


def slot_columns(rows):
    tall = jnp.transpose(jnp.concatenate(rows, axis=0))
    return [[tall[:, 4 * k + r : 4 * k + r + 1] for r in range(4)] for k in range(len(rows))]


def flat_cells(rows):
    row = jnp.concatenate([rows[r : r + 1] for r in range(4)], axis=1)
    return row.astype(jnp.int32) & 1023


def fill_far(far2, partner, live):
    lane = lax.broadcasted_iota(jnp.int32, (NZ, NZ), 1)
    for r in range(4):
        rows = slice(r * NZ, (r + 1) * NZ)
        match = (partner[r].astype(jnp.int32) & 127) == lane
        high = live[r].astype(bf16).astype(f32)
        far2[rows, 0:NZ] = jnp.where(match, high, 0.0).astype(bf16)
        far2[rows, NZ : 2 * NZ] = jnp.where(match, live[r] - high, 0.0).astype(bf16)


def flat_rows(rows):
    return jnp.concatenate([rows[r : r + 1] for r in range(4)], axis=1)


def colour_sums(hot, beyond, live):
    e16 = lax.broadcasted_iota(jnp.int32, (16, SLOTS), 0)
    tint = colour(flat_rows(beyond).astype(jnp.int32) & 127)
    live = flat_rows(live)
    high = live.astype(bf16).astype(f32)
    value = jnp.where((e16 == tint) | (e16 == 5), high, 0.0)
    value = jnp.where((e16 == tint + 8) | (e16 == 13), live - high, value)
    got = dot_nt(value.astype(bf16), hot)
    return got[:8] + got[8:]


def diagonals(hot, own, far, live):
    d24 = lax.broadcasted_iota(jnp.int32, (24, SLOTS), 0)
    step = (flat_rows(far).astype(jnp.int32) & 127) - (flat_rows(own).astype(jnp.int32) & 127)
    live = flat_rows(live)
    high = live.astype(bf16).astype(f32)
    match = step + REACH == d24
    both = [jnp.where(match, value, 0.0) for value in (high, live - high)]
    got = dot_nt(jnp.concatenate(both, axis=0).astype(bf16), hot)
    return got[:24] + got[24:]


def fill_hot(hot, cells, columns):
    z128 = lax.broadcasted_iota(jnp.int32, (NZ, SLOTS), 0)
    for k, y in enumerate(columns):
        value = jnp.where(cells == z128 + y * NZ, 1.0, 0.0)
        hot[k * NZ : (k + 1) * NZ, :] = value.astype(bf16)


def pair_matrix(both):
    z8 = lax.broadcasted_iota(jnp.int32, (8, NZ), 1)
    e8 = lax.broadcasted_iota(jnp.int32, (8, NZ), 0)
    one = jnp.where((e8 == colour(z8)) | (e8 == 5), 1.0, 0.0).astype(bf16)
    one2 = jnp.concatenate([one, one], axis=1)
    matrix = both[:, :NZ] + both[:, NZ:]
    f2 = jnp.concatenate(split(matrix), axis=0)
    ft2 = jnp.concatenate(split(jnp.transpose(matrix)), axis=0)
    return f2, ft2, dot_nn(one2, ft2), dot_nn(one2, f2)


def fault_kernel(own, cells, f2, ft2, rf, band, far2, hot, both):
    partner, live = slot_columns([partner_rows(cells), own[228:232, :]])
    fill_far(far2, partner, live)
    fill_hot(hot, flat_cells(own[224:228, :]), range(CY))
    both[...] = dot_nn(hot[...], far2[...])
    for y in range(CY):
        f2[y], ft2[y], rf[0, y], rf[1, y] = pair_matrix(both[y * NZ : (y + 1) * NZ, :])
    for k, y in enumerate((0, CY - 1)):
        band[k] = diagonals(
            hot[y * NZ : (y + 1) * NZ, :], own[224:228, :], partner_rows(cells), own[228:232, :]
        )


def through(value, matrix2):
    rows = value.shape[0]
    high, low = split(value)
    left = jnp.concatenate(
        [jnp.concatenate([high, high], axis=1), jnp.concatenate([low, low], axis=1)], axis=0
    )
    got = dot_nn(left, matrix2)
    return got[:rows] + got[rows:]


class Place:
    def __init__(self):
        self.gx = lax.axis_index("gx")
        self.gy = lax.axis_index("gy")
        par = lax.rem(self.gx, 2)
        even = par == 0
        self.sgn = 1 - 2 * par
        self.p_own = jnp.where(even, 3, 2)
        self.p_far = jnp.where(even, 4, 1)
        self.p_third = jnp.where(even, 0, 5)
        self.p_fault = (self.p_own, self.p_far, self.p_third)
        self.x_coarse = lax.rem(self.gx, 5) + 5

    def a_of(self, d):
        return lax.rem(self.x_coarse + d, 5)

    def b_of(self, coarse_y, d):
        return lax.rem(self.gy * (CY // 2) + coarse_y + d + 5, 5)


def roll_weights(w, wr, first, count):
    for p in range(7):
        for o, step in enumerate(FORWARD):
            if step[2] == 0 or (p == 0 and o < 4):
                continue
            at = (p * PER + o) * ROWS + first
            distance = 1 if step[2] == 1 else NZ - 1
            wr[at : at + count, :] = pltpu.roll(w[at : at + count, :], distance, 1)


def smooth(w, wr, fd, qc, inv, diag, first, count):
    even_y = (lax.broadcasted_iota(jnp.int32, (count, NZ), 0) & 1) == 0
    even_z = (lax.broadcasted_iota(jnp.int32, (count, NZ), 1) & 1) == 0
    for p in range(6):
        base = p + 1

        def weight(dx, dy, dz):
            if (dx, dy, dz) in OFFSET:
                start = (base * PER + OFFSET[dx, dy, dz]) * ROWS + 1 + first
                return w[start : start + count, :]
            o = OFFSET[-dx, -dy, -dz]
            start = ((base + dx) * PER + o) * ROWS + 1 + first + dy
            return (w if dz == 0 else wr)[start : start + count, :]

        near = 1 if p % 2 == 0 else -1
        sums = {}
        for dz in (-1, 0, 1):
            got = {}
            for dx in (-1, 0, 1):
                below, above = weight(dx, -1, dz), weight(dx, 1, dz)
                got[dx, 0] = jnp.where(even_y, above, below)
                if (dx, dz) != (0, 0):
                    got[dx, 0] = got[dx, 0] + weight(dx, 0, dz)
                got[dx, 1] = jnp.where(even_y, below, above)
            for sy in range(2):
                sums[0, sy, dz] = got[0, sy] + got[near, sy]
                sums[1, sy, dz] = got[-near, sy]
        start = (base * PER + 13) * ROWS + 1 + first
        at = p * 16 + first
        total = w[start : start + count, :] + fd[at : at + count, :]
        r = []
        for sx in range(2):
            for sy in range(2):
                down, same, up = (sums[sx, sy, dz] for dz in (-1, 0, 1))
                r.append(same + jnp.where(even_z, up, down))
                r.append(jnp.where(even_z, down, up))
        for value in r:
            total = total + value
        total = jnp.where(total == 0.0, 1.0, total)
        scale = damping / total
        diag[at : at + count, :] = total
        inv[at : at + count, :] = scale
        for k, value in enumerate(r):
            value = value * scale
            if k == 0:
                value = value + (1.0 - damping)
            at = (p * 8 + k) * 16 + first
            qc[at : at + count, :] = value


def spread(here, qc, inv, qe, rf_at, columns, count):
    z8 = lax.broadcasted_iota(jnp.int32, (8, NZ), 1)
    e8 = lax.broadcasted_iota(jnp.int32, (8, NZ), 0)
    beside = jnp.where((z8 & 1) == 0, z8 - 1, z8 + 1)
    mask_own = jnp.where(e8 == colour(z8), 1.0, 0.0)
    mask_oth = jnp.where(e8 == colour(beside + 10), 1.0, 0.0)
    rows5 = jnp.where(e8 < 5, 1.0, 0.0)

    def one(k, carry):
        c = columns(k)
        for p in range(6):
            for lat in range(4):
                at = (p * 8 + 2 * lat) * 16 + c
                qe[p, c, lat] = (
                    qc[pl.ds(at, 1), :] * mask_own + qc[pl.ds(at + 16, 1), :] * mask_oth
                )
        for k, plane in enumerate(here.p_fault):
            qe[plane, c, 2] = qe[plane, c, 2] + rf_at(k, c) * (
                inv[pl.ds(plane * 16 + c, 1), :] * rows5
            )
        return carry

    lax.fori_loop(0, count, one, 0)


def apply_column(w, wr, diag, qe, ap, p, y, odd_x, odd_y):
    acc = {}
    for dx in (-1, 0, 1):
        for dy in (-1, 0, 1):
            q = [qe[p + dx, y + dy, lat] for lat in range(4)]
            own_x = dx if (dx == 1 and odd_x) or (dx == -1 and not odd_x) else 0
            own_y = dy if (dy == 1 and odd_y) or (dy == -1 and not odd_y) else 0
            oth_x = own_x + (1 if (odd_x + dx) % 2 else -1)
            oth_y = own_y + (1 if (odd_y + dy) % 2 else -1)
            for dz in (-1, 0, 1):
                if (dx, dy, dz) == (0, 0, 0):
                    continue
                if (dx, dy, dz) in OFFSET:
                    at = ((p + 1) * PER + OFFSET[dx, dy, dz]) * ROWS + y + 1
                    ref = w if dz == 0 else wr
                else:
                    at = ((p + 1 + dx) * PER + OFFSET[-dx, -dy, -dz]) * ROWS + y + 1 + dy
                    ref = w
                wt = ref[pl.ds(at, 1), :]
                for lat in range(4):
                    lx = oth_x if lat >= 2 else own_x
                    ly = oth_y if lat % 2 else own_y
                    value = wt * q[lat]
                    key = (lx, ly, dz)
                    acc[key] = acc[key] + value if key in acc else value
    centre = diag[pl.ds(p * 16 + y, 1), :]
    for lx in (-1, 0, 1):
        for ly in (-1, 0, 1):
            total = acc[lx, ly, 0]
            total = total + pltpu.roll(acc[lx, ly, 1], NZ - 1, 1)
            total = total + pltpu.roll(acc[lx, ly, -1], 1, 1)
            own_lat = None
            sx = {0: 0, (1 if odd_x else -1): 1}.get(lx)
            sy = {0: 0, (1 if odd_y else -1): 1}.get(ly)
            if sx is not None and sy is not None:
                own_lat = 2 * sx + sy
            if own_lat is None:
                total = -total
            else:
                total = centre * qe[p, y, own_lat] - total
            ap[p - 1, y - 1, lx + 1, ly + 1] = total


def fault_apply(here, qe, ap, c, f2c, ft2c):
    ly_oth = 2 * (c % 2)
    for plane, source, x_own, matrix in (
        (here.p_own, here.p_far, 1 + here.sgn, ft2c),
        (here.p_far, here.p_own, 1 - here.sgn, f2c),
    ):
        total = through(qe[source, c].reshape(32, NZ), matrix)
        for lat in range(4):
            lx = 1 if lat >= 2 else x_own
            ly = ly_oth if lat % 2 else 1
            ap[plane - 1, c - 1, lx, ly] = ap[plane - 1, c - 1, lx, ly] - total[8 * lat : 8 * lat + 8]


def fault_apply_band(here, qe, ap, c, band):
    ly_oth = 2 * (c % 2)
    to_own, to_far = [0.0] * 4, [0.0] * 4
    for d in range(DIAGONALS):
        weight = band[d : d + 1, :]
        for lat in range(4):
            ahead = pltpu.roll(qe[here.p_far, c, lat], (REACH - d) % NZ, 1)
            to_own[lat] = to_own[lat] + weight * ahead
            back = weight * qe[here.p_own, c, lat]
            to_far[lat] = to_far[lat] + pltpu.roll(back, (d - REACH) % NZ, 1)
    for plane, x_own, total in (
        (here.p_own, 1 + here.sgn, to_own),
        (here.p_far, 1 - here.sgn, to_far),
    ):
        for lat in range(4):
            lx = 1 if lat >= 2 else x_own
            ly = ly_oth if lat % 2 else 1
            ap[plane - 1, c - 1, lx, ly] = ap[plane - 1, c - 1, lx, ly] - total[lat]


def gather(here, qc, ap, tt, coarse_y, rows, add):
    shift = (-1, 0, 0, 1)
    for zk in range(2):
        acc = {}
        for x in range(-1, 3):
            for y in rows:
                lat = 2 * (x not in (0, 1)) + (y not in (0, 1))
                c = 2 * coarse_y + y + 2
                at = ((x + 2) * 8 + 2 * lat + zk) * 16 + c
                q = qc[at : at + 1, :]
                for lx in range(3):
                    for ly in range(3):
                        value = q * ap[x + 1, c - 1, lx, ly]
                        key = (shift[x + 1] + lx - 1, shift[y + 1] + ly - 1)
                        acc[key] = acc[key] + value if key in acc else value
        lane = (coarse_y % 2) * 256 + zk * NZ
        for (dx, dy), value in acc.items():
            at = (coarse_y // 2, here.a_of(dx), here.b_of(coarse_y, dy), slice(None), slice(lane, lane + NZ))
            tt[at] = tt[at] + value if add else value


def gather_fault(here, inv, ap, tt, y, ft2c):
    c = y + 2
    coarse_y = y // 2
    lane = (coarse_y % 2) * 256
    value = ap[here.p_far - 1, c - 1].reshape(72, NZ) * inv[pl.ds(here.p_far * 16 + c, 1), :]
    total = through(value, ft2c)
    for lx in range(3):
        a = here.a_of(lx - 1 + here.sgn)
        for ly in range(3):
            at = (coarse_y // 2, a, here.b_of(coarse_y, ly - 1), slice(None), slice(lane, lane + NZ))
            row = 8 * (3 * lx + ly)
            tt[at] = tt[at] + total[row : row + 8]


INNER = (2, 3, 4, 5)


def rows_of(coarse_y, inner):
    return [y for y in range(-1, 3) if (2 * coarse_y + y in INNER) == inner]


def inner_kernel(
    peers, own, rp, ro, rs, f2, ft2, rf_pair, w, wr, qe, ap, tt, rf_third, qc, inv, diag, fd, hot
):
    here = Place()
    ro = Masked(ro, has_other("gx", peers[0]))

    def place(ref, count, first):
        for k in range(count):
            base = (first + k) * ROWS
            w[base + 3 : base + 11, :] = ref[8 * k : 8 * k + 8, :]

    def place_x(odd):
        lo, hi = (rp, ro) if odd else (ro, rp)
        place(lo, 28, PER)
        place(hi, 28, 5 * PER)

    by_parity("gx", place_x)
    place(Masked(rs, here.gx >= 2), 9, 4)
    place(own, 28, 3 * PER)

    fill_hot(hot, flat_cells(ro[224:228, :]), range(CY))
    got = colour_sums(hot[...], ro[232:236, :], ro[228:232, :])
    fd[...] = jnp.zeros_like(fd)
    for y in range(CY):
        rf_third[y] = got[:, y * NZ : (y + 1) * NZ]
        for plane, value in zip(here.p_fault, (rf_pair[0, y], rf_pair[1, y], rf_third[y])):
            fd[pl.ds(plane * 16 + y + 2, 1), :] = value[5:6, :]

    roll_weights(w, wr, 3, 8)
    smooth(w, wr, fd, qc, inv, diag, 2, 8)
    spread(
        here, qc, inv, qe, lambda k, c: rf_third[c - 2] if k == 2 else rf_pair[k, c - 2], lambda k: k + 3, 6
    )

    def pair(k, carry):
        for p in range(1, 5):
            apply_column(w, wr, diag, qe, ap, p, 2 * k + 4, p % 2, 0)
            apply_column(w, wr, diag, qe, ap, p, 2 * k + 5, p % 2, 1)
        return carry

    lax.fori_loop(0, 2, pair, 0)
    for y in INNER:
        fault_apply(here, qe, ap, y + 2, f2[y], ft2[y])
    tt[...] = jnp.zeros_like(tt)
    for coarse_y in range(CY // 2):
        gather(here, qc, ap, tt, coarse_y, rows_of(coarse_y, True), False)
    for y in INNER:
        gather_fault(here, inv, ap, tt, y, ft2[y])


def side(high, halo, f2, ft2, rf_pair, rf_third, work, fields, rf, band, hot):
    here = Place()
    w, wr, qe, ap, tt = work
    qc, inv, diag, fd = fields
    first = 6 if high else 0
    columns = (10, 11) if high else (0, 1)
    row, third, runs = (11, 13, (4,)) if high else (1, 0, (1, 10))

    for c in range(2):
        base = c * COLBLOCK
        w[pl.ds(4 * ROWS + row + c, 9, stride=ROWS), :] = halo[base : base + 9, :]
        w[pl.ds(PER * ROWS + row + c, 84, stride=ROWS), :] = halo[base + 9 : base + 93, :]
    at = THIRD
    for plane in range(7):
        for o in runs[-1:] if plane == 0 else runs:
            start = (plane * PER + o) * ROWS + third
            w[pl.ds(start, 3, stride=ROWS), :] = halo[at : at + 3, :]
            at += 3
    roll_weights(w, wr, 8 if high else 0, 8)

    fd[...] = jnp.zeros_like(fd)

    def put(column, k, value):
        rf[k, column - first] = value
        fd[pl.ds(here.p_fault[k] * 16 + column, 1), :] = value[5:6, :]

    for column in range(first, first + 8):
        y = column - 2
        if 0 <= y < CY:
            put(column, 0, rf_pair[0, y])
            put(column, 1, rf_pair[1, y])
            put(column, 2, rf_third[y])
    band[0:DIAGONALS, :] = halo[BAND_ROW : BAND_ROW + DIAGONALS, :]
    lists = halo[FAULT_ROW : FAULT_ROW + 12, :]
    fill_hot(hot, flat_cells(lists[0:4]), (0, 1) if high else (CY - 2, CY - 1))
    got = colour_sums(hot[...], lists[4:8], lists[8:12])
    for c, column in enumerate(columns):
        for k in range(2):
            at = SUM_ROW + (2 * c + k) * 6
            value = halo[at : at + 6, :]
            put(column, k, jnp.concatenate([value, jnp.zeros((2, NZ), f32)], axis=0))
        put(column, 2, got[:, c * NZ : (c + 1) * NZ])

    smooth(w, wr, fd, qc, inv, diag, first, 8)
    spread(
        here, qc, inv, qe, lambda k, c: rf[k, c - first], lambda k: k + (9 if high else 0), 3
    )

    def planes(k, carry):
        for odd_x in (1, 0):
            p = 2 * k + 2 - odd_x
            for y in (8, 9, 10) if high else (1, 2, 3):
                apply_column(w, wr, diag, qe, ap, p, y, odd_x, y % 2)
        return carry

    lax.fori_loop(0, 2, planes, 0)
    own = (6, 7) if high else (0, 1)
    for y in own:
        fault_apply(here, qe, ap, y + 2, f2[y], ft2[y])
    fault_apply_band(here, qe, ap, 10 if high else 1, band)
    parts = ((3, (0, 1, 2)), (2, (2,))) if high else ((0, (-1, 0, 1)), (1, (-1,)))
    for coarse_y, rows in parts:
        gather(here, qc, ap, tt, coarse_y, rows, True)
    for y in own:
        gather_fault(here, inv, ap, tt, y, ft2[y])


def finish(tt, pair, store):
    kz = lax.broadcasted_iota(jnp.int32, (512, NZ), 0)
    kout = lax.broadcasted_iota(jnp.int32, (512, NZ), 1)
    z_in = kz & 127
    is_oth = ((kz >> 7) & 1) == 1
    target = jnp.where(
        is_oth, (z_in >> 1) + jnp.where((z_in & 1) == 0, -1, 1), z_in >> 1
    )
    fits = (target == (kout & 63)) & ((kz >> 8) == (kout >> 6))
    collect = jnp.where(fits, 1.0, 0.0).astype(bf16)
    high, low = split(tt[pair].reshape(200, 512))
    got = (dot_nn(high, collect) + dot_nn(low, collect)) * 0.125
    for k in range(25):
        store(5 * k, got[8 * k : 8 * k + 5])


def core_kernel(halo, f2, ft2, rf_pair, rf_third, *refs):
    half, work, fields, rest = refs[5], refs[6:11], refs[11:15], refs[15:]

    def body(odd):
        side(not odd, halo, f2, ft2, rf_pair, rf_third, work, fields, *rest)

        def store(row, value):
            half[row : row + 5, :] = value

        finish(work[4], 0 if odd else 1, store)

    by_parity("gy", body)


def main_kernel(peers, halo, f2, ft2, rf_pair, rf_third, half, *refs):
    out, work, fields, rest = refs[5], refs[6:11], refs[11:15], refs[15:]
    halo = Masked(halo, has_other("gy", peers[1]))

    def body(odd):
        side(odd, halo, f2, ft2, rf_pair, rf_third, work, fields, *rest)
        lanes = [slice(0, NZ), slice(NZ, 2 * NZ)]

        def store(row, value):
            out[row : row + 5, 0, lanes[odd]] = value
            out[row : row + 5, 0, lanes[1 - odd]] = half[row : row + 5, :]

        finish(work[4], odd, store)

    by_parity("gy", body)


def send(value, target):
    size_x, size_y = lax.axis_size("gx"), lax.axis_size("gy")
    pairs = []
    for x in range(size_x):
        for y in range(size_y):
            to_x, to_y = target(x, y)
            pairs.append((x * size_y + y, to_x * size_y + to_y))
    return lax.ppermute(value, ("gx", "gy"), pairs)


def x_partner(x, y):
    return x ^ 1, y


def core_partner(x, y):
    return x, y ^ 1


def x_other(size_x):
    def target(x, y):
        other = x + 1 if x % 2 else x - 1
        return (other, y) if 0 <= other < size_x else core_partner(x, y)

    return target


def chip_other(size_y):
    def target(x, y):
        other = y + 1 if y % 2 else y - 1
        return (x, other) if 0 <= other < size_y else x_partner(x, y)

    return target


def x_ahead(size_x):
    return lambda x, y: ((x + 2) % size_x, y)


VMEM = pl.BlockSpec(memory_space=pltpu.VMEM)
HBM = pl.BlockSpec(memory_space=pltpu.HBM)


def params(mib):
    return pltpu.CompilerParams(vmem_limit_bytes=mib * 1024 * 1024)


def sds(*shape, dtype=f32):
    return jax.ShapeDtypeStruct(shape, dtype)


def per_device(trans, storage, fault_cells, fault_count, fault_trans):
    peers = (lax.axis_size("gx"), lax.axis_size("gy"))
    cells = send(fault_cells, x_partner)
    sources = [
        pltpu.with_memory_space_constraint(array, pltpu.HBM)
        for array in (trans, storage, fault_cells, fault_trans)
    ]
    own, plane = pl.pallas_call(
        functools.partial(pack_kernel, peers),
        out_shape=(sds(232, NZ), sds(72, NZ)),
        in_specs=[pl.BlockSpec(memory_space=pltpu.SMEM)] + [HBM] * 4,
        out_specs=(VMEM,) * 2,
        scratch_shapes=[pltpu.VMEM(array.shape, array.dtype) for array in sources]
        + [pltpu.SemaphoreType.DMA((4,))],
        compiler_params=params(16),
        name="pack",
    )(fault_count, *sources)
    rs = send(plane, x_ahead(peers[0]))
    joined = pl.pallas_call(
        join_kernel,
        out_shape=sds(240, NZ),
        in_specs=[VMEM] * 2,
        out_specs=VMEM,
        compiler_params=params(16),
        name="join",
    )(own, cells)
    ro = send(joined, x_other(peers[0]))
    rp = send(own, x_partner)
    pieces = sds(CY, 2 * NZ, NZ, dtype=bf16)
    f2, ft2, rf_pair, band = pl.pallas_call(
        fault_kernel,
        out_shape=(pieces, pieces, sds(2, CY, 8, NZ), sds(2, 24, NZ)),
        in_specs=[VMEM] * 2,
        out_specs=(VMEM,) * 4,
        scratch_shapes=[
            pltpu.VMEM((SLOTS, 2 * NZ), bf16),
            pltpu.VMEM((CY * NZ, SLOTS), bf16),
            pltpu.VMEM((CY * NZ, 2 * NZ), f32),
        ],
        compiler_params=params(16),
        cost_estimate=pl.CostEstimate(flops=2 * 10**9, bytes_accessed=2**21, transcendentals=0),
        name="faults",
    )(own, cells)
    to_core, to_chip = pl.pallas_call(
        functools.partial(column_kernel, peers),
        out_shape=(sds(Y_ROWS, NZ), sds(Y_ROWS, NZ)),
        in_specs=[VMEM] * 6,
        out_specs=(VMEM,) * 2,
        compiler_params=params(16),
        name="columns",
    )(own, rp, ro, rs, band, rf_pair)
    from_chip = send(to_chip, chip_other(peers[1]))
    from_core = send(to_core, core_partner)
    work = (
        sds(7 * PER * ROWS, NZ),
        sds(7 * PER * ROWS, NZ),
        sds(6, 12, 4, 8, NZ),
        sds(4, 10, 3, 3, 8, NZ),
        sds(2, 5, 5, 8, 512),
    )
    fields = [
        pltpu.VMEM((6 * 8 * 16, NZ), f32),
        pltpu.VMEM((6 * 16, NZ), f32),
        pltpu.VMEM((6 * 16, NZ), f32),
        pltpu.VMEM((6 * 16, NZ), f32),
    ]
    *work_in, rf_third = pl.pallas_call(
        functools.partial(inner_kernel, peers),
        out_shape=work + (sds(CY, 8, NZ),),
        in_specs=[VMEM] * 7,
        out_specs=(VMEM,) * 6,
        scratch_shapes=fields + [pltpu.VMEM((CY * NZ, SLOTS), bf16)],
        compiler_params=params(16),
        cost_estimate=pl.CostEstimate(flops=4 * 10**9, bytes_accessed=2**21, transcendentals=0),
        name="inner",
    )(own, rp, ro, rs, f2, ft2, rf_pair)
    side_scratch = fields + [
        pltpu.VMEM((3, 8, 8, NZ), f32),
        pltpu.VMEM((24, NZ), f32),
        pltpu.VMEM((2 * NZ, SLOTS), bf16),
    ]
    half, *work_in = pl.pallas_call(
        core_kernel,
        out_shape=(sds(125, NZ),) + work,
        in_specs=[VMEM] * 10,
        out_specs=(VMEM,) * 6,
        scratch_shapes=side_scratch,
        input_output_aliases={5 + k: 1 + k for k in range(5)},
        compiler_params=params(16),
        cost_estimate=pl.CostEstimate(flops=2 * 10**9, bytes_accessed=2**20, transcendentals=0),
        name="core_side",
    )(from_core, f2, ft2, rf_pair, rf_third, *work_in)
    result, *_ = pl.pallas_call(
        functools.partial(main_kernel, peers),
        out_shape=(sds(125, 1, 256),) + work,
        in_specs=[VMEM] * 11,
        out_specs=(VMEM,) * 6,
        scratch_shapes=side_scratch,
        input_output_aliases={6 + k: 1 + k for k in range(5)},
        compiler_params=params(16),
        name="chip_side",
    )(from_chip, f2, ft2, rf_pair, rf_third, half, *work_in)
    return result


def solution(mesh):
    placed = (
        P(None, "gx", "gy"),
        P("gx", "gy"),
        P("gx", "gy", None),
        P("gx", "gy"),
        P("gx", "gy", None),
    )
    return jax.shard_map(
        per_device, mesh=mesh, in_specs=placed, out_specs=P(None, "gx", "gy"), check_vma=False
    )
```

```python
import functools

import jax
import jax.numpy as jnp
from jax import lax
from jax.experimental import pallas as pl
from jax.experimental.pallas import tpu as pltpu
from jax.sharding import PartitionSpec as P

NZ = 128
CY = 8
SLOTS = 512

FORWARD = (
    (0, 0, 1),
    (0, 1, -1),
    (0, 1, 0),
    (0, 1, 1),
    (1, -1, -1),
    (1, -1, 0),
    (1, -1, 1),
    (1, 0, -1),
    (1, 0, 0),
    (1, 0, 1),
    (1, 1, -1),
    (1, 1, 0),
    (1, 1, 1),
)
OFFSET = {step: k for k, step in enumerate(FORWARD)}
damping = 2.0 / 3.0

ROWS = 24
PER = 14
COLBLOCK = 93
THIRD = 2 * COLBLOCK
FAULT_ROW = 225
BAND_ROW, SUM_ROW, Y_ROWS = 237, 254, 280
REACH = 8
DIAGONALS = 2 * REACH + 1

f32 = jnp.float32
bf16 = jnp.bfloat16


def dot_nt(a, b):
    return lax.dot_general(a, b, (((1,), (1,)), ((), ())), preferred_element_type=f32)


def dot_nn(a, b):
    return lax.dot_general(a, b, (((1,), (0,)), ((), ())), preferred_element_type=f32)


def split(value):
    high = value.astype(bf16)
    return high, (value - high.astype(f32)).astype(bf16)


def pack_kernel(peers, count, *refs):
    sources, (block, plane, tile), targets, sems = refs[:4], refs[4:7], refs[7:11], refs[11]
    copies = [
        pltpu.make_async_copy(src, dst, sems.at[k])
        for k, (src, dst) in enumerate(zip(sources, targets))
    ]
    for copy in copies:
        copy.start()
    for copy in copies:
        copy.wait()
    trans, storage, cells, ftrans = targets
    last_x = lax.axis_index("gx") == peers[0] - 1
    first_y = lax.axis_index("gy") == 0
    last_y = lax.axis_index("gy") == peers[1] - 1
    depth = lax.broadcasted_iota(jnp.int32, (8, NZ), 1)
    row = lax.broadcasted_iota(jnp.int32, (8, NZ), 0)
    for x in range(2):
        for o in range(PER):
            base = (x * PER + o) * 8
            for y in range(CY):
                lanes = slice(y * NZ, (y + 1) * NZ)
                if o < 13:
                    value = trans[o, x : x + 1, lanes]
                else:
                    value = storage[x : x + 1, lanes]
                block[base + y : base + y + 1, :] = value
            if o == 13:
                continue
            step = FORWARD[o]
            keep = None
            if step[2] == 1:
                keep = depth < NZ - 1
            if step[2] == -1:
                keep = depth > 0
            if step[1] == 1:
                inside = (row < CY - 1) | jnp.logical_not(last_y)
                keep = inside if keep is None else keep & inside
            if step[1] == -1:
                inside = (row > 0) | jnp.logical_not(first_y)
                keep = inside if keep is None else keep & inside
            if step[0] == 1 and x == 1:
                inside = (row >= 0) & jnp.logical_not(last_x)
                keep = inside if keep is None else keep & inside
            if keep is not None:
                block[base : base + 8, :] = jnp.where(keep, block[base : base + 8, :], 0.0)
    live = count[0, 0]
    lane = lax.broadcasted_iota(jnp.int32, (1, NZ), 1)
    for r in range(4):
        lanes = slice(r * NZ, (r + 1) * NZ)
        tile[r : r + 1, :] = cells[0, :, lanes].astype(f32)
        tile[4 + r : 5 + r, :] = jnp.where(
            lane + r * NZ < live, ftrans[0, :, lanes], 0.0
        )
    plane[...] = block[(PER + 4) * 8 : (PER + 13) * 8, :]


def partner_rows(cells):
    return jnp.concatenate(
        [cells[0, :, r * NZ : (r + 1) * NZ] for r in range(4)], axis=0
    ).astype(f32)


def join_kernel(own, tile, cells, joined):
    joined[0:224, :] = own[...]
    joined[224:232, :] = tile[...]
    joined[232:236, :] = partner_rows(cells)
    joined[236:240, :] = jnp.zeros((4, NZ), f32)


def by_parity(axis, body):
    odd = lax.rem(lax.axis_index(axis), 2)
    for k in range(2):
        pl.when(odd == k)(functools.partial(body, k))


class Masked:
    def __init__(self, ref, due):
        self.ref, self.due = ref, due

    def __getitem__(self, index):
        return jnp.where(self.due, self.ref[index], 0.0)


class Behind:
    def __init__(self, first, second):
        self.refs, self.at = (first, second), lax.axis_index("gx")

    def __getitem__(self, index):
        first, second = (ref[index] for ref in self.refs)
        value = jnp.where(lax.rem(self.at // 2, 2) == 1, first, second)
        return jnp.where(self.at >= 2, value, 0.0)


def has_other(axis, peers):
    at = lax.axis_index(axis)
    return jnp.where(lax.rem(at, 2) == 0, at > 0, at < peers - 1)


def column_kernel(peers, own, rp, ro, ra, rb, band, sums, to_core, to_chip):
    ro = Masked(ro, has_other("gx", peers[0]))
    lo2 = Behind(ra, rb)

    def fill(out, lo, hi, first, third, runs):
        for c in range(2):
            y = first + c
            base = c * COLBLOCK
            out[base : base + 9, :] = lo2[pl.ds(y, 9, stride=8), :]
            for k, ref in enumerate((lo, own, hi)):
                start = base + 9 + 28 * k
                out[start : start + 28, :] = ref[pl.ds(y, 28, stride=8), :]
        at = THIRD
        out[at : at + 3, :] = lo2[pl.ds((runs[-1] - 4) * 8 + third, 3, stride=8), :]
        at += 3
        for ref in (lo, own, hi):
            for x in range(2):
                for o in runs:
                    out[at : at + 3, :] = ref[pl.ds((x * PER + o) * 8 + third, 3, stride=8), :]
                    at += 3
        for k, start in enumerate((224, 232, 228)):
            out[FAULT_ROW + 4 * k : FAULT_ROW + 4 * k + 4, :] = ro[start : start + 4, :]
        out[BAND_ROW : BAND_ROW + DIAGONALS, :] = band[int(first > 0), 0:DIAGONALS, :]
        for c in range(2):
            for k in range(2):
                at = SUM_ROW + (2 * c + k) * 6
                out[at : at + 6, :] = sums[k, first + c, 0:6, :]
        out[SUM_ROW + 24 : Y_ROWS, :] = jnp.zeros((Y_ROWS - SUM_ROW - 24, NZ), f32)

    def for_x(odd_x):
        lo, hi = (rp, ro) if odd_x else (ro, rp)

        def for_y(odd_y):
            up, down = (to_chip, to_core) if odd_y else (to_core, to_chip)
            fill(up, lo, hi, CY - 2, CY - 3, (1, 10))
            fill(down, lo, hi, 0, 2, (4,))

        by_parity("gy", for_y)

    by_parity("gx", for_x)


def colour(z):
    half = z >> 1
    return half - 5 * ((half * 205) >> 10)


def slot_columns(rows):
    tall = jnp.transpose(jnp.concatenate(rows, axis=0))
    return [[tall[:, 4 * k + r : 4 * k + r + 1] for r in range(4)] for k in range(len(rows))]


def flat_cells(rows):
    row = jnp.concatenate([rows[r : r + 1] for r in range(4)], axis=1)
    return row.astype(jnp.int32) & 1023


def fill_far(far2, partner, live):
    lane = lax.broadcasted_iota(jnp.int32, (NZ, NZ), 1)
    for r in range(4):
        rows = slice(r * NZ, (r + 1) * NZ)
        match = (partner[r].astype(jnp.int32) & 127) == lane
        high = live[r].astype(bf16).astype(f32)
        far2[rows, 0:NZ] = jnp.where(match, high, 0.0).astype(bf16)
        far2[rows, NZ : 2 * NZ] = jnp.where(match, live[r] - high, 0.0).astype(bf16)


def flat_rows(rows):
    return jnp.concatenate([rows[r : r + 1] for r in range(4)], axis=1)


def colour_sums(hot, beyond, live):
    e16 = lax.broadcasted_iota(jnp.int32, (16, SLOTS), 0)
    tint = colour(flat_rows(beyond).astype(jnp.int32) & 127)
    live = flat_rows(live)
    high = live.astype(bf16).astype(f32)
    value = jnp.where((e16 == tint) | (e16 == 5), high, 0.0)
    value = jnp.where((e16 == tint + 8) | (e16 == 13), live - high, value)
    got = dot_nt(value.astype(bf16), hot)
    return got[:8] + got[8:]


def diagonals(hot, own, far, live):
    d24 = lax.broadcasted_iota(jnp.int32, (24, SLOTS), 0)
    step = (flat_rows(far).astype(jnp.int32) & 127) - (flat_rows(own).astype(jnp.int32) & 127)
    live = flat_rows(live)
    high = live.astype(bf16).astype(f32)
    match = step + REACH == d24
    both = [jnp.where(match, value, 0.0) for value in (high, live - high)]
    got = dot_nt(jnp.concatenate(both, axis=0).astype(bf16), hot)
    return got[:24] + got[24:]


def fill_hot(hot, cells, columns):
    z128 = lax.broadcasted_iota(jnp.int32, (NZ, SLOTS), 0)
    for k, y in enumerate(columns):
        value = jnp.where(cells == z128 + y * NZ, 1.0, 0.0)
        hot[k * NZ : (k + 1) * NZ, :] = value.astype(bf16)


def pair_matrix(both):
    z8 = lax.broadcasted_iota(jnp.int32, (8, NZ), 1)
    e8 = lax.broadcasted_iota(jnp.int32, (8, NZ), 0)
    one = jnp.where((e8 == colour(z8)) | (e8 == 5), 1.0, 0.0).astype(bf16)
    one2 = jnp.concatenate([one, one], axis=1)
    matrix = both[:, :NZ] + both[:, NZ:]
    f2 = jnp.concatenate(split(matrix), axis=0)
    ft2 = jnp.concatenate(split(jnp.transpose(matrix)), axis=0)
    return f2, ft2, dot_nn(one2, ft2), dot_nn(one2, f2)


def fault_kernel(tile, plane, cells, f2, ft2, rf, band, plane_out, far2, hot, both):
    plane_out[...] = plane[...]
    partner, live = slot_columns([partner_rows(cells), tile[4:8, :]])
    fill_far(far2, partner, live)
    fill_hot(hot, flat_cells(tile[0:4, :]), range(CY))
    both[...] = dot_nn(hot[...], far2[...])
    for y in range(CY):
        f2[y], ft2[y], rf[0, y], rf[1, y] = pair_matrix(both[y * NZ : (y + 1) * NZ, :])
    for k, y in enumerate((0, CY - 1)):
        band[k] = diagonals(
            hot[y * NZ : (y + 1) * NZ, :], tile[0:4, :], partner_rows(cells), tile[4:8, :]
        )


def through(value, matrix2):
    rows = value.shape[0]
    high, low = split(value)
    left = jnp.concatenate(
        [jnp.concatenate([high, high], axis=1), jnp.concatenate([low, low], axis=1)], axis=0
    )
    got = dot_nn(left, matrix2)
    return got[:rows] + got[rows:]


class Place:
    def __init__(self):
        self.gx = lax.axis_index("gx")
        self.gy = lax.axis_index("gy")
        par = lax.rem(self.gx, 2)
        even = par == 0
        self.sgn = 1 - 2 * par
        self.p_own = jnp.where(even, 3, 2)
        self.p_far = jnp.where(even, 4, 1)
        self.p_third = jnp.where(even, 0, 5)
        self.p_fault = (self.p_own, self.p_far, self.p_third)
        self.x_coarse = lax.rem(self.gx, 5) + 5

    def a_of(self, d):
        return lax.rem(self.x_coarse + d, 5)

    def b_of(self, coarse_y, d):
        return lax.rem(self.gy * (CY // 2) + coarse_y + d + 5, 5)


def roll_weights(w, wr, first, count):
    for p in range(7):
        for o, step in enumerate(FORWARD):
            if step[2] == 0 or (p == 0 and o < 4):
                continue
            at = (p * PER + o) * ROWS + first
            distance = 1 if step[2] == 1 else NZ - 1
            wr[at : at + count, :] = pltpu.roll(w[at : at + count, :], distance, 1)


def smooth(w, wr, fd, qc, inv, diag, first, count):
    even_y = (lax.broadcasted_iota(jnp.int32, (count, NZ), 0) & 1) == 0
    even_z = (lax.broadcasted_iota(jnp.int32, (count, NZ), 1) & 1) == 0
    for p in range(6):
        base = p + 1

        def weight(dx, dy, dz):
            if (dx, dy, dz) in OFFSET:
                start = (base * PER + OFFSET[dx, dy, dz]) * ROWS + 1 + first
                return w[start : start + count, :]
            o = OFFSET[-dx, -dy, -dz]
            start = ((base + dx) * PER + o) * ROWS + 1 + first + dy
            return (w if dz == 0 else wr)[start : start + count, :]

        near = 1 if p % 2 == 0 else -1
        sums = {}
        for dz in (-1, 0, 1):
            got = {}
            for dx in (-1, 0, 1):
                below, above = weight(dx, -1, dz), weight(dx, 1, dz)
                got[dx, 0] = jnp.where(even_y, above, below)
                if (dx, dz) != (0, 0):
                    got[dx, 0] = got[dx, 0] + weight(dx, 0, dz)
                got[dx, 1] = jnp.where(even_y, below, above)
            for sy in range(2):
                sums[0, sy, dz] = got[0, sy] + got[near, sy]
                sums[1, sy, dz] = got[-near, sy]
        start = (base * PER + 13) * ROWS + 1 + first
        at = p * 16 + first
        total = w[start : start + count, :] + fd[at : at + count, :]
        r = []
        for sx in range(2):
            for sy in range(2):
                down, same, up = (sums[sx, sy, dz] for dz in (-1, 0, 1))
                r.append(same + jnp.where(even_z, up, down))
                r.append(jnp.where(even_z, down, up))
        for value in r:
            total = total + value
        total = jnp.where(total == 0.0, 1.0, total)
        scale = damping / total
        diag[at : at + count, :] = total
        inv[at : at + count, :] = scale
        for k, value in enumerate(r):
            value = value * scale
            if k == 0:
                value = value + (1.0 - damping)
            at = (p * 8 + k) * 16 + first
            qc[at : at + count, :] = value


def spread(here, qc, inv, qe, rf_at, columns, count):
    z8 = lax.broadcasted_iota(jnp.int32, (8, NZ), 1)
    e8 = lax.broadcasted_iota(jnp.int32, (8, NZ), 0)
    beside = jnp.where((z8 & 1) == 0, z8 - 1, z8 + 1)
    mask_own = jnp.where(e8 == colour(z8), 1.0, 0.0)
    mask_oth = jnp.where(e8 == colour(beside + 10), 1.0, 0.0)
    rows5 = jnp.where(e8 < 5, 1.0, 0.0)

    def one(k, carry):
        c = columns(k)
        for p in range(6):
            for lat in range(4):
                at = (p * 8 + 2 * lat) * 16 + c
                qe[p, c, lat] = (
                    qc[pl.ds(at, 1), :] * mask_own + qc[pl.ds(at + 16, 1), :] * mask_oth
                )
        for k, plane in enumerate(here.p_fault):
            qe[plane, c, 2] = qe[plane, c, 2] + rf_at(k, c) * (
                inv[pl.ds(plane * 16 + c, 1), :] * rows5
            )
        return carry

    lax.fori_loop(0, count, one, 0)


def apply_column(w, wr, diag, qe, ap, p, y, odd_x, odd_y):
    acc = {}
    for dx in (-1, 0, 1):
        for dy in (-1, 0, 1):
            q = [qe[p + dx, y + dy, lat] for lat in range(4)]
            own_x = dx if (dx == 1 and odd_x) or (dx == -1 and not odd_x) else 0
            own_y = dy if (dy == 1 and odd_y) or (dy == -1 and not odd_y) else 0
            oth_x = own_x + (1 if (odd_x + dx) % 2 else -1)
            oth_y = own_y + (1 if (odd_y + dy) % 2 else -1)
            for dz in (-1, 0, 1):
                if (dx, dy, dz) == (0, 0, 0):
                    continue
                if (dx, dy, dz) in OFFSET:
                    at = ((p + 1) * PER + OFFSET[dx, dy, dz]) * ROWS + y + 1
                    ref = w if dz == 0 else wr
                else:
                    at = ((p + 1 + dx) * PER + OFFSET[-dx, -dy, -dz]) * ROWS + y + 1 + dy
                    ref = w
                wt = ref[pl.ds(at, 1), :]
                for lat in range(4):
                    lx = oth_x if lat >= 2 else own_x
                    ly = oth_y if lat % 2 else own_y
                    value = wt * q[lat]
                    key = (lx, ly, dz)
                    acc[key] = acc[key] + value if key in acc else value
    centre = diag[pl.ds(p * 16 + y, 1), :]
    for lx in (-1, 0, 1):
        for ly in (-1, 0, 1):
            total = acc[lx, ly, 0]
            total = total + pltpu.roll(acc[lx, ly, 1], NZ - 1, 1)
            total = total + pltpu.roll(acc[lx, ly, -1], 1, 1)
            own_lat = None
            sx = {0: 0, (1 if odd_x else -1): 1}.get(lx)
            sy = {0: 0, (1 if odd_y else -1): 1}.get(ly)
            if sx is not None and sy is not None:
                own_lat = 2 * sx + sy
            if own_lat is None:
                total = -total
            else:
                total = centre * qe[p, y, own_lat] - total
            ap[p - 1, y - 1, lx + 1, ly + 1] = total


def fault_apply(here, qe, ap, c, f2c, ft2c):
    ly_oth = 2 * (c % 2)
    for plane, source, x_own, matrix in (
        (here.p_own, here.p_far, 1 + here.sgn, ft2c),
        (here.p_far, here.p_own, 1 - here.sgn, f2c),
    ):
        total = through(qe[source, c].reshape(32, NZ), matrix)
        for lat in range(4):
            lx = 1 if lat >= 2 else x_own
            ly = ly_oth if lat % 2 else 1
            ap[plane - 1, c - 1, lx, ly] = ap[plane - 1, c - 1, lx, ly] - total[8 * lat : 8 * lat + 8]


def fault_apply_band(here, qe, ap, c, band):
    ly_oth = 2 * (c % 2)
    to_own, to_far = [0.0] * 4, [0.0] * 4
    for d in range(DIAGONALS):
        weight = band[d : d + 1, :]
        for lat in range(4):
            ahead = pltpu.roll(qe[here.p_far, c, lat], (REACH - d) % NZ, 1)
            to_own[lat] = to_own[lat] + weight * ahead
            back = weight * qe[here.p_own, c, lat]
            to_far[lat] = to_far[lat] + pltpu.roll(back, (d - REACH) % NZ, 1)
    for plane, x_own, total in (
        (here.p_own, 1 + here.sgn, to_own),
        (here.p_far, 1 - here.sgn, to_far),
    ):
        for lat in range(4):
            lx = 1 if lat >= 2 else x_own
            ly = ly_oth if lat % 2 else 1
            ap[plane - 1, c - 1, lx, ly] = ap[plane - 1, c - 1, lx, ly] - total[lat]


def gather(here, qc, ap, tt, coarse_y, rows, add):
    shift = (-1, 0, 0, 1)
    for zk in range(2):
        acc = {}
        for x in range(-1, 3):
            for y in rows:
                lat = 2 * (x not in (0, 1)) + (y not in (0, 1))
                c = 2 * coarse_y + y + 2
                at = ((x + 2) * 8 + 2 * lat + zk) * 16 + c
                q = qc[at : at + 1, :]
                for lx in range(3):
                    for ly in range(3):
                        value = q * ap[x + 1, c - 1, lx, ly]
                        key = (shift[x + 1] + lx - 1, shift[y + 1] + ly - 1)
                        acc[key] = acc[key] + value if key in acc else value
        lane = (coarse_y % 2) * 256 + zk * NZ
        for (dx, dy), value in acc.items():
            at = (coarse_y // 2, here.a_of(dx), here.b_of(coarse_y, dy), slice(None), slice(lane, lane + NZ))
            tt[at] = tt[at] + value if add else value


def gather_fault(here, inv, ap, tt, y, ft2c):
    c = y + 2
    coarse_y = y // 2
    lane = (coarse_y % 2) * 256
    value = ap[here.p_far - 1, c - 1].reshape(72, NZ) * inv[pl.ds(here.p_far * 16 + c, 1), :]
    total = through(value, ft2c)
    for lx in range(3):
        a = here.a_of(lx - 1 + here.sgn)
        for ly in range(3):
            at = (coarse_y // 2, a, here.b_of(coarse_y, ly - 1), slice(None), slice(lane, lane + NZ))
            row = 8 * (3 * lx + ly)
            tt[at] = tt[at] + total[row : row + 8]


INNER = (2, 3, 4, 5)


def rows_of(coarse_y, inner):
    return [y for y in range(-1, 3) if (2 * coarse_y + y in INNER) == inner]


def inner_kernel(
    peers, own, rp, ro, ra, rb, f2, ft2, rf_pair, w, wr, qe, ap, tt, rf_third, qc, inv, diag, fd, hot
):
    here = Place()
    ro = Masked(ro, has_other("gx", peers[0]))

    def place(ref, count, first):
        for k in range(count):
            base = (first + k) * ROWS
            w[base + 3 : base + 11, :] = ref[8 * k : 8 * k + 8, :]

    def place_x(odd):
        lo, hi = (rp, ro) if odd else (ro, rp)
        place(lo, 28, PER)
        place(hi, 28, 5 * PER)

    by_parity("gx", place_x)
    place(Behind(ra, rb), 9, 4)
    place(own, 28, 3 * PER)

    fill_hot(hot, flat_cells(ro[224:228, :]), range(CY))
    got = colour_sums(hot[...], ro[232:236, :], ro[228:232, :])
    fd[...] = jnp.zeros_like(fd)
    for y in range(CY):
        rf_third[y] = got[:, y * NZ : (y + 1) * NZ]
        for plane, value in zip(here.p_fault, (rf_pair[0, y], rf_pair[1, y], rf_third[y])):
            fd[pl.ds(plane * 16 + y + 2, 1), :] = value[5:6, :]

    roll_weights(w, wr, 3, 8)
    smooth(w, wr, fd, qc, inv, diag, 2, 8)
    spread(
        here, qc, inv, qe, lambda k, c: rf_third[c - 2] if k == 2 else rf_pair[k, c - 2], lambda k: k + 3, 6
    )

    def pair(k, carry):
        for p in range(1, 5):
            apply_column(w, wr, diag, qe, ap, p, 2 * k + 4, p % 2, 0)
            apply_column(w, wr, diag, qe, ap, p, 2 * k + 5, p % 2, 1)
        return carry

    lax.fori_loop(0, 2, pair, 0)
    for y in INNER:
        fault_apply(here, qe, ap, y + 2, f2[y], ft2[y])
    tt[...] = jnp.zeros_like(tt)
    for coarse_y in range(CY // 2):
        gather(here, qc, ap, tt, coarse_y, rows_of(coarse_y, True), False)
    for y in INNER:
        gather_fault(here, inv, ap, tt, y, ft2[y])


def side(high, halo, f2, ft2, rf_pair, rf_third, work, fields, rf, band, hot):
    here = Place()
    w, wr, qe, ap, tt = work
    qc, inv, diag, fd = fields
    first = 6 if high else 0
    columns = (10, 11) if high else (0, 1)
    row, third, runs = (11, 13, (4,)) if high else (1, 0, (1, 10))

    for c in range(2):
        base = c * COLBLOCK
        w[pl.ds(4 * ROWS + row + c, 9, stride=ROWS), :] = halo[base : base + 9, :]
        w[pl.ds(PER * ROWS + row + c, 84, stride=ROWS), :] = halo[base + 9 : base + 93, :]
    at = THIRD
    for plane in range(7):
        for o in runs[-1:] if plane == 0 else runs:
            start = (plane * PER + o) * ROWS + third
            w[pl.ds(start, 3, stride=ROWS), :] = halo[at : at + 3, :]
            at += 3
    roll_weights(w, wr, 8 if high else 0, 8)

    fd[...] = jnp.zeros_like(fd)

    def put(column, k, value):
        rf[k, column - first] = value
        fd[pl.ds(here.p_fault[k] * 16 + column, 1), :] = value[5:6, :]

    for column in range(first, first + 8):
        y = column - 2
        if 0 <= y < CY:
            put(column, 0, rf_pair[0, y])
            put(column, 1, rf_pair[1, y])
            put(column, 2, rf_third[y])
    band[0:DIAGONALS, :] = halo[BAND_ROW : BAND_ROW + DIAGONALS, :]
    lists = halo[FAULT_ROW : FAULT_ROW + 12, :]
    fill_hot(hot, flat_cells(lists[0:4]), (0, 1) if high else (CY - 2, CY - 1))
    got = colour_sums(hot[...], lists[4:8], lists[8:12])
    for c, column in enumerate(columns):
        for k in range(2):
            at = SUM_ROW + (2 * c + k) * 6
            value = halo[at : at + 6, :]
            put(column, k, jnp.concatenate([value, jnp.zeros((2, NZ), f32)], axis=0))
        put(column, 2, got[:, c * NZ : (c + 1) * NZ])

    smooth(w, wr, fd, qc, inv, diag, first, 8)
    spread(
        here, qc, inv, qe, lambda k, c: rf[k, c - first], lambda k: k + (9 if high else 0), 3
    )

    def planes(k, carry):
        for odd_x in (1, 0):
            p = 2 * k + 2 - odd_x
            for y in (8, 9, 10) if high else (1, 2, 3):
                apply_column(w, wr, diag, qe, ap, p, y, odd_x, y % 2)
        return carry

    lax.fori_loop(0, 2, planes, 0)
    own = (6, 7) if high else (0, 1)
    for y in own:
        fault_apply(here, qe, ap, y + 2, f2[y], ft2[y])
    fault_apply_band(here, qe, ap, 10 if high else 1, band)
    parts = ((3, (0, 1, 2)), (2, (2,))) if high else ((0, (-1, 0, 1)), (1, (-1,)))
    for coarse_y, rows in parts:
        gather(here, qc, ap, tt, coarse_y, rows, True)
    for y in own:
        gather_fault(here, inv, ap, tt, y, ft2[y])


def finish(tt, pair, store):
    kz = lax.broadcasted_iota(jnp.int32, (512, NZ), 0)
    kout = lax.broadcasted_iota(jnp.int32, (512, NZ), 1)
    z_in = kz & 127
    is_oth = ((kz >> 7) & 1) == 1
    target = jnp.where(
        is_oth, (z_in >> 1) + jnp.where((z_in & 1) == 0, -1, 1), z_in >> 1
    )
    fits = (target == (kout & 63)) & ((kz >> 8) == (kout >> 6))
    collect = jnp.where(fits, 1.0, 0.0).astype(bf16)
    high, low = split(tt[pair].reshape(200, 512))
    got = (dot_nn(high, collect) + dot_nn(low, collect)) * 0.125
    for k in range(25):
        store(5 * k, got[8 * k : 8 * k + 5])


def core_kernel(halo, f2, ft2, rf_pair, rf_third, *refs):
    half, work, fields, rest = refs[5], refs[6:11], refs[11:15], refs[15:]

    def body(odd):
        side(not odd, halo, f2, ft2, rf_pair, rf_third, work, fields, *rest)

        def store(row, value):
            half[row : row + 5, :] = value

        finish(work[4], 0 if odd else 1, store)

    by_parity("gy", body)


def main_kernel(peers, halo, f2, ft2, rf_pair, rf_third, half, *refs):
    out, work, fields, rest = refs[5], refs[6:11], refs[11:15], refs[15:]
    halo = Masked(halo, has_other("gy", peers[1]))

    def body(odd):
        side(odd, halo, f2, ft2, rf_pair, rf_third, work, fields, *rest)
        lanes = [slice(0, NZ), slice(NZ, 2 * NZ)]

        def store(row, value):
            out[row : row + 5, 0, lanes[odd]] = value
            out[row : row + 5, 0, lanes[1 - odd]] = half[row : row + 5, :]

        finish(work[4], odd, store)

    by_parity("gy", body)


def send(value, target):
    size_x, size_y = lax.axis_size("gx"), lax.axis_size("gy")
    pairs = []
    for x in range(size_x):
        for y in range(size_y):
            to_x, to_y = target(x, y)
            pairs.append((x * size_y + y, to_x * size_y + to_y))
    return lax.ppermute(value, ("gx", "gy"), pairs)


def x_partner(x, y):
    return x ^ 1, y


def core_partner(x, y):
    return x, y ^ 1


def x_other(size_x):
    def target(x, y):
        other = x + 1 if x % 2 else x - 1
        return (other, y) if 0 <= other < size_x else core_partner(x, y)

    return target


def chip_other(size_y):
    def target(x, y):
        other = y + 1 if y % 2 else y - 1
        return (x, other) if 0 <= other < size_y else x_partner(x, y)

    return target


def z_partner(size_x):
    def target(x, y):
        other = x ^ 2
        return (other, y) if other < size_x else x_partner(x, y)

    return target


def z_other(size_x):
    def target(x, y):
        other = x + 2 if x % 4 >= 2 else x - 2
        return (other, y) if 0 <= other < size_x else x_partner(x, y)

    return target


VMEM = pl.BlockSpec(memory_space=pltpu.VMEM)
HBM = pl.BlockSpec(memory_space=pltpu.HBM)


def params(mib):
    return pltpu.CompilerParams(vmem_limit_bytes=mib * 1024 * 1024)


def sds(*shape, dtype=f32):
    return jax.ShapeDtypeStruct(shape, dtype)


def per_device(trans, storage, fault_cells, fault_count, fault_trans):
    peers = (lax.axis_size("gx"), lax.axis_size("gy"))
    cells = send(fault_cells, x_partner)
    sources = [
        pltpu.with_memory_space_constraint(array, pltpu.HBM)
        for array in (trans, storage, fault_cells, fault_trans)
    ]
    own, plane, tile = pl.pallas_call(
        functools.partial(pack_kernel, peers),
        out_shape=(sds(224, NZ), sds(72, NZ), sds(8, NZ)),
        in_specs=[pl.BlockSpec(memory_space=pltpu.SMEM)] + [HBM] * 4,
        out_specs=(VMEM,) * 3,
        scratch_shapes=[pltpu.VMEM(array.shape, array.dtype) for array in sources]
        + [pltpu.SemaphoreType.DMA((4,))],
        compiler_params=params(16),
        name="pack",
    )(fault_count, *sources)
    joined = pl.pallas_call(
        join_kernel,
        out_shape=sds(240, NZ),
        in_specs=[VMEM] * 3,
        out_specs=VMEM,
        compiler_params=params(16),
        name="join",
    )(own, tile, cells)
    ro = send(joined, x_other(peers[0]))
    rp = send(own, x_partner)
    pieces = sds(CY, 2 * NZ, NZ, dtype=bf16)
    f2, ft2, rf_pair, band, plane = pl.pallas_call(
        fault_kernel,
        out_shape=(pieces, pieces, sds(2, CY, 8, NZ), sds(2, 24, NZ), sds(72, NZ)),
        in_specs=[VMEM] * 3,
        out_specs=(VMEM,) * 5,
        scratch_shapes=[
            pltpu.VMEM((SLOTS, 2 * NZ), bf16),
            pltpu.VMEM((CY * NZ, SLOTS), bf16),
            pltpu.VMEM((CY * NZ, 2 * NZ), f32),
        ],
        compiler_params=params(16),
        cost_estimate=pl.CostEstimate(flops=2 * 10**9, bytes_accessed=2**21, transcendentals=0),
        name="faults",
    )(tile, plane, cells)
    ra = send(plane, z_partner(peers[0]))
    rb = send(plane, z_other(peers[0]))
    to_core, to_chip = pl.pallas_call(
        functools.partial(column_kernel, peers),
        out_shape=(sds(Y_ROWS, NZ), sds(Y_ROWS, NZ)),
        in_specs=[VMEM] * 7,
        out_specs=(VMEM,) * 2,
        compiler_params=params(16),
        name="columns",
    )(own, rp, ro, ra, rb, band, rf_pair)
    from_chip = send(to_chip, chip_other(peers[1]))
    from_core = send(to_core, core_partner)
    work = (
        sds(7 * PER * ROWS, NZ),
        sds(7 * PER * ROWS, NZ),
        sds(6, 12, 4, 8, NZ),
        sds(4, 10, 3, 3, 8, NZ),
        sds(2, 5, 5, 8, 512),
    )
    fields = [
        pltpu.VMEM((6 * 8 * 16, NZ), f32),
        pltpu.VMEM((6 * 16, NZ), f32),
        pltpu.VMEM((6 * 16, NZ), f32),
        pltpu.VMEM((6 * 16, NZ), f32),
    ]
    *work_in, rf_third = pl.pallas_call(
        functools.partial(inner_kernel, peers),
        out_shape=work + (sds(CY, 8, NZ),),
        in_specs=[VMEM] * 8,
        out_specs=(VMEM,) * 6,
        scratch_shapes=fields + [pltpu.VMEM((CY * NZ, SLOTS), bf16)],
        compiler_params=params(16),
        cost_estimate=pl.CostEstimate(flops=4 * 10**9, bytes_accessed=2**21, transcendentals=0),
        name="inner",
    )(own, rp, ro, ra, rb, f2, ft2, rf_pair)
    side_scratch = fields + [
        pltpu.VMEM((3, 8, 8, NZ), f32),
        pltpu.VMEM((24, NZ), f32),
        pltpu.VMEM((2 * NZ, SLOTS), bf16),
    ]
    half, *work_in = pl.pallas_call(
        core_kernel,
        out_shape=(sds(125, NZ),) + work,
        in_specs=[VMEM] * 10,
        out_specs=(VMEM,) * 6,
        scratch_shapes=side_scratch,
        input_output_aliases={5 + k: 1 + k for k in range(5)},
        compiler_params=params(16),
        cost_estimate=pl.CostEstimate(flops=2 * 10**9, bytes_accessed=2**20, transcendentals=0),
        name="core_side",
    )(from_core, f2, ft2, rf_pair, rf_third, *work_in)
    result, *_ = pl.pallas_call(
        functools.partial(main_kernel, peers),
        out_shape=(sds(125, 1, 256),) + work,
        in_specs=[VMEM] * 11,
        out_specs=(VMEM,) * 6,
        scratch_shapes=side_scratch,
        input_output_aliases={6 + k: 1 + k for k in range(5)},
        compiler_params=params(16),
        name="chip_side",
    )(from_chip, f2, ft2, rf_pair, rf_third, half, *work_in)
    return result


def solution(mesh):
    placed = (
        P(None, "gx", "gy"),
        P("gx", "gy"),
        P("gx", "gy", None),
        P("gx", "gy"),
        P("gx", "gy", None),
    )
    return jax.shard_map(
        per_device, mesh=mesh, in_specs=placed, out_specs=P(None, "gx", "gy"), check_vma=False
    )
```

```python
import functools

import jax
import jax.numpy as jnp
from jax import lax
from jax.experimental import pallas as pl
from jax.experimental.pallas import tpu as pltpu
from jax.sharding import PartitionSpec as P

NZ = 128
CY = 8
SLOTS = 512

FORWARD = (
    (0, 0, 1),
    (0, 1, -1),
    (0, 1, 0),
    (0, 1, 1),
    (1, -1, -1),
    (1, -1, 0),
    (1, -1, 1),
    (1, 0, -1),
    (1, 0, 0),
    (1, 0, 1),
    (1, 1, -1),
    (1, 1, 0),
    (1, 1, 1),
)
OFFSET = {step: k for k, step in enumerate(FORWARD)}
damping = 2.0 / 3.0

ROWS = 24
PER = 14
COLBLOCK = 93
THIRD = 2 * COLBLOCK
FAULT_ROW = 225
BAND_ROW, SUM_ROW, Y_ROWS = 237, 254, 280
REACH = 8
DIAGONALS = 2 * REACH + 1

f32 = jnp.float32
bf16 = jnp.bfloat16


def dot_nt(a, b):
    return lax.dot_general(a, b, (((1,), (1,)), ((), ())), preferred_element_type=f32)


def dot_nn(a, b):
    return lax.dot_general(a, b, (((1,), (0,)), ((), ())), preferred_element_type=f32)


def split(value):
    high = value.astype(bf16)
    return high, (value - high.astype(f32)).astype(bf16)


def pack_kernel(peers, count, *refs):
    sources, (block, plane, tile), targets, sems = refs[:4], refs[4:7], refs[7:11], refs[11]
    copies = [
        pltpu.make_async_copy(src, dst, sems.at[k])
        for k, (src, dst) in enumerate(zip(sources, targets))
    ]
    for copy in copies:
        copy.start()
    for copy in copies:
        copy.wait()
    trans, storage, cells, ftrans = targets
    last_x = lax.axis_index("gx") == peers[0] - 1
    first_y = lax.axis_index("gy") == 0
    last_y = lax.axis_index("gy") == peers[1] - 1
    depth = lax.broadcasted_iota(jnp.int32, (8, NZ), 1)
    row = lax.broadcasted_iota(jnp.int32, (8, NZ), 0)
    for x in range(2):
        for o in range(PER):
            base = (x * PER + o) * 8
            for y in range(CY):
                lanes = slice(y * NZ, (y + 1) * NZ)
                if o < 13:
                    value = trans[o, x : x + 1, lanes]
                else:
                    value = storage[x : x + 1, lanes]
                block[base + y : base + y + 1, :] = value
            if o == 13:
                continue
            step = FORWARD[o]
            keep = None
            if step[2] == 1:
                keep = depth < NZ - 1
            if step[2] == -1:
                keep = depth > 0
            if step[1] == 1:
                inside = (row < CY - 1) | jnp.logical_not(last_y)
                keep = inside if keep is None else keep & inside
            if step[1] == -1:
                inside = (row > 0) | jnp.logical_not(first_y)
                keep = inside if keep is None else keep & inside
            if step[0] == 1 and x == 1:
                inside = (row >= 0) & jnp.logical_not(last_x)
                keep = inside if keep is None else keep & inside
            if keep is not None:
                block[base : base + 8, :] = jnp.where(keep, block[base : base + 8, :], 0.0)
    live = count[0, 0]
    lane = lax.broadcasted_iota(jnp.int32, (1, NZ), 1)
    for r in range(4):
        lanes = slice(r * NZ, (r + 1) * NZ)
        tile[r : r + 1, :] = cells[0, :, lanes].astype(f32)
        tile[4 + r : 5 + r, :] = jnp.where(
            lane + r * NZ < live, ftrans[0, :, lanes], 0.0
        )
    plane[...] = block[(PER + 4) * 8 : (PER + 13) * 8, :]


def partner_rows(cells):
    return jnp.concatenate(
        [cells[0, :, r * NZ : (r + 1) * NZ] for r in range(4)], axis=0
    ).astype(f32)


def join_kernel(own, tile, plane, cells, joined, plane_out):
    plane_out[...] = plane[...]
    joined[0:224, :] = own[...]
    joined[224:232, :] = tile[...]
    joined[232:236, :] = partner_rows(cells)
    joined[236:240, :] = jnp.zeros((4, NZ), f32)


def by_parity(axis, body):
    odd = lax.rem(lax.axis_index(axis), 2)
    for k in range(2):
        pl.when(odd == k)(functools.partial(body, k))


class Masked:
    def __init__(self, ref, due):
        self.ref, self.due = ref, due

    def __getitem__(self, index):
        return jnp.where(self.due, self.ref[index], 0.0)


def has_other(axis, peers):
    at = lax.axis_index(axis)
    return jnp.where(lax.rem(at, 2) == 0, at > 0, at < peers - 1)


def column_kernel(peers, own, rp, ro, rs, band, sums, to_core, to_chip):
    ro = Masked(ro, has_other("gx", peers[0]))
    lo2 = Masked(rs, lax.axis_index("gx") >= 2)

    def fill(out, lo, hi, first, third, runs):
        for c in range(2):
            y = first + c
            base = c * COLBLOCK
            out[base : base + 9, :] = lo2[pl.ds(y, 9, stride=8), :]
            for k, ref in enumerate((lo, own, hi)):
                start = base + 9 + 28 * k
                out[start : start + 28, :] = ref[pl.ds(y, 28, stride=8), :]
        at = THIRD
        out[at : at + 3, :] = lo2[pl.ds((runs[-1] - 4) * 8 + third, 3, stride=8), :]
        at += 3
        for ref in (lo, own, hi):
            for x in range(2):
                for o in runs:
                    out[at : at + 3, :] = ref[pl.ds((x * PER + o) * 8 + third, 3, stride=8), :]
                    at += 3
        for k, start in enumerate((224, 232, 228)):
            out[FAULT_ROW + 4 * k : FAULT_ROW + 4 * k + 4, :] = ro[start : start + 4, :]
        out[BAND_ROW : BAND_ROW + DIAGONALS, :] = band[int(first > 0), 0:DIAGONALS, :]
        for c in range(2):
            for k in range(2):
                at = SUM_ROW + (2 * c + k) * 6
                out[at : at + 6, :] = sums[k, first + c, 0:6, :]
        out[SUM_ROW + 24 : Y_ROWS, :] = jnp.zeros((Y_ROWS - SUM_ROW - 24, NZ), f32)

    def for_x(odd_x):
        lo, hi = (rp, ro) if odd_x else (ro, rp)

        def for_y(odd_y):
            up, down = (to_chip, to_core) if odd_y else (to_core, to_chip)
            fill(up, lo, hi, CY - 2, CY - 3, (1, 10))
            fill(down, lo, hi, 0, 2, (4,))

        by_parity("gy", for_y)

    by_parity("gx", for_x)


def colour(z):
    half = z >> 1
    return half - 5 * ((half * 205) >> 10)


def slot_columns(rows):
    tall = jnp.transpose(jnp.concatenate(rows, axis=0))
    return [[tall[:, 4 * k + r : 4 * k + r + 1] for r in range(4)] for k in range(len(rows))]


def flat_cells(rows):
    row = jnp.concatenate([rows[r : r + 1] for r in range(4)], axis=1)
    return row.astype(jnp.int32) & 1023


def fill_far(far2, partner, live):
    lane = lax.broadcasted_iota(jnp.int32, (NZ, NZ), 1)
    for r in range(4):
        rows = slice(r * NZ, (r + 1) * NZ)
        match = (partner[r].astype(jnp.int32) & 127) == lane
        high = live[r].astype(bf16).astype(f32)
        far2[rows, 0:NZ] = jnp.where(match, high, 0.0).astype(bf16)
        far2[rows, NZ : 2 * NZ] = jnp.where(match, live[r] - high, 0.0).astype(bf16)


def flat_rows(rows):
    return jnp.concatenate([rows[r : r + 1] for r in range(4)], axis=1)


def colour_sums(hot, beyond, live):
    e16 = lax.broadcasted_iota(jnp.int32, (16, SLOTS), 0)
    tint = colour(flat_rows(beyond).astype(jnp.int32) & 127)
    live = flat_rows(live)
    high = live.astype(bf16).astype(f32)
    value = jnp.where((e16 == tint) | (e16 == 5), high, 0.0)
    value = jnp.where((e16 == tint + 8) | (e16 == 13), live - high, value)
    got = dot_nt(value.astype(bf16), hot)
    return got[:8] + got[8:]


def diagonals(hot, own, far, live):
    d24 = lax.broadcasted_iota(jnp.int32, (24, SLOTS), 0)
    step = (flat_rows(far).astype(jnp.int32) & 127) - (flat_rows(own).astype(jnp.int32) & 127)
    live = flat_rows(live)
    high = live.astype(bf16).astype(f32)
    match = step + REACH == d24
    both = [jnp.where(match, value, 0.0) for value in (high, live - high)]
    got = dot_nt(jnp.concatenate(both, axis=0).astype(bf16), hot)
    return got[:24] + got[24:]


def fill_hot(hot, cells, columns):
    z128 = lax.broadcasted_iota(jnp.int32, (NZ, SLOTS), 0)
    for k, y in enumerate(columns):
        value = jnp.where(cells == z128 + y * NZ, 1.0, 0.0)
        hot[k * NZ : (k + 1) * NZ, :] = value.astype(bf16)


def pair_matrix(both):
    z8 = lax.broadcasted_iota(jnp.int32, (8, NZ), 1)
    e8 = lax.broadcasted_iota(jnp.int32, (8, NZ), 0)
    one = jnp.where((e8 == colour(z8)) | (e8 == 5), 1.0, 0.0).astype(bf16)
    one2 = jnp.concatenate([one, one], axis=1)
    matrix = both[:, :NZ] + both[:, NZ:]
    f2 = jnp.concatenate(split(matrix), axis=0)
    ft2 = jnp.concatenate(split(jnp.transpose(matrix)), axis=0)
    return f2, ft2, dot_nn(one2, ft2), dot_nn(one2, f2)


def fault_kernel(tile, cells, f2, ft2, rf, band, far2, hot, both):
    partner, live = slot_columns([partner_rows(cells), tile[4:8, :]])
    fill_far(far2, partner, live)
    fill_hot(hot, flat_cells(tile[0:4, :]), range(CY))
    both[...] = dot_nn(hot[...], far2[...])
    for y in range(CY):
        f2[y], ft2[y], rf[0, y], rf[1, y] = pair_matrix(both[y * NZ : (y + 1) * NZ, :])
    for k, y in enumerate((0, CY - 1)):
        band[k] = diagonals(
            hot[y * NZ : (y + 1) * NZ, :], tile[0:4, :], partner_rows(cells), tile[4:8, :]
        )


def through(value, matrix2):
    rows = value.shape[0]
    high, low = split(value)
    left = jnp.concatenate(
        [jnp.concatenate([high, high], axis=1), jnp.concatenate([low, low], axis=1)], axis=0
    )
    got = dot_nn(left, matrix2)
    return got[:rows] + got[rows:]


class Place:
    def __init__(self):
        self.gx = lax.axis_index("gx")
        self.gy = lax.axis_index("gy")
        par = lax.rem(self.gx, 2)
        even = par == 0
        self.sgn = 1 - 2 * par
        self.p_own = jnp.where(even, 3, 2)
        self.p_far = jnp.where(even, 4, 1)
        self.p_third = jnp.where(even, 0, 5)
        self.p_fault = (self.p_own, self.p_far, self.p_third)
        self.x_coarse = lax.rem(self.gx, 5) + 5

    def a_of(self, d):
        return lax.rem(self.x_coarse + d, 5)

    def b_of(self, coarse_y, d):
        return lax.rem(self.gy * (CY // 2) + coarse_y + d + 5, 5)


def roll_weights(w, wr, first, count):
    for p in range(7):
        for o, step in enumerate(FORWARD):
            if step[2] == 0 or (p == 0 and o < 4):
                continue
            at = (p * PER + o) * ROWS + first
            distance = 1 if step[2] == 1 else NZ - 1
            wr[at : at + count, :] = pltpu.roll(w[at : at + count, :], distance, 1)


def smooth(w, wr, fd, qc, inv, diag, first, count):
    even_y = (lax.broadcasted_iota(jnp.int32, (count, NZ), 0) & 1) == 0
    even_z = (lax.broadcasted_iota(jnp.int32, (count, NZ), 1) & 1) == 0
    for p in range(6):
        base = p + 1

        def weight(dx, dy, dz):
            if (dx, dy, dz) in OFFSET:
                start = (base * PER + OFFSET[dx, dy, dz]) * ROWS + 1 + first
                return w[start : start + count, :]
            o = OFFSET[-dx, -dy, -dz]
            start = ((base + dx) * PER + o) * ROWS + 1 + first + dy
            return (w if dz == 0 else wr)[start : start + count, :]

        near = 1 if p % 2 == 0 else -1
        sums = {}
        for dz in (-1, 0, 1):
            got = {}
            for dx in (-1, 0, 1):
                below, above = weight(dx, -1, dz), weight(dx, 1, dz)
                got[dx, 0] = jnp.where(even_y, above, below)
                if (dx, dz) != (0, 0):
                    got[dx, 0] = got[dx, 0] + weight(dx, 0, dz)
                got[dx, 1] = jnp.where(even_y, below, above)
            for sy in range(2):
                sums[0, sy, dz] = got[0, sy] + got[near, sy]
                sums[1, sy, dz] = got[-near, sy]
        start = (base * PER + 13) * ROWS + 1 + first
        at = p * 16 + first
        total = w[start : start + count, :] + fd[at : at + count, :]
        r = []
        for sx in range(2):
            for sy in range(2):
                down, same, up = (sums[sx, sy, dz] for dz in (-1, 0, 1))
                r.append(same + jnp.where(even_z, up, down))
                r.append(jnp.where(even_z, down, up))
        for value in r:
            total = total + value
        total = jnp.where(total == 0.0, 1.0, total)
        scale = damping / total
        diag[at : at + count, :] = total
        inv[at : at + count, :] = scale
        for k, value in enumerate(r):
            value = value * scale
            if k == 0:
                value = value + (1.0 - damping)
            at = (p * 8 + k) * 16 + first
            qc[at : at + count, :] = value


def spread(here, qc, inv, qe, rf_at, columns, count):
    z8 = lax.broadcasted_iota(jnp.int32, (8, NZ), 1)
    e8 = lax.broadcasted_iota(jnp.int32, (8, NZ), 0)
    beside = jnp.where((z8 & 1) == 0, z8 - 1, z8 + 1)
    mask_own = jnp.where(e8 == colour(z8), 1.0, 0.0)
    mask_oth = jnp.where(e8 == colour(beside + 10), 1.0, 0.0)
    rows5 = jnp.where(e8 < 5, 1.0, 0.0)

    def one(k, carry):
        c = columns(k)
        for p in range(6):
            for lat in range(4):
                at = (p * 8 + 2 * lat) * 16 + c
                qe[p, c, lat] = (
                    qc[pl.ds(at, 1), :] * mask_own + qc[pl.ds(at + 16, 1), :] * mask_oth
                )
        for k, plane in enumerate(here.p_fault):
            qe[plane, c, 2] = qe[plane, c, 2] + rf_at(k, c) * (
                inv[pl.ds(plane * 16 + c, 1), :] * rows5
            )
        return carry

    lax.fori_loop(0, count, one, 0)


def apply_column(w, wr, diag, qe, ap, p, y, odd_x, odd_y):
    acc = {}
    for dx in (-1, 0, 1):
        for dy in (-1, 0, 1):
            q = [qe[p + dx, y + dy, lat] for lat in range(4)]
            own_x = dx if (dx == 1 and odd_x) or (dx == -1 and not odd_x) else 0
            own_y = dy if (dy == 1 and odd_y) or (dy == -1 and not odd_y) else 0
            oth_x = own_x + (1 if (odd_x + dx) % 2 else -1)
            oth_y = own_y + (1 if (odd_y + dy) % 2 else -1)
            for dz in (-1, 0, 1):
                if (dx, dy, dz) == (0, 0, 0):
                    continue
                if (dx, dy, dz) in OFFSET:
                    at = ((p + 1) * PER + OFFSET[dx, dy, dz]) * ROWS + y + 1
                    ref = w if dz == 0 else wr
                else:
                    at = ((p + 1 + dx) * PER + OFFSET[-dx, -dy, -dz]) * ROWS + y + 1 + dy
                    ref = w
                wt = ref[pl.ds(at, 1), :]
                for lat in range(4):
                    lx = oth_x if lat >= 2 else own_x
                    ly = oth_y if lat % 2 else own_y
                    value = wt * q[lat]
                    key = (lx, ly, dz)
                    acc[key] = acc[key] + value if key in acc else value
    centre = diag[pl.ds(p * 16 + y, 1), :]
    for lx in (-1, 0, 1):
        for ly in (-1, 0, 1):
            total = acc[lx, ly, 0]
            total = total + pltpu.roll(acc[lx, ly, 1], NZ - 1, 1)
            total = total + pltpu.roll(acc[lx, ly, -1], 1, 1)
            own_lat = None
            sx = {0: 0, (1 if odd_x else -1): 1}.get(lx)
            sy = {0: 0, (1 if odd_y else -1): 1}.get(ly)
            if sx is not None and sy is not None:
                own_lat = 2 * sx + sy
            if own_lat is None:
                total = -total
            else:
                total = centre * qe[p, y, own_lat] - total
            ap[p - 1, y - 1, lx + 1, ly + 1] = total


def fault_apply(here, qe, ap, c, f2c, ft2c):
    ly_oth = 2 * (c % 2)
    for plane, source, x_own, matrix in (
        (here.p_own, here.p_far, 1 + here.sgn, ft2c),
        (here.p_far, here.p_own, 1 - here.sgn, f2c),
    ):
        total = through(qe[source, c].reshape(32, NZ), matrix)
        for lat in range(4):
            lx = 1 if lat >= 2 else x_own
            ly = ly_oth if lat % 2 else 1
            ap[plane - 1, c - 1, lx, ly] = ap[plane - 1, c - 1, lx, ly] - total[8 * lat : 8 * lat + 8]


def fault_apply_band(here, qe, ap, c, band):
    ly_oth = 2 * (c % 2)
    to_own, to_far = [0.0] * 4, [0.0] * 4
    for d in range(DIAGONALS):
        weight = band[d : d + 1, :]
        for lat in range(4):
            ahead = pltpu.roll(qe[here.p_far, c, lat], (REACH - d) % NZ, 1)
            to_own[lat] = to_own[lat] + weight * ahead
            back = weight * qe[here.p_own, c, lat]
            to_far[lat] = to_far[lat] + pltpu.roll(back, (d - REACH) % NZ, 1)
    for plane, x_own, total in (
        (here.p_own, 1 + here.sgn, to_own),
        (here.p_far, 1 - here.sgn, to_far),
    ):
        for lat in range(4):
            lx = 1 if lat >= 2 else x_own
            ly = ly_oth if lat % 2 else 1
            ap[plane - 1, c - 1, lx, ly] = ap[plane - 1, c - 1, lx, ly] - total[lat]


def gather(here, qc, ap, tt, coarse_y, rows, add):
    shift = (-1, 0, 0, 1)
    for zk in range(2):
        acc = {}
        for x in range(-1, 3):
            for y in rows:
                lat = 2 * (x not in (0, 1)) + (y not in (0, 1))
                c = 2 * coarse_y + y + 2
                at = ((x + 2) * 8 + 2 * lat + zk) * 16 + c
                q = qc[at : at + 1, :]
                for lx in range(3):
                    for ly in range(3):
                        value = q * ap[x + 1, c - 1, lx, ly]
                        key = (shift[x + 1] + lx - 1, shift[y + 1] + ly - 1)
                        acc[key] = acc[key] + value if key in acc else value
        lane = (coarse_y % 2) * 256 + zk * NZ
        for (dx, dy), value in acc.items():
            at = (coarse_y // 2, here.a_of(dx), here.b_of(coarse_y, dy), slice(None), slice(lane, lane + NZ))
            tt[at] = tt[at] + value if add else value


def gather_fault(here, inv, ap, tt, y, ft2c):
    c = y + 2
    coarse_y = y // 2
    lane = (coarse_y % 2) * 256
    value = ap[here.p_far - 1, c - 1].reshape(72, NZ) * inv[pl.ds(here.p_far * 16 + c, 1), :]
    total = through(value, ft2c)
    for lx in range(3):
        a = here.a_of(lx - 1 + here.sgn)
        for ly in range(3):
            at = (coarse_y // 2, a, here.b_of(coarse_y, ly - 1), slice(None), slice(lane, lane + NZ))
            row = 8 * (3 * lx + ly)
            tt[at] = tt[at] + total[row : row + 8]


INNER = (2, 3, 4, 5)


def rows_of(coarse_y, inner):
    return [y for y in range(-1, 3) if (2 * coarse_y + y in INNER) == inner]


def inner_kernel(
    peers, own, rp, ro, rs, f2, ft2, rf_pair, w, wr, qe, ap, tt, rf_third, qc, inv, diag, fd, hot
):
    here = Place()
    ro = Masked(ro, has_other("gx", peers[0]))

    def place(ref, count, first):
        for k in range(count):
            base = (first + k) * ROWS
            w[base + 3 : base + 11, :] = ref[8 * k : 8 * k + 8, :]

    def place_x(odd):
        lo, hi = (rp, ro) if odd else (ro, rp)
        place(lo, 28, PER)
        place(hi, 28, 5 * PER)

    by_parity("gx", place_x)
    place(Masked(rs, here.gx >= 2), 9, 4)
    place(own, 28, 3 * PER)

    fill_hot(hot, flat_cells(ro[224:228, :]), range(CY))
    got = colour_sums(hot[...], ro[232:236, :], ro[228:232, :])
    fd[...] = jnp.zeros_like(fd)
    for y in range(CY):
        rf_third[y] = got[:, y * NZ : (y + 1) * NZ]
        for plane, value in zip(here.p_fault, (rf_pair[0, y], rf_pair[1, y], rf_third[y])):
            fd[pl.ds(plane * 16 + y + 2, 1), :] = value[5:6, :]

    roll_weights(w, wr, 3, 8)
    smooth(w, wr, fd, qc, inv, diag, 2, 8)
    spread(
        here, qc, inv, qe, lambda k, c: rf_third[c - 2] if k == 2 else rf_pair[k, c - 2], lambda k: k + 3, 6
    )

    def pair(k, carry):
        for p in range(1, 5):
            apply_column(w, wr, diag, qe, ap, p, 2 * k + 4, p % 2, 0)
            apply_column(w, wr, diag, qe, ap, p, 2 * k + 5, p % 2, 1)
        return carry

    lax.fori_loop(0, 2, pair, 0)
    for y in INNER:
        fault_apply(here, qe, ap, y + 2, f2[y], ft2[y])
    tt[...] = jnp.zeros_like(tt)
    for coarse_y in range(CY // 2):
        gather(here, qc, ap, tt, coarse_y, rows_of(coarse_y, True), False)
    for y in INNER:
        gather_fault(here, inv, ap, tt, y, ft2[y])


def side(high, halo, f2, ft2, rf_pair, rf_third, work, fields, rf, band, hot):
    here = Place()
    w, wr, qe, ap, tt = work
    qc, inv, diag, fd = fields
    first = 6 if high else 0
    columns = (10, 11) if high else (0, 1)
    row, third, runs = (11, 13, (4,)) if high else (1, 0, (1, 10))

    for c in range(2):
        base = c * COLBLOCK
        w[pl.ds(4 * ROWS + row + c, 9, stride=ROWS), :] = halo[base : base + 9, :]
        w[pl.ds(PER * ROWS + row + c, 84, stride=ROWS), :] = halo[base + 9 : base + 93, :]
    at = THIRD
    for plane in range(7):
        for o in runs[-1:] if plane == 0 else runs:
            start = (plane * PER + o) * ROWS + third
            w[pl.ds(start, 3, stride=ROWS), :] = halo[at : at + 3, :]
            at += 3
    roll_weights(w, wr, 8 if high else 0, 8)

    fd[...] = jnp.zeros_like(fd)

    def put(column, k, value):
        rf[k, column - first] = value
        fd[pl.ds(here.p_fault[k] * 16 + column, 1), :] = value[5:6, :]

    for column in range(first, first + 8):
        y = column - 2
        if 0 <= y < CY:
            put(column, 0, rf_pair[0, y])
            put(column, 1, rf_pair[1, y])
            put(column, 2, rf_third[y])
    band[0:DIAGONALS, :] = halo[BAND_ROW : BAND_ROW + DIAGONALS, :]
    lists = halo[FAULT_ROW : FAULT_ROW + 12, :]
    fill_hot(hot, flat_cells(lists[0:4]), (0, 1) if high else (CY - 2, CY - 1))
    got = colour_sums(hot[...], lists[4:8], lists[8:12])
    for c, column in enumerate(columns):
        for k in range(2):
            at = SUM_ROW + (2 * c + k) * 6
            value = halo[at : at + 6, :]
            put(column, k, jnp.concatenate([value, jnp.zeros((2, NZ), f32)], axis=0))
        put(column, 2, got[:, c * NZ : (c + 1) * NZ])

    smooth(w, wr, fd, qc, inv, diag, first, 8)
    spread(
        here, qc, inv, qe, lambda k, c: rf[k, c - first], lambda k: k + (9 if high else 0), 3
    )

    def planes(k, carry):
        for odd_x in (1, 0):
            p = 2 * k + 2 - odd_x
            for y in (8, 9, 10) if high else (1, 2, 3):
                apply_column(w, wr, diag, qe, ap, p, y, odd_x, y % 2)
        return carry

    lax.fori_loop(0, 2, planes, 0)
    own = (6, 7) if high else (0, 1)
    for y in own:
        fault_apply(here, qe, ap, y + 2, f2[y], ft2[y])
    fault_apply_band(here, qe, ap, 10 if high else 1, band)
    parts = ((3, (0, 1, 2)), (2, (2,))) if high else ((0, (-1, 0, 1)), (1, (-1,)))
    for coarse_y, rows in parts:
        gather(here, qc, ap, tt, coarse_y, rows, True)
    for y in own:
        gather_fault(here, inv, ap, tt, y, ft2[y])


def finish(tt, pair, store):
    kz = lax.broadcasted_iota(jnp.int32, (512, NZ), 0)
    kout = lax.broadcasted_iota(jnp.int32, (512, NZ), 1)
    z_in = kz & 127
    is_oth = ((kz >> 7) & 1) == 1
    target = jnp.where(
        is_oth, (z_in >> 1) + jnp.where((z_in & 1) == 0, -1, 1), z_in >> 1
    )
    fits = (target == (kout & 63)) & ((kz >> 8) == (kout >> 6))
    collect = jnp.where(fits, 1.0, 0.0).astype(bf16)
    high, low = split(tt[pair].reshape(200, 512))
    got = (dot_nn(high, collect) + dot_nn(low, collect)) * 0.125
    for k in range(25):
        store(5 * k, got[8 * k : 8 * k + 5])


def core_kernel(halo, f2, ft2, rf_pair, rf_third, *refs):
    half, work, fields, rest = refs[5], refs[6:11], refs[11:15], refs[15:]

    def body(odd):
        side(not odd, halo, f2, ft2, rf_pair, rf_third, work, fields, *rest)

        def store(row, value):
            half[row : row + 5, :] = value

        finish(work[4], 0 if odd else 1, store)

    by_parity("gy", body)


def main_kernel(peers, halo, f2, ft2, rf_pair, rf_third, half, *refs):
    out, work, fields, rest = refs[5], refs[6:11], refs[11:15], refs[15:]
    halo = Masked(halo, has_other("gy", peers[1]))

    def body(odd):
        side(odd, halo, f2, ft2, rf_pair, rf_third, work, fields, *rest)
        lanes = [slice(0, NZ), slice(NZ, 2 * NZ)]

        def store(row, value):
            out[row : row + 5, 0, lanes[odd]] = value
            out[row : row + 5, 0, lanes[1 - odd]] = half[row : row + 5, :]

        finish(work[4], odd, store)

    by_parity("gy", body)


def send(value, target):
    size_x, size_y = lax.axis_size("gx"), lax.axis_size("gy")
    pairs = []
    for x in range(size_x):
        for y in range(size_y):
            to_x, to_y = target(x, y)
            pairs.append((x * size_y + y, to_x * size_y + to_y))
    return lax.ppermute(value, ("gx", "gy"), pairs)


def x_partner(x, y):
    return x ^ 1, y


def core_partner(x, y):
    return x, y ^ 1


def x_other(size_x):
    def target(x, y):
        other = x + 1 if x % 2 else x - 1
        return (other, y) if 0 <= other < size_x else core_partner(x, y)

    return target


def chip_other(size_y):
    def target(x, y):
        other = y + 1 if y % 2 else y - 1
        return (x, other) if 0 <= other < size_y else x_partner(x, y)

    return target


def x_ahead(size_x):
    return lambda x, y: ((x + 2) % size_x, y)


VMEM = pl.BlockSpec(memory_space=pltpu.VMEM)
HBM = pl.BlockSpec(memory_space=pltpu.HBM)


def params(mib):
    return pltpu.CompilerParams(vmem_limit_bytes=mib * 1024 * 1024)


def sds(*shape, dtype=f32):
    return jax.ShapeDtypeStruct(shape, dtype)


def per_device(trans, storage, fault_cells, fault_count, fault_trans):
    peers = (lax.axis_size("gx"), lax.axis_size("gy"))
    cells = send(fault_cells, x_partner)
    sources = [
        pltpu.with_memory_space_constraint(array, pltpu.HBM)
        for array in (trans, storage, fault_cells, fault_trans)
    ]
    own, plane, tile = pl.pallas_call(
        functools.partial(pack_kernel, peers),
        out_shape=(sds(224, NZ), sds(72, NZ), sds(8, NZ)),
        in_specs=[pl.BlockSpec(memory_space=pltpu.SMEM)] + [HBM] * 4,
        out_specs=(VMEM,) * 3,
        scratch_shapes=[pltpu.VMEM(array.shape, array.dtype) for array in sources]
        + [pltpu.SemaphoreType.DMA((4,))],
        compiler_params=params(16),
        name="pack",
    )(fault_count, *sources)
    joined, plane = pl.pallas_call(
        join_kernel,
        out_shape=(sds(240, NZ), sds(72, NZ)),
        in_specs=[VMEM] * 4,
        out_specs=(VMEM,) * 2,
        compiler_params=params(16),
        name="join",
    )(own, tile, plane, cells)
    rs = send(plane, x_ahead(peers[0]))
    ro = send(joined, x_other(peers[0]))
    rp = send(own, x_partner)
    pieces = sds(CY, 2 * NZ, NZ, dtype=bf16)
    f2, ft2, rf_pair, band = pl.pallas_call(
        fault_kernel,
        out_shape=(pieces, pieces, sds(2, CY, 8, NZ), sds(2, 24, NZ)),
        in_specs=[VMEM] * 2,
        out_specs=(VMEM,) * 4,
        scratch_shapes=[
            pltpu.VMEM((SLOTS, 2 * NZ), bf16),
            pltpu.VMEM((CY * NZ, SLOTS), bf16),
            pltpu.VMEM((CY * NZ, 2 * NZ), f32),
        ],
        compiler_params=params(16),
        cost_estimate=pl.CostEstimate(flops=2 * 10**9, bytes_accessed=2**21, transcendentals=0),
        name="faults",
    )(tile, cells)
    to_core, to_chip = pl.pallas_call(
        functools.partial(column_kernel, peers),
        out_shape=(sds(Y_ROWS, NZ), sds(Y_ROWS, NZ)),
        in_specs=[VMEM] * 6,
        out_specs=(VMEM,) * 2,
        compiler_params=params(16),
        name="columns",
    )(own, rp, ro, rs, band, rf_pair)
    from_chip = send(to_chip, chip_other(peers[1]))
    from_core = send(to_core, core_partner)
    work = (
        sds(7 * PER * ROWS, NZ),
        sds(7 * PER * ROWS, NZ),
        sds(6, 12, 4, 8, NZ),
        sds(4, 10, 3, 3, 8, NZ),
        sds(2, 5, 5, 8, 512),
    )
    fields = [
        pltpu.VMEM((6 * 8 * 16, NZ), f32),
        pltpu.VMEM((6 * 16, NZ), f32),
        pltpu.VMEM((6 * 16, NZ), f32),
        pltpu.VMEM((6 * 16, NZ), f32),
    ]
    *work_in, rf_third = pl.pallas_call(
        functools.partial(inner_kernel, peers),
        out_shape=work + (sds(CY, 8, NZ),),
        in_specs=[VMEM] * 7,
        out_specs=(VMEM,) * 6,
        scratch_shapes=fields + [pltpu.VMEM((CY * NZ, SLOTS), bf16)],
        compiler_params=params(16),
        cost_estimate=pl.CostEstimate(flops=4 * 10**9, bytes_accessed=2**21, transcendentals=0),
        name="inner",
    )(own, rp, ro, rs, f2, ft2, rf_pair)
    side_scratch = fields + [
        pltpu.VMEM((3, 8, 8, NZ), f32),
        pltpu.VMEM((24, NZ), f32),
        pltpu.VMEM((2 * NZ, SLOTS), bf16),
    ]
    half, *work_in = pl.pallas_call(
        core_kernel,
        out_shape=(sds(125, NZ),) + work,
        in_specs=[VMEM] * 10,
        out_specs=(VMEM,) * 6,
        scratch_shapes=side_scratch,
        input_output_aliases={5 + k: 1 + k for k in range(5)},
        compiler_params=params(16),
        cost_estimate=pl.CostEstimate(flops=2 * 10**9, bytes_accessed=2**20, transcendentals=0),
        name="core_side",
    )(from_core, f2, ft2, rf_pair, rf_third, *work_in)
    result, *_ = pl.pallas_call(
        functools.partial(main_kernel, peers),
        out_shape=(sds(125, 1, 256),) + work,
        in_specs=[VMEM] * 11,
        out_specs=(VMEM,) * 6,
        scratch_shapes=side_scratch,
        input_output_aliases={6 + k: 1 + k for k in range(5)},
        compiler_params=params(16),
        name="chip_side",
    )(from_chip, f2, ft2, rf_pair, rf_third, half, *work_in)
    return result


def solution(mesh):
    placed = (
        P(None, "gx", "gy"),
        P("gx", "gy"),
        P("gx", "gy", None),
        P("gx", "gy"),
        P("gx", "gy", None),
    )
    return jax.shard_map(
        per_device, mesh=mesh, in_specs=placed, out_specs=P(None, "gx", "gy"), check_vma=False
    )
```

```python
import functools

import jax
import jax.numpy as jnp
from jax import lax
from jax.experimental import pallas as pl
from jax.experimental.pallas import tpu as pltpu
from jax.sharding import PartitionSpec as P

NZ = 128
CY = 8
SLOTS = 512

FORWARD = (
    (0, 0, 1),
    (0, 1, -1),
    (0, 1, 0),
    (0, 1, 1),
    (1, -1, -1),
    (1, -1, 0),
    (1, -1, 1),
    (1, 0, -1),
    (1, 0, 0),
    (1, 0, 1),
    (1, 1, -1),
    (1, 1, 0),
    (1, 1, 1),
)
OFFSET = {step: k for k, step in enumerate(FORWARD)}
damping = 2.0 / 3.0

ROWS = 24
PER = 14
COLBLOCK = 93
THIRD = 2 * COLBLOCK
FAULT_ROW = 225
BAND_ROW, SUM_ROW, Y_ROWS = 237, 254, 280
REACH = 8
DIAGONALS = 2 * REACH + 1

f32 = jnp.float32
bf16 = jnp.bfloat16


def dot_nt(a, b):
    return lax.dot_general(a, b, (((1,), (1,)), ((), ())), preferred_element_type=f32)


def dot_nn(a, b):
    return lax.dot_general(a, b, (((1,), (0,)), ((), ())), preferred_element_type=f32)


def split(value):
    high = value.astype(bf16)
    return high, (value - high.astype(f32)).astype(bf16)


def pack_kernel(peers, count, *refs):
    sources, (block, plane, tile), targets, sems = refs[:4], refs[4:7], refs[7:11], refs[11]
    copies = [
        pltpu.make_async_copy(src, dst, sems.at[k])
        for k, (src, dst) in enumerate(zip(sources, targets))
    ]
    for copy in copies:
        copy.start()
    for copy in copies:
        copy.wait()
    trans, storage, cells, ftrans = targets
    last_x = lax.axis_index("gx") == peers[0] - 1
    first_y = lax.axis_index("gy") == 0
    last_y = lax.axis_index("gy") == peers[1] - 1
    depth = lax.broadcasted_iota(jnp.int32, (8, NZ), 1)
    row = lax.broadcasted_iota(jnp.int32, (8, NZ), 0)
    for x in range(2):
        for o in range(PER):
            base = (x * PER + o) * 8
            for y in range(CY):
                lanes = slice(y * NZ, (y + 1) * NZ)
                if o < 13:
                    value = trans[o, x : x + 1, lanes]
                else:
                    value = storage[x : x + 1, lanes]
                block[base + y : base + y + 1, :] = value
            if o == 13:
                continue
            step = FORWARD[o]
            keep = None
            if step[2] == 1:
                keep = depth < NZ - 1
            if step[2] == -1:
                keep = depth > 0
            if step[1] == 1:
                inside = (row < CY - 1) | jnp.logical_not(last_y)
                keep = inside if keep is None else keep & inside
            if step[1] == -1:
                inside = (row > 0) | jnp.logical_not(first_y)
                keep = inside if keep is None else keep & inside
            if step[0] == 1 and x == 1:
                inside = (row >= 0) & jnp.logical_not(last_x)
                keep = inside if keep is None else keep & inside
            if keep is not None:
                block[base : base + 8, :] = jnp.where(keep, block[base : base + 8, :], 0.0)
    live = count[0, 0]
    lane = lax.broadcasted_iota(jnp.int32, (1, NZ), 1)
    for r in range(4):
        lanes = slice(r * NZ, (r + 1) * NZ)
        tile[r : r + 1, :] = cells[0, :, lanes].astype(f32)
        tile[4 + r : 5 + r, :] = jnp.where(
            lane + r * NZ < live, ftrans[0, :, lanes], 0.0
        )
    plane[...] = block[(PER + 4) * 8 : (PER + 13) * 8, :]


def partner_rows(cells):
    return jnp.concatenate(
        [cells[0, :, r * NZ : (r + 1) * NZ] for r in range(4)], axis=0
    ).astype(f32)


def join_kernel(own, tile, plane, cells, joined, plane_out):
    plane_out[...] = plane[...]
    joined[0:224, :] = own[...]
    joined[224:232, :] = tile[...]
    joined[232:236, :] = partner_rows(cells)
    joined[236:240, :] = jnp.zeros((4, NZ), f32)


def by_parity(axis, body):
    odd = lax.rem(lax.axis_index(axis), 2)
    for k in range(2):
        pl.when(odd == k)(functools.partial(body, k))


class Masked:
    def __init__(self, ref, due):
        self.ref, self.due = ref, due

    def __getitem__(self, index):
        return jnp.where(self.due, self.ref[index], 0.0)


def has_other(axis, peers):
    at = lax.axis_index(axis)
    return jnp.where(lax.rem(at, 2) == 0, at > 0, at < peers - 1)


def column_kernel(peers, own, rp, ro, rs, band, sums, to_core, to_chip):
    ro = Masked(ro, has_other("gx", peers[0]))
    lo2 = Masked(rs, lax.axis_index("gx") >= 2)

    def fill(out, lo, hi, first, third, runs):
        for c in range(2):
            y = first + c
            base = c * COLBLOCK
            out[base : base + 9, :] = lo2[pl.ds(y, 9, stride=8), :]
            for k, ref in enumerate((lo, own, hi)):
                start = base + 9 + 28 * k
                out[start : start + 28, :] = ref[pl.ds(y, 28, stride=8), :]
        at = THIRD
        out[at : at + 3, :] = lo2[pl.ds((runs[-1] - 4) * 8 + third, 3, stride=8), :]
        at += 3
        for ref in (lo, own, hi):
            for x in range(2):
                for o in runs:
                    out[at : at + 3, :] = ref[pl.ds((x * PER + o) * 8 + third, 3, stride=8), :]
                    at += 3
        for k, start in enumerate((224, 232, 228)):
            out[FAULT_ROW + 4 * k : FAULT_ROW + 4 * k + 4, :] = ro[start : start + 4, :]
        out[BAND_ROW : BAND_ROW + DIAGONALS, :] = band[int(first > 0), 0:DIAGONALS, :]
        for c in range(2):
            for k in range(2):
                at = SUM_ROW + (2 * c + k) * 6
                out[at : at + 6, :] = sums[k, first + c, 0:6, :]
        out[SUM_ROW + 24 : Y_ROWS, :] = jnp.zeros((Y_ROWS - SUM_ROW - 24, NZ), f32)

    def for_x(odd_x):
        lo, hi = (rp, ro) if odd_x else (ro, rp)

        def for_y(odd_y):
            up, down = (to_chip, to_core) if odd_y else (to_core, to_chip)
            fill(up, lo, hi, CY - 2, CY - 3, (1, 10))
            fill(down, lo, hi, 0, 2, (4,))

        by_parity("gy", for_y)

    by_parity("gx", for_x)


def colour(z):
    half = z >> 1
    return half - 5 * ((half * 205) >> 10)


def slot_columns(rows):
    tall = jnp.transpose(jnp.concatenate(rows, axis=0))
    return [[tall[:, 4 * k + r : 4 * k + r + 1] for r in range(4)] for k in range(len(rows))]


def flat_cells(rows):
    row = jnp.concatenate([rows[r : r + 1] for r in range(4)], axis=1)
    return row.astype(jnp.int32) & 1023


def fill_far(far2, partner, live):
    lane = lax.broadcasted_iota(jnp.int32, (NZ, NZ), 1)
    for r in range(4):
        rows = slice(r * NZ, (r + 1) * NZ)
        match = (partner[r].astype(jnp.int32) & 127) == lane
        high = live[r].astype(bf16).astype(f32)
        far2[rows, 0:NZ] = jnp.where(match, high, 0.0).astype(bf16)
        far2[rows, NZ : 2 * NZ] = jnp.where(match, live[r] - high, 0.0).astype(bf16)


def flat_rows(rows):
    return jnp.concatenate([rows[r : r + 1] for r in range(4)], axis=1)


def colour_sums(hot, beyond, live):
    e16 = lax.broadcasted_iota(jnp.int32, (16, SLOTS), 0)
    tint = colour(flat_rows(beyond).astype(jnp.int32) & 127)
    live = flat_rows(live)
    high = live.astype(bf16).astype(f32)
    value = jnp.where((e16 == tint) | (e16 == 5), high, 0.0)
    value = jnp.where((e16 == tint + 8) | (e16 == 13), live - high, value)
    got = dot_nt(value.astype(bf16), hot)
    return got[:8] + got[8:]


def diagonals(hot, own, far, live):
    d24 = lax.broadcasted_iota(jnp.int32, (24, SLOTS), 0)
    step = (flat_rows(far).astype(jnp.int32) & 127) - (flat_rows(own).astype(jnp.int32) & 127)
    live = flat_rows(live)
    high = live.astype(bf16).astype(f32)
    match = step + REACH == d24
    both = [jnp.where(match, value, 0.0) for value in (high, live - high)]
    got = dot_nt(jnp.concatenate(both, axis=0).astype(bf16), hot)
    return got[:24] + got[24:]


def fill_hot(hot, cells, columns):
    z128 = lax.broadcasted_iota(jnp.int32, (NZ, SLOTS), 0)
    for k, y in enumerate(columns):
        value = jnp.where(cells == z128 + y * NZ, 1.0, 0.0)
        hot[k * NZ : (k + 1) * NZ, :] = value.astype(bf16)


def pair_matrix(both):
    z8 = lax.broadcasted_iota(jnp.int32, (8, NZ), 1)
    e8 = lax.broadcasted_iota(jnp.int32, (8, NZ), 0)
    one = jnp.where((e8 == colour(z8)) | (e8 == 5), 1.0, 0.0).astype(bf16)
    one2 = jnp.concatenate([one, one], axis=1)
    matrix = both[:, :NZ] + both[:, NZ:]
    f2 = jnp.concatenate(split(matrix), axis=0)
    ft2 = jnp.concatenate(split(jnp.transpose(matrix)), axis=0)
    return f2, ft2, dot_nn(one2, ft2), dot_nn(one2, f2)


def fill_collect(collect):
    kz = lax.broadcasted_iota(jnp.int32, (512, NZ), 0)
    kout = lax.broadcasted_iota(jnp.int32, (512, NZ), 1)
    z_in = kz & 127
    is_oth = ((kz >> 7) & 1) == 1
    target = jnp.where(
        is_oth, (z_in >> 1) + jnp.where((z_in & 1) == 0, -1, 1), z_in >> 1
    )
    fits = (target == (kout & 63)) & ((kz >> 8) == (kout >> 6))
    collect[...] = jnp.where(fits, 1.0, 0.0).astype(bf16)


def fault_kernel(tile, cells, f2, ft2, rf, band, collect, far2, hot, both):
    fill_collect(collect)
    partner, live = slot_columns([partner_rows(cells), tile[4:8, :]])
    fill_far(far2, partner, live)
    fill_hot(hot, flat_cells(tile[0:4, :]), range(CY))
    both[...] = dot_nn(hot[...], far2[...])
    for y in range(CY):
        f2[y], ft2[y], rf[0, y], rf[1, y] = pair_matrix(both[y * NZ : (y + 1) * NZ, :])
    for k, y in enumerate((0, CY - 1)):
        band[k] = diagonals(
            hot[y * NZ : (y + 1) * NZ, :], tile[0:4, :], partner_rows(cells), tile[4:8, :]
        )


def through(value, matrix2):
    rows = value.shape[0]
    high, low = split(value)
    left = jnp.concatenate(
        [jnp.concatenate([high, high], axis=1), jnp.concatenate([low, low], axis=1)], axis=0
    )
    got = dot_nn(left, matrix2)
    return got[:rows] + got[rows:]


class Place:
    def __init__(self):
        self.gx = lax.axis_index("gx")
        self.gy = lax.axis_index("gy")
        par = lax.rem(self.gx, 2)
        even = par == 0
        self.sgn = 1 - 2 * par
        self.p_own = jnp.where(even, 3, 2)
        self.p_far = jnp.where(even, 4, 1)
        self.p_third = jnp.where(even, 0, 5)
        self.p_fault = (self.p_own, self.p_far, self.p_third)
        self.x_coarse = lax.rem(self.gx, 5) + 5

    def a_of(self, d):
        return lax.rem(self.x_coarse + d, 5)

    def b_of(self, coarse_y, d):
        return lax.rem(self.gy * (CY // 2) + coarse_y + d + 5, 5)


def roll_weights(w, wr, first, count):
    for p in range(7):
        for o, step in enumerate(FORWARD):
            if step[2] == 0 or (p == 0 and o < 4):
                continue
            at = (p * PER + o) * ROWS + first
            distance = 1 if step[2] == 1 else NZ - 1
            wr[at : at + count, :] = pltpu.roll(w[at : at + count, :], distance, 1)


def smooth(w, wr, fd, qc, inv, diag, first, count):
    even_y = (lax.broadcasted_iota(jnp.int32, (count, NZ), 0) & 1) == 0
    even_z = (lax.broadcasted_iota(jnp.int32, (count, NZ), 1) & 1) == 0
    for p in range(6):
        base = p + 1

        def weight(dx, dy, dz):
            if (dx, dy, dz) in OFFSET:
                start = (base * PER + OFFSET[dx, dy, dz]) * ROWS + 1 + first
                return w[start : start + count, :]
            o = OFFSET[-dx, -dy, -dz]
            start = ((base + dx) * PER + o) * ROWS + 1 + first + dy
            return (w if dz == 0 else wr)[start : start + count, :]

        near = 1 if p % 2 == 0 else -1
        sums = {}
        for dz in (-1, 0, 1):
            got = {}
            for dx in (-1, 0, 1):
                below, above = weight(dx, -1, dz), weight(dx, 1, dz)
                got[dx, 0] = jnp.where(even_y, above, below)
                if (dx, dz) != (0, 0):
                    got[dx, 0] = got[dx, 0] + weight(dx, 0, dz)
                got[dx, 1] = jnp.where(even_y, below, above)
            for sy in range(2):
                sums[0, sy, dz] = got[0, sy] + got[near, sy]
                sums[1, sy, dz] = got[-near, sy]
        start = (base * PER + 13) * ROWS + 1 + first
        at = p * 16 + first
        total = w[start : start + count, :] + fd[at : at + count, :]
        r = []
        for sx in range(2):
            for sy in range(2):
                down, same, up = (sums[sx, sy, dz] for dz in (-1, 0, 1))
                r.append(same + jnp.where(even_z, up, down))
                r.append(jnp.where(even_z, down, up))
        for value in r:
            total = total + value
        total = jnp.where(total == 0.0, 1.0, total)
        scale = damping / total
        diag[at : at + count, :] = total
        inv[at : at + count, :] = scale
        for k, value in enumerate(r):
            value = value * scale
            if k == 0:
                value = value + (1.0 - damping)
            at = (p * 8 + k) * 16 + first
            qc[at : at + count, :] = value


def spread(here, qc, inv, qe, rf_at, columns):
    z8 = lax.broadcasted_iota(jnp.int32, (8, NZ), 1)
    e8 = lax.broadcasted_iota(jnp.int32, (8, NZ), 0)
    beside = jnp.where((z8 & 1) == 0, z8 - 1, z8 + 1)
    mask_own = jnp.where(e8 == colour(z8), 1.0, 0.0)
    mask_oth = jnp.where(e8 == colour(beside + 10), 1.0, 0.0)
    rows5 = jnp.where(e8 < 5, 1.0, 0.0)

    for c in columns:
        for p in range(6):
            for lat in range(4):
                at = (p * 8 + 2 * lat) * 16 + c
                qe[p, c, lat] = qc[at : at + 1, :] * mask_own + qc[at + 16 : at + 17, :] * mask_oth
        for k, plane in enumerate(here.p_fault):
            qe[plane, c, 2] = qe[plane, c, 2] + rf_at(k, c) * (
                inv[pl.ds(plane * 16 + c, 1), :] * rows5
            )


def apply_column(w, wr, diag, qe, ap, p, y):
    odd_x, odd_y = p % 2, y % 2
    acc = {}
    for dx in (-1, 0, 1):
        for dy in (-1, 0, 1):
            q = [qe[p + dx, y + dy, lat] for lat in range(4)]
            own_x = dx if (dx == 1 and odd_x) or (dx == -1 and not odd_x) else 0
            own_y = dy if (dy == 1 and odd_y) or (dy == -1 and not odd_y) else 0
            oth_x = own_x + (1 if (odd_x + dx) % 2 else -1)
            oth_y = own_y + (1 if (odd_y + dy) % 2 else -1)
            for dz in (-1, 0, 1):
                if (dx, dy, dz) == (0, 0, 0):
                    continue
                if (dx, dy, dz) in OFFSET:
                    at = ((p + 1) * PER + OFFSET[dx, dy, dz]) * ROWS + y + 1
                    ref = w if dz == 0 else wr
                else:
                    at = ((p + 1 + dx) * PER + OFFSET[-dx, -dy, -dz]) * ROWS + y + 1 + dy
                    ref = w
                wt = ref[at : at + 1, :]
                for lat in range(4):
                    lx = oth_x if lat >= 2 else own_x
                    ly = oth_y if lat % 2 else own_y
                    value = wt * q[lat]
                    key = (lx, ly, dz)
                    acc[key] = acc[key] + value if key in acc else value
    centre = diag[p * 16 + y : p * 16 + y + 1, :]
    for lx in (-1, 0, 1):
        for ly in (-1, 0, 1):
            total = acc[lx, ly, 0]
            total = total + pltpu.roll(acc[lx, ly, 1], NZ - 1, 1)
            total = total + pltpu.roll(acc[lx, ly, -1], 1, 1)
            own_lat = None
            sx = {0: 0, (1 if odd_x else -1): 1}.get(lx)
            sy = {0: 0, (1 if odd_y else -1): 1}.get(ly)
            if sx is not None and sy is not None:
                own_lat = 2 * sx + sy
            if own_lat is None:
                total = -total
            else:
                total = centre * qe[p, y, own_lat] - total
            ap[p - 1, y - 1, lx + 1, ly + 1] = total


def fault_apply(here, qe, ap, c, f2c, ft2c):
    ly_oth = 2 * (c % 2)
    for plane, source, x_own, matrix in (
        (here.p_own, here.p_far, 1 + here.sgn, ft2c),
        (here.p_far, here.p_own, 1 - here.sgn, f2c),
    ):
        total = through(qe[source, c].reshape(32, NZ), matrix)
        for lat in range(4):
            lx = 1 if lat >= 2 else x_own
            ly = ly_oth if lat % 2 else 1
            ap[plane - 1, c - 1, lx, ly] = ap[plane - 1, c - 1, lx, ly] - total[8 * lat : 8 * lat + 8]


def fault_apply_band(here, qe, ap, c, band):
    ly_oth = 2 * (c % 2)
    to_own, to_far = [0.0] * 4, [0.0] * 4
    for d in range(DIAGONALS):
        weight = band[d : d + 1, :]
        for lat in range(4):
            ahead = pltpu.roll(qe[here.p_far, c, lat], (REACH - d) % NZ, 1)
            to_own[lat] = to_own[lat] + weight * ahead
            back = weight * qe[here.p_own, c, lat]
            to_far[lat] = to_far[lat] + pltpu.roll(back, (d - REACH) % NZ, 1)
    for plane, x_own, total in (
        (here.p_own, 1 + here.sgn, to_own),
        (here.p_far, 1 - here.sgn, to_far),
    ):
        for lat in range(4):
            lx = 1 if lat >= 2 else x_own
            ly = ly_oth if lat % 2 else 1
            ap[plane - 1, c - 1, lx, ly] = ap[plane - 1, c - 1, lx, ly] - total[lat]


def gather(here, qc, ap, tt, coarse_y, rows, add):
    shift = (-1, 0, 0, 1)
    for zk in range(2):
        acc = {}
        for x in range(-1, 3):
            for y in rows:
                lat = 2 * (x not in (0, 1)) + (y not in (0, 1))
                c = 2 * coarse_y + y + 2
                at = ((x + 2) * 8 + 2 * lat + zk) * 16 + c
                q = qc[at : at + 1, :]
                for lx in range(3):
                    for ly in range(3):
                        value = q * ap[x + 1, c - 1, lx, ly]
                        key = (shift[x + 1] + lx - 1, shift[y + 1] + ly - 1)
                        acc[key] = acc[key] + value if key in acc else value
        lane = (coarse_y % 2) * 256 + zk * NZ
        for (dx, dy), value in acc.items():
            at = (coarse_y // 2, here.a_of(dx), here.b_of(coarse_y, dy), slice(None), slice(lane, lane + NZ))
            tt[at] = tt[at] + value if add else value


def gather_fault(here, inv, ap, tt, y, ft2c):
    c = y + 2
    coarse_y = y // 2
    lane = (coarse_y % 2) * 256
    value = ap[here.p_far - 1, c - 1].reshape(72, NZ) * inv[pl.ds(here.p_far * 16 + c, 1), :]
    total = through(value, ft2c)
    for lx in range(3):
        a = here.a_of(lx - 1 + here.sgn)
        for ly in range(3):
            at = (coarse_y // 2, a, here.b_of(coarse_y, ly - 1), slice(None), slice(lane, lane + NZ))
            row = 8 * (3 * lx + ly)
            tt[at] = tt[at] + total[row : row + 8]


INNER = (2, 3, 4, 5)


def rows_of(coarse_y, inner):
    return [y for y in range(-1, 3) if (2 * coarse_y + y in INNER) == inner]


def inner_kernel(
    peers, own, rp, ro, rs, f2, ft2, rf_pair, w, wr, qe, ap, tt, rf_third, qc, inv, diag, fd, hot
):
    here = Place()
    ro = Masked(ro, has_other("gx", peers[0]))

    def place(ref, count, first):
        for k in range(count):
            base = (first + k) * ROWS
            w[base + 3 : base + 11, :] = ref[8 * k : 8 * k + 8, :]

    def place_x(odd):
        lo, hi = (rp, ro) if odd else (ro, rp)
        place(lo, 28, PER)
        place(hi, 28, 5 * PER)

    by_parity("gx", place_x)
    place(Masked(rs, here.gx >= 2), 9, 4)
    place(own, 28, 3 * PER)

    fill_hot(hot, flat_cells(ro[224:228, :]), range(CY))
    got = colour_sums(hot[...], ro[232:236, :], ro[228:232, :])
    fd[...] = jnp.zeros_like(fd)
    for y in range(CY):
        rf_third[y] = got[:, y * NZ : (y + 1) * NZ]
        for plane, value in zip(here.p_fault, (rf_pair[0, y], rf_pair[1, y], rf_third[y])):
            fd[pl.ds(plane * 16 + y + 2, 1), :] = value[5:6, :]

    roll_weights(w, wr, 3, 8)
    smooth(w, wr, fd, qc, inv, diag, 2, 8)
    spread(
        here, qc, inv, qe, lambda k, c: rf_third[c - 2] if k == 2 else rf_pair[k, c - 2], range(3, 9)
    )
    for p in range(1, 5):
        for y in INNER:
            apply_column(w, wr, diag, qe, ap, p, y + 2)
    for y in INNER:
        fault_apply(here, qe, ap, y + 2, f2[y], ft2[y])
    tt[...] = jnp.zeros_like(tt)
    for coarse_y in range(CY // 2):
        gather(here, qc, ap, tt, coarse_y, rows_of(coarse_y, True), False)
    for y in INNER:
        gather_fault(here, inv, ap, tt, y, ft2[y])


def side(high, halo, f2, ft2, rf_pair, rf_third, work, fields, rf, band, hot):
    here = Place()
    w, wr, qe, ap, tt = work
    qc, inv, diag, fd = fields
    first = 6 if high else 0
    columns = (10, 11) if high else (0, 1)
    row, third, runs = (11, 13, (4,)) if high else (1, 0, (1, 10))

    for c in range(2):
        base = c * COLBLOCK
        w[pl.ds(4 * ROWS + row + c, 9, stride=ROWS), :] = halo[base : base + 9, :]
        w[pl.ds(PER * ROWS + row + c, 84, stride=ROWS), :] = halo[base + 9 : base + 93, :]
    at = THIRD
    for plane in range(7):
        for o in runs[-1:] if plane == 0 else runs:
            start = (plane * PER + o) * ROWS + third
            w[pl.ds(start, 3, stride=ROWS), :] = halo[at : at + 3, :]
            at += 3
    roll_weights(w, wr, 8 if high else 0, 8)

    fd[...] = jnp.zeros_like(fd)

    def put(column, k, value):
        rf[k, column - first] = value
        fd[pl.ds(here.p_fault[k] * 16 + column, 1), :] = value[5:6, :]

    own = (6, 7) if high else (0, 1)
    for y in own:
        put(y + 2, 0, rf_pair[0, y])
        put(y + 2, 1, rf_pair[1, y])
        put(y + 2, 2, rf_third[y])
    band[0:DIAGONALS, :] = halo[BAND_ROW : BAND_ROW + DIAGONALS, :]
    lists = halo[FAULT_ROW : FAULT_ROW + 12, :]
    fill_hot(hot, flat_cells(lists[0:4]), (0, 1) if high else (CY - 2, CY - 1))
    got = colour_sums(hot[...], lists[4:8], lists[8:12])
    for c, column in enumerate(columns):
        for k in range(2):
            at = SUM_ROW + (2 * c + k) * 6
            value = halo[at : at + 6, :]
            put(column, k, jnp.concatenate([value, jnp.zeros((2, NZ), f32)], axis=0))
        put(column, 2, got[:, c * NZ : (c + 1) * NZ])

    smooth(w, wr, fd, qc, inv, diag, first, 8)
    spread(
        here, qc, inv, qe, lambda k, c: rf[k, c - first], (9, 10, 11) if high else (0, 1, 2)
    )
    for p in range(1, 5):
        for y in (8, 9, 10) if high else (1, 2, 3):
            apply_column(w, wr, diag, qe, ap, p, y)
    for y in own:
        fault_apply(here, qe, ap, y + 2, f2[y], ft2[y])
    fault_apply_band(here, qe, ap, 10 if high else 1, band)
    parts = ((3, (0, 1, 2)), (2, (2,))) if high else ((0, (-1, 0, 1)), (1, (-1,)))
    for coarse_y, rows in parts:
        gather(here, qc, ap, tt, coarse_y, rows, True)
    for y in own:
        gather_fault(here, inv, ap, tt, y, ft2[y])


def finish(tt, pair, collect, store):
    high, low = split(tt[pair].reshape(200, 512))
    got = (dot_nn(high, collect[...]) + dot_nn(low, collect[...])) * 0.125
    for k in range(25):
        store(5 * k, got[8 * k : 8 * k + 5])


def core_kernel(halo, f2, ft2, rf_pair, rf_third, collect, *refs):
    half, work, fields, rest = refs[5], refs[6:11], refs[11:15], refs[15:]

    def body(odd):
        side(not odd, halo, f2, ft2, rf_pair, rf_third, work, fields, *rest)

        def store(row, value):
            half[row : row + 5, :] = value

        finish(work[4], 0 if odd else 1, collect, store)

    by_parity("gy", body)


def main_kernel(peers, halo, f2, ft2, rf_pair, rf_third, collect, half, *refs):
    out, work, fields, rest = refs[5], refs[6:11], refs[11:15], refs[15:]
    halo = Masked(halo, has_other("gy", peers[1]))

    def body(odd):
        side(odd, halo, f2, ft2, rf_pair, rf_third, work, fields, *rest)
        lanes = [slice(0, NZ), slice(NZ, 2 * NZ)]

        def store(row, value):
            out[row : row + 5, 0, lanes[odd]] = value
            out[row : row + 5, 0, lanes[1 - odd]] = half[row : row + 5, :]

        finish(work[4], odd, collect, store)

    by_parity("gy", body)


def send(value, target):
    size_x, size_y = lax.axis_size("gx"), lax.axis_size("gy")
    pairs = []
    for x in range(size_x):
        for y in range(size_y):
            to_x, to_y = target(x, y)
            pairs.append((x * size_y + y, to_x * size_y + to_y))
    return lax.ppermute(value, ("gx", "gy"), pairs)


def x_partner(x, y):
    return x ^ 1, y


def core_partner(x, y):
    return x, y ^ 1


def x_other(size_x):
    def target(x, y):
        other = x + 1 if x % 2 else x - 1
        return (other, y) if 0 <= other < size_x else core_partner(x, y)

    return target


def chip_other(size_y):
    def target(x, y):
        other = y + 1 if y % 2 else y - 1
        return (x, other) if 0 <= other < size_y else x_partner(x, y)

    return target


def x_ahead(size_x):
    return lambda x, y: ((x + 2) % size_x, y)


VMEM = pl.BlockSpec(memory_space=pltpu.VMEM)
HBM = pl.BlockSpec(memory_space=pltpu.HBM)


def params(mib):
    return pltpu.CompilerParams(vmem_limit_bytes=mib * 1024 * 1024)


def sds(*shape, dtype=f32):
    return jax.ShapeDtypeStruct(shape, dtype)


def per_device(trans, storage, fault_cells, fault_count, fault_trans):
    peers = (lax.axis_size("gx"), lax.axis_size("gy"))
    cells = send(fault_cells, x_partner)
    sources = [
        pltpu.with_memory_space_constraint(array, pltpu.HBM)
        for array in (trans, storage, fault_cells, fault_trans)
    ]
    own, plane, tile = pl.pallas_call(
        functools.partial(pack_kernel, peers),
        out_shape=(sds(224, NZ), sds(72, NZ), sds(8, NZ)),
        in_specs=[pl.BlockSpec(memory_space=pltpu.SMEM)] + [HBM] * 4,
        out_specs=(VMEM,) * 3,
        scratch_shapes=[pltpu.VMEM(array.shape, array.dtype) for array in sources]
        + [pltpu.SemaphoreType.DMA((4,))],
        compiler_params=params(16),
        name="pack",
    )(fault_count, *sources)
    joined, plane = pl.pallas_call(
        join_kernel,
        out_shape=(sds(240, NZ), sds(72, NZ)),
        in_specs=[VMEM] * 4,
        out_specs=(VMEM,) * 2,
        compiler_params=params(16),
        name="join",
    )(own, tile, plane, cells)
    rs = send(plane, x_ahead(peers[0]))
    ro = send(joined, x_other(peers[0]))
    rp = send(own, x_partner)
    pieces = sds(CY, 2 * NZ, NZ, dtype=bf16)
    f2, ft2, rf_pair, band, collect = pl.pallas_call(
        fault_kernel,
        out_shape=(
            pieces,
            pieces,
            sds(2, CY, 8, NZ),
            sds(2, 24, NZ),
            sds(512, NZ, dtype=bf16),
        ),
        in_specs=[VMEM] * 2,
        out_specs=(VMEM,) * 5,
        scratch_shapes=[
            pltpu.VMEM((SLOTS, 2 * NZ), bf16),
            pltpu.VMEM((CY * NZ, SLOTS), bf16),
            pltpu.VMEM((CY * NZ, 2 * NZ), f32),
        ],
        compiler_params=params(16),
        cost_estimate=pl.CostEstimate(flops=2 * 10**9, bytes_accessed=2**21, transcendentals=0),
        name="faults",
    )(tile, cells)
    to_core, to_chip = pl.pallas_call(
        functools.partial(column_kernel, peers),
        out_shape=(sds(Y_ROWS, NZ), sds(Y_ROWS, NZ)),
        in_specs=[VMEM] * 6,
        out_specs=(VMEM,) * 2,
        compiler_params=params(16),
        name="columns",
    )(own, rp, ro, rs, band, rf_pair)
    from_chip = send(to_chip, chip_other(peers[1]))
    from_core = send(to_core, core_partner)
    work = (
        sds(7 * PER * ROWS, NZ),
        sds(7 * PER * ROWS, NZ),
        sds(6, 12, 4, 8, NZ),
        sds(4, 10, 3, 3, 8, NZ),
        sds(2, 5, 5, 8, 512),
    )
    fields = [
        pltpu.VMEM((6 * 8 * 16, NZ), f32),
        pltpu.VMEM((6 * 16, NZ), f32),
        pltpu.VMEM((6 * 16, NZ), f32),
        pltpu.VMEM((6 * 16, NZ), f32),
    ]
    *work_in, rf_third = pl.pallas_call(
        functools.partial(inner_kernel, peers),
        out_shape=work + (sds(CY, 8, NZ),),
        in_specs=[VMEM] * 7,
        out_specs=(VMEM,) * 6,
        scratch_shapes=fields + [pltpu.VMEM((CY * NZ, SLOTS), bf16)],
        compiler_params=params(16),
        cost_estimate=pl.CostEstimate(flops=4 * 10**9, bytes_accessed=2**21, transcendentals=0),
        name="inner",
    )(own, rp, ro, rs, f2, ft2, rf_pair)
    side_scratch = fields + [
        pltpu.VMEM((3, 8, 8, NZ), f32),
        pltpu.VMEM((24, NZ), f32),
        pltpu.VMEM((2 * NZ, SLOTS), bf16),
    ]
    half, *work_in = pl.pallas_call(
        core_kernel,
        out_shape=(sds(125, NZ),) + work,
        in_specs=[VMEM] * 11,
        out_specs=(VMEM,) * 6,
        scratch_shapes=side_scratch,
        input_output_aliases={6 + k: 1 + k for k in range(5)},
        compiler_params=params(16),
        cost_estimate=pl.CostEstimate(flops=2 * 10**9, bytes_accessed=2**20, transcendentals=0),
        name="core_side",
    )(from_core, f2, ft2, rf_pair, rf_third, collect, *work_in)
    result, *_ = pl.pallas_call(
        functools.partial(main_kernel, peers),
        out_shape=(sds(125, 1, 256),) + work,
        in_specs=[VMEM] * 12,
        out_specs=(VMEM,) * 6,
        scratch_shapes=side_scratch,
        input_output_aliases={7 + k: 1 + k for k in range(5)},
        compiler_params=params(16),
        name="chip_side",
    )(from_chip, f2, ft2, rf_pair, rf_third, collect, half, *work_in)
    return result


def solution(mesh):
    placed = (
        P(None, "gx", "gy"),
        P("gx", "gy"),
        P("gx", "gy", None),
        P("gx", "gy"),
        P("gx", "gy", None),
    )
    return jax.shard_map(
        per_device, mesh=mesh, in_specs=placed, out_specs=P(None, "gx", "gy"), check_vma=False
    )
```

```python
import functools

import jax
import jax.numpy as jnp
from jax import lax
from jax.experimental import pallas as pl
from jax.experimental.pallas import tpu as pltpu
from jax.sharding import PartitionSpec as P

NZ = 128
CY = 8
SLOTS = 512

FORWARD = (
    (0, 0, 1),
    (0, 1, -1),
    (0, 1, 0),
    (0, 1, 1),
    (1, -1, -1),
    (1, -1, 0),
    (1, -1, 1),
    (1, 0, -1),
    (1, 0, 0),
    (1, 0, 1),
    (1, 1, -1),
    (1, 1, 0),
    (1, 1, 1),
)
OFFSET = {step: k for k, step in enumerate(FORWARD)}
damping = 2.0 / 3.0

ROWS = 24
PER = 14
COLBLOCK = 93
THIRD = 2 * COLBLOCK
FAULT_ROW = 225
BAND_ROW, SUM_ROW, Y_ROWS = 237, 254, 280
REACH = 8
DIAGONALS = 2 * REACH + 1

f32 = jnp.float32
bf16 = jnp.bfloat16


def dot_nt(a, b):
    return lax.dot_general(a, b, (((1,), (1,)), ((), ())), preferred_element_type=f32)


def dot_nn(a, b):
    return lax.dot_general(a, b, (((1,), (0,)), ((), ())), preferred_element_type=f32)


def split(value):
    high = value.astype(bf16)
    return high, (value - high.astype(f32)).astype(bf16)


def pack_kernel(peers, count, *refs):
    sources, (block, plane, tile), targets, sems = refs[:4], refs[4:7], refs[7:11], refs[11]
    copies = [
        pltpu.make_async_copy(src, dst, sems.at[k])
        for k, (src, dst) in enumerate(zip(sources, targets))
    ]
    for copy in copies:
        copy.start()
    for copy in copies:
        copy.wait()
    trans, storage, cells, ftrans = targets
    last_x = lax.axis_index("gx") == peers[0] - 1
    first_y = lax.axis_index("gy") == 0
    last_y = lax.axis_index("gy") == peers[1] - 1
    depth = lax.broadcasted_iota(jnp.int32, (8, NZ), 1)
    row = lax.broadcasted_iota(jnp.int32, (8, NZ), 0)
    for x in range(2):
        for o in range(PER):
            base = (x * PER + o) * 8
            for y in range(CY):
                lanes = slice(y * NZ, (y + 1) * NZ)
                if o < 13:
                    value = trans[o, x : x + 1, lanes]
                else:
                    value = storage[x : x + 1, lanes]
                block[base + y : base + y + 1, :] = value
            if o == 13:
                continue
            step = FORWARD[o]
            keep = None
            if step[2] == 1:
                keep = depth < NZ - 1
            if step[2] == -1:
                keep = depth > 0
            if step[1] == 1:
                inside = (row < CY - 1) | jnp.logical_not(last_y)
                keep = inside if keep is None else keep & inside
            if step[1] == -1:
                inside = (row > 0) | jnp.logical_not(first_y)
                keep = inside if keep is None else keep & inside
            if step[0] == 1 and x == 1:
                inside = (row >= 0) & jnp.logical_not(last_x)
                keep = inside if keep is None else keep & inside
            if keep is not None:
                block[base : base + 8, :] = jnp.where(keep, block[base : base + 8, :], 0.0)
    live = count[0, 0]
    lane = lax.broadcasted_iota(jnp.int32, (1, NZ), 1)
    for r in range(4):
        lanes = slice(r * NZ, (r + 1) * NZ)
        tile[r : r + 1, :] = cells[0, :, lanes].astype(f32)
        tile[4 + r : 5 + r, :] = jnp.where(
            lane + r * NZ < live, ftrans[0, :, lanes], 0.0
        )
    plane[...] = block[(PER + 4) * 8 : (PER + 13) * 8, :]


def partner_rows(cells):
    return jnp.concatenate(
        [cells[0, :, r * NZ : (r + 1) * NZ] for r in range(4)], axis=0
    ).astype(f32)


def join_kernel(own, tile, plane, cells, joined, plane_out):
    plane_out[...] = plane[...]
    joined[0:224, :] = own[...]
    joined[224:232, :] = tile[...]
    joined[232:236, :] = partner_rows(cells)
    joined[236:240, :] = jnp.zeros((4, NZ), f32)


def by_parity(axis, body):
    odd = lax.rem(lax.axis_index(axis), 2)
    for k in range(2):
        pl.when(odd == k)(functools.partial(body, k))


class Masked:
    def __init__(self, ref, due):
        self.ref, self.due = ref, due

    def __getitem__(self, index):
        return jnp.where(self.due, self.ref[index], 0.0)


def has_other(axis, peers):
    at = lax.axis_index(axis)
    return jnp.where(lax.rem(at, 2) == 0, at > 0, at < peers - 1)


def column_kernel(peers, own, rp, ro, rs, band, sums, after, to_core, to_chip):
    del after
    ro = Masked(ro, has_other("gx", peers[0]))
    lo2 = Masked(rs, lax.axis_index("gx") >= 2)

    def fill(out, lo, hi, first, third, runs):
        for c in range(2):
            y = first + c
            base = c * COLBLOCK
            out[base : base + 9, :] = lo2[pl.ds(y, 9, stride=8), :]
            for k, ref in enumerate((lo, own, hi)):
                start = base + 9 + 28 * k
                out[start : start + 28, :] = ref[pl.ds(y, 28, stride=8), :]
        at = THIRD
        out[at : at + 3, :] = lo2[pl.ds((runs[-1] - 4) * 8 + third, 3, stride=8), :]
        at += 3
        for ref in (lo, own, hi):
            for x in range(2):
                for o in runs:
                    out[at : at + 3, :] = ref[pl.ds((x * PER + o) * 8 + third, 3, stride=8), :]
                    at += 3
        for k, start in enumerate((224, 232, 228)):
            out[FAULT_ROW + 4 * k : FAULT_ROW + 4 * k + 4, :] = ro[start : start + 4, :]
        out[BAND_ROW : BAND_ROW + DIAGONALS, :] = band[int(first > 0), 0:DIAGONALS, :]
        for c in range(2):
            for k in range(2):
                at = SUM_ROW + (2 * c + k) * 6
                out[at : at + 6, :] = sums[k, first + c, 0:6, :]
        out[SUM_ROW + 24 : Y_ROWS, :] = jnp.zeros((Y_ROWS - SUM_ROW - 24, NZ), f32)

    def for_x(odd_x):
        lo, hi = (rp, ro) if odd_x else (ro, rp)

        def for_y(odd_y):
            up, down = (to_chip, to_core) if odd_y else (to_core, to_chip)
            fill(up, lo, hi, CY - 2, CY - 3, (1, 10))
            fill(down, lo, hi, 0, 2, (4,))

        by_parity("gy", for_y)

    by_parity("gx", for_x)


def colour(z):
    half = z >> 1
    return half - 5 * ((half * 205) >> 10)


def slot_columns(rows):
    tall = jnp.transpose(jnp.concatenate(rows, axis=0))
    return [[tall[:, 4 * k + r : 4 * k + r + 1] for r in range(4)] for k in range(len(rows))]


def flat_cells(rows):
    row = jnp.concatenate([rows[r : r + 1] for r in range(4)], axis=1)
    return row.astype(jnp.int32) & 1023


def fill_far(far2, partner, live):
    lane = lax.broadcasted_iota(jnp.int32, (NZ, NZ), 1)
    for r in range(4):
        rows = slice(r * NZ, (r + 1) * NZ)
        match = (partner[r].astype(jnp.int32) & 127) == lane
        high = live[r].astype(bf16).astype(f32)
        far2[rows, 0:NZ] = jnp.where(match, high, 0.0).astype(bf16)
        far2[rows, NZ : 2 * NZ] = jnp.where(match, live[r] - high, 0.0).astype(bf16)


def flat_rows(rows):
    return jnp.concatenate([rows[r : r + 1] for r in range(4)], axis=1)


def colour_sums(hot, beyond, live):
    e16 = lax.broadcasted_iota(jnp.int32, (16, SLOTS), 0)
    tint = colour(flat_rows(beyond).astype(jnp.int32) & 127)
    live = flat_rows(live)
    high = live.astype(bf16).astype(f32)
    value = jnp.where((e16 == tint) | (e16 == 5), high, 0.0)
    value = jnp.where((e16 == tint + 8) | (e16 == 13), live - high, value)
    got = dot_nt(value.astype(bf16), hot)
    return got[:8] + got[8:]


def diagonals(hot, own, far, live):
    d24 = lax.broadcasted_iota(jnp.int32, (24, SLOTS), 0)
    step = (flat_rows(far).astype(jnp.int32) & 127) - (flat_rows(own).astype(jnp.int32) & 127)
    live = flat_rows(live)
    high = live.astype(bf16).astype(f32)
    match = step + REACH == d24
    both = [jnp.where(match, value, 0.0) for value in (high, live - high)]
    got = dot_nt(jnp.concatenate(both, axis=0).astype(bf16), hot)
    return got[:24] + got[24:]


def fill_hot(hot, cells, columns):
    z128 = lax.broadcasted_iota(jnp.int32, (NZ, SLOTS), 0)
    for k, y in enumerate(columns):
        value = jnp.where(cells == z128 + y * NZ, 1.0, 0.0)
        hot[k * NZ : (k + 1) * NZ, :] = value.astype(bf16)


def pair_matrix(both):
    z8 = lax.broadcasted_iota(jnp.int32, (8, NZ), 1)
    e8 = lax.broadcasted_iota(jnp.int32, (8, NZ), 0)
    one = jnp.where((e8 == colour(z8)) | (e8 == 5), 1.0, 0.0).astype(bf16)
    one2 = jnp.concatenate([one, one], axis=1)
    matrix = both[:, :NZ] + both[:, NZ:]
    f2 = jnp.concatenate(split(matrix), axis=0)
    ft2 = jnp.concatenate(split(jnp.transpose(matrix)), axis=0)
    return f2, ft2, dot_nn(one2, ft2), dot_nn(one2, f2)


def fill_collect(collect):
    kz = lax.broadcasted_iota(jnp.int32, (512, NZ), 0)
    kout = lax.broadcasted_iota(jnp.int32, (512, NZ), 1)
    z_in = kz & 127
    is_oth = ((kz >> 7) & 1) == 1
    target = jnp.where(
        is_oth, (z_in >> 1) + jnp.where((z_in & 1) == 0, -1, 1), z_in >> 1
    )
    fits = (target == (kout & 63)) & ((kz >> 8) == (kout >> 6))
    collect[...] = jnp.where(fits, 1.0, 0.0).astype(bf16)


def fault_kernel(tile, cells, f2, ft2, rf, band, collect, far2, hot, both):
    fill_collect(collect)
    partner, live = slot_columns([partner_rows(cells), tile[4:8, :]])
    fill_far(far2, partner, live)
    fill_hot(hot, flat_cells(tile[0:4, :]), range(CY))
    both[...] = dot_nn(hot[...], far2[...])
    for y in range(CY):
        f2[y], ft2[y], rf[0, y], rf[1, y] = pair_matrix(both[y * NZ : (y + 1) * NZ, :])
    for k, y in enumerate((0, CY - 1)):
        band[k] = diagonals(
            hot[y * NZ : (y + 1) * NZ, :], tile[0:4, :], partner_rows(cells), tile[4:8, :]
        )


def through(value, matrix2):
    rows = value.shape[0]
    high, low = split(value)
    left = jnp.concatenate(
        [jnp.concatenate([high, high], axis=1), jnp.concatenate([low, low], axis=1)], axis=0
    )
    got = dot_nn(left, matrix2)
    return got[:rows] + got[rows:]


class Place:
    def __init__(self):
        self.gx = lax.axis_index("gx")
        self.gy = lax.axis_index("gy")
        par = lax.rem(self.gx, 2)
        even = par == 0
        self.sgn = 1 - 2 * par
        self.p_own = jnp.where(even, 3, 2)
        self.p_far = jnp.where(even, 4, 1)
        self.p_third = jnp.where(even, 0, 5)
        self.p_fault = (self.p_own, self.p_far, self.p_third)
        self.x_coarse = lax.rem(self.gx, 5) + 5

    def a_of(self, d):
        return lax.rem(self.x_coarse + d, 5)

    def b_of(self, coarse_y, d):
        return lax.rem(self.gy * (CY // 2) + coarse_y + d + 5, 5)


def roll_weights(w, wr, first, count):
    for p in range(7):
        for o, step in enumerate(FORWARD):
            if step[2] == 0 or (p == 0 and o < 4):
                continue
            at = (p * PER + o) * ROWS + first
            distance = 1 if step[2] == 1 else NZ - 1
            wr[at : at + count, :] = pltpu.roll(w[at : at + count, :], distance, 1)


def smooth(w, wr, fd, qc, inv, diag, first, count):
    even_y = (lax.broadcasted_iota(jnp.int32, (count, NZ), 0) & 1) == 0
    even_z = (lax.broadcasted_iota(jnp.int32, (count, NZ), 1) & 1) == 0
    for p in range(6):
        base = p + 1

        def weight(dx, dy, dz):
            if (dx, dy, dz) in OFFSET:
                start = (base * PER + OFFSET[dx, dy, dz]) * ROWS + 1 + first
                return w[start : start + count, :]
            o = OFFSET[-dx, -dy, -dz]
            start = ((base + dx) * PER + o) * ROWS + 1 + first + dy
            return (w if dz == 0 else wr)[start : start + count, :]

        near = 1 if p % 2 == 0 else -1
        sums = {}
        for dz in (-1, 0, 1):
            got = {}
            for dx in (-1, 0, 1):
                below, above = weight(dx, -1, dz), weight(dx, 1, dz)
                got[dx, 0] = jnp.where(even_y, above, below)
                if (dx, dz) != (0, 0):
                    got[dx, 0] = got[dx, 0] + weight(dx, 0, dz)
                got[dx, 1] = jnp.where(even_y, below, above)
            for sy in range(2):
                sums[0, sy, dz] = got[0, sy] + got[near, sy]
                sums[1, sy, dz] = got[-near, sy]
        start = (base * PER + 13) * ROWS + 1 + first
        at = p * 16 + first
        total = w[start : start + count, :] + fd[at : at + count, :]
        r = []
        for sx in range(2):
            for sy in range(2):
                down, same, up = (sums[sx, sy, dz] for dz in (-1, 0, 1))
                r.append(same + jnp.where(even_z, up, down))
                r.append(jnp.where(even_z, down, up))
        for value in r:
            total = total + value
        total = jnp.where(total == 0.0, 1.0, total)
        scale = damping / total
        diag[at : at + count, :] = total
        inv[at : at + count, :] = scale
        for k, value in enumerate(r):
            value = value * scale
            if k == 0:
                value = value + (1.0 - damping)
            at = (p * 8 + k) * 16 + first
            qc[at : at + count, :] = value


def spread(here, qc, inv, qe, rf_at, columns):
    z8 = lax.broadcasted_iota(jnp.int32, (8, NZ), 1)
    e8 = lax.broadcasted_iota(jnp.int32, (8, NZ), 0)
    beside = jnp.where((z8 & 1) == 0, z8 - 1, z8 + 1)
    mask_own = jnp.where(e8 == colour(z8), 1.0, 0.0)
    mask_oth = jnp.where(e8 == colour(beside + 10), 1.0, 0.0)
    rows5 = jnp.where(e8 < 5, 1.0, 0.0)

    for c in columns:
        for p in range(6):
            for lat in range(4):
                at = (p * 8 + 2 * lat) * 16 + c
                qe[p, c, lat] = qc[at : at + 1, :] * mask_own + qc[at + 16 : at + 17, :] * mask_oth
        for k, plane in enumerate(here.p_fault):
            qe[plane, c, 2] = qe[plane, c, 2] + rf_at(k, c) * (
                inv[pl.ds(plane * 16 + c, 1), :] * rows5
            )


def apply_column(w, wr, diag, qe, ap, p, y):
    odd_x, odd_y = p % 2, y % 2
    acc = {}
    for dx in (-1, 0, 1):
        for dy in (-1, 0, 1):
            q = [qe[p + dx, y + dy, lat] for lat in range(4)]
            own_x = dx if (dx == 1 and odd_x) or (dx == -1 and not odd_x) else 0
            own_y = dy if (dy == 1 and odd_y) or (dy == -1 and not odd_y) else 0
            oth_x = own_x + (1 if (odd_x + dx) % 2 else -1)
            oth_y = own_y + (1 if (odd_y + dy) % 2 else -1)
            for dz in (-1, 0, 1):
                if (dx, dy, dz) == (0, 0, 0):
                    continue
                if (dx, dy, dz) in OFFSET:
                    at = ((p + 1) * PER + OFFSET[dx, dy, dz]) * ROWS + y + 1
                    ref = w if dz == 0 else wr
                else:
                    at = ((p + 1 + dx) * PER + OFFSET[-dx, -dy, -dz]) * ROWS + y + 1 + dy
                    ref = w
                wt = ref[at : at + 1, :]
                for lat in range(4):
                    lx = oth_x if lat >= 2 else own_x
                    ly = oth_y if lat % 2 else own_y
                    value = wt * q[lat]
                    key = (lx, ly, dz)
                    acc[key] = acc[key] + value if key in acc else value
    centre = diag[p * 16 + y : p * 16 + y + 1, :]
    for lx in (-1, 0, 1):
        for ly in (-1, 0, 1):
            total = acc[lx, ly, 0]
            total = total + pltpu.roll(acc[lx, ly, 1], NZ - 1, 1)
            total = total + pltpu.roll(acc[lx, ly, -1], 1, 1)
            own_lat = None
            sx = {0: 0, (1 if odd_x else -1): 1}.get(lx)
            sy = {0: 0, (1 if odd_y else -1): 1}.get(ly)
            if sx is not None and sy is not None:
                own_lat = 2 * sx + sy
            if own_lat is None:
                total = -total
            else:
                total = centre * qe[p, y, own_lat] - total
            ap[p - 1, y - 1, lx + 1, ly + 1] = total


def fault_apply(here, qe, ap, c, f2c, ft2c):
    ly_oth = 2 * (c % 2)
    for plane, source, x_own, matrix in (
        (here.p_own, here.p_far, 1 + here.sgn, ft2c),
        (here.p_far, here.p_own, 1 - here.sgn, f2c),
    ):
        total = through(qe[source, c].reshape(32, NZ), matrix)
        for lat in range(4):
            lx = 1 if lat >= 2 else x_own
            ly = ly_oth if lat % 2 else 1
            ap[plane - 1, c - 1, lx, ly] = ap[plane - 1, c - 1, lx, ly] - total[8 * lat : 8 * lat + 8]


def fault_apply_band(here, qe, ap, c, band):
    ly_oth = 2 * (c % 2)
    to_own, to_far = [0.0] * 4, [0.0] * 4
    for d in range(DIAGONALS):
        weight = band[d : d + 1, :]
        for lat in range(4):
            ahead = pltpu.roll(qe[here.p_far, c, lat], (REACH - d) % NZ, 1)
            to_own[lat] = to_own[lat] + weight * ahead
            back = weight * qe[here.p_own, c, lat]
            to_far[lat] = to_far[lat] + pltpu.roll(back, (d - REACH) % NZ, 1)
    for plane, x_own, total in (
        (here.p_own, 1 + here.sgn, to_own),
        (here.p_far, 1 - here.sgn, to_far),
    ):
        for lat in range(4):
            lx = 1 if lat >= 2 else x_own
            ly = ly_oth if lat % 2 else 1
            ap[plane - 1, c - 1, lx, ly] = ap[plane - 1, c - 1, lx, ly] - total[lat]


def gather(here, qc, ap, tt, coarse_y, rows, add):
    shift = (-1, 0, 0, 1)
    for zk in range(2):
        acc = {}
        for x in range(-1, 3):
            for y in rows:
                lat = 2 * (x not in (0, 1)) + (y not in (0, 1))
                c = 2 * coarse_y + y + 2
                at = ((x + 2) * 8 + 2 * lat + zk) * 16 + c
                q = qc[at : at + 1, :]
                for lx in range(3):
                    for ly in range(3):
                        value = q * ap[x + 1, c - 1, lx, ly]
                        key = (shift[x + 1] + lx - 1, shift[y + 1] + ly - 1)
                        acc[key] = acc[key] + value if key in acc else value
        lane = (coarse_y % 2) * 256 + zk * NZ
        for (dx, dy), value in acc.items():
            at = (coarse_y // 2, here.a_of(dx), here.b_of(coarse_y, dy), slice(None), slice(lane, lane + NZ))
            tt[at] = tt[at] + value if add else value


def gather_fault(here, inv, ap, tt, y, ft2c):
    c = y + 2
    coarse_y = y // 2
    lane = (coarse_y % 2) * 256
    value = ap[here.p_far - 1, c - 1].reshape(72, NZ) * inv[pl.ds(here.p_far * 16 + c, 1), :]
    total = through(value, ft2c)
    for lx in range(3):
        a = here.a_of(lx - 1 + here.sgn)
        for ly in range(3):
            at = (coarse_y // 2, a, here.b_of(coarse_y, ly - 1), slice(None), slice(lane, lane + NZ))
            row = 8 * (3 * lx + ly)
            tt[at] = tt[at] + total[row : row + 8]


INNER = (2, 3, 4, 5)


def rows_of(coarse_y, inner):
    return [y for y in range(-1, 3) if (2 * coarse_y + y in INNER) == inner]


def has_time(peers):
    at = lax.axis_index("gx")
    return (lax.rem(lax.axis_index("gy"), 2) == 1) | (at == 0) | (at == peers[0] - 1)


def early_kernel(peers, *refs):
    pl.when(has_time(peers))(functools.partial(inner_part, peers, *refs))


def late_kernel(peers, *refs):
    refs = refs[:7] + refs[13:]
    pl.when(jnp.logical_not(has_time(peers)))(functools.partial(inner_part, peers, *refs))


def inner_part(
    peers, own, rp, ro, rs, f2, ft2, rf_pair, w, wr, qe, ap, tt, rf_third, qc, inv, diag, fd, hot
):
    here = Place()
    ro = Masked(ro, has_other("gx", peers[0]))

    def place(ref, count, first):
        for k in range(count):
            base = (first + k) * ROWS
            w[base + 3 : base + 11, :] = ref[8 * k : 8 * k + 8, :]

    def place_x(odd):
        lo, hi = (rp, ro) if odd else (ro, rp)
        place(lo, 28, PER)
        place(hi, 28, 5 * PER)

    by_parity("gx", place_x)
    place(Masked(rs, here.gx >= 2), 9, 4)
    place(own, 28, 3 * PER)

    fill_hot(hot, flat_cells(ro[224:228, :]), range(CY))
    got = colour_sums(hot[...], ro[232:236, :], ro[228:232, :])
    fd[...] = jnp.zeros_like(fd)
    for y in range(CY):
        rf_third[y] = got[:, y * NZ : (y + 1) * NZ]
        for plane, value in zip(here.p_fault, (rf_pair[0, y], rf_pair[1, y], rf_third[y])):
            fd[pl.ds(plane * 16 + y + 2, 1), :] = value[5:6, :]

    roll_weights(w, wr, 3, 8)
    smooth(w, wr, fd, qc, inv, diag, 2, 8)
    spread(
        here, qc, inv, qe, lambda k, c: rf_third[c - 2] if k == 2 else rf_pair[k, c - 2], range(3, 9)
    )
    for p in range(1, 5):
        for y in INNER:
            apply_column(w, wr, diag, qe, ap, p, y + 2)
    for y in INNER:
        fault_apply(here, qe, ap, y + 2, f2[y], ft2[y])
    tt[...] = jnp.zeros_like(tt)
    for coarse_y in range(CY // 2):
        gather(here, qc, ap, tt, coarse_y, rows_of(coarse_y, True), False)
    for y in INNER:
        gather_fault(here, inv, ap, tt, y, ft2[y])


def side(high, halo, f2, ft2, rf_pair, rf_third, work, fields, rf, band, hot):
    here = Place()
    w, wr, qe, ap, tt = work
    qc, inv, diag, fd = fields
    first = 6 if high else 0
    columns = (10, 11) if high else (0, 1)
    row, third, runs = (11, 13, (4,)) if high else (1, 0, (1, 10))

    for c in range(2):
        base = c * COLBLOCK
        w[pl.ds(4 * ROWS + row + c, 9, stride=ROWS), :] = halo[base : base + 9, :]
        w[pl.ds(PER * ROWS + row + c, 84, stride=ROWS), :] = halo[base + 9 : base + 93, :]
    at = THIRD
    for plane in range(7):
        for o in runs[-1:] if plane == 0 else runs:
            start = (plane * PER + o) * ROWS + third
            w[pl.ds(start, 3, stride=ROWS), :] = halo[at : at + 3, :]
            at += 3
    roll_weights(w, wr, 8 if high else 0, 8)

    fd[...] = jnp.zeros_like(fd)

    def put(column, k, value):
        rf[k, column - first] = value
        fd[pl.ds(here.p_fault[k] * 16 + column, 1), :] = value[5:6, :]

    own = (6, 7) if high else (0, 1)
    for y in own:
        put(y + 2, 0, rf_pair[0, y])
        put(y + 2, 1, rf_pair[1, y])
        put(y + 2, 2, rf_third[y])
    band[0:DIAGONALS, :] = halo[BAND_ROW : BAND_ROW + DIAGONALS, :]
    lists = halo[FAULT_ROW : FAULT_ROW + 12, :]
    fill_hot(hot, flat_cells(lists[0:4]), (0, 1) if high else (CY - 2, CY - 1))
    got = colour_sums(hot[...], lists[4:8], lists[8:12])
    for c, column in enumerate(columns):
        for k in range(2):
            at = SUM_ROW + (2 * c + k) * 6
            value = halo[at : at + 6, :]
            put(column, k, jnp.concatenate([value, jnp.zeros((2, NZ), f32)], axis=0))
        put(column, 2, got[:, c * NZ : (c + 1) * NZ])

    smooth(w, wr, fd, qc, inv, diag, first, 8)
    spread(
        here, qc, inv, qe, lambda k, c: rf[k, c - first], (9, 10, 11) if high else (0, 1, 2)
    )
    for p in range(1, 5):
        for y in (8, 9, 10) if high else (1, 2, 3):
            apply_column(w, wr, diag, qe, ap, p, y)
    for y in own:
        fault_apply(here, qe, ap, y + 2, f2[y], ft2[y])
    fault_apply_band(here, qe, ap, 10 if high else 1, band)
    parts = ((3, (0, 1, 2)), (2, (2,))) if high else ((0, (-1, 0, 1)), (1, (-1,)))
    for coarse_y, rows in parts:
        gather(here, qc, ap, tt, coarse_y, rows, True)
    for y in own:
        gather_fault(here, inv, ap, tt, y, ft2[y])


def finish(tt, pair, collect, store):
    high, low = split(tt[pair].reshape(200, 512))
    got = (dot_nn(high, collect[...]) + dot_nn(low, collect[...])) * 0.125
    for k in range(25):
        store(5 * k, got[8 * k : 8 * k + 5])


def core_kernel(halo, f2, ft2, rf_pair, rf_third, collect, *refs):
    half, work, fields, rest = refs[5], refs[6:11], refs[11:15], refs[15:]

    def body(odd):
        side(not odd, halo, f2, ft2, rf_pair, rf_third, work, fields, *rest)

        def store(row, value):
            half[row : row + 5, :] = value

        finish(work[4], 0 if odd else 1, collect, store)

    by_parity("gy", body)


def main_kernel(peers, halo, f2, ft2, rf_pair, rf_third, collect, half, *refs):
    out, work, fields, rest = refs[5], refs[6:11], refs[11:15], refs[15:]
    halo = Masked(halo, has_other("gy", peers[1]))

    def body(odd):
        side(odd, halo, f2, ft2, rf_pair, rf_third, work, fields, *rest)
        lanes = [slice(0, NZ), slice(NZ, 2 * NZ)]

        def store(row, value):
            out[row : row + 5, 0, lanes[odd]] = value
            out[row : row + 5, 0, lanes[1 - odd]] = half[row : row + 5, :]

        finish(work[4], odd, collect, store)

    by_parity("gy", body)


def send(value, target):
    size_x, size_y = lax.axis_size("gx"), lax.axis_size("gy")
    pairs = []
    for x in range(size_x):
        for y in range(size_y):
            to_x, to_y = target(x, y)
            pairs.append((x * size_y + y, to_x * size_y + to_y))
    return lax.ppermute(value, ("gx", "gy"), pairs)


def x_partner(x, y):
    return x ^ 1, y


def core_partner(x, y):
    return x, y ^ 1


def x_other(size_x):
    def target(x, y):
        other = x + 1 if x % 2 else x - 1
        return (other, y) if 0 <= other < size_x else core_partner(x, y)

    return target


def chip_other(size_y):
    def target(x, y):
        other = y + 1 if y % 2 else y - 1
        return (x, other) if 0 <= other < size_y else x_partner(x, y)

    return target


def x_ahead(size_x):
    return lambda x, y: ((x + 2) % size_x, y)


VMEM = pl.BlockSpec(memory_space=pltpu.VMEM)
HBM = pl.BlockSpec(memory_space=pltpu.HBM)


def params(mib):
    return pltpu.CompilerParams(vmem_limit_bytes=mib * 1024 * 1024)


def sds(*shape, dtype=f32):
    return jax.ShapeDtypeStruct(shape, dtype)


def per_device(trans, storage, fault_cells, fault_count, fault_trans):
    peers = (lax.axis_size("gx"), lax.axis_size("gy"))
    cells = send(fault_cells, x_partner)
    sources = [
        pltpu.with_memory_space_constraint(array, pltpu.HBM)
        for array in (trans, storage, fault_cells, fault_trans)
    ]
    own, plane, tile = pl.pallas_call(
        functools.partial(pack_kernel, peers),
        out_shape=(sds(224, NZ), sds(72, NZ), sds(8, NZ)),
        in_specs=[pl.BlockSpec(memory_space=pltpu.SMEM)] + [HBM] * 4,
        out_specs=(VMEM,) * 3,
        scratch_shapes=[pltpu.VMEM(array.shape, array.dtype) for array in sources]
        + [pltpu.SemaphoreType.DMA((4,))],
        compiler_params=params(16),
        name="pack",
    )(fault_count, *sources)
    joined, plane = pl.pallas_call(
        join_kernel,
        out_shape=(sds(240, NZ), sds(72, NZ)),
        in_specs=[VMEM] * 4,
        out_specs=(VMEM,) * 2,
        compiler_params=params(16),
        name="join",
    )(own, tile, plane, cells)
    rs = send(plane, x_ahead(peers[0]))
    ro = send(joined, x_other(peers[0]))
    rp = send(own, x_partner)
    pieces = sds(CY, 2 * NZ, NZ, dtype=bf16)
    f2, ft2, rf_pair, band, collect = pl.pallas_call(
        fault_kernel,
        out_shape=(
            pieces,
            pieces,
            sds(2, CY, 8, NZ),
            sds(2, 24, NZ),
            sds(512, NZ, dtype=bf16),
        ),
        in_specs=[VMEM] * 2,
        out_specs=(VMEM,) * 5,
        scratch_shapes=[
            pltpu.VMEM((SLOTS, 2 * NZ), bf16),
            pltpu.VMEM((CY * NZ, SLOTS), bf16),
            pltpu.VMEM((CY * NZ, 2 * NZ), f32),
        ],
        compiler_params=params(16),
        cost_estimate=pl.CostEstimate(flops=2 * 10**9, bytes_accessed=2**21, transcendentals=0),
        name="faults",
    )(tile, cells)
    work = (
        sds(7 * PER * ROWS, NZ),
        sds(7 * PER * ROWS, NZ),
        sds(6, 12, 4, 8, NZ),
        sds(4, 10, 3, 3, 8, NZ),
        sds(2, 5, 5, 8, 512),
    )
    inner = work + (sds(CY, 8, NZ),)
    fields = [
        pltpu.VMEM((6 * 8 * 16, NZ), f32),
        pltpu.VMEM((6 * 16, NZ), f32),
        pltpu.VMEM((6 * 16, NZ), f32),
        pltpu.VMEM((6 * 16, NZ), f32),
    ]
    inner_args = (own, rp, ro, rs, f2, ft2, rf_pair)
    inner_scratch = fields + [pltpu.VMEM((CY * NZ, SLOTS), bf16)]
    filled = pl.pallas_call(
        functools.partial(early_kernel, peers),
        out_shape=inner,
        in_specs=[VMEM] * 7,
        out_specs=(VMEM,) * 6,
        scratch_shapes=inner_scratch,
        compiler_params=params(16),
        name="inner_early",
    )(*inner_args)
    to_core, to_chip = pl.pallas_call(
        functools.partial(column_kernel, peers),
        out_shape=(sds(Y_ROWS, NZ), sds(Y_ROWS, NZ)),
        in_specs=[VMEM] * 7,
        out_specs=(VMEM,) * 2,
        compiler_params=params(16),
        name="columns",
    )(own, rp, ro, rs, band, rf_pair, filled[5])
    from_chip = send(to_chip, chip_other(peers[1]))
    from_core = send(to_core, core_partner)
    *work_in, rf_third = pl.pallas_call(
        functools.partial(late_kernel, peers),
        out_shape=inner,
        in_specs=[VMEM] * 13,
        out_specs=(VMEM,) * 6,
        scratch_shapes=inner_scratch,
        input_output_aliases={7 + k: k for k in range(6)},
        compiler_params=params(16),
        cost_estimate=pl.CostEstimate(flops=4 * 10**9, bytes_accessed=2**21, transcendentals=0),
        name="inner_late",
    )(*inner_args, *filled)
    side_scratch = fields + [
        pltpu.VMEM((3, 8, 8, NZ), f32),
        pltpu.VMEM((24, NZ), f32),
        pltpu.VMEM((2 * NZ, SLOTS), bf16),
    ]
    half, *work_in = pl.pallas_call(
        core_kernel,
        out_shape=(sds(125, NZ),) + work,
        in_specs=[VMEM] * 11,
        out_specs=(VMEM,) * 6,
        scratch_shapes=side_scratch,
        input_output_aliases={6 + k: 1 + k for k in range(5)},
        compiler_params=params(16),
        cost_estimate=pl.CostEstimate(flops=2 * 10**9, bytes_accessed=2**20, transcendentals=0),
        name="core_side",
    )(from_core, f2, ft2, rf_pair, rf_third, collect, *work_in)
    result, *_ = pl.pallas_call(
        functools.partial(main_kernel, peers),
        out_shape=(sds(125, 1, 256),) + work,
        in_specs=[VMEM] * 12,
        out_specs=(VMEM,) * 6,
        scratch_shapes=side_scratch,
        input_output_aliases={7 + k: 1 + k for k in range(5)},
        compiler_params=params(16),
        name="chip_side",
    )(from_chip, f2, ft2, rf_pair, rf_third, collect, half, *work_in)
    return result


def solution(mesh):
    placed = (
        P(None, "gx", "gy"),
        P("gx", "gy"),
        P("gx", "gy", None),
        P("gx", "gy"),
        P("gx", "gy", None),
    )
    return jax.shard_map(
        per_device, mesh=mesh, in_specs=placed, out_specs=P(None, "gx", "gy"), check_vma=False
    )
```

```python
import functools

import jax
import jax.numpy as jnp
from jax import lax
from jax.experimental import pallas as pl
from jax.experimental.pallas import tpu as pltpu
from jax.sharding import PartitionSpec as P

NZ = 128
CY = 8
SLOTS = 512

FORWARD = (
    (0, 0, 1),
    (0, 1, -1),
    (0, 1, 0),
    (0, 1, 1),
    (1, -1, -1),
    (1, -1, 0),
    (1, -1, 1),
    (1, 0, -1),
    (1, 0, 0),
    (1, 0, 1),
    (1, 1, -1),
    (1, 1, 0),
    (1, 1, 1),
)
OFFSET = {step: k for k, step in enumerate(FORWARD)}
damping = 2.0 / 3.0

ROWS = 24
PER = 14
COLBLOCK = 93
THIRD = 2 * COLBLOCK
FAULT_ROW = 225
BAND_ROW, SUM_ROW, Y_ROWS = 237, 254, 280
REACH = 8
DIAGONALS = 2 * REACH + 1

f32 = jnp.float32
bf16 = jnp.bfloat16


def dot_nt(a, b):
    return lax.dot_general(a, b, (((1,), (1,)), ((), ())), preferred_element_type=f32)


def dot_nn(a, b):
    return lax.dot_general(a, b, (((1,), (0,)), ((), ())), preferred_element_type=f32)


def split(value):
    high = value.astype(bf16)
    return high, (value - high.astype(f32)).astype(bf16)


def pack_kernel(peers, count, *refs):
    sources, (block, plane), targets, sems = refs[:4], refs[4:6], refs[6:10], refs[10]
    copies = [
        pltpu.make_async_copy(src, dst, sems.at[k])
        for k, (src, dst) in enumerate(zip(sources, targets))
    ]
    for copy in copies:
        copy.start()
    for copy in copies:
        copy.wait()
    trans, storage, cells, ftrans = targets
    last_x = lax.axis_index("gx") == peers[0] - 1
    first_y = lax.axis_index("gy") == 0
    last_y = lax.axis_index("gy") == peers[1] - 1
    depth = lax.broadcasted_iota(jnp.int32, (8, NZ), 1)
    row = lax.broadcasted_iota(jnp.int32, (8, NZ), 0)
    for x in range(2):
        for o in range(PER):
            base = (x * PER + o) * 8
            for y in range(CY):
                lanes = slice(y * NZ, (y + 1) * NZ)
                if o < 13:
                    value = trans[o, x : x + 1, lanes]
                else:
                    value = storage[x : x + 1, lanes]
                block[base + y : base + y + 1, :] = value
            if o == 13:
                continue
            step = FORWARD[o]
            keep = None
            if step[2] == 1:
                keep = depth < NZ - 1
            if step[2] == -1:
                keep = depth > 0
            if step[1] == 1:
                inside = (row < CY - 1) | jnp.logical_not(last_y)
                keep = inside if keep is None else keep & inside
            if step[1] == -1:
                inside = (row > 0) | jnp.logical_not(first_y)
                keep = inside if keep is None else keep & inside
            if step[0] == 1 and x == 1:
                inside = (row >= 0) & jnp.logical_not(last_x)
                keep = inside if keep is None else keep & inside
            if keep is not None:
                block[base : base + 8, :] = jnp.where(keep, block[base : base + 8, :], 0.0)
    live = count[0, 0]
    lane = lax.broadcasted_iota(jnp.int32, (1, NZ), 1)
    for r in range(4):
        lanes = slice(r * NZ, (r + 1) * NZ)
        at = 2 * PER * 8 + r
        block[at : at + 1, :] = cells[0, :, lanes].astype(f32)
        block[at + 4 : at + 5, :] = jnp.where(
            lane + r * NZ < live, ftrans[0, :, lanes], 0.0
        )
    plane[0:72, :] = block[(PER + 4) * 8 : (PER + 13) * 8, :]
    plane[72:80, :] = block[224:232, :]


def pass_kernel(own, plane, own_out, plane_out):
    own_out[...] = own[...]
    plane_out[...] = plane[...]


def by_parity(axis, body):
    odd = lax.rem(lax.axis_index(axis), 2)
    for k in range(2):
        pl.when(odd == k)(functools.partial(body, k))


class Masked:
    def __init__(self, ref, due):
        self.ref, self.due = ref, due

    def __getitem__(self, index):
        return jnp.where(self.due, self.ref[index], 0.0)


class Behind:
    def __init__(self, rd, re):
        self.refs, self.at = (rd, re), lax.axis_index("gx")

    def __getitem__(self, index):
        even, odd = (ref[index] for ref in self.refs)
        value = jnp.where(lax.rem(self.at, 2) == 0, even, odd)
        return jnp.where(self.at >= 2, value, 0.0)


def has_other(axis, peers):
    at = lax.axis_index(axis)
    return jnp.where(lax.rem(at, 2) == 0, at > 0, at < peers - 1)


def column_kernel(peers, own, rp, ro, rd, re, band, sums, after, to_core, to_chip):
    del after
    ro = Masked(ro, has_other("gx", peers[0]))
    lo2 = Behind(rd, re)

    def fill(out, lo, hi, first, third, runs):
        for c in range(2):
            y = first + c
            base = c * COLBLOCK
            out[base : base + 9, :] = lo2[pl.ds(y, 9, stride=8), :]
            for k, ref in enumerate((lo, own, hi)):
                start = base + 9 + 28 * k
                out[start : start + 28, :] = ref[pl.ds(y, 28, stride=8), :]
        at = THIRD
        out[at : at + 3, :] = lo2[pl.ds((runs[-1] - 4) * 8 + third, 3, stride=8), :]
        at += 3
        for ref in (lo, own, hi):
            for x in range(2):
                for o in runs:
                    out[at : at + 3, :] = ref[pl.ds((x * PER + o) * 8 + third, 3, stride=8), :]
                    at += 3
        for k, rows in enumerate((ro[224:228, :], rd[72:76, :], ro[228:232, :])):
            out[FAULT_ROW + 4 * k : FAULT_ROW + 4 * k + 4, :] = rows
        out[BAND_ROW : BAND_ROW + DIAGONALS, :] = band[int(first > 0), 0:DIAGONALS, :]
        for c in range(2):
            for k in range(2):
                at = SUM_ROW + (2 * c + k) * 6
                out[at : at + 6, :] = sums[k, first + c, 0:6, :]
        out[SUM_ROW + 24 : Y_ROWS, :] = jnp.zeros((Y_ROWS - SUM_ROW - 24, NZ), f32)

    def for_x(odd_x):
        lo, hi = (rp, ro) if odd_x else (ro, rp)

        def for_y(odd_y):
            up, down = (to_chip, to_core) if odd_y else (to_core, to_chip)
            fill(up, lo, hi, CY - 2, CY - 3, (1, 10))
            fill(down, lo, hi, 0, 2, (4,))

        by_parity("gy", for_y)

    by_parity("gx", for_x)


def colour(z):
    half = z >> 1
    return half - 5 * ((half * 205) >> 10)


def slot_columns(rows):
    tall = jnp.transpose(jnp.concatenate(rows, axis=0))
    return [[tall[:, 4 * k + r : 4 * k + r + 1] for r in range(4)] for k in range(len(rows))]


def flat_cells(rows):
    row = jnp.concatenate([rows[r : r + 1] for r in range(4)], axis=1)
    return row.astype(jnp.int32) & 1023


def fill_far(far2, partner, live):
    lane = lax.broadcasted_iota(jnp.int32, (NZ, NZ), 1)
    for r in range(4):
        rows = slice(r * NZ, (r + 1) * NZ)
        match = (partner[r].astype(jnp.int32) & 127) == lane
        high = live[r].astype(bf16).astype(f32)
        far2[rows, 0:NZ] = jnp.where(match, high, 0.0).astype(bf16)
        far2[rows, NZ : 2 * NZ] = jnp.where(match, live[r] - high, 0.0).astype(bf16)


def flat_rows(rows):
    return jnp.concatenate([rows[r : r + 1] for r in range(4)], axis=1)


def colour_sums(hot, beyond, live):
    e16 = lax.broadcasted_iota(jnp.int32, (16, SLOTS), 0)
    tint = colour(flat_rows(beyond).astype(jnp.int32) & 127)
    live = flat_rows(live)
    high = live.astype(bf16).astype(f32)
    value = jnp.where((e16 == tint) | (e16 == 5), high, 0.0)
    value = jnp.where((e16 == tint + 8) | (e16 == 13), live - high, value)
    got = dot_nt(value.astype(bf16), hot)
    return got[:8] + got[8:]


def diagonals(hot, own, far, live):
    d24 = lax.broadcasted_iota(jnp.int32, (24, SLOTS), 0)
    step = (flat_rows(far).astype(jnp.int32) & 127) - (flat_rows(own).astype(jnp.int32) & 127)
    live = flat_rows(live)
    high = live.astype(bf16).astype(f32)
    match = step + REACH == d24
    both = [jnp.where(match, value, 0.0) for value in (high, live - high)]
    got = dot_nt(jnp.concatenate(both, axis=0).astype(bf16), hot)
    return got[:24] + got[24:]


def fill_hot(hot, cells, columns):
    z128 = lax.broadcasted_iota(jnp.int32, (NZ, SLOTS), 0)
    for k, y in enumerate(columns):
        value = jnp.where(cells == z128 + y * NZ, 1.0, 0.0)
        hot[k * NZ : (k + 1) * NZ, :] = value.astype(bf16)


def pair_matrix(both):
    z8 = lax.broadcasted_iota(jnp.int32, (8, NZ), 1)
    e8 = lax.broadcasted_iota(jnp.int32, (8, NZ), 0)
    one = jnp.where((e8 == colour(z8)) | (e8 == 5), 1.0, 0.0).astype(bf16)
    one2 = jnp.concatenate([one, one], axis=1)
    matrix = both[:, :NZ] + both[:, NZ:]
    f2 = jnp.concatenate(split(matrix), axis=0)
    ft2 = jnp.concatenate(split(jnp.transpose(matrix)), axis=0)
    return f2, ft2, dot_nn(one2, ft2), dot_nn(one2, f2)


def fill_collect(collect):
    kz = lax.broadcasted_iota(jnp.int32, (512, NZ), 0)
    kout = lax.broadcasted_iota(jnp.int32, (512, NZ), 1)
    z_in = kz & 127
    is_oth = ((kz >> 7) & 1) == 1
    target = jnp.where(
        is_oth, (z_in >> 1) + jnp.where((z_in & 1) == 0, -1, 1), z_in >> 1
    )
    fits = (target == (kout & 63)) & ((kz >> 8) == (kout >> 6))
    collect[...] = jnp.where(fits, 1.0, 0.0).astype(bf16)


def fault_kernel(own, rp, f2, ft2, rf, band, collect, far2, hot, both):
    fill_collect(collect)
    partner, live = slot_columns([rp[224:228, :], own[228:232, :]])
    fill_far(far2, partner, live)
    fill_hot(hot, flat_cells(own[224:228, :]), range(CY))
    both[...] = dot_nn(hot[...], far2[...])
    for y in range(CY):
        f2[y], ft2[y], rf[0, y], rf[1, y] = pair_matrix(both[y * NZ : (y + 1) * NZ, :])
    for k, y in enumerate((0, CY - 1)):
        band[k] = diagonals(
            hot[y * NZ : (y + 1) * NZ, :], own[224:228, :], rp[224:228, :], own[228:232, :]
        )


def through(value, matrix2):
    rows = value.shape[0]
    high, low = split(value)
    left = jnp.concatenate(
        [jnp.concatenate([high, high], axis=1), jnp.concatenate([low, low], axis=1)], axis=0
    )
    got = dot_nn(left, matrix2)
    return got[:rows] + got[rows:]


class Place:
    def __init__(self):
        self.gx = lax.axis_index("gx")
        self.gy = lax.axis_index("gy")
        par = lax.rem(self.gx, 2)
        even = par == 0
        self.sgn = 1 - 2 * par
        self.p_own = jnp.where(even, 3, 2)
        self.p_far = jnp.where(even, 4, 1)
        self.p_third = jnp.where(even, 0, 5)
        self.p_fault = (self.p_own, self.p_far, self.p_third)
        self.x_coarse = lax.rem(self.gx, 5) + 5

    def a_of(self, d):
        return lax.rem(self.x_coarse + d, 5)

    def b_of(self, coarse_y, d):
        return lax.rem(self.gy * (CY // 2) + coarse_y + d + 5, 5)


def roll_weights(w, wr, first, count):
    for p in range(7):
        for o, step in enumerate(FORWARD):
            if step[2] == 0 or (p == 0 and o < 4):
                continue
            at = (p * PER + o) * ROWS + first
            distance = 1 if step[2] == 1 else NZ - 1
            wr[at : at + count, :] = pltpu.roll(w[at : at + count, :], distance, 1)


def smooth(w, wr, fd, qc, inv, diag, first, count):
    even_y = (lax.broadcasted_iota(jnp.int32, (count, NZ), 0) & 1) == 0
    even_z = (lax.broadcasted_iota(jnp.int32, (count, NZ), 1) & 1) == 0
    for p in range(6):
        base = p + 1

        def weight(dx, dy, dz):
            if (dx, dy, dz) in OFFSET:
                start = (base * PER + OFFSET[dx, dy, dz]) * ROWS + 1 + first
                return w[start : start + count, :]
            o = OFFSET[-dx, -dy, -dz]
            start = ((base + dx) * PER + o) * ROWS + 1 + first + dy
            return (w if dz == 0 else wr)[start : start + count, :]

        near = 1 if p % 2 == 0 else -1
        sums = {}
        for dz in (-1, 0, 1):
            got = {}
            for dx in (-1, 0, 1):
                below, above = weight(dx, -1, dz), weight(dx, 1, dz)
                got[dx, 0] = jnp.where(even_y, above, below)
                if (dx, dz) != (0, 0):
                    got[dx, 0] = got[dx, 0] + weight(dx, 0, dz)
                got[dx, 1] = jnp.where(even_y, below, above)
            for sy in range(2):
                sums[0, sy, dz] = got[0, sy] + got[near, sy]
                sums[1, sy, dz] = got[-near, sy]
        start = (base * PER + 13) * ROWS + 1 + first
        at = p * 16 + first
        total = w[start : start + count, :] + fd[at : at + count, :]
        r = []
        for sx in range(2):
            for sy in range(2):
                down, same, up = (sums[sx, sy, dz] for dz in (-1, 0, 1))
                r.append(same + jnp.where(even_z, up, down))
                r.append(jnp.where(even_z, down, up))
        for value in r:
            total = total + value
        total = jnp.where(total == 0.0, 1.0, total)
        scale = damping / total
        diag[at : at + count, :] = total
        inv[at : at + count, :] = scale
        for k, value in enumerate(r):
            value = value * scale
            if k == 0:
                value = value + (1.0 - damping)
            at = (p * 8 + k) * 16 + first
            qc[at : at + count, :] = value


def spread(here, qc, inv, qe, rf_at, columns):
    z8 = lax.broadcasted_iota(jnp.int32, (8, NZ), 1)
    e8 = lax.broadcasted_iota(jnp.int32, (8, NZ), 0)
    beside = jnp.where((z8 & 1) == 0, z8 - 1, z8 + 1)
    mask_own = jnp.where(e8 == colour(z8), 1.0, 0.0)
    mask_oth = jnp.where(e8 == colour(beside + 10), 1.0, 0.0)
    rows5 = jnp.where(e8 < 5, 1.0, 0.0)

    for c in columns:
        for p in range(6):
            for lat in range(4):
                at = (p * 8 + 2 * lat) * 16 + c
                qe[p, c, lat] = qc[at : at + 1, :] * mask_own + qc[at + 16 : at + 17, :] * mask_oth
        for k, plane in enumerate(here.p_fault):
            qe[plane, c, 2] = qe[plane, c, 2] + rf_at(k, c) * (
                inv[pl.ds(plane * 16 + c, 1), :] * rows5
            )


def apply_column(w, wr, diag, qe, ap, p, y):
    odd_x, odd_y = p % 2, y % 2
    acc = {}
    for dx in (-1, 0, 1):
        for dy in (-1, 0, 1):
            q = [qe[p + dx, y + dy, lat] for lat in range(4)]
            own_x = dx if (dx == 1 and odd_x) or (dx == -1 and not odd_x) else 0
            own_y = dy if (dy == 1 and odd_y) or (dy == -1 and not odd_y) else 0
            oth_x = own_x + (1 if (odd_x + dx) % 2 else -1)
            oth_y = own_y + (1 if (odd_y + dy) % 2 else -1)
            for dz in (-1, 0, 1):
                if (dx, dy, dz) == (0, 0, 0):
                    continue
                if (dx, dy, dz) in OFFSET:
                    at = ((p + 1) * PER + OFFSET[dx, dy, dz]) * ROWS + y + 1
                    ref = w if dz == 0 else wr
                else:
                    at = ((p + 1 + dx) * PER + OFFSET[-dx, -dy, -dz]) * ROWS + y + 1 + dy
                    ref = w
                wt = ref[at : at + 1, :]
                for lat in range(4):
                    lx = oth_x if lat >= 2 else own_x
                    ly = oth_y if lat % 2 else own_y
                    value = wt * q[lat]
                    key = (lx, ly, dz)
                    acc[key] = acc[key] + value if key in acc else value
    centre = diag[p * 16 + y : p * 16 + y + 1, :]
    for lx in (-1, 0, 1):
        for ly in (-1, 0, 1):
            total = acc[lx, ly, 0]
            total = total + pltpu.roll(acc[lx, ly, 1], NZ - 1, 1)
            total = total + pltpu.roll(acc[lx, ly, -1], 1, 1)
            own_lat = None
            sx = {0: 0, (1 if odd_x else -1): 1}.get(lx)
            sy = {0: 0, (1 if odd_y else -1): 1}.get(ly)
            if sx is not None and sy is not None:
                own_lat = 2 * sx + sy
            if own_lat is None:
                total = -total
            else:
                total = centre * qe[p, y, own_lat] - total
            ap[p - 1, y - 1, lx + 1, ly + 1] = total


def fault_apply(here, qe, ap, c, f2c, ft2c):
    ly_oth = 2 * (c % 2)
    for plane, source, x_own, matrix in (
        (here.p_own, here.p_far, 1 + here.sgn, ft2c),
        (here.p_far, here.p_own, 1 - here.sgn, f2c),
    ):
        total = through(qe[source, c].reshape(32, NZ), matrix)
        for lat in range(4):
            lx = 1 if lat >= 2 else x_own
            ly = ly_oth if lat % 2 else 1
            ap[plane - 1, c - 1, lx, ly] = ap[plane - 1, c - 1, lx, ly] - total[8 * lat : 8 * lat + 8]


def fault_apply_band(here, qe, ap, c, band):
    ly_oth = 2 * (c % 2)
    to_own, to_far = [0.0] * 4, [0.0] * 4
    for d in range(DIAGONALS):
        weight = band[d : d + 1, :]
        for lat in range(4):
            ahead = pltpu.roll(qe[here.p_far, c, lat], (REACH - d) % NZ, 1)
            to_own[lat] = to_own[lat] + weight * ahead
            back = weight * qe[here.p_own, c, lat]
            to_far[lat] = to_far[lat] + pltpu.roll(back, (d - REACH) % NZ, 1)
    for plane, x_own, total in (
        (here.p_own, 1 + here.sgn, to_own),
        (here.p_far, 1 - here.sgn, to_far),
    ):
        for lat in range(4):
            lx = 1 if lat >= 2 else x_own
            ly = ly_oth if lat % 2 else 1
            ap[plane - 1, c - 1, lx, ly] = ap[plane - 1, c - 1, lx, ly] - total[lat]


def gather(here, qc, ap, tt, coarse_y, rows, add):
    shift = (-1, 0, 0, 1)
    for zk in range(2):
        acc = {}
        for x in range(-1, 3):
            for y in rows:
                lat = 2 * (x not in (0, 1)) + (y not in (0, 1))
                c = 2 * coarse_y + y + 2
                at = ((x + 2) * 8 + 2 * lat + zk) * 16 + c
                q = qc[at : at + 1, :]
                for lx in range(3):
                    for ly in range(3):
                        value = q * ap[x + 1, c - 1, lx, ly]
                        key = (shift[x + 1] + lx - 1, shift[y + 1] + ly - 1)
                        acc[key] = acc[key] + value if key in acc else value
        lane = (coarse_y % 2) * 256 + zk * NZ
        for (dx, dy), value in acc.items():
            at = (coarse_y // 2, here.a_of(dx), here.b_of(coarse_y, dy), slice(None), slice(lane, lane + NZ))
            tt[at] = tt[at] + value if add else value


def gather_fault(here, inv, ap, tt, y, ft2c):
    c = y + 2
    coarse_y = y // 2
    lane = (coarse_y % 2) * 256
    value = ap[here.p_far - 1, c - 1].reshape(72, NZ) * inv[pl.ds(here.p_far * 16 + c, 1), :]
    total = through(value, ft2c)
    for lx in range(3):
        a = here.a_of(lx - 1 + here.sgn)
        for ly in range(3):
            at = (coarse_y // 2, a, here.b_of(coarse_y, ly - 1), slice(None), slice(lane, lane + NZ))
            row = 8 * (3 * lx + ly)
            tt[at] = tt[at] + total[row : row + 8]


INNER = (2, 3, 4, 5)


def rows_of(coarse_y, inner):
    return [y for y in range(-1, 3) if (2 * coarse_y + y in INNER) == inner]


def has_time(peers):
    at = lax.axis_index("gx")
    return (lax.rem(lax.axis_index("gy"), 2) == 1) | (at == 0) | (at == peers[0] - 1)


def early_kernel(peers, *refs):
    pl.when(has_time(peers))(functools.partial(inner_part, peers, *refs))


def late_kernel(peers, *refs):
    refs = refs[:8] + refs[14:]
    pl.when(jnp.logical_not(has_time(peers)))(functools.partial(inner_part, peers, *refs))


def inner_part(
    peers, own, rp, ro, rd, re, f2, ft2, rf_pair, w, wr, qe, ap, tt, rf_third, qc, inv, diag, fd, hot
):
    here = Place()
    ro = Masked(ro, has_other("gx", peers[0]))

    def place(ref, count, first):
        for k in range(count):
            base = (first + k) * ROWS
            w[base + 3 : base + 11, :] = ref[8 * k : 8 * k + 8, :]

    def place_x(odd):
        lo, hi = (rp, ro) if odd else (ro, rp)
        place(lo, 28, PER)
        place(hi, 28, 5 * PER)

    by_parity("gx", place_x)
    place(Behind(rd, re), 9, 4)
    place(own, 28, 3 * PER)

    fill_hot(hot, flat_cells(ro[224:228, :]), range(CY))
    got = colour_sums(hot[...], rd[72:76, :], ro[228:232, :])
    fd[...] = jnp.zeros_like(fd)
    for y in range(CY):
        rf_third[y] = got[:, y * NZ : (y + 1) * NZ]
        for plane, value in zip(here.p_fault, (rf_pair[0, y], rf_pair[1, y], rf_third[y])):
            fd[pl.ds(plane * 16 + y + 2, 1), :] = value[5:6, :]

    roll_weights(w, wr, 3, 8)
    smooth(w, wr, fd, qc, inv, diag, 2, 8)
    spread(
        here, qc, inv, qe, lambda k, c: rf_third[c - 2] if k == 2 else rf_pair[k, c - 2], range(3, 9)
    )
    for p in range(1, 5):
        for y in INNER:
            apply_column(w, wr, diag, qe, ap, p, y + 2)
    for y in INNER:
        fault_apply(here, qe, ap, y + 2, f2[y], ft2[y])
    tt[...] = jnp.zeros_like(tt)
    for coarse_y in range(CY // 2):
        gather(here, qc, ap, tt, coarse_y, rows_of(coarse_y, True), False)
    for y in INNER:
        gather_fault(here, inv, ap, tt, y, ft2[y])


def side(high, halo, f2, ft2, rf_pair, rf_third, work, fields, rf, band, hot):
    here = Place()
    w, wr, qe, ap, tt = work
    qc, inv, diag, fd = fields
    first = 6 if high else 0
    columns = (10, 11) if high else (0, 1)
    row, third, runs = (11, 13, (4,)) if high else (1, 0, (1, 10))

    for c in range(2):
        base = c * COLBLOCK
        w[pl.ds(4 * ROWS + row + c, 9, stride=ROWS), :] = halo[base : base + 9, :]
        w[pl.ds(PER * ROWS + row + c, 84, stride=ROWS), :] = halo[base + 9 : base + 93, :]
    at = THIRD
    for plane in range(7):
        for o in runs[-1:] if plane == 0 else runs:
            start = (plane * PER + o) * ROWS + third
            w[pl.ds(start, 3, stride=ROWS), :] = halo[at : at + 3, :]
            at += 3
    roll_weights(w, wr, 8 if high else 0, 8)

    fd[...] = jnp.zeros_like(fd)

    def put(column, k, value):
        rf[k, column - first] = value
        fd[pl.ds(here.p_fault[k] * 16 + column, 1), :] = value[5:6, :]

    own = (6, 7) if high else (0, 1)
    for y in own:
        put(y + 2, 0, rf_pair[0, y])
        put(y + 2, 1, rf_pair[1, y])
        put(y + 2, 2, rf_third[y])
    band[0:DIAGONALS, :] = halo[BAND_ROW : BAND_ROW + DIAGONALS, :]
    lists = halo[FAULT_ROW : FAULT_ROW + 12, :]
    fill_hot(hot, flat_cells(lists[0:4]), (0, 1) if high else (CY - 2, CY - 1))
    got = colour_sums(hot[...], lists[4:8], lists[8:12])
    for c, column in enumerate(columns):
        for k in range(2):
            at = SUM_ROW + (2 * c + k) * 6
            value = halo[at : at + 6, :]
            put(column, k, jnp.concatenate([value, jnp.zeros((2, NZ), f32)], axis=0))
        put(column, 2, got[:, c * NZ : (c + 1) * NZ])

    smooth(w, wr, fd, qc, inv, diag, first, 8)
    spread(
        here, qc, inv, qe, lambda k, c: rf[k, c - first], (9, 10, 11) if high else (0, 1, 2)
    )
    for p in range(1, 5):
        for y in (8, 9, 10) if high else (1, 2, 3):
            apply_column(w, wr, diag, qe, ap, p, y)
    for y in own:
        fault_apply(here, qe, ap, y + 2, f2[y], ft2[y])
    fault_apply_band(here, qe, ap, 10 if high else 1, band)
    parts = ((3, (0, 1, 2)), (2, (2,))) if high else ((0, (-1, 0, 1)), (1, (-1,)))
    for coarse_y, rows in parts:
        gather(here, qc, ap, tt, coarse_y, rows, True)
    for y in own:
        gather_fault(here, inv, ap, tt, y, ft2[y])


def finish(tt, pair, collect, store):
    high, low = split(tt[pair].reshape(200, 512))
    got = (dot_nn(high, collect[...]) + dot_nn(low, collect[...])) * 0.125
    for k in range(25):
        store(5 * k, got[8 * k : 8 * k + 5])


def core_kernel(halo, f2, ft2, rf_pair, rf_third, collect, *refs):
    half, work, fields, rest = refs[5], refs[6:11], refs[11:15], refs[15:]

    def body(odd):
        side(not odd, halo, f2, ft2, rf_pair, rf_third, work, fields, *rest)

        def store(row, value):
            half[row : row + 5, :] = value

        finish(work[4], 0 if odd else 1, collect, store)

    by_parity("gy", body)


def main_kernel(peers, halo, f2, ft2, rf_pair, rf_third, collect, half, *refs):
    out, work, fields, rest = refs[5], refs[6:11], refs[11:15], refs[15:]
    halo = Masked(halo, has_other("gy", peers[1]))

    def body(odd):
        side(odd, halo, f2, ft2, rf_pair, rf_third, work, fields, *rest)
        lanes = [slice(0, NZ), slice(NZ, 2 * NZ)]

        def store(row, value):
            out[row : row + 5, 0, lanes[odd]] = value
            out[row : row + 5, 0, lanes[1 - odd]] = half[row : row + 5, :]

        finish(work[4], odd, collect, store)

    by_parity("gy", body)


def send(value, target):
    size_x, size_y = lax.axis_size("gx"), lax.axis_size("gy")
    pairs = []
    for x in range(size_x):
        for y in range(size_y):
            to_x, to_y = target(x, y)
            pairs.append((x * size_y + y, to_x * size_y + to_y))
    return lax.ppermute(value, ("gx", "gy"), pairs)


def x_partner(x, y):
    return x ^ 1, y


def core_partner(x, y):
    return x, y ^ 1


def x_other(size_x):
    def target(x, y):
        other = x + 1 if x % 2 else x - 1
        return (other, y) if 0 <= other < size_x else core_partner(x, y)

    return target


def chip_other(size_x, size_y):
    def target(x, y):
        other = y + 1 if y % 2 else y - 1
        if 0 <= other < size_y:
            return x, other
        beside = x + 1 if x % 2 else x - 1
        return (beside, y) if 0 <= beside < size_x else (x, size_y - 1 - y)

    return target


def x_two(size_x, up):
    def target(x, y):
        other = x + 2 if x % 2 == up else x - 2
        return (other, y) if 0 <= other < size_x else x_partner(x, y)

    return target


VMEM = pl.BlockSpec(memory_space=pltpu.VMEM)
HBM = pl.BlockSpec(memory_space=pltpu.HBM)


def params(mib):
    return pltpu.CompilerParams(vmem_limit_bytes=mib * 1024 * 1024)


def sds(*shape, dtype=f32):
    return jax.ShapeDtypeStruct(shape, dtype)


def per_device(trans, storage, fault_cells, fault_count, fault_trans):
    peers = (lax.axis_size("gx"), lax.axis_size("gy"))
    sources = [
        pltpu.with_memory_space_constraint(array, pltpu.HBM)
        for array in (trans, storage, fault_cells, fault_trans)
    ]
    own, plane = pl.pallas_call(
        functools.partial(pack_kernel, peers),
        out_shape=(sds(232, NZ), sds(80, NZ)),
        in_specs=[pl.BlockSpec(memory_space=pltpu.SMEM)] + [HBM] * 4,
        out_specs=(VMEM,) * 2,
        scratch_shapes=[pltpu.VMEM(array.shape, array.dtype) for array in sources]
        + [pltpu.SemaphoreType.DMA((4,))],
        compiler_params=params(16),
        name="pack",
    )(fault_count, *sources)
    rp = send(own, x_partner)
    own_again, plane = pl.pallas_call(
        pass_kernel,
        out_shape=(sds(232, NZ), sds(80, NZ)),
        in_specs=[VMEM] * 2,
        out_specs=(VMEM,) * 2,
        compiler_params=params(16),
        name="pass",
    )(own, plane)
    rd = send(plane, x_two(peers[0], 0))
    re = send(plane, x_two(peers[0], 1))
    ro = send(own_again, x_other(peers[0]))
    pieces = sds(CY, 2 * NZ, NZ, dtype=bf16)
    f2, ft2, rf_pair, band, collect = pl.pallas_call(
        fault_kernel,
        out_shape=(
            pieces,
            pieces,
            sds(2, CY, 8, NZ),
            sds(2, 24, NZ),
            sds(512, NZ, dtype=bf16),
        ),
        in_specs=[VMEM] * 2,
        out_specs=(VMEM,) * 5,
        scratch_shapes=[
            pltpu.VMEM((SLOTS, 2 * NZ), bf16),
            pltpu.VMEM((CY * NZ, SLOTS), bf16),
            pltpu.VMEM((CY * NZ, 2 * NZ), f32),
        ],
        compiler_params=params(16),
        cost_estimate=pl.CostEstimate(flops=2 * 10**9, bytes_accessed=2**21, transcendentals=0),
        name="faults",
    )(own, rp)
    work = (
        sds(7 * PER * ROWS, NZ),
        sds(7 * PER * ROWS, NZ),
        sds(6, 12, 4, 8, NZ),
        sds(4, 10, 3, 3, 8, NZ),
        sds(2, 5, 5, 8, 512),
    )
    inner = work + (sds(CY, 8, NZ),)
    fields = [
        pltpu.VMEM((6 * 8 * 16, NZ), f32),
        pltpu.VMEM((6 * 16, NZ), f32),
        pltpu.VMEM((6 * 16, NZ), f32),
        pltpu.VMEM((6 * 16, NZ), f32),
    ]
    inner_args = (own, rp, ro, rd, re, f2, ft2, rf_pair)
    inner_scratch = fields + [pltpu.VMEM((CY * NZ, SLOTS), bf16)]
    filled = pl.pallas_call(
        functools.partial(early_kernel, peers),
        out_shape=inner,
        in_specs=[VMEM] * 8,
        out_specs=(VMEM,) * 6,
        scratch_shapes=inner_scratch,
        compiler_params=params(16),
        name="inner_early",
    )(*inner_args)
    to_core, to_chip = pl.pallas_call(
        functools.partial(column_kernel, peers),
        out_shape=(sds(Y_ROWS, NZ), sds(Y_ROWS, NZ)),
        in_specs=[VMEM] * 8,
        out_specs=(VMEM,) * 2,
        compiler_params=params(16),
        name="columns",
    )(own, rp, ro, rd, re, band, rf_pair, filled[5])
    from_chip = send(to_chip, chip_other(*peers))
    from_core = send(to_core, core_partner)
    *work_in, rf_third = pl.pallas_call(
        functools.partial(late_kernel, peers),
        out_shape=inner,
        in_specs=[VMEM] * 14,
        out_specs=(VMEM,) * 6,
        scratch_shapes=inner_scratch,
        input_output_aliases={8 + k: k for k in range(6)},
        compiler_params=params(16),
        cost_estimate=pl.CostEstimate(flops=4 * 10**9, bytes_accessed=2**21, transcendentals=0),
        name="inner_late",
    )(*inner_args, *filled)
    side_scratch = fields + [
        pltpu.VMEM((3, 8, 8, NZ), f32),
        pltpu.VMEM((24, NZ), f32),
        pltpu.VMEM((2 * NZ, SLOTS), bf16),
    ]
    half, *work_in = pl.pallas_call(
        core_kernel,
        out_shape=(sds(125, NZ),) + work,
        in_specs=[VMEM] * 11,
        out_specs=(VMEM,) * 6,
        scratch_shapes=side_scratch,
        input_output_aliases={6 + k: 1 + k for k in range(5)},
        compiler_params=params(16),
        cost_estimate=pl.CostEstimate(flops=2 * 10**9, bytes_accessed=2**20, transcendentals=0),
        name="core_side",
    )(from_core, f2, ft2, rf_pair, rf_third, collect, *work_in)
    result, *_ = pl.pallas_call(
        functools.partial(main_kernel, peers),
        out_shape=(sds(125, 1, 256),) + work,
        in_specs=[VMEM] * 12,
        out_specs=(VMEM,) * 6,
        scratch_shapes=side_scratch,
        input_output_aliases={7 + k: 1 + k for k in range(5)},
        compiler_params=params(16),
        name="chip_side",
    )(from_chip, f2, ft2, rf_pair, rf_third, collect, half, *work_in)
    return result


def solution(mesh):
    placed = (
        P(None, "gx", "gy"),
        P("gx", "gy"),
        P("gx", "gy", None),
        P("gx", "gy"),
        P("gx", "gy", None),
    )
    return jax.shard_map(
        per_device, mesh=mesh, in_specs=placed, out_specs=P(None, "gx", "gy"), check_vma=False
    )
```

```python
import functools

import jax
import jax.numpy as jnp
from jax import lax
from jax.experimental import pallas as pl
from jax.experimental.pallas import tpu as pltpu
from jax.sharding import PartitionSpec as P

NZ = 128
CY = 8
SLOTS = 512

FORWARD = (
    (0, 0, 1),
    (0, 1, -1),
    (0, 1, 0),
    (0, 1, 1),
    (1, -1, -1),
    (1, -1, 0),
    (1, -1, 1),
    (1, 0, -1),
    (1, 0, 0),
    (1, 0, 1),
    (1, 1, -1),
    (1, 1, 0),
    (1, 1, 1),
)
OFFSET = {step: k for k, step in enumerate(FORWARD)}
damping = 2.0 / 3.0

ROWS = 24
PER = 14
COLBLOCK = 93
THIRD = 2 * COLBLOCK
FAULT_ROW = 225
BAND_ROW, SUM_ROW, Y_ROWS = 237, 254, 280
REACH = 8
DIAGONALS = 2 * REACH + 1

f32 = jnp.float32
bf16 = jnp.bfloat16


def dot_nt(a, b):
    return lax.dot_general(a, b, (((1,), (1,)), ((), ())), preferred_element_type=f32)


def dot_nn(a, b):
    return lax.dot_general(a, b, (((1,), (0,)), ((), ())), preferred_element_type=f32)


def split(value):
    high = value.astype(bf16)
    return high, (value - high.astype(f32)).astype(bf16)


def pack_kernel(peers, *refs):
    sources, (block, plane), targets, sems = refs[:4], refs[4:6], refs[6:10], refs[10]
    copies = [
        pltpu.make_async_copy(src, dst, sems.at[k])
        for k, (src, dst) in enumerate(zip(sources, targets))
    ]
    for copy in copies:
        copy.start()
    for copy in copies:
        copy.wait()
    trans, storage, cells, ftrans = targets
    last_x = lax.axis_index("gx") == peers[0] - 1
    first_y = lax.axis_index("gy") == 0
    last_y = lax.axis_index("gy") == peers[1] - 1
    depth = lax.broadcasted_iota(jnp.int32, (8, NZ), 1)
    row = lax.broadcasted_iota(jnp.int32, (8, NZ), 0)
    for x in range(2):
        for o in range(PER):
            base = (x * PER + o) * 8
            for y in range(CY):
                lanes = slice(y * NZ, (y + 1) * NZ)
                if o < 13:
                    value = trans[o, x : x + 1, lanes]
                else:
                    value = storage[x : x + 1, lanes]
                block[base + y : base + y + 1, :] = value
            if o == 13:
                continue
            step = FORWARD[o]
            keep = None
            if step[2] == 1:
                keep = depth < NZ - 1
            if step[2] == -1:
                keep = depth > 0
            if step[1] == 1:
                inside = (row < CY - 1) | jnp.logical_not(last_y)
                keep = inside if keep is None else keep & inside
            if step[1] == -1:
                inside = (row > 0) | jnp.logical_not(first_y)
                keep = inside if keep is None else keep & inside
            if step[0] == 1 and x == 1:
                inside = (row >= 0) & jnp.logical_not(last_x)
                keep = inside if keep is None else keep & inside
            if keep is not None:
                block[base : base + 8, :] = jnp.where(keep, block[base : base + 8, :], 0.0)
    for r in range(4):
        lanes = slice(r * NZ, (r + 1) * NZ)
        at = 2 * PER * 8 + r
        block[at : at + 1, :] = cells[0, :, lanes].astype(f32)
        block[at + 4 : at + 5, :] = ftrans[0, :, lanes]
    plane[0:72, :] = block[(PER + 4) * 8 : (PER + 13) * 8, :]
    plane[72:80, :] = block[224:232, :]


def live_kernel(count, own, own_out):
    own_out[0:228, :] = own[0:228, :]
    slot = lax.broadcasted_iota(jnp.int32, (4, NZ), 0) * NZ
    slot = slot + lax.broadcasted_iota(jnp.int32, (4, NZ), 1)
    own_out[228:232, :] = jnp.where(slot < count[0, 0], own[228:232, :], 0.0)


def by_parity(axis, body):
    odd = lax.rem(lax.axis_index(axis), 2)
    for k in range(2):
        pl.when(odd == k)(functools.partial(body, k))


class Masked:
    def __init__(self, ref, due):
        self.ref, self.due = ref, due

    def __getitem__(self, index):
        return jnp.where(self.due, self.ref[index], 0.0)


class Behind:
    def __init__(self, rd, re):
        self.refs, self.at = (rd, re), lax.axis_index("gx")

    def __getitem__(self, index):
        even, odd = (ref[index] for ref in self.refs)
        value = jnp.where(lax.rem(self.at, 2) == 0, even, odd)
        return jnp.where(self.at >= 2, value, 0.0)


def has_other(axis, peers):
    at = lax.axis_index(axis)
    return jnp.where(lax.rem(at, 2) == 0, at > 0, at < peers - 1)


def column_kernel(peers, own, rp, ro, rd, re, band, sums, after, to_core, to_chip):
    del after
    ro = Masked(ro, has_other("gx", peers[0]))
    lo2 = Behind(rd, re)

    def fill(out, lo, hi, first, third, runs):
        for c in range(2):
            y = first + c
            base = c * COLBLOCK
            out[base : base + 9, :] = lo2[pl.ds(y, 9, stride=8), :]
            for k, ref in enumerate((lo, own, hi)):
                start = base + 9 + 28 * k
                out[start : start + 28, :] = ref[pl.ds(y, 28, stride=8), :]
        at = THIRD
        out[at : at + 3, :] = lo2[pl.ds((runs[-1] - 4) * 8 + third, 3, stride=8), :]
        at += 3
        for ref in (lo, own, hi):
            for x in range(2):
                for o in runs:
                    out[at : at + 3, :] = ref[pl.ds((x * PER + o) * 8 + third, 3, stride=8), :]
                    at += 3
        for k, rows in enumerate((ro[224:228, :], rd[72:76, :], ro[228:232, :])):
            out[FAULT_ROW + 4 * k : FAULT_ROW + 4 * k + 4, :] = rows
        out[BAND_ROW : BAND_ROW + DIAGONALS, :] = band[int(first > 0), 0:DIAGONALS, :]
        for c in range(2):
            for k in range(2):
                at = SUM_ROW + (2 * c + k) * 6
                out[at : at + 6, :] = sums[k, first + c, 0:6, :]
        out[SUM_ROW + 24 : Y_ROWS, :] = jnp.zeros((Y_ROWS - SUM_ROW - 24, NZ), f32)

    def for_x(odd_x):
        lo, hi = (rp, ro) if odd_x else (ro, rp)

        def for_y(odd_y):
            up, down = (to_chip, to_core) if odd_y else (to_core, to_chip)
            fill(up, lo, hi, CY - 2, CY - 3, (1, 10))
            fill(down, lo, hi, 0, 2, (4,))

        by_parity("gy", for_y)

    by_parity("gx", for_x)


def colour(z):
    half = z >> 1
    return half - 5 * ((half * 205) >> 10)


def slot_columns(rows):
    tall = jnp.transpose(jnp.concatenate(rows, axis=0))
    return [[tall[:, 4 * k + r : 4 * k + r + 1] for r in range(4)] for k in range(len(rows))]


def flat_cells(rows):
    row = jnp.concatenate([rows[r : r + 1] for r in range(4)], axis=1)
    return row.astype(jnp.int32) & 1023


def fill_far(far2, partner, live):
    lane = lax.broadcasted_iota(jnp.int32, (NZ, NZ), 1)
    for r in range(4):
        rows = slice(r * NZ, (r + 1) * NZ)
        match = (partner[r].astype(jnp.int32) & 127) == lane
        high = live[r].astype(bf16).astype(f32)
        far2[rows, 0:NZ] = jnp.where(match, high, 0.0).astype(bf16)
        far2[rows, NZ : 2 * NZ] = jnp.where(match, live[r] - high, 0.0).astype(bf16)


def flat_rows(rows):
    return jnp.concatenate([rows[r : r + 1] for r in range(4)], axis=1)


def colour_sums(hot, beyond, live):
    e16 = lax.broadcasted_iota(jnp.int32, (16, SLOTS), 0)
    tint = colour(flat_rows(beyond).astype(jnp.int32) & 127)
    live = flat_rows(live)
    high = live.astype(bf16).astype(f32)
    value = jnp.where((e16 == tint) | (e16 == 5), high, 0.0)
    value = jnp.where((e16 == tint + 8) | (e16 == 13), live - high, value)
    got = dot_nt(value.astype(bf16), hot)
    return got[:8] + got[8:]


def diagonals(hot, own, far, live):
    d24 = lax.broadcasted_iota(jnp.int32, (24, SLOTS), 0)
    step = (flat_rows(far).astype(jnp.int32) & 127) - (flat_rows(own).astype(jnp.int32) & 127)
    live = flat_rows(live)
    high = live.astype(bf16).astype(f32)
    match = step + REACH == d24
    both = [jnp.where(match, value, 0.0) for value in (high, live - high)]
    got = dot_nt(jnp.concatenate(both, axis=0).astype(bf16), hot)
    return got[:24] + got[24:]


def fill_hot(hot, cells, columns):
    z128 = lax.broadcasted_iota(jnp.int32, (NZ, SLOTS), 0)
    for k, y in enumerate(columns):
        value = jnp.where(cells == z128 + y * NZ, 1.0, 0.0)
        hot[k * NZ : (k + 1) * NZ, :] = value.astype(bf16)


def pair_matrix(both):
    z8 = lax.broadcasted_iota(jnp.int32, (8, NZ), 1)
    e8 = lax.broadcasted_iota(jnp.int32, (8, NZ), 0)
    one = jnp.where((e8 == colour(z8)) | (e8 == 5), 1.0, 0.0).astype(bf16)
    one2 = jnp.concatenate([one, one], axis=1)
    matrix = both[:, :NZ] + both[:, NZ:]
    f2 = jnp.concatenate(split(matrix), axis=0)
    ft2 = jnp.concatenate(split(jnp.transpose(matrix)), axis=0)
    return f2, ft2, dot_nn(one2, ft2), dot_nn(one2, f2)


def fill_collect(collect):
    kz = lax.broadcasted_iota(jnp.int32, (512, NZ), 0)
    kout = lax.broadcasted_iota(jnp.int32, (512, NZ), 1)
    z_in = kz & 127
    is_oth = ((kz >> 7) & 1) == 1
    target = jnp.where(
        is_oth, (z_in >> 1) + jnp.where((z_in & 1) == 0, -1, 1), z_in >> 1
    )
    fits = (target == (kout & 63)) & ((kz >> 8) == (kout >> 6))
    collect[...] = jnp.where(fits, 1.0, 0.0).astype(bf16)


def fault_kernel(own, rp, f2, ft2, rf, band, collect, far2, hot, both):
    fill_collect(collect)
    partner, live = slot_columns([rp[224:228, :], own[228:232, :]])
    fill_far(far2, partner, live)
    fill_hot(hot, flat_cells(own[224:228, :]), range(CY))
    both[...] = dot_nn(hot[...], far2[...])
    for y in range(CY):
        f2[y], ft2[y], rf[0, y], rf[1, y] = pair_matrix(both[y * NZ : (y + 1) * NZ, :])
    for k, y in enumerate((0, CY - 1)):
        band[k] = diagonals(
            hot[y * NZ : (y + 1) * NZ, :], own[224:228, :], rp[224:228, :], own[228:232, :]
        )


def through(value, matrix2):
    rows = value.shape[0]
    high, low = split(value)
    left = jnp.concatenate(
        [jnp.concatenate([high, high], axis=1), jnp.concatenate([low, low], axis=1)], axis=0
    )
    got = dot_nn(left, matrix2)
    return got[:rows] + got[rows:]


class Place:
    def __init__(self):
        self.gx = lax.axis_index("gx")
        self.gy = lax.axis_index("gy")
        par = lax.rem(self.gx, 2)
        even = par == 0
        self.sgn = 1 - 2 * par
        self.p_own = jnp.where(even, 3, 2)
        self.p_far = jnp.where(even, 4, 1)
        self.p_third = jnp.where(even, 0, 5)
        self.p_fault = (self.p_own, self.p_far, self.p_third)
        self.x_coarse = lax.rem(self.gx, 5) + 5

    def a_of(self, d):
        return lax.rem(self.x_coarse + d, 5)

    def b_of(self, coarse_y, d):
        return lax.rem(self.gy * (CY // 2) + coarse_y + d + 5, 5)


def roll_weights(w, wr, first, count):
    for p in range(7):
        for o, step in enumerate(FORWARD):
            if step[2] == 0 or (p == 0 and o < 4):
                continue
            at = (p * PER + o) * ROWS + first
            distance = 1 if step[2] == 1 else NZ - 1
            wr[at : at + count, :] = pltpu.roll(w[at : at + count, :], distance, 1)


def smooth(w, wr, fd, qc, inv, diag, first, count):
    even_y = (lax.broadcasted_iota(jnp.int32, (count, NZ), 0) & 1) == 0
    even_z = (lax.broadcasted_iota(jnp.int32, (count, NZ), 1) & 1) == 0
    for p in range(6):
        base = p + 1

        def weight(dx, dy, dz):
            if (dx, dy, dz) in OFFSET:
                start = (base * PER + OFFSET[dx, dy, dz]) * ROWS + 1 + first
                return w[start : start + count, :]
            o = OFFSET[-dx, -dy, -dz]
            start = ((base + dx) * PER + o) * ROWS + 1 + first + dy
            return (w if dz == 0 else wr)[start : start + count, :]

        near = 1 if p % 2 == 0 else -1
        sums = {}
        for dz in (-1, 0, 1):
            got = {}
            for dx in (-1, 0, 1):
                below, above = weight(dx, -1, dz), weight(dx, 1, dz)
                got[dx, 0] = jnp.where(even_y, above, below)
                if (dx, dz) != (0, 0):
                    got[dx, 0] = got[dx, 0] + weight(dx, 0, dz)
                got[dx, 1] = jnp.where(even_y, below, above)
            for sy in range(2):
                sums[0, sy, dz] = got[0, sy] + got[near, sy]
                sums[1, sy, dz] = got[-near, sy]
        start = (base * PER + 13) * ROWS + 1 + first
        at = p * 16 + first
        total = w[start : start + count, :] + fd[at : at + count, :]
        r = []
        for sx in range(2):
            for sy in range(2):
                down, same, up = (sums[sx, sy, dz] for dz in (-1, 0, 1))
                r.append(same + jnp.where(even_z, up, down))
                r.append(jnp.where(even_z, down, up))
        for value in r:
            total = total + value
        total = jnp.where(total == 0.0, 1.0, total)
        scale = damping / total
        diag[at : at + count, :] = total
        inv[at : at + count, :] = scale
        for k, value in enumerate(r):
            value = value * scale
            if k == 0:
                value = value + (1.0 - damping)
            at = (p * 8 + k) * 16 + first
            qc[at : at + count, :] = value


def spread(here, qc, inv, qe, rf_at, columns):
    z8 = lax.broadcasted_iota(jnp.int32, (8, NZ), 1)
    e8 = lax.broadcasted_iota(jnp.int32, (8, NZ), 0)
    beside = jnp.where((z8 & 1) == 0, z8 - 1, z8 + 1)
    mask_own = jnp.where(e8 == colour(z8), 1.0, 0.0)
    mask_oth = jnp.where(e8 == colour(beside + 10), 1.0, 0.0)
    rows5 = jnp.where(e8 < 5, 1.0, 0.0)

    for c in columns:
        for p in range(6):
            for lat in range(4):
                at = (p * 8 + 2 * lat) * 16 + c
                qe[p, c, lat] = qc[at : at + 1, :] * mask_own + qc[at + 16 : at + 17, :] * mask_oth
        for k, plane in enumerate(here.p_fault):
            qe[plane, c, 2] = qe[plane, c, 2] + rf_at(k, c) * (
                inv[pl.ds(plane * 16 + c, 1), :] * rows5
            )


def apply_column(w, wr, diag, qe, ap, p, y):
    odd_x, odd_y = p % 2, y % 2
    acc = {}
    for dx in (-1, 0, 1):
        for dy in (-1, 0, 1):
            q = [qe[p + dx, y + dy, lat] for lat in range(4)]
            own_x = dx if (dx == 1 and odd_x) or (dx == -1 and not odd_x) else 0
            own_y = dy if (dy == 1 and odd_y) or (dy == -1 and not odd_y) else 0
            oth_x = own_x + (1 if (odd_x + dx) % 2 else -1)
            oth_y = own_y + (1 if (odd_y + dy) % 2 else -1)
            for dz in (-1, 0, 1):
                if (dx, dy, dz) == (0, 0, 0):
                    continue
                if (dx, dy, dz) in OFFSET:
                    at = ((p + 1) * PER + OFFSET[dx, dy, dz]) * ROWS + y + 1
                    ref = w if dz == 0 else wr
                else:
                    at = ((p + 1 + dx) * PER + OFFSET[-dx, -dy, -dz]) * ROWS + y + 1 + dy
                    ref = w
                wt = ref[at : at + 1, :]
                for lat in range(4):
                    lx = oth_x if lat >= 2 else own_x
                    ly = oth_y if lat % 2 else own_y
                    value = wt * q[lat]
                    key = (lx, ly, dz)
                    acc[key] = acc[key] + value if key in acc else value
    centre = diag[p * 16 + y : p * 16 + y + 1, :]
    for lx in (-1, 0, 1):
        for ly in (-1, 0, 1):
            total = acc[lx, ly, 0]
            total = total + pltpu.roll(acc[lx, ly, 1], NZ - 1, 1)
            total = total + pltpu.roll(acc[lx, ly, -1], 1, 1)
            own_lat = None
            sx = {0: 0, (1 if odd_x else -1): 1}.get(lx)
            sy = {0: 0, (1 if odd_y else -1): 1}.get(ly)
            if sx is not None and sy is not None:
                own_lat = 2 * sx + sy
            if own_lat is None:
                total = -total
            else:
                total = centre * qe[p, y, own_lat] - total
            ap[p - 1, y - 1, lx + 1, ly + 1] = total


def fault_apply(here, qe, ap, c, f2c, ft2c):
    ly_oth = 2 * (c % 2)
    for plane, source, x_own, matrix in (
        (here.p_own, here.p_far, 1 + here.sgn, ft2c),
        (here.p_far, here.p_own, 1 - here.sgn, f2c),
    ):
        total = through(qe[source, c].reshape(32, NZ), matrix)
        for lat in range(4):
            lx = 1 if lat >= 2 else x_own
            ly = ly_oth if lat % 2 else 1
            ap[plane - 1, c - 1, lx, ly] = ap[plane - 1, c - 1, lx, ly] - total[8 * lat : 8 * lat + 8]


def fault_apply_band(here, qe, ap, c, band):
    ly_oth = 2 * (c % 2)
    to_own, to_far = [0.0] * 4, [0.0] * 4
    for d in range(DIAGONALS):
        weight = band[d : d + 1, :]
        for lat in range(4):
            ahead = pltpu.roll(qe[here.p_far, c, lat], (REACH - d) % NZ, 1)
            to_own[lat] = to_own[lat] + weight * ahead
            back = weight * qe[here.p_own, c, lat]
            to_far[lat] = to_far[lat] + pltpu.roll(back, (d - REACH) % NZ, 1)
    for plane, x_own, total in (
        (here.p_own, 1 + here.sgn, to_own),
        (here.p_far, 1 - here.sgn, to_far),
    ):
        for lat in range(4):
            lx = 1 if lat >= 2 else x_own
            ly = ly_oth if lat % 2 else 1
            ap[plane - 1, c - 1, lx, ly] = ap[plane - 1, c - 1, lx, ly] - total[lat]


def gather(here, qc, ap, tt, coarse_y, rows, add):
    shift = (-1, 0, 0, 1)
    for zk in range(2):
        acc = {}
        for x in range(-1, 3):
            for y in rows:
                lat = 2 * (x not in (0, 1)) + (y not in (0, 1))
                c = 2 * coarse_y + y + 2
                at = ((x + 2) * 8 + 2 * lat + zk) * 16 + c
                q = qc[at : at + 1, :]
                for lx in range(3):
                    for ly in range(3):
                        value = q * ap[x + 1, c - 1, lx, ly]
                        key = (shift[x + 1] + lx - 1, shift[y + 1] + ly - 1)
                        acc[key] = acc[key] + value if key in acc else value
        lane = (coarse_y % 2) * 256 + zk * NZ
        for (dx, dy), value in acc.items():
            at = (coarse_y // 2, here.a_of(dx), here.b_of(coarse_y, dy), slice(None), slice(lane, lane + NZ))
            tt[at] = tt[at] + value if add else value


def gather_fault(here, inv, ap, tt, y, ft2c):
    c = y + 2
    coarse_y = y // 2
    lane = (coarse_y % 2) * 256
    value = ap[here.p_far - 1, c - 1].reshape(72, NZ) * inv[pl.ds(here.p_far * 16 + c, 1), :]
    total = through(value, ft2c)
    for lx in range(3):
        a = here.a_of(lx - 1 + here.sgn)
        for ly in range(3):
            at = (coarse_y // 2, a, here.b_of(coarse_y, ly - 1), slice(None), slice(lane, lane + NZ))
            row = 8 * (3 * lx + ly)
            tt[at] = tt[at] + total[row : row + 8]


INNER = (2, 3, 4, 5)


def rows_of(coarse_y, inner):
    return [y for y in range(-1, 3) if (2 * coarse_y + y in INNER) == inner]


def has_time(peers):
    at = lax.axis_index("gx")
    return (lax.rem(lax.axis_index("gy"), 2) == 1) | (at == 0) | (at == peers[0] - 1)


def early_kernel(peers, *refs):
    pl.when(has_time(peers))(functools.partial(inner_part, peers, *refs))


def late_kernel(peers, *refs):
    refs = refs[:8] + refs[14:]
    pl.when(jnp.logical_not(has_time(peers)))(functools.partial(inner_part, peers, *refs))


def inner_part(
    peers, own, rp, ro, rd, re, f2, ft2, rf_pair, w, wr, qe, ap, tt, rf_third, qc, inv, diag, fd, hot
):
    here = Place()
    ro = Masked(ro, has_other("gx", peers[0]))

    def place(ref, count, first):
        for k in range(count):
            base = (first + k) * ROWS
            w[base + 3 : base + 11, :] = ref[8 * k : 8 * k + 8, :]

    def place_x(odd):
        lo, hi = (rp, ro) if odd else (ro, rp)
        place(lo, 28, PER)
        place(hi, 28, 5 * PER)

    by_parity("gx", place_x)
    place(Behind(rd, re), 9, 4)
    place(own, 28, 3 * PER)

    fill_hot(hot, flat_cells(ro[224:228, :]), range(CY))
    got = colour_sums(hot[...], rd[72:76, :], ro[228:232, :])
    fd[...] = jnp.zeros_like(fd)
    for y in range(CY):
        rf_third[y] = got[:, y * NZ : (y + 1) * NZ]
        for plane, value in zip(here.p_fault, (rf_pair[0, y], rf_pair[1, y], rf_third[y])):
            fd[pl.ds(plane * 16 + y + 2, 1), :] = value[5:6, :]

    roll_weights(w, wr, 3, 8)
    smooth(w, wr, fd, qc, inv, diag, 2, 8)
    spread(
        here, qc, inv, qe, lambda k, c: rf_third[c - 2] if k == 2 else rf_pair[k, c - 2], range(3, 9)
    )
    for p in range(1, 5):
        for y in INNER:
            apply_column(w, wr, diag, qe, ap, p, y + 2)
    for y in INNER:
        fault_apply(here, qe, ap, y + 2, f2[y], ft2[y])
    tt[...] = jnp.zeros_like(tt)
    for coarse_y in range(CY // 2):
        gather(here, qc, ap, tt, coarse_y, rows_of(coarse_y, True), False)
    for y in INNER:
        gather_fault(here, inv, ap, tt, y, ft2[y])


def side(high, halo, f2, ft2, rf_pair, rf_third, work, fields, rf, band, hot):
    here = Place()
    w, wr, qe, ap, tt = work
    qc, inv, diag, fd = fields
    first = 6 if high else 0
    columns = (10, 11) if high else (0, 1)
    row, third, runs = (11, 13, (4,)) if high else (1, 0, (1, 10))

    for c in range(2):
        base = c * COLBLOCK
        w[pl.ds(4 * ROWS + row + c, 9, stride=ROWS), :] = halo[base : base + 9, :]
        w[pl.ds(PER * ROWS + row + c, 84, stride=ROWS), :] = halo[base + 9 : base + 93, :]
    at = THIRD
    for plane in range(7):
        for o in runs[-1:] if plane == 0 else runs:
            start = (plane * PER + o) * ROWS + third
            w[pl.ds(start, 3, stride=ROWS), :] = halo[at : at + 3, :]
            at += 3
    roll_weights(w, wr, 8 if high else 0, 8)

    fd[...] = jnp.zeros_like(fd)

    def put(column, k, value):
        rf[k, column - first] = value
        fd[pl.ds(here.p_fault[k] * 16 + column, 1), :] = value[5:6, :]

    own = (6, 7) if high else (0, 1)
    for y in own:
        put(y + 2, 0, rf_pair[0, y])
        put(y + 2, 1, rf_pair[1, y])
        put(y + 2, 2, rf_third[y])
    band[0:DIAGONALS, :] = halo[BAND_ROW : BAND_ROW + DIAGONALS, :]
    lists = halo[FAULT_ROW : FAULT_ROW + 12, :]
    fill_hot(hot, flat_cells(lists[0:4]), (0, 1) if high else (CY - 2, CY - 1))
    got = colour_sums(hot[...], lists[4:8], lists[8:12])
    for c, column in enumerate(columns):
        for k in range(2):
            at = SUM_ROW + (2 * c + k) * 6
            value = halo[at : at + 6, :]
            put(column, k, jnp.concatenate([value, jnp.zeros((2, NZ), f32)], axis=0))
        put(column, 2, got[:, c * NZ : (c + 1) * NZ])

    smooth(w, wr, fd, qc, inv, diag, first, 8)
    spread(
        here, qc, inv, qe, lambda k, c: rf[k, c - first], (9, 10, 11) if high else (0, 1, 2)
    )
    for p in range(1, 5):
        for y in (8, 9, 10) if high else (1, 2, 3):
            apply_column(w, wr, diag, qe, ap, p, y)
    for y in own:
        fault_apply(here, qe, ap, y + 2, f2[y], ft2[y])
    fault_apply_band(here, qe, ap, 10 if high else 1, band)
    parts = ((3, (0, 1, 2)), (2, (2,))) if high else ((0, (-1, 0, 1)), (1, (-1,)))
    for coarse_y, rows in parts:
        gather(here, qc, ap, tt, coarse_y, rows, True)
    for y in own:
        gather_fault(here, inv, ap, tt, y, ft2[y])


def finish(tt, pair, collect, store):
    high, low = split(tt[pair].reshape(200, 512))
    got = (dot_nn(high, collect[...]) + dot_nn(low, collect[...])) * 0.125
    for k in range(25):
        store(5 * k, got[8 * k : 8 * k + 5])


def core_kernel(halo, f2, ft2, rf_pair, rf_third, collect, *refs):
    half, work, fields, rest = refs[5], refs[6:11], refs[11:15], refs[15:]

    def body(odd):
        side(not odd, halo, f2, ft2, rf_pair, rf_third, work, fields, *rest)

        def store(row, value):
            half[row : row + 5, :] = value

        finish(work[4], 0 if odd else 1, collect, store)

    by_parity("gy", body)


def main_kernel(peers, halo, f2, ft2, rf_pair, rf_third, collect, half, *refs):
    out, work, fields, rest = refs[5], refs[6:11], refs[11:15], refs[15:]
    halo = Masked(halo, has_other("gy", peers[1]))

    def body(odd):
        side(odd, halo, f2, ft2, rf_pair, rf_third, work, fields, *rest)
        lanes = [slice(0, NZ), slice(NZ, 2 * NZ)]

        def store(row, value):
            out[row : row + 5, 0, lanes[odd]] = value
            out[row : row + 5, 0, lanes[1 - odd]] = half[row : row + 5, :]

        finish(work[4], odd, collect, store)

    by_parity("gy", body)


def send(value, target):
    size_x, size_y = lax.axis_size("gx"), lax.axis_size("gy")
    pairs = []
    for x in range(size_x):
        for y in range(size_y):
            to_x, to_y = target(x, y)
            pairs.append((x * size_y + y, to_x * size_y + to_y))
    return lax.ppermute(value, ("gx", "gy"), pairs)


def x_partner(x, y):
    return x ^ 1, y


def core_partner(x, y):
    return x, y ^ 1


def x_other(size_x):
    def target(x, y):
        other = x + 1 if x % 2 else x - 1
        return (other, y) if 0 <= other < size_x else core_partner(x, y)

    return target


def chip_other(size_x, size_y):
    def target(x, y):
        other = y + 1 if y % 2 else y - 1
        if 0 <= other < size_y:
            return x, other
        beside = x + 1 if x % 2 else x - 1
        return (beside, y) if 0 <= beside < size_x else (x, size_y - 1 - y)

    return target


def x_two(size_x, up):
    def target(x, y):
        other = x + 2 if x % 2 == up else x - 2
        return (other, y) if 0 <= other < size_x else x_partner(x, y)

    return target


VMEM = pl.BlockSpec(memory_space=pltpu.VMEM)
HBM = pl.BlockSpec(memory_space=pltpu.HBM)


def params(mib):
    return pltpu.CompilerParams(vmem_limit_bytes=mib * 1024 * 1024)


def sds(*shape, dtype=f32):
    return jax.ShapeDtypeStruct(shape, dtype)


def per_device(trans, storage, fault_cells, fault_count, fault_trans):
    peers = (lax.axis_size("gx"), lax.axis_size("gy"))
    sources = [
        pltpu.with_memory_space_constraint(array, pltpu.HBM)
        for array in (trans, storage, fault_cells, fault_trans)
    ]
    own, plane = pl.pallas_call(
        functools.partial(pack_kernel, peers),
        out_shape=(sds(232, NZ), sds(80, NZ)),
        in_specs=[HBM] * 4,
        out_specs=(VMEM,) * 2,
        scratch_shapes=[pltpu.VMEM(array.shape, array.dtype) for array in sources]
        + [pltpu.SemaphoreType.DMA((4,))],
        compiler_params=params(16),
        name="pack",
    )(*sources)
    rp = send(own, x_partner)
    rd = send(plane, x_two(peers[0], 0))
    re = send(plane, x_two(peers[0], 1))
    live = pl.pallas_call(
        live_kernel,
        out_shape=sds(232, NZ),
        in_specs=[pl.BlockSpec(memory_space=pltpu.SMEM), VMEM],
        out_specs=VMEM,
        compiler_params=params(16),
        name="live",
    )(fault_count, own)
    ro = send(live, x_other(peers[0]))
    pieces = sds(CY, 2 * NZ, NZ, dtype=bf16)
    f2, ft2, rf_pair, band, collect = pl.pallas_call(
        fault_kernel,
        out_shape=(
            pieces,
            pieces,
            sds(2, CY, 8, NZ),
            sds(2, 24, NZ),
            sds(512, NZ, dtype=bf16),
        ),
        in_specs=[VMEM] * 2,
        out_specs=(VMEM,) * 5,
        scratch_shapes=[
            pltpu.VMEM((SLOTS, 2 * NZ), bf16),
            pltpu.VMEM((CY * NZ, SLOTS), bf16),
            pltpu.VMEM((CY * NZ, 2 * NZ), f32),
        ],
        compiler_params=params(16),
        cost_estimate=pl.CostEstimate(flops=2 * 10**9, bytes_accessed=2**21, transcendentals=0),
        name="faults",
    )(live, rp)
    work = (
        sds(7 * PER * ROWS, NZ),
        sds(7 * PER * ROWS, NZ),
        sds(6, 12, 4, 8, NZ),
        sds(4, 10, 3, 3, 8, NZ),
        sds(2, 5, 5, 8, 512),
    )
    inner = work + (sds(CY, 8, NZ),)
    fields = [
        pltpu.VMEM((6 * 8 * 16, NZ), f32),
        pltpu.VMEM((6 * 16, NZ), f32),
        pltpu.VMEM((6 * 16, NZ), f32),
        pltpu.VMEM((6 * 16, NZ), f32),
    ]
    inner_args = (own, rp, ro, rd, re, f2, ft2, rf_pair)
    inner_scratch = fields + [pltpu.VMEM((CY * NZ, SLOTS), bf16)]
    filled = pl.pallas_call(
        functools.partial(early_kernel, peers),
        out_shape=inner,
        in_specs=[VMEM] * 8,
        out_specs=(VMEM,) * 6,
        scratch_shapes=inner_scratch,
        compiler_params=params(16),
        name="inner_early",
    )(*inner_args)
    to_core, to_chip = pl.pallas_call(
        functools.partial(column_kernel, peers),
        out_shape=(sds(Y_ROWS, NZ), sds(Y_ROWS, NZ)),
        in_specs=[VMEM] * 8,
        out_specs=(VMEM,) * 2,
        compiler_params=params(16),
        name="columns",
    )(own, rp, ro, rd, re, band, rf_pair, filled[5])
    from_chip = send(to_chip, chip_other(*peers))
    from_core = send(to_core, core_partner)
    *work_in, rf_third = pl.pallas_call(
        functools.partial(late_kernel, peers),
        out_shape=inner,
        in_specs=[VMEM] * 14,
        out_specs=(VMEM,) * 6,
        scratch_shapes=inner_scratch,
        input_output_aliases={8 + k: k for k in range(6)},
        compiler_params=params(16),
        cost_estimate=pl.CostEstimate(flops=4 * 10**9, bytes_accessed=2**21, transcendentals=0),
        name="inner_late",
    )(*inner_args, *filled)
    side_scratch = fields + [
        pltpu.VMEM((3, 8, 8, NZ), f32),
        pltpu.VMEM((24, NZ), f32),
        pltpu.VMEM((2 * NZ, SLOTS), bf16),
    ]
    half, *work_in = pl.pallas_call(
        core_kernel,
        out_shape=(sds(125, NZ),) + work,
        in_specs=[VMEM] * 11,
        out_specs=(VMEM,) * 6,
        scratch_shapes=side_scratch,
        input_output_aliases={6 + k: 1 + k for k in range(5)},
        compiler_params=params(16),
        cost_estimate=pl.CostEstimate(flops=2 * 10**9, bytes_accessed=2**20, transcendentals=0),
        name="core_side",
    )(from_core, f2, ft2, rf_pair, rf_third, collect, *work_in)
    result, *_ = pl.pallas_call(
        functools.partial(main_kernel, peers),
        out_shape=(sds(125, 1, 256),) + work,
        in_specs=[VMEM] * 12,
        out_specs=(VMEM,) * 6,
        scratch_shapes=side_scratch,
        input_output_aliases={7 + k: 1 + k for k in range(5)},
        compiler_params=params(16),
        name="chip_side",
    )(from_chip, f2, ft2, rf_pair, rf_third, collect, half, *work_in)
    return result


def solution(mesh):
    placed = (
        P(None, "gx", "gy"),
        P("gx", "gy"),
        P("gx", "gy", None),
        P("gx", "gy"),
        P("gx", "gy", None),
    )
    return jax.shard_map(
        per_device, mesh=mesh, in_specs=placed, out_specs=P(None, "gx", "gy"), check_vma=False
    )
```
